32 devices in a mesh: dp: 2 (over x), rep: 16 (over z, y, core).
Axes of the slice: x: 2, y: 2, z: 4, core: 2. Of those that a mesh axis runs over, the one named last changes fastest.
Arguments:
- block_in: bfloat16 [160, 196, 768], P(('dp', 'rep')), may hold values from -6 to 6
- tissue: int32 [160, 196], P(('dp', 'rep')), may hold values from 0 to 1, as said below
- text_emb: bfloat16 [160, 512], P(('dp', 'rep')), may hold values from -6 to 6
- text_order: int32 [160], replicated, may hold values from 0 to 159, each once
- owner_list: int32 [77], replicated, may hold values from 0 to 15, as said below
- master: float32 [16, 8, 128, 768], P('rep', None, 'dp'), as said below
- first_moment: float32 [16, 8, 128, 768], P('rep', None, 'dp'), as said below
- second_moment: float32 [16, 8, 128, 768], P('rep', None, 'dp'), as said below
Outputs:
- block_out: bfloat16 [160, 196, 768], P(('dp', 'rep'))
- input_grad: float32 [160, 196, 768], P(('dp', 'rep'))
- new_master: float32 [16, 8, 128, 768], P('rep', None, 'dp')
- new_first: float32 [16, 8, 128, 768], P('rep', None, 'dp')
- new_second: float32 [16, 8, 128, 768], P('rep', None, 'dp')
The draws below stay inside these ranges and needn't reach their ends.
Inputs may be any that keep to these rules, and one draw needn't show every extreme that they name: owner_list[t] is the owner along rep of tile t of the weights' row view; no owner holds more than 8 tiles and some owner holds exactly 8. Every image has at least one twelfth of 196 tissue slots, rounded down, and never fewer than one; some image has all 196. `master`: slot s of owner r holds the tile that is the s-th of that owner's tiles in increasing tile order; slots that no tile takes hold values that are updated like the rest. `first_moment`: laid out as master. `second_moment`: laid out as master; positive.
All inputs are finite; a program needn't handle non-finite values.
Results may differ from the reference program's by a relative error of at most 0.011.
The reference program's roundings to bfloat16 on the way count: a program that leaves them out, or rounds other values in their place, can miss the bound.
Values may be sent and summed in bfloat16 or wider, within the bound.
No kernel may reach another device: no remote copies, remote signals or barrier semaphores. Data moves between devices by JAX's collectives and lax.ppermute only.
A program may use at most 192 MiB of HBM per device.

```python
import math
import jax
import jax.numpy as jnp
from jax import lax

D = 768
HEADS = 12
HEAD = 64
FF = 3072
EMB = 512
PATCHES = 196
IMG_DEV = 5
TR = 128
STEP = 10
IMAGES = 160
TILES = 77
SLOTS = 8
N_REP = 16


logit_scale = 50.0


def owner_table(key):
    key = jax.random.fold_in(key, 101)
    pick_key, rank_key, order_key = jax.random.split(key, 3)
    slot_total = N_REP * SLOTS
    crowded = jax.random.randint(pick_key, (), 0, N_REP)
    numbers = jnp.arange(slot_total, dtype=jnp.int32)
    priority = jax.random.permutation(rank_key, slot_total).astype(jnp.int32)
    priority = jnp.where(numbers // SLOTS == crowded, -1 - numbers, priority)
    chosen = jnp.argsort(priority, stable=True)[:TILES].astype(jnp.int32)
    owners = chosen // SLOTS
    return owners[jax.random.permutation(order_key, TILES)].astype(jnp.int32)


def slot_layout(key):
    owners = owner_table(key)
    earlier = jnp.tril(jnp.ones((TILES, TILES), jnp.int32), -1)
    same_owner = (owners[:, None] == owners[None, :]).astype(jnp.int32)
    placed = owners * SLOTS + jnp.sum(same_owner * earlier, axis=1)
    numbers = jnp.arange(N_REP * SLOTS, dtype=jnp.int32)
    hits = placed[None, :] == numbers[:, None]
    tile_of = jnp.sum(jnp.where(hits, jnp.arange(TILES, dtype=jnp.int32)[None, :], 0), axis=1)
    row_of = tile_of[:, None] * TR + jnp.arange(TR, dtype=jnp.int32)[None, :]
    used = jnp.any(hits, axis=1)
    return jnp.where(used[:, None], row_of, -1)


def grad_unit():
    return 0.5 * logit_scale / (EMB * math.sqrt(IMAGES))


def moment_scale(key):
    global_row = slot_layout(key)
    query_bias_row = 4 * D + 2 * FF + EMB + 4
    factor = jnp.where(global_row == query_bias_row, 0.125, 1.0)
    return (grad_unit() * factor).reshape(N_REP, SLOTS, TR, 1).astype(jnp.float32)


def draw_owner_list(key, part):
    return owner_table(key)


def draw_tissue(key, part):
    key = jax.random.fold_in(key, 11)
    count_key, slot_key, full_key = jax.random.split(key, 3)
    least = max(1, PATCHES // 12)
    counts = jax.random.randint(count_key, (IMAGES,), least, PATCHES + 1)
    fullest = jax.random.randint(full_key, (), 0, IMAGES)
    counts = jnp.where(jnp.arange(IMAGES) == fullest, PATCHES, counts)
    ranks = jax.vmap(lambda one_key: jax.random.permutation(one_key, PATCHES))(jax.random.split(slot_key, IMAGES))
    return (ranks < counts[:, None]).astype(jnp.int32)


def draw_master(key, part):
    global_row = slot_layout(key)
    key = jax.random.fold_in(key, 5)
    normal_key, gain_key = jax.random.split(key)
    full_shape = (N_REP * SLOTS, TR, D)
    noise = jax.random.normal(normal_key, full_shape, jnp.float32)
    wobble = jax.random.uniform(gain_key, full_shape, jnp.float32, minval=-1.0, maxval=1.0)
    vector_base = 4 * D + 2 * FF + EMB
    offset = global_row - vector_base
    row_scale = jnp.where(global_row < 3 * D, D ** (-0.5), jnp.where(global_row < 4 * D, 0.5 * math.sqrt(PATCHES) * D ** (-0.5), jnp.where(global_row < 4 * D + FF, D ** (-0.5), jnp.where(global_row < 4 * D + 2 * FF, FF ** (-0.5), jnp.where(global_row < vector_base, D ** (-0.5), 0.2)))))
    row_scale = jnp.where(global_row < 0, 0.05, row_scale)
    row_scale = jnp.where(offset >= 8 + FF // D, 0.05, row_scale)
    is_gain = (offset == 0) | (offset == 2)
    drawn = jnp.where(is_gain[..., None], 1.0 + 0.3 * wobble, row_scale[..., None].astype(jnp.float32) * noise)
    return drawn.reshape(N_REP, SLOTS, TR, D).astype(jnp.float32)


def draw_first_moment(key, part):
    unit = moment_scale(key)
    key = jax.random.fold_in(key, 7)
    sign_key, size_key = jax.random.split(key)
    full_shape = (N_REP, SLOTS, TR, D)
    signs = jnp.where(jax.random.bernoulli(sign_key, 0.5, full_shape), 1.0, -1.0)
    magnitude = jax.random.uniform(size_key, full_shape, jnp.float32, minval=0.5, maxval=2.0)
    return (signs * magnitude * (unit / 9.0)).astype(jnp.float32)


def draw_second_moment(key, part):
    unit = moment_scale(key)
    key = jax.random.fold_in(key, 13)
    level_key, size_key = jax.random.split(key)
    full_shape = (N_REP, SLOTS, TR, D)
    level = jnp.exp(jax.random.uniform(level_key, full_shape, jnp.float32, minval=0.0, maxval=math.log(4.0)))
    magnitude = jnp.exp(jax.random.uniform(size_key, full_shape, jnp.float32, minval=math.log(0.5), maxval=math.log(2.0)))
    scaled = unit * magnitude
    return (level * 0.001 * scaled * scaled).astype(jnp.float32)


def level_of(own_key, shape, cuts, low, top_value):
    loudness, own = 1.0, jax.random.fold_in(own_key, 6)
    for axis_at, blocks in cuts:
        heights = jnp.exp(jax.random.uniform(jax.random.fold_in(own, axis_at), (blocks,), jnp.float32, low / len(cuts), top_value / len(cuts)))
        loudness = loudness * jnp.repeat(heights, shape[axis_at] // blocks).reshape([-1 if axis == axis_at else 1 for axis in range(len(shape))])
    return loudness


def bell_draw(stream_key, dims, scale, most, cuts=(), held_as=jnp.bfloat16):
    loudness = level_of(stream_key, dims, cuts, -0.22, 0.18) if cuts else 1.0
    values = jax.random.normal(stream_key, dims, jnp.float32) * scale * loudness
    return jnp.minimum(jnp.maximum(values, -most), most).astype(held_as)


def setup_inputs(seed: int = 0) -> dict:
    splits = jax.random.split(jax.random.key(seed), 9)
    block_in = bell_draw(splits[0], (IMAGES, PATCHES, D), 1.0, 6.0, ((0, 32),))
    tissue = draw_tissue(jax.random.fold_in(splits[8], 71), 0)
    text_emb = bell_draw(splits[2], (IMAGES, EMB), 1.0, 6.0, ((0, 32),))
    text_order = jax.random.permutation(splits[3], IMAGES).astype(jnp.int32)
    owner_list = draw_owner_list(jax.random.fold_in(splits[8], 71), 0)
    master = draw_master(jax.random.fold_in(splits[8], 71), 0)
    first_moment = draw_first_moment(jax.random.fold_in(splits[8], 71), 0)
    second_moment = draw_second_moment(jax.random.fold_in(splits[8], 71), 0)
    return {"block_in": block_in, "tissue": tissue, "text_emb": text_emb, "text_order": text_order, "owner_list": owner_list, "master": master, "first_moment": first_moment, "second_moment": second_moment}


logit_scale = 50.0
learn_rate = 0.03
beta_one = 0.9
beta_two = 0.999
adam_eps = 1e-08
decay_rate = 0.05
norm_eps = 1e-05
unit_eps = 1e-06
highest = lax.Precision.HIGHEST

@jax.custom_vjp
def low(v):
    return lax.optimization_barrier(v.astype(jnp.bfloat16)).astype(jnp.float32)

@jax.custom_vjp
def low_back(v):
    return v

def low_keep(v):
    return (low(v), None)

def low_pass(kept, grad):
    return (grad,)

def back_keep(v):
    return (v, None)

def back_low(kept, grad):
    return (low(grad),)
low.defvjp(low_keep, low_pass)
low_back.defvjp(back_keep, back_low)

def rounded_both(tensor):
    return low(low_back(tensor))

def matmul_right(left_side, right_side):
    return jnp.einsum('...k,nk->...n', left_side, right_side, precision=highest)

def layer_norm(tensor, gain_row, shift_row):
    center = tensor - lax.optimization_barrier(jnp.mean(tensor, axis=-1, keepdims=True))
    spread = lax.optimization_barrier(jnp.mean(center * center, axis=-1, keepdims=True))
    return center * lax.rsqrt(spread + norm_eps) * gain_row + shift_row

def unit_rows(tensor):
    return tensor * lax.rsqrt(lax.optimization_barrier(jnp.sum(tensor * tensor, axis=-1, keepdims=True)) + unit_eps)

def log_sum_exp(tensor, axis_index):
    top_score = lax.optimization_barrier(jnp.max(tensor, axis=axis_index, keepdims=True))
    summed = lax.optimization_barrier(jnp.sum(jnp.exp(tensor - top_score), axis=axis_index, keepdims=True))
    return jnp.squeeze(top_score + jnp.log(summed), axis=axis_index)

def slot_place(owner_list, slot_count):
    tile_count = owner_list.shape[0]
    earlier = jnp.tril(jnp.ones((tile_count, tile_count), jnp.int32), -1)
    same_owner = (owner_list[:, None] == owner_list[None, :]).astype(jnp.int32)
    return (owner_list * slot_count + lax.optimization_barrier(jnp.sum(same_owner * earlier, axis=1))).astype(jnp.int32)

def unpack(weight_rows):
    vector_base = 4 * D + 2 * FF + EMB
    vector_rows = weight_rows[vector_base:]
    qkv_w = weight_rows[:3 * D]
    out_w = weight_rows[3 * D:4 * D]
    up_w = weight_rows[4 * D:4 * D + FF]
    down_w = weight_rows[4 * D + FF:4 * D + 2 * FF].reshape(D, FF)
    proj_w = weight_rows[4 * D + 2 * FF:vector_base]
    bias_up = vector_rows[7:7 + FF // D].reshape(FF)
    return (qkv_w, out_w, up_w, down_w, proj_w, vector_rows[0], vector_rows[1], vector_rows[2], vector_rows[3], vector_rows[4], vector_rows[5], vector_rows[6], bias_up, vector_rows[7 + FF // D])

def block_layer(params, inputs, valid_mask):
    qkv_w, out_w, up_w, down_w, proj_w, gain_one, shift_one, gain_two, shift_two, bias_q, bias_v, bias_o, bias_up, bias_down = params
    group_size = inputs.shape[0]
    normed = low(layer_norm(inputs, gain_one, shift_one))
    merged_qkv = matmul_right(normed, qkv_w)
    queries = rounded_both(merged_qkv[..., :D] + bias_q).reshape(group_size, PATCHES, HEADS, HEAD)
    key_heads = rounded_both(merged_qkv[..., D:2 * D]).reshape(group_size, PATCHES, HEADS, HEAD)
    value_heads = rounded_both(merged_qkv[..., 2 * D:] + bias_v).reshape(group_size, PATCHES, HEADS, HEAD)
    raw_scores = jnp.einsum('gqhd,gkhd->ghqk', queries, key_heads, precision=highest) * HEAD ** (-0.5)
    scores = low_back(jnp.where(valid_mask[:, None, None, :] > 0, raw_scores, -1000000000.0))
    top_score = lax.optimization_barrier(jnp.max(scores, axis=-1, keepdims=True))
    expo = jnp.exp(scores - top_score)
    attention = expo / lax.optimization_barrier(jnp.sum(expo, axis=-1, keepdims=True))
    mixed_heads = jnp.einsum('ghqk,gkhd->gqhd', low(attention), value_heads, precision=highest)
    attended = rounded_both(mixed_heads.reshape(group_size, PATCHES, D))
    middle = inputs + low_back(matmul_right(attended, out_w) + bias_o)
    normed_two = low(layer_norm(middle, gain_two, shift_two))
    hidden_pre = low_back(matmul_right(normed_two, up_w) + bias_up)
    hidden_act = low(jax.nn.gelu(hidden_pre, approximate=False))
    return low(middle + low_back(matmul_right(hidden_act, down_w) + bias_down))

def contrastive(weight_rows, inputs, valid_mask, text_emb, text_order):
    params = unpack(low(weight_rows))
    proj_w = params[4]
    group_size = 4 * IMG_DEV

    def one_group(pieces):
        group_in, group_mask = pieces
        group_out = block_layer(params, group_in, group_mask)
        counts = lax.optimization_barrier(jnp.sum(group_mask, axis=1))
        pooled = lax.optimization_barrier(jnp.sum(group_mask[..., None] * group_out, axis=1)) / counts[:, None]
        return (group_out, pooled)
    block_out, pooled = lax.map(jax.checkpoint(one_group), (inputs.reshape(-1, group_size, PATCHES, D), valid_mask.reshape(-1, group_size, PATCHES)))
    pooled = pooled.reshape(-1, D)
    image_total = pooled.shape[0]
    projected = low_back(matmul_right(low(pooled), proj_w))
    image_unit = low(unit_rows(projected))
    text_unit = low(unit_rows(text_emb.astype(jnp.float32)))
    rows_sim = low_back(logit_scale * matmul_right(image_unit, text_unit))
    cols_sim = low_back(logit_scale * matmul_right(image_unit, text_unit))
    rows_lse = log_sum_exp(rows_sim, 1)
    cols_lse = log_sum_exp(cols_sim, 0)
    rows_pos = jnp.take_along_axis(rows_sim, text_order[:, None], axis=1)[:, 0]
    cols_pos = jnp.take_along_axis(cols_sim, text_order[:, None], axis=1)[:, 0]
    loss_value = (jnp.sum(rows_lse - rows_pos) + jnp.sum(cols_lse) - jnp.sum(cols_pos)) / (2.0 * image_total)
    return (loss_value, block_out.reshape(image_total, PATCHES, D))

def reference(block_in, tissue, text_emb, text_order, owner_list, master, first_moment, second_moment):
    slot_count = master.shape[1]
    flat_master = master.reshape(-1, TR, D)
    placed = slot_place(owner_list, slot_count)
    weight_rows = flat_master[placed].reshape(TILES * TR, D)
    inputs = block_in.astype(jnp.float32)
    valid_mask = tissue.astype(jnp.float32)

    def objective(rows_in, acts_in):
        return contrastive(rows_in, acts_in, valid_mask, text_emb, text_order)
    loss_value, pullback, block_out = jax.vjp(objective, weight_rows, inputs, has_aux=True)
    rows_grad, input_grad = pullback(jnp.ones_like(loss_value))
    reduced = jnp.zeros_like(flat_master).at[placed].set(rows_grad.reshape(TILES, TR, D)).reshape(master.shape)
    new_first = beta_one * first_moment + (1.0 - beta_one) * reduced
    new_second = beta_two * second_moment + (1.0 - beta_two) * reduced * reduced
    step_dir = new_first / (1.0 - beta_one ** STEP)
    step_norm = jnp.sqrt(new_second / (1.0 - beta_two ** STEP)) + adam_eps
    new_master = master - learn_rate * (step_dir / step_norm + decay_rate * master)
    return (block_out.astype(jnp.bfloat16), input_grad, new_master, new_first, new_second)
```

```python
import functools

import jax
import jax.numpy as jnp
from jax import lax
from jax.experimental import pallas as pl
from jax.experimental.pallas import tpu as pltpu
from jax.sharding import PartitionSpec as P

D = 768
HEADS = 12
HEAD = 64
FF = 3072
EMB = 512
PATCHES = 196
STEP = 10
ROWS = 208
TR = 128

logit_scale = 50.0
learn_rate = 0.03
beta_one = 0.9
beta_two = 0.999
adam_eps = 1e-08
decay_rate = 0.05
norm_eps = 1e-05
unit_eps = 1e-06
masked_score = -1000000000.0

bf16 = jnp.bfloat16
f32 = jnp.float32
AXES = ("dp", "rep")
MIB = 1 << 20

X, Z, Y, CORE = range(4)
PIECES = [(x, z, y) for x in range(2) for z in range(4) for y in range(2)]

QKV_TILES = 3 * D // TR
OUT_TILES = D // TR
UP_TILES = FF // TR
DOWN_TILES = FF // TR
PROJ_TILES = EMB // TR
DOWN_FIRST = QKV_TILES + OUT_TILES + UP_TILES
PROJ_FIRST = DOWN_FIRST + DOWN_TILES
VEC_TILE = PROJ_FIRST + PROJ_TILES
PACK = (D + FF) // 3
CHUNK_TILES = (
    (QKV_TILES // 2, 0),
    (OUT_TILES // 2, QKV_TILES),
    (UP_TILES // 2, QKV_TILES + OUT_TILES),
    (DOWN_TILES // 2, DOWN_FIRST),
    (PROJ_TILES // 2, PROJ_FIRST),
)
CHUNK_AT = ((0, 0), (0, 9), (1, 0), (2, 0), (2, 12))
SAME_CORE = [[i * 2 + c for i in range(8)] for c in range(2)]


def nn(a, b):
    return lax.dot_general(a, b, (((1,), (0,)), ((), ())), preferred_element_type=f32)


def nt(a, b):
    return lax.dot_general(a, b, (((1,), (1,)), ((), ())), preferred_element_type=f32)


def tn(a, b):
    return lax.dot_general(a, b, (((0,), (0,)), ((), ())), preferred_element_type=f32)


def call(kernel, outs, ins, in_specs, out_specs, grid=None, scratch=(), flops=0, vmem=56, prefetch=0):
    moved = sum(a.size * a.dtype.itemsize for a in ins) + sum(o.size * o.dtype.itemsize for o in outs)
    params = pltpu.CompilerParams(
        vmem_limit_bytes=vmem * MIB,
        dimension_semantics=("arbitrary",) * len(grid or ()) or None,
    )
    return pl.pallas_call(
        kernel,
        out_shape=tuple(outs),
        grid_spec=pltpu.PrefetchScalarGridSpec(
            num_scalar_prefetch=prefetch,
            grid=grid or (1,),
            in_specs=in_specs,
            out_specs=tuple(out_specs),
            scratch_shapes=list(scratch),
        ),
        compiler_params=params,
        cost_estimate=pl.CostEstimate(flops=int(flops), bytes_accessed=int(moved), transcendentals=0),
    )(*ins)


def whole(shape):
    return pl.BlockSpec(shape, lambda *_: (0,) * len(shape))


def rows_at(rows, cols):
    return pl.BlockSpec((rows, cols), lambda i, *_: (i, 0))


def cols_at(rows, cols):
    return pl.BlockSpec((rows, cols), lambda i, *_: (0, i))


def sds(shape, dtype):
    return jax.ShapeDtypeStruct(shape, dtype)


class Weight:
    def __init__(self, arrays, tiles, first=0, quarters=False):
        self.arrays, self.tiles, self.first, self.quarters = tuple(arrays), tiles, first, quarters
        self.pieces = len(arrays) > 1
        self.specs = [pl.BlockSpec(memory_space=pl.ANY)] * len(arrays)
        shape = (tiles, TR // 4, FF) if quarters else (tiles, TR, D)
        self.scratch = [pltpu.VMEM(shape, bf16), pltpu.SemaphoreType.DMA((32 if self.pieces else 1,))]

    def copies(self, me, refs, out, sems):
        if not self.pieces:
            return [pltpu.make_async_copy(refs[0], out, sems.at[0])]
        copies = []
        half = self.tiles // 2
        for at, (c, x, y) in enumerate(sources(me)):
            for back in range(4):
                z = me[Z] ^ back
                if self.quarters:
                    row, col = x * 16, z * D + y * 384
                else:
                    row, col = x * 64 + z * 16, y * 384
                rows = pl.ds(pl.multiple_of(row, 16), 16)
                cols = pl.ds(pl.multiple_of(col, 128), 384)
                source = refs[at].at[back, pl.ds(self.first, half)]
                copies.append(
                    pltpu.make_async_copy(source, out.at[pl.ds(half * c, half), rows, cols], sems.at[len(copies)])
                )
        return copies

    def load(self, me, refs, out, sems):
        @pl.when(pl.program_id(0) == 0)
        def _():
            copies = self.copies(me, refs, out, sems)
            for copy in copies:
                copy.start()
            for copy in copies:
                copy.wait()


def normalized(x):
    center = x - jnp.mean(x, axis=-1, keepdims=True)
    spread = jnp.mean(center * center, axis=-1, keepdims=True)
    inverse = lax.rsqrt(spread + norm_eps)
    return center * inverse, inverse


def norm_back(grad, hat, inverse, gain):
    scaled = grad * gain
    first = jnp.mean(scaled, axis=-1, keepdims=True)
    second = jnp.mean(scaled * hat, axis=-1, keepdims=True)
    return inverse * (scaled - first - hat * second)


def column_sum(x):
    return jnp.sum(x, axis=0, keepdims=True)


def qkv_kernel(images, weight, me_ref, *refs):
    count = len(weight.arrays)
    pieces = refs[:count]
    x_ref, vec_in_ref, a_ref, qkv_ref, vec_ref, w_ref, sems, vec_half, vec_sems = refs[count:]
    j = pl.program_id(0)

    @pl.when(j == 0)
    def _():
        copies = weight.copies(me_ref, pieces, w_ref, sems)
        for copy in copies:
            copy.start()
        if weight.pieces:
            parts = []
            for at, (_, x, y) in list(enumerate(sources(me_ref)))[:4]:
                for back in range(4):
                    copy = pltpu.make_async_copy(pieces[at].at[back, 12], vec_half.at[y], vec_sems.at[len(parts)])
                    parts.append(((x == 0) & ((me_ref[Z] ^ back) == 0), copy))
            for here, copy in parts:
                pl.when(here)(copy.start)
            for here, copy in parts:
                pl.when(here)(copy.wait)
            vec_ref[...] = jnp.concatenate([vec_half[0], vec_half[1]], axis=1).astype(f32)
        else:
            vec_ref[...] = vec_in_ref[...]
        for i in range(images):
            hat, _ = normalized(x_ref[pl.ds(i * ROWS, ROWS), :].astype(f32))
            a_ref[pl.ds(i * ROWS, ROWS), :] = (hat * vec_ref[0:1, :] + vec_ref[1:2, :]).astype(bf16)
        for copy in copies:
            copy.wait()

    bias = jnp.where(j == 0, vec_ref[4:5, :], jnp.where(j == 2, vec_ref[5:6, :], 0.0))
    scale = jnp.where(j == 0, f32(HEAD**-0.5), f32(1.0))
    w = w_ref[pl.ds(6 * j, 6)].reshape(D, D)
    qkv_ref[...] = ((nt(a_ref[...], w) + bias) * scale).astype(bf16)


def qkv_forward(images, x, vec, weight, me):
    n = images * ROWS
    return call(
        functools.partial(qkv_kernel, images, weight),
        (sds((n, D), bf16), sds((n, 3 * D), bf16), sds((16, D), f32)),
        (me, *weight.arrays, x, vec),
        weight.specs + [whole((n, D)), whole((16, D))],
        [whole((n, D)), cols_at(n, D), whole((16, D))],
        grid=(3,),
        scratch=weight.scratch + [pltpu.VMEM((2, 16, 384), bf16), pltpu.SemaphoreType.DMA((16,))],
        flops=2 * n * D * 3 * D,
        prefetch=1,
    )


def attention_kernel(qkv_ref, mask_ref, o_ref, lse_ref):
    lane = lax.broadcasted_iota(jnp.int32, (ROWS, 2 * HEAD), 1)
    low_half = lane < HEAD
    valid = mask_ref[0] > 0.0
    lse_all = jnp.zeros((ROWS, 128), f32)
    for pair in range(HEADS // 2):
        at = pair * 2 * HEAD
        q = qkv_ref[:, at : at + 2 * HEAD]
        k = qkv_ref[:, D + at : D + at + 2 * HEAD]
        v = qkv_ref[:, 2 * D + at : 2 * D + at + 2 * HEAD]
        mixed = []
        for half in range(2):
            keep = low_half if half == 0 else jnp.logical_not(low_half)
            s = nt(q, jnp.where(keep, k, jnp.zeros_like(k)))
            s = jnp.where(valid, s, masked_score)
            top = jnp.max(s, axis=-1, keepdims=True)
            e = jnp.exp(s - top)
            total = jnp.sum(e, axis=-1, keepdims=True)
            p = e * (1.0 / total)
            mixed.append(nn(p.astype(bf16), v))
            lse_all = jnp.where(lane == 2 * pair + half, top + jnp.log(total), lse_all)
        o_ref[:, at : at + 2 * HEAD] = jnp.where(low_half, mixed[0], mixed[1]).astype(bf16)
    lse_ref[0] = jnp.transpose(lse_all)[0:16, :]


def attention_forward(images, qkv, mask_row):
    n = images * ROWS
    return call(
        attention_kernel,
        (sds((n, D), bf16), sds((images, 16, ROWS), f32)),
        (qkv, mask_row),
        [rows_at(ROWS, 3 * D), pl.BlockSpec((1, 1, ROWS), lambda i: (i, 0, 0))],
        [rows_at(ROWS, D), pl.BlockSpec((1, 16, ROWS), lambda i: (i, 0, 0))],
        grid=(images,),
        flops=4 * n * ROWS * D,
    )


def middle_kernel(weight, me_ref, *refs):
    count = len(weight.arrays)
    x_ref, o_ref, vec_ref, h_ref, m_ref, w_ref, sems = refs[count:]
    weight.load(me_ref, refs[:count], w_ref, sems)
    part = nt(o_ref[...], w_ref[...].reshape(D, D)) + vec_ref[6:7, :]
    middle = x_ref[...].astype(f32) + part
    h_ref[...] = middle
    hat, _ = normalized(middle)
    m_ref[...] = (hat * vec_ref[2:3, :] + vec_ref[3:4, :]).astype(bf16)


def middle_forward(images, x, o, vec, weight, me):
    n = images * ROWS
    return call(
        functools.partial(middle_kernel, weight),
        (sds((n, D), f32), sds((n, D), bf16)),
        (me, *weight.arrays, x, o, vec),
        weight.specs + [rows_at(ROWS, D), rows_at(ROWS, D), whole((16, D))],
        [rows_at(ROWS, D), rows_at(ROWS, D)],
        grid=(images,),
        scratch=weight.scratch,
        flops=2 * n * D * D,
        prefetch=1,
    )


def gelu_parts(u):
    r = jnp.abs(u) * 0.7071067811865476
    t = 1.0 / (1.0 + 0.3275911 * r)
    poly = t * (0.127414796 + t * (-0.142248368 + t * (0.7107068705 + t * (-0.7265760135 + t * 0.5307027145))))
    e = jnp.exp(-0.5 * u * u)
    tail = poly * e
    phi = jnp.where(u >= 0.0, 1.0 - tail, tail)
    return u * phi, phi + u * e * 0.3989422804014327


def up_kernel(images, weight, me_ref, *refs):
    count = len(weight.arrays)
    m_ref, bias_ref, sel_ref, act_ref, slope_ref, sum_ref, w_ref, sems = refs[count:]
    weight.load(me_ref, refs[:count], w_ref, sems)
    w = w_ref[pl.ds(6 * pl.program_id(0), 6)].reshape(D, D)
    total = jnp.zeros((16, D), f32)
    for i in range(images):
        at = pl.ds(i * ROWS, ROWS)
        u = nt(m_ref[at, :], w) + bias_ref[0]
        act, slope = gelu_parts(u)
        act = act.astype(bf16)
        act_ref[at, :] = act
        slope_ref[at, :] = slope.astype(bf16)
        total += nn(sel_ref[i], act)
    sum_ref[...] = total


def up_forward(images, m, weight, bias, sel, me):
    n = images * ROWS
    return call(
        functools.partial(up_kernel, images, weight),
        (sds((n, FF), bf16), sds((n, FF), bf16), sds((16, FF), f32)),
        (me, *weight.arrays, m, bias, sel),
        weight.specs
        + [whole((n, D)), pl.BlockSpec((1, 1, D), lambda j, *_: (j, 0, 0)), whole((images, 16, ROWS))],
        [cols_at(n, D), cols_at(n, D), cols_at(16, D)],
        grid=(FF // D,),
        scratch=weight.scratch,
        flops=2 * n * D * FF,
        prefetch=1,
    )


def down_kernel(weight, me_ref, *refs):
    count = len(weight.arrays)
    act_ref, h_ref, vec_ref, sel_ref, inv_ref, out_ref, pooled_ref, w_ref, sems, sum_ref = refs[count:]
    i = pl.program_id(0)
    weight.load(me_ref, refs[:count], w_ref, sems)
    y = nt(act_ref[...], w_ref[...].reshape(D, FF)) + vec_ref[11:12, :]
    out = (h_ref[...] + y).astype(bf16)
    out_ref[0] = out[0:PATCHES, :]
    part = nn(sel_ref[0], out)

    @pl.when(i == 0)
    def _():
        sum_ref[...] = part

    @pl.when(i > 0)
    def _():
        sum_ref[...] += part

    pooled_ref[...] = (sum_ref[...] * inv_ref[:, 0:1]).astype(bf16)


def down_forward(images, act, weight, h, vec, sel, inv_count, me):
    n = images * ROWS
    return call(
        functools.partial(down_kernel, weight),
        (sds((images, PATCHES, D), bf16), sds((16, D), bf16)),
        (me, *weight.arrays, act, h, vec, sel, inv_count),
        weight.specs
        + [
            rows_at(ROWS, FF),
            rows_at(ROWS, D),
            whole((16, D)),
            pl.BlockSpec((1, 16, ROWS), lambda i, *_: (i, 0, 0)),
            whole((16, 128)),
        ],
        [pl.BlockSpec((1, PATCHES, D), lambda i, *_: (i, 0, 0)), whole((16, D))],
        grid=(images,),
        scratch=weight.scratch + [pltpu.VMEM((16, D), f32)],
        flops=2 * n * D * FF,
        prefetch=1,
    )


def loss_kernel(total_images, proj, down, me_ref, first_ref, *refs):
    count = len(proj.arrays)
    pieces = refs[:count]
    if proj.pieces:
        down_pieces, rest = pieces, refs[count:]
    else:
        down_pieces, rest = refs[count : count + 1], refs[count + 1 :]
    text_ref, pooled_ref, order_ref, inv_ref, dz_ref, rank_ref, spread_ref, hidden_ref = rest[:8]
    proj_ref, proj_sems, down_ref, down_sems = rest[8:12]
    down_copies = down.copies(me_ref, down_pieces, down_ref, down_sems)
    proj_copies = proj.copies(me_ref, pieces, proj_ref, proj_sems)
    if proj.pieces:
        slab_ref, slab_sems = rest[12:]
        for at, (c, x, y) in enumerate(sources(me_ref)):
            for back in range(4):
                device = x * 16 + (me_ref[Z] ^ back) * 4 + y * 2 + c
                out = slab_ref.at[pl.ds(pl.multiple_of(device * 16, 16), 16)]
                proj_copies.append(pltpu.make_async_copy(pieces[at].at[back, 14], out, slab_sems.at[at * 4 + back]))
    for copy in proj_copies + down_copies:
        copy.start()
    for copy in proj_copies:
        copy.wait()
    if proj.pieces:
        images = total_images // 32
        shape = (total_images, 512)
        row = lax.broadcasted_iota(jnp.int32, shape, 0)
        col = lax.broadcasted_iota(jnp.int32, shape, 1)
        start = row // images * 16 + row % images
        held = slab_ref[...]
        left = nn(jnp.where(col == start, 1.0, 0.0).astype(bf16), held)
        right = nn(jnp.where(col == start + 8, 1.0, 0.0).astype(bf16), held[:, 0:128])
        text = jnp.concatenate([left, right], axis=1).astype(bf16)
    else:
        text = text_ref[...]
    proj_w = proj_ref[...].reshape(EMB, D)
    z = nt(pooled_ref[...], proj_w)
    square = jnp.sum(z * z, axis=-1, keepdims=True) + unit_eps
    inverse = lax.rsqrt(square)
    image = (z * inverse).astype(bf16)
    s = logit_scale * nt(image, text)
    shape = (total_images, total_images)
    hit = jnp.where(order_ref[:, 0:1] == lax.broadcasted_iota(jnp.int32, shape, 1), 1.0, 0.0)
    part = 1.0 / (2.0 * total_images)

    def grad_of(axis):
        top = jnp.max(s, axis=axis, keepdims=True)
        lse = top + jnp.log(jnp.sum(jnp.exp(s - top), axis=axis, keepdims=True))
        return ((jnp.exp(s - lse) - hit) * part).astype(bf16)

    de = logit_scale * (nn(grad_of(1), text) + nn(grad_of(0), text))
    dz = inverse * de - z * (inverse * inverse * inverse * jnp.sum(z * de, axis=-1, keepdims=True))
    dz = dz.astype(bf16)
    dz_ref[...] = dz
    pick = lax.broadcasted_iota(jnp.int32, (16, total_images), 1) == (
        first_ref[0] + lax.broadcasted_iota(jnp.int32, (16, total_images), 0)
    )
    own = nn(jnp.where(pick, 1.0, 0.0).astype(bf16), dz).astype(bf16)
    spread = nn(own, proj_w) * inv_ref[:, 0:1]
    spread_ref[...] = spread
    rank = spread.astype(bf16)
    rank_ref[...] = rank
    for copy in down_copies:
        copy.wait()
    hidden_ref[...] = nn(rank, down_ref[...].reshape(D, FF))


def loss_backward(me, first, pooled, text, order, proj, down, inv_count):
    total = pooled.shape[0]
    if proj.pieces:
        arrays, extra = proj.arrays, [pltpu.VMEM((512, 384), bf16), pltpu.SemaphoreType.DMA((32,))]
    else:
        arrays, extra = proj.arrays + down.arrays, []
    return call(
        functools.partial(loss_kernel, total, proj, down),
        (sds((total, EMB), bf16), sds((16, D), bf16), sds((16, D), f32), sds((16, FF), f32)),
        (me, first, *arrays, text, pooled, order, inv_count),
        [pl.BlockSpec(memory_space=pl.ANY)] * len(arrays)
        + [whole(text.shape), whole((total, D)), whole((total, 128)), whole((16, 128))],
        [whole((total, EMB)), whole((16, D)), whole((16, D)), whole((16, FF))],
        scratch=proj.scratch + down.scratch + extra,
        flops=6 * total * total * EMB + 2 * total * D * EMB + 32 * D * FF,
        prefetch=2,
    )


def weave(ref, value):
    for t in range(value.shape[0] // TR):
        for x, z, y in PIECES:
            row = t * TR + x * 64 + z * 16
            ref[x * 8 + z * 2 + y, pl.ds(t * 16, 16), :] = value[row : row + 16, y * 384 : y * 384 + 384]


def half_block(j, me):
    return (j // 2 + 1 - me[CORE]) % 2 * 2 + j % 2


def up_back_kernel(images, weight, me_ref, *refs):
    count = len(weight.arrays)
    slope_ref, m_ref, hidden_ref, col_ref, dm_ref, db_ref = refs[count : count + 6]
    w_ref, sems, du_ref = refs[-3:]
    j = pl.program_id(0)
    weight.load(me_ref, refs[:count], w_ref, sems)
    w = w_ref[pl.ds(6 * half_block(j, me_ref), 6)].reshape(D, D)
    for i in range(images):
        at = pl.ds(i * ROWS, ROWS)
        du = (slope_ref[at, :].astype(f32) * (col_ref[at, 0:1] * hidden_ref[i : i + 1, :])).astype(bf16)
        du_ref[at, :] = du
        part = nn(du, w)

        @pl.when(j == 0)
        def _():
            dm_ref[at, :] = part

        @pl.when(j > 0)
        def _():
            dm_ref[at, :] += part

    du = du_ref[...]
    db_ref[...] = nn(jnp.ones((16, images * ROWS), bf16), du)
    dw = tn(du, m_ref[...]).astype(bf16)
    if not weight.pieces:
        refs[count + 6][...] = dw
        return
    send_ref, keep_ref = refs[count + 6 : count + 8]

    @pl.when(j < 2)
    def _():
        weave(send_ref, dw)

    @pl.when(j >= 2)
    def _():
        weave(keep_ref, dw)


def up_backward(images, slope, m, weight, hidden, col, me):
    n = images * ROWS

    def cols(rows):
        return pl.BlockSpec((rows, D), lambda j, me: (0, half_block(j, me)))

    if weight.pieces:
        shapes = (sds((16, 192, 384), bf16),) * 2
        specs = [
            pl.BlockSpec((16, 96, 384), lambda j, me: (0, jnp.minimum(j, 1), 0)),
            pl.BlockSpec((16, 96, 384), lambda j, me: (0, jnp.maximum(j - 2, 0), 0)),
        ]
    else:
        shapes = (sds((FF, D), bf16),)
        specs = [pl.BlockSpec((D, D), lambda j, me: (half_block(j, me), 0))]
    return call(
        functools.partial(up_back_kernel, images, weight),
        (sds((n, D), f32), sds((16, FF), f32)) + shapes,
        (me, *weight.arrays, slope, m, hidden, col),
        weight.specs + [cols(n), whole((n, D)), cols(16), whole((n, 128))],
        [whole((n, D)), cols(16)] + specs,
        grid=(FF // D,),
        scratch=weight.scratch + [pltpu.VMEM((n, D), bf16)],
        flops=4 * n * D * FF,
        prefetch=1,
    )


def accumulate(i, ref, value):
    @pl.when(i == 0)
    def _():
        ref[...] = value

    @pl.when(i > 0)
    def _():
        ref[...] += value


def middle_back_kernel(images, weight, me_ref, *refs):
    count = len(weight.arrays)
    h_ref, dm_ref, col_ref, spread_ref, o_ref, vec_ref = refs[count : count + 6]
    dh_ref, do_ref, dw_ref, dvec_ref, w_ref, sems, acc_ref = refs[count + 6 :]
    i = pl.program_id(0)
    weight.load(me_ref, refs[:count], w_ref, sems)
    hat, inverse = normalized(h_ref[...])
    dm = dm_ref[...]
    part = norm_back(dm, hat, inverse, vec_ref[2:3, :])
    here = spread_ref[pl.ds(i, 1), :]
    dh = col_ref[:, 0:1] * here + part
    dh_ref[...] = dh
    dat = dh.astype(bf16)
    do_ref[...] = nn(dat, w_ref[...].reshape(D, D)).astype(bf16)
    accumulate(i, acc_ref, tn(dat, o_ref[...]))
    sums = jnp.concatenate(
        [
            column_sum(dm * hat),
            column_sum(dm),
            column_sum(dat.astype(f32)),
            column_sum(col_ref[:, 0:1]) * here.astype(bf16).astype(f32),
            jnp.zeros((4, D), f32),
        ],
        axis=0,
    )
    accumulate(i, dvec_ref, sums)

    @pl.when(i == images - 1)
    def _():
        dw = acc_ref[...].astype(bf16)
        if weight.pieces:
            for half in range(2):
                weave(dw_ref.at[half], dw[half * 384 : half * 384 + 384])
        else:
            dw_ref[...] = dw


def middle_backward(images, h, dm, col, spread, o, weight, vec, me):
    n = images * ROWS
    dw_shape = (2, 16, 48, 384) if weight.pieces else (D, D)
    return call(
        functools.partial(middle_back_kernel, images, weight),
        (sds((n, D), f32), sds((n, D), bf16), sds(dw_shape, bf16), sds((8, D), f32)),
        (me, *weight.arrays, h, dm, col, spread, o, vec),
        weight.specs
        + [
            rows_at(ROWS, D),
            rows_at(ROWS, D),
            rows_at(ROWS, 128),
            whole((16, D)),
            rows_at(ROWS, D),
            whole((16, D)),
        ],
        [rows_at(ROWS, D), rows_at(ROWS, D), whole(dw_shape), whole((8, D))],
        grid=(images,),
        scratch=weight.scratch + [pltpu.VMEM((D, D), f32)],
        flops=4 * n * D * D,
        prefetch=1,
    )


def attention_back_kernel(qkv_ref, do_ref, lse_ref, col_ref, dqkv_ref, db_ref):
    i = pl.program_id(0)
    low_half = lax.broadcasted_iota(jnp.int32, (ROWS, 2 * HEAD), 1) < HEAD
    valid = jnp.broadcast_to(col_ref[:, 0:1], (ROWS, ROWS)) > 0.0
    for pair in range(HEADS // 2):
        at = pair * 2 * HEAD
        q = qkv_ref[:, at : at + 2 * HEAD]
        k = qkv_ref[:, D + at : D + at + 2 * HEAD]
        v = qkv_ref[:, 2 * D + at : 2 * D + at + 2 * HEAD]
        do = do_ref[:, at : at + 2 * HEAD]
        dv, dk, dq = [], [], []
        for half in range(2):
            keep = low_half if half == 0 else jnp.logical_not(low_half)
            only_k = jnp.where(keep, k, jnp.zeros_like(k))
            only_v = jnp.where(keep, v, jnp.zeros_like(v))
            head = 2 * pair + half
            s = jnp.where(valid, nt(only_k, q), masked_score)
            p = jnp.exp(s - lse_ref[0, head : head + 1, :])
            dp = nt(only_v, do)
            share = jnp.sum(p * dp, axis=0, keepdims=True)
            ds = (p * (dp - share)).astype(bf16)
            dv.append(nn(p.astype(bf16), do))
            dk.append(nn(ds, q))
            dq.append(tn(ds, only_k))
        dqkv_ref[:, at : at + 2 * HEAD] = ((dq[0] + dq[1]) * (HEAD**-0.5)).astype(bf16)
        dqkv_ref[:, D + at : D + at + 2 * HEAD] = jnp.where(low_half, dk[0], dk[1]).astype(bf16)
        dqkv_ref[:, 2 * D + at : 2 * D + at + 2 * HEAD] = jnp.where(low_half, dv[0], dv[1]).astype(bf16)
    accumulate(i, db_ref, nn(jnp.ones((16, ROWS), bf16), dqkv_ref[...]))


def attention_backward(images, qkv, do, lse, col):
    n = images * ROWS
    return call(
        attention_back_kernel,
        (sds((n, 3 * D), bf16), sds((16, 3 * D), f32)),
        (qkv, do, lse, col),
        [
            rows_at(ROWS, 3 * D),
            rows_at(ROWS, D),
            pl.BlockSpec((1, 16, ROWS), lambda i: (i, 0, 0)),
            rows_at(ROWS, 128),
        ],
        [rows_at(ROWS, 3 * D), whole((16, 3 * D))],
        grid=(images,),
        flops=10 * n * ROWS * D,
    )


def qkv_grad_kernel(dqkv_ref, a_ref, dw_ref):
    dw_ref[...] = tn(dqkv_ref[...], a_ref[...]).astype(bf16)


def qkv_weight_grad(images, dqkv, a):
    n = images * ROWS
    return call(
        qkv_grad_kernel,
        (sds((3 * D, D), bf16),),
        (dqkv, a),
        [cols_at(n, D), whole((n, D))],
        [rows_at(D, D)],
        grid=(3,),
        flops=6 * n * D * D,
    )[0]


def qkv_grad_fast_kernel(_, dqkv_ref, a_ref, out_ref, pieces_ref):
    j = pl.program_id(0)

    @pl.when(j < 3)
    def _():
        weave(pieces_ref, tn(dqkv_ref[...], a_ref[...]).astype(bf16))

    @pl.when(j == 3)
    def _():
        pieces_ref[...] = out_ref[0]


def qkv_weight_grad_fast(images, dqkv, a, dw_out, me, other):
    n = images * ROWS

    def half(me):
        return 1 - me[CORE] if other else me[CORE]

    return call(
        qkv_grad_fast_kernel,
        (sds((16, 192, 384), bf16),),
        (me, dqkv, a, dw_out),
        [
            pl.BlockSpec((n, 384), lambda j, me: (0, half(me) * 3 + jnp.minimum(j, 2))),
            whole((n, D)),
            pl.BlockSpec((1, 16, 48, 384), lambda j, me: (half(me), 0, 0, 0)),
        ],
        [pl.BlockSpec((16, 48, 384), lambda j, me: (0, j, 0))],
        grid=(4,),
        flops=3 * n * D * D,
        prefetch=1,
    )[0]


def input_back_kernel(weight, me_ref, *refs):
    count = len(weight.arrays)
    x_ref, dqkv_ref, dh_ref, vec_ref, out_ref, dvec_ref, w_ref, sems = refs[count:]
    i = pl.program_id(0)
    weight.load(me_ref, refs[:count], w_ref, sems)
    da = nn(dqkv_ref[...], w_ref[...].reshape(3 * D, D))
    hat, inverse = normalized(x_ref[...].astype(f32))
    out = dh_ref[...] + norm_back(da, hat, inverse, vec_ref[0:1, :])
    out_ref[0] = out[0:PATCHES, :]
    sums = jnp.concatenate([column_sum(da * hat), column_sum(da), jnp.zeros((6, D), f32)], axis=0)
    accumulate(i, dvec_ref, sums)


def input_backward(images, x, dqkv, weight, dh, vec, me):
    n = images * ROWS
    return call(
        functools.partial(input_back_kernel, weight),
        (sds((images, PATCHES, D), f32), sds((8, D), f32)),
        (me, *weight.arrays, x, dqkv, dh, vec),
        weight.specs + [rows_at(ROWS, D), rows_at(ROWS, 3 * D), rows_at(ROWS, D), whole((16, D))],
        [pl.BlockSpec((1, PATCHES, D), lambda i, *_: (i, 0, 0)), whole((8, D))],
        grid=(images,),
        scratch=weight.scratch,
        flops=6 * n * D * D,
        prefetch=1,
    )


SUMMED, DOWN, PROJ, NONE, VEC = 0, 1, 2, 3, 4


def adam_kernel(part_rows, fast, kind_ref, row_ref, *refs):
    master_ref, first_ref, second_ref, summed_ref, down_ref, proj_ref, vec_ref = refs[:7]
    new_master_ref, new_first_ref, new_second_ref, grad_ref, woven_ref = refs[7:]
    kind = kind_ref[pl.program_id(0)]
    wide = FF // D

    @pl.when(kind == SUMMED)
    def _():
        if fast:
            for z in range(4):
                for y in range(2):
                    grad_ref[16 * z : 16 * z + 16, 384 * y : 384 * y + 384] = summed_ref[2 * z + y, 0].astype(f32)
        else:
            grad_ref[...] = summed_ref[0].astype(f32)

    @pl.when(kind == VEC)
    def _():
        grad_ref[...] = jnp.zeros_like(grad_ref)
        grad_ref[0 : vec_ref.shape[0], :] = vec_ref[...]

    @pl.when(kind == DOWN)
    def _():
        block = down_ref[...] if fast else down_ref[0]
        for c in range(D // 128):
            for b in range(wide):
                lanes = slice(b * D + c * 128, b * D + c * 128 + 128)
                woven_ref[c, pl.ds(b, part_rows // wide, stride=wide), :] = block[0 : part_rows // wide, lanes]
            grad_ref[:, c * 128 : (c + 1) * 128] = woven_ref[c]

    @pl.when(kind == PROJ)
    def _():
        grad_ref[...] = proj_ref[...]

    @pl.when(kind == NONE)
    def _():
        grad_ref[...] = jnp.zeros_like(grad_ref)

    grad = grad_ref[...]
    master = master_ref[0, 0]
    first = beta_one * first_ref[0, 0] + (1.0 - beta_one) * grad
    second = beta_two * second_ref[0, 0] + (1.0 - beta_two) * grad * grad
    new_first_ref[0, 0] = first
    new_second_ref[0, 0] = second
    direction = first / (1.0 - beta_one**STEP)
    size = jnp.sqrt(second / (1.0 - beta_two**STEP)) + adam_eps
    new_master_ref[0, 0] = master - learn_rate * (direction / size + decay_rate * master)


def adam(kind, row, master, first, second, summed, down, proj, vec, fast):
    slots, part_rows = master.shape[1:3]
    block = pl.BlockSpec((1, 1, part_rows, D), lambda s, *_: (0, s, 0, 0))
    each = part_rows * D // FF
    if fast:
        summed_spec = pl.BlockSpec((8, 1, 16, 384), lambda s, *_: (0, s, 0, 0))
        down_spec = pl.BlockSpec((each, FF), lambda s, kind, row: (jnp.where(kind[s] == DOWN, row[s] // each, 0), 0))
    else:
        summed_spec = pl.BlockSpec((1, part_rows, D), lambda s, *_: (s, 0, 0))
        down_spec = pl.BlockSpec((1,) + down.shape[1:], lambda s, *_: (s, 0, 0))
    return call(
        functools.partial(adam_kernel, part_rows, fast),
        (sds(master.shape, f32),) * 3,
        (kind, row, master, first, second, summed, down, proj, vec),
        [
            block,
            block,
            block,
            summed_spec,
            down_spec,
            pl.BlockSpec((part_rows, D), lambda s, kind, row: (jnp.where(kind[s] == PROJ, row[s] // part_rows, 0), 0)),
            whole(vec.shape),
        ],
        [block] * 3,
        grid=(slots,),
        scratch=[pltpu.VMEM((part_rows, D), f32), pltpu.VMEM((D // 128, part_rows, 128), f32)],
        flops=20 * slots * part_rows * D,
        prefetch=2,
    )


def rank_grad_kernel(images, *refs):
    dz_ref, pooled_ref, down_ref, proj_ref = refs[-4:]
    held = jnp.concatenate([ref[...].reshape(64, PACK) for ref in refs[:-4]], axis=0)
    shape = (512, 512)
    row = lax.broadcasted_iota(jnp.int32, shape, 0)
    col = lax.broadcasted_iota(jnp.int32, shape, 1)
    first = 0
    for segment in range(3):
        here = (row - col == segment * images) & (row // 16 == col // 16) & (col % 16 < images)
        rank = nn(jnp.where(here, 1.0, 0.0).astype(bf16), held[:, 0:D]).astype(bf16)
        part = held[:, D:PACK] if segment == 0 else held
        down_ref[:, first : first + part.shape[1]] = tn(rank, part)
        first += part.shape[1]
    proj_ref[...] = tn(dz_ref[...], pooled_ref[...])


def rank_grads(images, arrays, dz, pooled):
    return call(
        functools.partial(rank_grad_kernel, images),
        (sds((D, FF), f32), sds((EMB, D), f32)),
        (*arrays, dz, pooled),
        [whole(a.shape) for a in arrays] + [whole(dz.shape), whole(pooled.shape)],
        [whole((D, FF)), whole((EMB, D))],
        flops=1024 * D * FF,
    )


def slot_place(owner_list, slot_count):
    tile_count = owner_list.shape[0]
    earlier = jnp.tril(jnp.ones((tile_count, tile_count), jnp.int32), -1)
    same_owner = (owner_list[:, None] == owner_list[None, :]).astype(jnp.int32)
    return owner_list * slot_count + jnp.sum(same_owner * earlier, axis=1)


def gather_weights(master, placed):
    n_dp, n_rep = lax.axis_size("dp"), lax.axis_size("rep")
    slots, part_rows = master.shape[1:3]
    gathered = lax.all_gather(master.astype(bf16), AXES, axis=0, tiled=True)
    gathered = gathered.reshape(n_dp, n_rep * slots, part_rows, D)
    return jnp.transpose(jnp.take(gathered, placed, axis=1), (1, 0, 2, 3)).reshape(-1, D)


def scatter_grads(tiles, tile_of_slot, slots, part_rows):
    n_dp, n_rep = lax.axis_size("dp"), lax.axis_size("rep")
    count = tiles.shape[0]
    tiles = jnp.concatenate([tiles, jnp.zeros((1, TR, D), tiles.dtype)], axis=0)
    index = jnp.where(tile_of_slot < count, tile_of_slot, count)
    buffer = jnp.take(tiles, index, axis=0).reshape(n_rep * slots, n_dp, part_rows, D)
    buffer = jnp.transpose(buffer, (1, 0, 2, 3)).reshape(n_dp * n_rep, slots, part_rows, D)
    return lax.psum_scatter(buffer, AXES, scatter_dimension=0, tiled=True)[0]


def pairs(move):
    def number(x, z, y, c):
        return x * 16 + z * 4 + y * 2 + c

    return [(number(x, z, y, c), number(*move(x, z, y, c))) for x, z, y in PIECES for c in range(2)]


SWAP_CORE = pairs(lambda x, z, y, c: (x, z, y, 1 - c))
SWAP_X = pairs(lambda x, z, y, c: (1 - x, z, y, c))
SWAP_Y = pairs(lambda x, z, y, c: (x, z, 1 - y, c))
SWAP_XY = pairs(lambda x, z, y, c: (1 - x, z, 1 - y, c))
ACROSS_Z = [pairs(lambda x, z, y, c, k=k: (x, z ^ k, y, c)) for k in (1, 2, 3)]
CROSS_ONE = pairs(lambda x, z, y, c: (1 - x, z, y, c) if c == 0 else (x, z, 1 - y, c))
CROSS_TWO = pairs(lambda x, z, y, c: (x, z, 1 - y, c) if c == 0 else (1 - x, z, y, c))


def send(value, permutation):
    return lax.ppermute(value, AXES, permutation)


def add_kernel(count, _, *refs):
    out_ref = refs[-1]
    pieces = out_ref.shape[0]
    for p in range(pieces):
        total = refs[p * count][0].astype(f32)
        for k in range(1, count):
            total += refs[p * count + k][0].astype(f32)
        out_ref[p] = total.astype(bf16)


def add_pieces(sources, me, pieces, steps):
    rows = sources[0][0].shape[1]
    each = pieces // steps
    arrays, specs = [], []
    for p in range(each):
        for array, at in sources:
            arrays.append(array)
            specs.append(pl.BlockSpec((1, rows, 384), lambda i, me, p=p, at=at: (at(i * each + p, me), 0, 0)))
    return call(
        functools.partial(add_kernel, len(sources)),
        (sds((pieces, rows, 384), bf16),),
        (me, *arrays),
        specs,
        [pl.BlockSpec((each, rows, 384), lambda i, me: (i, 0, 0))],
        grid=(steps,),
        flops=pieces * rows * D,
        prefetch=1,
    )[0]


class PieceSum:
    def __init__(self, other, me):
        self.me = me
        self.one = send(other, SWAP_CORE)

    def first_send(self, i, me):
        return jnp.where(me[CORE] == 0, (1 - me[X]) * 8 + i, i * 2 + 1 - me[Y])

    def kept(self, i, me):
        return jnp.where(me[CORE] == 0, me[X] * 8 + i, i * 2 + me[Y])

    def second_send(self, i, me):
        return jnp.where(me[CORE] == 0, 2 * i + 1 - me[Y], (1 - me[X]) * 4 + i)

    def second_keep(self, i, me):
        return jnp.where(me[CORE] == 0, 2 * i + me[Y], me[X] * 4 + i)

    def cross_one(self):
        self.two = send(add_pieces([(self.mine, self.first_send), (self.one, self.first_send)], self.me, 8, 2), CROSS_ONE)

    def cross_two(self):
        def own(i, me):
            return self.kept(self.second_send(i, me), me)

        parts = [(self.mine, own), (self.one, own), (self.two, self.second_send)]
        self.three = send(add_pieces(parts, self.me, 4, 1), CROSS_TWO)

    def along_z(self, first):
        def z_at(i, me):
            return me[Z] ^ (first + i)

        def crossed(i, me):
            return self.second_keep(z_at(i, me), me)

        def own(i, me):
            return self.kept(crossed(i, me), me)

        return [(self.mine, own), (self.one, own), (self.two, crossed), (self.three, z_at)]

    def cross_z(self):
        parts = add_pieces(self.along_z(1), self.me, 3, 1)
        self.last = [send(parts[k], ACROSS_Z[k]) for k in range(3)]

    def total(self):
        arrived = [(part[None], lambda i, me: 0) for part in self.last]
        return add_pieces(self.along_z(0) + arrived, self.me, 1, 1)


def place_kernel(index_ref, mine_ref, theirs_ref, out_ref):
    for k in range(out_ref.shape[0]):
        at = index_ref[k]

        @pl.when(at < 24)
        def _():
            out_ref[k] = mine_ref[at]

        @pl.when((at >= 24) & (at < 48))
        def _():
            out_ref[k] = theirs_ref[at - 24]

        @pl.when(at >= 48)
        def _():
            out_ref[k] = jnp.zeros((16, 384), bf16)


def return_to_owners(sums, place):
    placed = call(
        place_kernel,
        (sds((64, 16, 384), bf16),),
        (place, sums, send(sums, SWAP_CORE)),
        [whole((24, 16, 384)), whole((24, 16, 384))],
        [whole((64, 16, 384))],
        prefetch=1,
    )[0]
    return lax.all_to_all(placed.reshape(8, 8, 16, 384), "rep", 0, 0, axis_index_groups=SAME_CORE)


def plan_kernel(owner_ref, me_ref, pick_ref, place_ref, kind_ref, row_ref, counts, placed, tile_of):
    x, c = me_ref[X], me_ref[CORE]
    rep = me_ref[Z] * 4 + me_ref[Y] * 2 + c

    @pl.loop(0, 16)
    def _(r):
        counts[r] = 0

    @pl.loop(0, 128)
    def _(k):
        tile_of[k] = 1 << 20

    @pl.loop(0, VEC_TILE + 1)
    def _(t):
        owner = owner_ref[t]
        at = owner * 8 + counts[owner]
        counts[owner] = counts[owner] + 1
        placed[t] = at
        tile_of[at] = t

    def slab(t):
        at = placed[t]
        owner = at // 8
        return jnp.where(owner % 2 == c, 0, 64) + owner // 2 * 8 + at % 8

    def fill(first, count, tile):
        @pl.loop(0, count)
        def _(k):
            pick_ref[first + k] = slab(tile + k)

    base = 0
    for tiles, tile in CHUNK_TILES:
        fill(base, tiles, tile + tiles * c)
        base += tiles
    pick_ref[base] = slab(VEC_TILE)

    @pl.loop(0, 64)
    def _(k):
        t = tile_of[k // 8 * 16 + c * 8 + k % 8]
        u = t - QKV_TILES
        v = u - OUT_TILES
        half = jnp.where(t < QKV_TILES, t // 9, jnp.where(u < OUT_TILES, u // 3, v // 12))
        place = jnp.where(t < QKV_TILES, t % 9, jnp.where(u < OUT_TILES, 9 + u % 3, 12 + v % 12))
        place_ref[k] = jnp.where(t < DOWN_FIRST, jnp.where(half == c, place, 24 + place), 48)

    @pl.loop(0, 8)
    def _(k):
        t = tile_of[rep * 8 + k]
        is_down = (t >= DOWN_FIRST) & (t < PROJ_FIRST)
        is_proj = (t >= PROJ_FIRST) & (t < VEC_TILE)
        kind = jnp.where(t < DOWN_FIRST, SUMMED, jnp.where(is_down, DOWN, jnp.where(is_proj, PROJ, NONE)))
        kind_ref[k] = jnp.where((t == VEC_TILE) & (x == 0), VEC, kind)
        row_ref[k] = jnp.where(
            is_down, ((t - DOWN_FIRST) * TR + x * 64) // 4, jnp.where(is_proj, (t - PROJ_FIRST) * TR + x * 64, 0)
        )


def plan(owner_list, me):
    smem = pl.BlockSpec(memory_space=pltpu.SMEM)
    sizes = (sum(tiles for tiles, _ in CHUNK_TILES) + 1, 64, 8, 8)
    return pl.pallas_call(
        plan_kernel,
        out_shape=tuple(sds((size,), jnp.int32) for size in sizes),
        in_specs=[smem, smem],
        out_specs=(smem,) * 4,
        scratch_shapes=[pltpu.SMEM((16,), jnp.int32), pltpu.SMEM((128,), jnp.int32), pltpu.SMEM((128,), jnp.int32)],
    )(owner_list, me)


def prepare_kernel(owner_ref, me_ref, master_ref, out_ref, lanes_ref, tile_ref):
    rep = me_ref[Z] * 4 + me_ref[Y] * 2 + me_ref[CORE]
    for s in range(9):
        tile_ref[s] = 0

    def note(t, held):
        here = owner_ref[t] == rep

        @pl.when(here)
        def _():
            tile_ref[held] = t

        return held + jnp.where(here, 1, 0)

    lax.fori_loop(DOWN_FIRST, PROJ_FIRST, note, lax.fori_loop(0, DOWN_FIRST, note, 0))
    for s in range(8):
        down = (tile_ref[s] >= DOWN_FIRST) & (tile_ref[s] < PROJ_FIRST)

        @pl.when(jnp.logical_not(down))
        def _():
            for z in range(4):
                for y in range(2):
                    out_ref[2 * z + y, s] = master_ref[0, s, 16 * z : 16 * z + 16, 384 * y : 384 * y + 384].astype(bf16)

        @pl.when(down)
        def _():
            for k in range(6):
                lanes_ref[k] = master_ref[0, s, :, 128 * k : 128 * k + 128]
            for z in range(4):
                for k in range(6):
                    part = lanes_ref[k, pl.ds(z, 16, stride=4), :]
                    out_ref[2 * z + k // 3, s, :, k % 3 * 128 : k % 3 * 128 + 128] = part.astype(bf16)


def pick_kernel(index_ref, mine_ref, theirs_ref, text_ref, one_ref, two_ref, three_ref):
    def slab(k, ref, j):
        at = index_ref[k]

        @pl.when(at < 64)
        def _():
            ref[j] = mine_ref[at]

        @pl.when(at >= 64)
        def _():
            ref[j] = theirs_ref[at - 64]

    k = 0
    for (tiles, _), (chunk, first) in zip(CHUNK_TILES, CHUNK_AT, strict=True):
        for j in range(tiles):
            slab(k, (one_ref, two_ref, three_ref)[chunk], first + j)
            k += 1
    slab(k, one_ref, 12)
    text = text_ref[...].astype(f32)
    count = text.shape[0]
    text = (text * lax.rsqrt(jnp.sum(text * text, axis=-1, keepdims=True) + unit_eps)).astype(bf16)
    three_ref[14] = jnp.zeros((16, 384), bf16)
    three_ref[14, 0:count, :] = text[:, 0:384]
    three_ref[14, 8 : 8 + count, 0:128] = text[:, 384:512]


class Spread:
    def __init__(self, block):
        self.parts = [block] + [send(block, move) for move in ACROSS_Z]

    def cross_one(self):
        self.ring = jnp.stack(self.parts)
        self.one = send(self.ring, CROSS_ONE)
        self.two = send(self.ring, CROSS_TWO)

    def cross_two(self):
        self.both = send(self.one, CROSS_TWO)
        self.near = [send(v, SWAP_CORE) for v in (self.ring, self.one, self.two)]

    def finish(self):
        self.near.append(send(self.both, SWAP_CORE))

    def arrays(self):
        return (self.ring, self.one, self.two, self.both, *self.near)


def meet(*values):
    return lax.optimization_barrier(values)


def sources(me):
    for other in range(2):
        c = me[CORE] if other == 0 else 1 - me[CORE]
        for crossed in range(4):
            one, two = crossed % 2, crossed // 2
            flip_x = jnp.where(c == 0, one, two)
            flip_y = jnp.where(c == 0, two, one)
            yield c, me[X] + flip_x - 2 * me[X] * flip_x, me[Y] + flip_y - 2 * me[Y] * flip_y


def pick_slabs(master, text_emb, owner_list, me):
    prepared = call(
        prepare_kernel,
        (sds((8, 8, 16, 384), bf16),),
        (owner_list, me, master),
        [whole(master.shape)],
        [whole((8, 8, 16, 384))],
        scratch=[pltpu.VMEM((6, 64, 128), f32), pltpu.SMEM((16,), jnp.int32)],
        prefetch=2,
    )[0]
    pick, place, kind, row = plan(owner_list, me)
    mine = lax.all_to_all(prepared, "rep", 0, 0, axis_index_groups=SAME_CORE).reshape(64, 16, 384)
    blocks = call(
        pick_kernel,
        tuple(sds((slabs, 16, 384), bf16) for slabs in (13, 12, 15)),
        (pick, mine, send(mine, SWAP_CORE), text_emb),
        [whole((64, 16, 384)), whole((64, 16, 384)), whole(text_emb.shape)],
        [whole((slabs, 16, 384)) for slabs in (13, 12, 15)],
        prefetch=1,
    )
    return blocks, place, kind, row


def shards(block_in, tissue, text_emb, text_order, owner_list, master, first_moment, second_moment):
    n_dp = lax.axis_size("dp")
    n_rep = lax.axis_size("rep")
    images = block_in.shape[0]
    slots, part_rows = master.shape[1:3]
    image_total = text_order.shape[0]
    n = images * ROWS
    dp_at, rep_at = lax.axis_index("dp"), lax.axis_index("rep")
    first_image = lax.axis_index(AXES) * images

    x = jnp.pad(block_in, ((0, 0), (0, ROWS - PATCHES), (0, 0))).reshape(n, D)
    valid = jnp.pad((tissue > 0).astype(f32), ((0, 0), (0, ROWS - PATCHES)))
    mask_row = valid[:, None, :]
    col = jnp.broadcast_to(valid.reshape(n, 1), (n, 128))
    numbers = jnp.arange(images, dtype=jnp.int32)
    sel = jnp.where(
        numbers[:, None, None] == jnp.arange(16, dtype=jnp.int32)[None, :, None], valid[:, None, :], 0.0
    ).astype(bf16)
    inv_count = jnp.pad(1.0 / jnp.sum(valid, axis=1), (0, 16 - images))
    inv_count = jnp.broadcast_to(inv_count[:, None], (16, 128))
    order = jnp.broadcast_to(text_order[:, None], (image_total, 128))
    first_image = first_image.astype(jnp.int32)[None]

    fast = (n_dp, n_rep, slots, part_rows) == (2, 16, 8, 64)
    if fast:
        me = jnp.stack([dp_at, rep_at // 4, rep_at // 2 % 2, rep_at % 2]).astype(jnp.int32)
        (block_one, block_two, block_three), place, kind, row = pick_slabs(master, text_emb, owner_list, me)
        x, col, sel, inv_count, order, first_image, block_one = lax.optimization_barrier(
            (x, col, sel, inv_count, order, first_image, block_one)
        )
        one = Spread(block_one)
        *one.parts, block_two, block_three = meet(*one.parts, block_two, block_three)
        two = Spread(block_two)
        one.cross_one()
        one.ring, one.one, one.two, *two.parts, block_three = meet(one.ring, one.one, one.two, *two.parts, block_three)
        one.cross_two()
        three = Spread(block_three)
        one.both, *one.near = meet(one.both, *one.near)
        one.finish()
        near, *two.parts = meet(one.near[3], *two.parts)
        one.near[3] = near
        two.cross_one()
        w_qkv = Weight(one.arrays(), QKV_TILES)
        w_out = Weight(one.arrays(), OUT_TILES, 9)
        a, qkv, vec = qkv_forward(images, x, jnp.zeros((16, D), f32), w_qkv, me)
        qkv, two.ring, two.one, two.two, *three.parts = meet(qkv, two.ring, two.one, two.two, *three.parts)
        two.cross_two()
        three.cross_one()
        o, lse = attention_forward(images, qkv, mask_row)
        o, two.both, *two.near = meet(o, two.both, *two.near)
        two.finish()
        w_up = Weight(two.arrays(), UP_TILES)
        h, m = middle_forward(images, x, o, vec, w_out, me)
        h, m, two.near[3], three.ring, three.one, three.two = meet(h, m, two.near[3], three.ring, three.one, three.two)
        three.cross_two()
        bias_up = vec[7 : 7 + FF // D].reshape(FF // D, 1, D)
        w_up = Weight(two.arrays(), UP_TILES)
        act, slope, act_sum = up_forward(images, m, w_up, bias_up, sel, me)
        act, three.both, *three.near = meet(act, three.both, *three.near)
        three.finish()
        w_down = Weight(three.arrays(), DOWN_TILES, quarters=True)
        w_proj = Weight(three.arrays(), PROJ_TILES, 12)
        all_text = jnp.zeros((16, 128), bf16)
    else:
        me = jnp.zeros((4,), jnp.int32)
        placed = slot_place(owner_list, slots)
        hits = placed[None, :] == jnp.arange(n_rep * slots, dtype=jnp.int32)[:, None]
        tile_ids = jnp.arange(owner_list.shape[0], dtype=jnp.int32)[None, :]
        tile_of_slot = jnp.where(jnp.any(hits, axis=1), jnp.sum(jnp.where(hits, tile_ids, 0), axis=1), 1 << 20)
        text = text_emb.astype(f32)
        own_text = (text * lax.rsqrt(jnp.sum(text * text, axis=-1, keepdims=True) + unit_eps)).astype(bf16)
        all_text = lax.all_gather(own_text, AXES, axis=0, tiled=True)
        tiles = gather_weights(master, placed).reshape(-1, TR, D)
        w_qkv = Weight([tiles[:QKV_TILES]], QKV_TILES)
        w_out = Weight([tiles[QKV_TILES : QKV_TILES + OUT_TILES]], OUT_TILES)
        w_up = Weight([tiles[QKV_TILES + OUT_TILES : DOWN_FIRST]], UP_TILES)
        w_down = Weight([tiles[DOWN_FIRST:PROJ_FIRST].reshape(DOWN_TILES, TR // 4, FF)], DOWN_TILES, quarters=True)
        w_proj = Weight([tiles[PROJ_FIRST:VEC_TILE]], PROJ_TILES)
        a, qkv, vec = qkv_forward(images, x, tiles[VEC_TILE, :16].astype(f32), w_qkv, me)
        bias_up = vec[7 : 7 + FF // D].reshape(FF // D, 1, D)
        o, lse = attention_forward(images, qkv, mask_row)
        h, m = middle_forward(images, x, o, vec, w_out, me)
        act, slope, act_sum = up_forward(images, m, w_up, bias_up, sel, me)
    block_out, pooled = down_forward(images, act, w_down, h, vec, sel, inv_count, me)

    pooled_all = lax.all_to_all(
        jnp.broadcast_to(pooled[None, :images], (n_dp * n_rep, images, D)), AXES, 0, 0
    ).reshape(image_total, D)
    dz_all, rank, spread, hidden = loss_backward(
        me, first_image, pooled_all, all_text, order, w_proj, w_down, inv_count
    )

    def vectors(g_one, g_two, g_bias, g_bias_up):
        parts = [
            g_one[0:2],
            g_two[0:2],
            g_bias[0:1, :D],
            g_bias[0:1, 2 * D :],
            g_two[2:3],
            g_bias_up[0].reshape(FF // D, D),
            g_two[3:4],
            jnp.zeros((16 - 8 - FF // D, D), f32),
        ]
        return jnp.concatenate(parts, axis=0)

    both = jnp.concatenate([rank[:images], act_sum[:images].astype(bf16)], axis=1)
    if fast:
        packed = jnp.concatenate([both[:, at * PACK : (at + 1) * PACK] for at in range(3)], axis=0)
        ranks = Spread(jnp.pad(packed, ((0, 16 - 3 * images), (0, 0))))
        dm, g_bias_up, other, mine = up_backward(images, slope, m, w_up, hidden, col, me)
        dm, other, mine, *ranks.parts = meet(dm, other, mine, *ranks.parts)
        up_sum = PieceSum(other, me)
        ranks.cross_one()
        dh, do, g_out, g_two = middle_backward(images, h, dm, col, spread, o, w_out, vec, me)
        dh, do, up_sum.mine, up_sum.one, ranks.ring, ranks.one, ranks.two = meet(
            dh, do, mine, up_sum.one, ranks.ring, ranks.one, ranks.two
        )
        up_sum.cross_one()
        ranks.cross_two()
        dqkv, g_bias = attention_backward(images, qkv, do, lse, col)
        dqkv, up_sum.two, ranks.both, *ranks.near = meet(dqkv, up_sum.two, ranks.both, *ranks.near)
        up_sum.cross_two()
        ranks.finish()
        other = qkv_weight_grad_fast(images, dqkv, a, g_out, me, True)
        other, dqkv, up_sum.three, ranks.near[3] = meet(other, dqkv, up_sum.three, ranks.near[3])
        qkv_sum = PieceSum(other, me)
        up_sum.cross_z()
        mine = qkv_weight_grad_fast(images, dqkv, a, g_out, me, False)
        dqkv, qkv_sum.mine, qkv_sum.one = meet(dqkv, mine, qkv_sum.one)
        qkv_sum.cross_one()
        input_grad, g_one = input_backward(images, x, dqkv, w_qkv, dh, vec, me)
        vec_sum = vectors(g_one, g_two, g_bias, g_bias_up)
        vec_sum, qkv_sum.two, *up_sum.last = meet(vec_sum, qkv_sum.two, *up_sum.last)
        qkv_sum.cross_two()
        vec_sum += send(vec_sum, SWAP_CORE)
        up_total = up_sum.total()
        vec_sum, up_total, qkv_sum.three = meet(vec_sum, up_total, qkv_sum.three)
        qkv_sum.cross_z()
        vec_sum += send(vec_sum, SWAP_X) + send(vec_sum, SWAP_Y) + send(vec_sum, SWAP_XY)
        g_down, g_proj = rank_grads(images, ranks.arrays(), dz_all, pooled_all)
        vec_sum, g_down, g_proj, *qkv_sum.last = meet(vec_sum, g_down, g_proj, *qkv_sum.last)
        sums = jnp.concatenate([qkv_sum.total()[0], up_total[0]], axis=0).reshape(24, 16, 384)
        vec_total = vec_sum + send(vec_sum, ACROSS_Z[0]) + send(vec_sum, ACROSS_Z[1]) + send(vec_sum, ACROSS_Z[2])
        summed = return_to_owners(sums, place)
    else:
        both_all = lax.all_gather(both, AXES, axis=0, tiled=True)
        dm, g_bias_up, g_up = up_backward(images, slope, m, w_up, hidden, col, me)
        dh, do, g_out, g_two = middle_backward(images, h, dm, col, spread, o, w_out, vec, me)
        dqkv, g_bias = attention_backward(images, qkv, do, lse, col)
        g_qkv = qkv_weight_grad(images, dqkv, a)
        input_grad, g_one = input_backward(images, x, dqkv, w_qkv, dh, vec, me)
        vec_total = vectors(g_one, g_two, g_bias, g_bias_up)
        mine = lax.dynamic_slice_in_dim(tile_of_slot, rep_at * slots, slots)
        first_row = dp_at * part_rows
        is_down = (mine >= DOWN_FIRST) & (mine < PROJ_FIRST)
        is_proj = (mine >= PROJ_FIRST) & (mine < VEC_TILE)
        kind = jnp.where(is_down, DOWN, jnp.where(is_proj, PROJ, jnp.where(mine <= VEC_TILE, SUMMED, NONE)))
        kind = kind.astype(jnp.int32)
        each = part_rows * D // FF
        row = jnp.where(is_proj, (mine - PROJ_FIRST) * TR + first_row, 0)
        down_rows = jnp.clip(((mine - DOWN_FIRST) * TR + first_row) * D // FF, 0, D - each)
        g_down = tn(both_all[:, :D], both_all[:, D:])
        g_down = jnp.stack([lax.dynamic_slice_in_dim(g_down, at, each) for at in down_rows])
        g_down = jnp.pad(g_down, ((0, 0), (0, max(0, 8 - each)), (0, 0)))
        g_proj = tn(dz_all, pooled_all)
        last = jnp.pad(vec_total, ((0, TR - 16), (0, 0))).astype(bf16)
        tiles = jnp.concatenate([g_qkv, g_out, g_up, last], axis=0).reshape(-1, TR, D)
        index = jnp.where(tile_of_slot == VEC_TILE, DOWN_FIRST, jnp.where(tile_of_slot < DOWN_FIRST, tile_of_slot, 1 << 20))
        summed = scatter_grads(tiles, index, slots, part_rows)
    new_master, new_first, new_second = adam(
        kind, row, master, first_moment, second_moment, summed, g_down, g_proj, vec_total, fast
    )
    return block_out, input_grad, new_master, new_first, new_second


def solution(mesh):
    in_specs = (
        P(("dp", "rep"), None, None),
        P(("dp", "rep"), None),
        P(("dp", "rep"), None),
        P(),
        P(),
        P("rep", None, "dp", None),
        P("rep", None, "dp", None),
        P("rep", None, "dp", None),
    )
    out_specs = (
        P(("dp", "rep"), None, None),
        P(("dp", "rep"), None, None),
        P("rep", None, "dp", None),
        P("rep", None, "dp", None),
        P("rep", None, "dp", None),
    )
    return jax.shard_map(shards, mesh=mesh, in_specs=in_specs, out_specs=out_specs, check_vma=False)
```

```python
import functools

import jax
import jax.numpy as jnp
from jax import lax
from jax.experimental import pallas as pl
from jax.experimental.pallas import tpu as pltpu
from jax.sharding import PartitionSpec as P

D = 768
HEADS = 12
HEAD = 64
FF = 3072
EMB = 512
PATCHES = 196
STEP = 10
ROWS = 208
TR = 128

logit_scale = 50.0
learn_rate = 0.03
beta_one = 0.9
beta_two = 0.999
adam_eps = 1e-08
decay_rate = 0.05
norm_eps = 1e-05
unit_eps = 1e-06
masked_score = -1000000000.0

bf16 = jnp.bfloat16
f32 = jnp.float32
AXES = ("dp", "rep")
MIB = 1 << 20

X, Z, Y, CORE = range(4)
PIECES = [(x, z, y) for x in range(2) for z in range(4) for y in range(2)]

QKV_TILES = 3 * D // TR
OUT_TILES = D // TR
UP_TILES = FF // TR
DOWN_TILES = FF // TR
PROJ_TILES = EMB // TR
DOWN_FIRST = QKV_TILES + OUT_TILES + UP_TILES
PROJ_FIRST = DOWN_FIRST + DOWN_TILES
VEC_TILE = PROJ_FIRST + PROJ_TILES
PACK = (D + FF) // 3
CHUNK_TILES = (
    (QKV_TILES // 2, 0),
    (OUT_TILES // 2, QKV_TILES),
    (UP_TILES // 2, QKV_TILES + OUT_TILES),
    (DOWN_TILES // 2, DOWN_FIRST),
    (PROJ_TILES // 2, PROJ_FIRST),
)
CHUNK_AT = ((0, 0), (0, 9), (1, 0), (2, 0), (2, 12))
SAME_CORE = [[i * 2 + c for i in range(8)] for c in range(2)]


def nn(a, b):
    return lax.dot_general(a, b, (((1,), (0,)), ((), ())), preferred_element_type=f32)


def nt(a, b):
    return lax.dot_general(a, b, (((1,), (1,)), ((), ())), preferred_element_type=f32)


def tn(a, b):
    return lax.dot_general(a, b, (((0,), (0,)), ((), ())), preferred_element_type=f32)


def call(kernel, outs, ins, in_specs, out_specs, grid=None, scratch=(), flops=0, vmem=24, prefetch=0, in_hbm=()):
    ins = [
        pltpu.with_memory_space_constraint(a, pltpu.HBM) if k >= prefetch and (s.memory_space is pltpu.HBM or k in in_hbm) else a
        for k, (a, s) in enumerate(zip(ins, [None] * prefetch + list(in_specs), strict=True))
    ]
    moved = sum(a.size * a.dtype.itemsize for a in ins) + sum(o.size * o.dtype.itemsize for o in outs)
    params = pltpu.CompilerParams(
        vmem_limit_bytes=vmem * MIB,
        dimension_semantics=("arbitrary",) * len(grid or ()) or None,
    )
    return pl.pallas_call(
        kernel,
        out_shape=tuple(outs),
        grid_spec=pltpu.PrefetchScalarGridSpec(
            num_scalar_prefetch=prefetch,
            grid=grid or (1,),
            in_specs=in_specs,
            out_specs=tuple(out_specs),
            scratch_shapes=list(scratch),
        ),
        compiler_params=params,
        cost_estimate=pl.CostEstimate(flops=int(flops), bytes_accessed=int(moved), transcendentals=0),
    )(*ins)


def whole(shape):
    return pl.BlockSpec(shape, lambda *_: (0,) * len(shape))


def rows_at(rows, cols):
    return pl.BlockSpec((rows, cols), lambda i, *_: (i, 0))


def cols_at(rows, cols):
    return pl.BlockSpec((rows, cols), lambda i, *_: (0, i))


def sds(shape, dtype):
    return jax.ShapeDtypeStruct(shape, dtype)


class Weight:
    def __init__(self, arrays, tiles, first=0, quarters=False):
        self.arrays, self.tiles, self.first, self.quarters = tuple(arrays), tiles, first, quarters
        self.pieces = len(arrays) > 1
        self.specs = [pl.BlockSpec(memory_space=pltpu.HBM)] * len(arrays)
        shape = (tiles, TR // 4, FF) if quarters else (tiles, TR, D)
        self.scratch = [pltpu.VMEM(shape, bf16), pltpu.SemaphoreType.DMA((32 if self.pieces else 1,))]

    def copies(self, me, refs, out, sems):
        if not self.pieces:
            return [lambda: pltpu.make_async_copy(refs[0], out, sems.at[0])]
        copies = []
        half = self.tiles // 2
        for at, (c, x, y) in enumerate(sources(me)):
            for back in range(4):
                z = me[Z] ^ back
                if self.quarters:
                    row, col = x * 16, z * D + y * 384
                else:
                    row, col = x * 64 + z * 16, y * 384
                rows = pl.ds(pl.multiple_of(row, 16), 16)
                cols = pl.ds(pl.multiple_of(col, 128), 384)
                source = refs[at].at[back, pl.ds(self.first, half)]
                place = out.at[pl.ds(half * c, half), rows, cols]
                copies.append(functools.partial(pltpu.make_async_copy, source, place, sems.at[len(copies)]))
        return copies

    def start(self, me, refs, out, sems):
        for copy in self.copies(me, refs, out, sems):
            copy().start()

    def wait(self, me, refs, out, sems, part=None, parts=1):
        copies = self.copies(me, refs, out, sems)
        if part is not None and not self.pieces:
            copies = copies if part == 0 else []
        elif part is not None:
            copies = copies[16 * part : 16 * part + 16] if parts == 2 else copies[part::4]
        for copy in copies:
            copy().wait()

    def load(self, me, refs, out, sems):
        @pl.when(pl.program_id(0) == 0)
        def _():
            self.start(me, refs, out, sems)
            self.wait(me, refs, out, sems)


def normalized(x):
    center = x - jnp.mean(x, axis=-1, keepdims=True)
    spread = jnp.mean(center * center, axis=-1, keepdims=True)
    inverse = lax.rsqrt(spread + norm_eps)
    return center * inverse, inverse


def norm_back(grad, hat, inverse, gain):
    scaled = grad * gain
    first = jnp.mean(scaled, axis=-1, keepdims=True)
    second = jnp.mean(scaled * hat, axis=-1, keepdims=True)
    return inverse * (scaled - first - hat * second)


def accumulate(i, ref, value):
    @pl.when(i == 0)
    def _():
        ref[...] = value

    @pl.when(i > 0)
    def _():
        ref[...] += value


def column_sum(x):
    return jnp.sum(x, axis=0, keepdims=True)


def qkv_block(j, me):
    return jnp.where(me[CORE] == 0, j, 2 - j)


def qkv_kernel(images, weight, me_ref, *refs):
    count = len(weight.arrays)
    pieces = refs[:count]
    x_ref, vec_in_ref, a_ref, qkv_ref, vec_ref, w_ref, sems, vec_half, vec_sems = refs[count:]
    j = pl.program_id(0)

    @pl.when(j == 0)
    def _():
        weight.start(me_ref, pieces, w_ref, sems)
        if weight.pieces:
            parts = []
            for at, (_, x, y) in list(enumerate(sources(me_ref)))[:4]:
                for back in range(4):
                    copy = pltpu.make_async_copy(pieces[at].at[back, 12], vec_half.at[y], vec_sems.at[len(parts)])
                    parts.append(((x == 0) & ((me_ref[Z] ^ back) == 0), copy))
            for here, copy in parts:
                pl.when(here)(copy.start)
            for here, copy in parts:
                pl.when(here)(copy.wait)
            vec_ref[...] = jnp.concatenate([vec_half[0], vec_half[1]], axis=1).astype(f32)
        else:
            vec_ref[...] = vec_in_ref[...]
        for i in range(images):
            hat, _ = normalized(x_ref[pl.ds(i * ROWS, ROWS), :].astype(f32))
            a_ref[pl.ds(i * ROWS, ROWS), :] = (hat * vec_ref[0:1, :] + vec_ref[1:2, :]).astype(bf16)
        weight.wait(me_ref, pieces, w_ref, sems, 0, 2)

    @pl.when(j == 1)
    def _():
        weight.wait(me_ref, pieces, w_ref, sems, 1, 2)

    j = qkv_block(j, me_ref)
    bias = jnp.where(j == 0, vec_ref[4:5, :], jnp.where(j == 2, vec_ref[5:6, :], 0.0))
    scale = jnp.where(j == 0, f32(HEAD**-0.5), f32(1.0))
    w = w_ref[pl.ds(6 * j, 6)].reshape(D, D)
    qkv_ref[...] = ((nt(a_ref[...], w) + bias) * scale).astype(bf16)


def qkv_forward(images, x, vec, weight, me):
    n = images * ROWS
    return call(
        functools.partial(qkv_kernel, images, weight),
        (sds((n, D), bf16), sds((n, 3 * D), bf16), sds((16, D), f32)),
        (me, *weight.arrays, x, vec),
        weight.specs + [whole((n, D)), whole((16, D))],
        [whole((n, D)), pl.BlockSpec((n, D), lambda j, me: (0, qkv_block(j, me))), whole((16, D))],
        grid=(3,),
        scratch=weight.scratch + [pltpu.VMEM((2, 16, 384), bf16), pltpu.SemaphoreType.DMA((16,))],
        flops=2 * n * D * 3 * D,
        prefetch=1,
    )


def attention_kernel(qkv_ref, mask_ref, o_ref, lse_ref):
    lane = lax.broadcasted_iota(jnp.int32, (ROWS, 2 * HEAD), 1)
    low_half = lane < HEAD
    valid = mask_ref[0] > 0.0
    lse_all = jnp.zeros((ROWS, 128), f32)
    for pair in range(HEADS // 2):
        at = pair * 2 * HEAD
        q = qkv_ref[:, at : at + 2 * HEAD]
        k = qkv_ref[:, D + at : D + at + 2 * HEAD]
        v = qkv_ref[:, 2 * D + at : 2 * D + at + 2 * HEAD]
        mixed = []
        for half in range(2):
            keep = low_half if half == 0 else jnp.logical_not(low_half)
            s = nt(q, jnp.where(keep, k, jnp.zeros_like(k)))
            s = jnp.where(valid, s, masked_score)
            top = jnp.max(s, axis=-1, keepdims=True)
            e = jnp.exp(s - top)
            total = jnp.sum(e, axis=-1, keepdims=True)
            p = e * (1.0 / total)
            mixed.append(nn(p.astype(bf16), v))
            lse_all = jnp.where(lane == 2 * pair + half, top + jnp.log(total), lse_all)
        o_ref[:, at : at + 2 * HEAD] = jnp.where(low_half, mixed[0], mixed[1]).astype(bf16)
    lse_ref[0] = jnp.transpose(lse_all)[0:16, :]


def attention_forward(images, qkv, mask_row):
    n = images * ROWS
    return call(
        attention_kernel,
        (sds((n, D), bf16), sds((images, 16, ROWS), f32)),
        (qkv, mask_row),
        [rows_at(ROWS, 3 * D), pl.BlockSpec((1, 1, ROWS), lambda i: (i, 0, 0))],
        [rows_at(ROWS, D), pl.BlockSpec((1, 16, ROWS), lambda i: (i, 0, 0))],
        grid=(images,),
        flops=4 * n * ROWS * D,
    )


def middle_kernel(weight, me_ref, *refs):
    count = len(weight.arrays)
    x_ref, o_ref, vec_ref, h_ref, m_ref, w_ref, sems = refs[count:]
    weight.load(me_ref, refs[:count], w_ref, sems)
    part = nt(o_ref[...], w_ref[...].reshape(D, D)) + vec_ref[6:7, :]
    middle = x_ref[...].astype(f32) + part
    h_ref[...] = middle
    hat, _ = normalized(middle)
    m_ref[...] = (hat * vec_ref[2:3, :] + vec_ref[3:4, :]).astype(bf16)


def middle_forward(images, x, o, vec, weight, me):
    n = images * ROWS
    return call(
        functools.partial(middle_kernel, weight),
        (sds((n, D), f32), sds((n, D), bf16)),
        (me, *weight.arrays, x, o, vec),
        weight.specs + [rows_at(ROWS, D), rows_at(ROWS, D), whole((16, D))],
        [rows_at(ROWS, D), rows_at(ROWS, D)],
        grid=(images,),
        scratch=weight.scratch,
        flops=2 * n * D * D,
        prefetch=1,
    )


def gelu_parts(u):
    size = jnp.abs(u)
    t = 1.0 / (1.0 + 0.23164189 * size)
    poly = t * (0.127414796 + t * (-0.142248368 + t * (0.7107068705 + t * (-0.7265760135 + t * 0.5307027145))))
    e = jnp.exp2(u * u * -0.7213475204444817)
    act = jnp.maximum(u, 0.0) - size * (poly * e)
    w = e * (poly - 0.3989422804014327 * size)
    return act, jnp.where(u >= 0.0, 1.0 - w, w)


def own_block(j, me):
    return (j // 2 + me[CORE]) % 2 * 2 + j % 2


def up_kernel(images, weight, me_ref, *refs):
    count = len(weight.arrays)
    m_ref, bias_ref, act_ref, slope_ref, w_ref, sems = refs[count:]
    j = pl.program_id(0)

    @pl.when(j == 0)
    def _():
        weight.start(me_ref, refs[:count], w_ref, sems)
        weight.wait(me_ref, refs[:count], w_ref, sems, 0, 2)

    @pl.when(j == 2)
    def _():
        weight.wait(me_ref, refs[:count], w_ref, sems, 1, 2)

    w = w_ref[pl.ds(6 * own_block(j, me_ref), 6)].reshape(D, D)
    for i in range(images):
        at = pl.ds(i * ROWS, ROWS)
        act, slope = gelu_parts(nt(m_ref[at, :], w) + bias_ref[0])
        act_ref[at, :] = act.astype(bf16)
        slope_ref[at, :] = slope.astype(bf16)


def up_forward(images, m, weight, bias, me):
    n = images * ROWS
    cols = pl.BlockSpec((n, D), lambda j, me: (0, own_block(j, me)))
    return call(
        functools.partial(up_kernel, images, weight),
        (sds((n, FF), bf16), sds((n, FF), bf16)),
        (me, *weight.arrays, m, bias),
        weight.specs + [whole((n, D)), pl.BlockSpec((1, 1, D), lambda j, me: (own_block(j, me), 0, 0))],
        [cols, cols],
        grid=(FF // D,),
        scratch=weight.scratch,
        flops=2 * n * D * FF,
        prefetch=1,
    )


def act_sum_kernel(images, act_ref, sel_ref, sum_ref):
    total = jnp.zeros(sum_ref.shape, f32)
    for i in range(images):
        total += nn(sel_ref[i], act_ref[pl.ds(i * ROWS, ROWS), :])
    sum_ref[...] = total.astype(bf16)


def act_sums(images, act, sel):
    n = images * ROWS
    return call(
        functools.partial(act_sum_kernel, images),
        (sds((16, FF), bf16),),
        (act, sel),
        [cols_at(n, D), whole((images, 16, ROWS))],
        [cols_at(16, D)],
        grid=(FF // D,),
        flops=32 * n * FF,
    )[0]


def down_kernel(images, weight, me_ref, *refs):
    count = len(weight.arrays)
    act_ref, h_ref, vec_ref, sel_ref, inv_ref, out_ref, pooled_ref, w_ref, sems, sum_ref, y_ref = refs[count:]
    k = pl.program_id(0)
    quarters = FF // D

    @pl.when(k == 0)
    def _():
        weight.start(me_ref, refs[:count], w_ref, sems)

    for part in range(quarters):

        @pl.when(k == part)
        def _():
            weight.wait(me_ref, refs[:count], w_ref, sems, part, quarters)

    @pl.when(k < quarters)
    def _():
        cols = pl.ds(pl.multiple_of((me_ref[Z] ^ k) * D, 128), D)
        accumulate(k, y_ref, nt(act_ref[...], w_ref[:, :, cols].reshape(D, D)))

    @pl.when(k >= quarters)
    def _():
        i = k - quarters
        y = y_ref[pl.ds(pl.multiple_of(i * ROWS, 16), ROWS), :] + vec_ref[11:12, :]
        out = (h_ref[...] + y).astype(bf16)
        out_ref[0] = out[0:PATCHES, :]
        accumulate(i, sum_ref, nn(sel_ref[0], out))
        pooled_ref[...] = (sum_ref[...] * inv_ref[:, 0:1]).astype(bf16)


def down_forward(images, act, weight, h, vec, sel, inv_count, me):
    n = images * ROWS
    quarters = FF // D

    def image(k):
        return jnp.maximum(k - quarters, 0)

    return call(
        functools.partial(down_kernel, images, weight),
        (sds((images, PATCHES, D), bf16), sds((16, D), bf16)),
        (me, *weight.arrays, act, h, vec, sel, inv_count),
        weight.specs
        + [
            pl.BlockSpec((n, D), lambda k, me: (0, me[Z] ^ jnp.minimum(k, quarters - 1))),
            pl.BlockSpec((ROWS, D), lambda k, me: (image(k), 0)),
            whole((16, D)),
            pl.BlockSpec((1, 16, ROWS), lambda k, me: (image(k), 0, 0)),
            whole((16, 128)),
        ],
        [pl.BlockSpec((1, PATCHES, D), lambda k, me: (image(k), 0, 0)), whole((16, D))],
        grid=(quarters + images,),
        scratch=weight.scratch + [pltpu.VMEM((16, D), f32), pltpu.VMEM((n, D), f32)],
        flops=2 * n * D * FF,
        prefetch=1,
    )


def loss_kernel(total_images, proj, down, me_ref, first_ref, *refs):
    count = len(proj.arrays)
    pieces = refs[:count]
    if proj.pieces:
        down_pieces, rest = pieces, refs[count:]
    else:
        down_pieces, rest = refs[count : count + 1], refs[count + 1 :]
    text_ref, pooled_ref, order_ref, inv_ref, dz_ref, rank_ref, spread_ref, hidden_ref, all_ref = rest[:9]
    proj_ref, proj_sems, down_ref, down_sems, rows_ref = rest[9:14]
    down_copies = down.copies(me_ref, down_pieces, down_ref, down_sems)
    proj_copies = proj.copies(me_ref, pieces, proj_ref, proj_sems)
    if proj.pieces:
        slab_ref, slab_sems = rest[14:]
        for at, (c, x, y) in enumerate(sources(me_ref)):
            for back in range(4):
                device = x * 16 + (me_ref[Z] ^ back) * 4 + y * 2 + c
                out = slab_ref.at[pl.ds(pl.multiple_of(device * 16, 16), 16)]
                source = pieces[at].at[back, 14]
                proj_copies.append(
                    functools.partial(pltpu.make_async_copy, source, out, slab_sems.at[at * 4 + back])
                )
    for copy in proj_copies + down_copies:
        copy().start()
    for copy in proj_copies:
        copy().wait()
    if proj.pieces:
        images = total_images // 32
        shape = (total_images, 512)
        row = lax.broadcasted_iota(jnp.int32, shape, 0)
        col = lax.broadcasted_iota(jnp.int32, shape, 1)
        start = row // images * 16 + row % images
        held = slab_ref[...]
        left = nn(jnp.where(col == start, 1.0, 0.0).astype(bf16), held)
        right = nn(jnp.where(col == start + 8, 1.0, 0.0).astype(bf16), held[:, 0:128])
        text = jnp.concatenate([left, right], axis=1).astype(bf16)
    else:
        text = text_ref[...]
    proj_w = proj_ref[...].reshape(EMB, D)
    each = total_images // pooled_ref.shape[0]
    for d in range(pooled_ref.shape[0]):
        rows_ref[d * each : d * each + each, :] = pooled_ref[d].astype(f32)
    pooled = rows_ref[...].astype(bf16)
    all_ref[...] = pooled
    z = nt(pooled, proj_w)
    square = jnp.sum(z * z, axis=-1, keepdims=True) + unit_eps
    inverse = lax.rsqrt(square)
    image = (z * inverse).astype(bf16)
    s = logit_scale * nt(image, text)
    shape = (total_images, total_images)
    hit = jnp.where(order_ref[:, 0:1] == lax.broadcasted_iota(jnp.int32, shape, 1), 1.0, 0.0)
    part = 1.0 / (2.0 * total_images)

    def grad_of(axis):
        top = jnp.max(s, axis=axis, keepdims=True)
        lse = top + jnp.log(jnp.sum(jnp.exp(s - top), axis=axis, keepdims=True))
        return ((jnp.exp(s - lse) - hit) * part).astype(bf16)

    de = logit_scale * (nn(grad_of(1), text) + nn(grad_of(0), text))
    dz = inverse * de - z * (inverse * inverse * inverse * jnp.sum(z * de, axis=-1, keepdims=True))
    dz = dz.astype(bf16)
    dz_ref[...] = dz
    pick = lax.broadcasted_iota(jnp.int32, (16, total_images), 1) == (
        first_ref[0] + lax.broadcasted_iota(jnp.int32, (16, total_images), 0)
    )
    own = nn(jnp.where(pick, 1.0, 0.0).astype(bf16), dz).astype(bf16)
    spread = nn(own, proj_w) * inv_ref[:, 0:1]
    spread_ref[...] = spread
    rank = spread.astype(bf16)
    rank_ref[...] = rank
    for copy in down_copies:
        copy().wait()
    hidden_ref[...] = nn(rank, down_ref[...].reshape(D, FF))


def loss_backward(me, first, pooled, text, order, proj, down, inv_count):
    total = pooled.shape[0] * pooled.shape[1]
    if proj.pieces:
        arrays, extra = proj.arrays, [pltpu.VMEM((512, 384), bf16), pltpu.SemaphoreType.DMA((32,))]
    else:
        arrays, extra = proj.arrays + down.arrays, []
    return call(
        functools.partial(loss_kernel, total, proj, down),
        (sds((total, EMB), bf16), sds((16, D), bf16), sds((16, D), f32), sds((16, FF), f32), sds((total, D), bf16)),
        (me, first, *arrays, text, pooled, order, inv_count),
        [pl.BlockSpec(memory_space=pltpu.HBM)] * len(arrays)
        + [whole(text.shape), whole(pooled.shape), whole((total, 128)), whole((16, 128))],
        [whole((total, EMB)), whole((16, D)), whole((16, D)), whole((16, FF)), whole((total, D))],
        scratch=proj.scratch + down.scratch + [pltpu.VMEM((total, D), f32)] + extra,
        flops=6 * total * total * EMB + 2 * total * D * EMB + 32 * D * FF,
        vmem=32,
        prefetch=2,
    )


def weave(ref, value):
    for t in range(value.shape[0] // TR):
        for x, z, y in PIECES:
            row = t * TR + x * 64 + z * 16
            ref[x * 8 + z * 2 + y, pl.ds(t * 16, 16), :] = value[row : row + 16, y * 384 : y * 384 + 384]


def half_block(j, me):
    return (j // 2 + 1 - me[CORE]) % 2 * 2 + j % 2


SPLIT = 528


def up_back_kernel(images, weight, me_ref, *refs):
    count = len(weight.arrays)
    slope_ref, m_ref, hidden_ref, col_ref, dm_ref, db_ref = refs[count : count + 6]
    w_ref, sems, du_ref = refs[-3:]
    j = pl.program_id(0)
    blocks = FF // D

    @pl.when(j == 0)
    def _():
        weight.start(me_ref, refs[:count], w_ref, sems)

    @pl.when(j < blocks)
    def _():
        cols = pl.ds(pl.multiple_of(half_block(j, me_ref) * D, 128), D)
        total = jnp.zeros((1, D), f32)
        for i in range(images):
            at = pl.ds(i * ROWS, ROWS)
            du = (slope_ref[at, :].astype(f32) * (col_ref[at, 0:1] * hidden_ref[i : i + 1, :])).astype(bf16)
            du_ref[at, cols] = du
            total += column_sum(du.astype(f32))
        db_ref[...] = jnp.broadcast_to(total, db_ref.shape)
        dw = tn(du_ref[pl.ds(0, images * ROWS), cols], m_ref[...]).astype(bf16)
        if not weight.pieces:
            refs[count + 6][...] = dw
            return
        send_ref, keep_ref = refs[count + 6 : count + 8]

        @pl.when(j < 2)
        def _():
            weave(send_ref, dw)

        @pl.when(j >= 2)
        def _():
            weave(keep_ref, dw)

    @pl.when(j == blocks)
    def _():
        weight.wait(me_ref, refs[:count], w_ref, sems)

    @pl.when(j >= blocks)
    def _():
        rows = pl.ds(pl.multiple_of((j - blocks) * SPLIT, 16), SPLIT)
        dm_ref[...] = nn(du_ref[rows, :], w_ref[...].reshape(FF, D))


def up_backward(images, slope, m, weight, hidden, col, me):
    n = images * ROWS
    blocks = FF // D
    steps = -(-n // SPLIT)

    def block(j, me):
        return half_block(jnp.minimum(j, blocks - 1), me)

    def cols(rows):
        return pl.BlockSpec((rows, D), lambda j, me: (0, block(j, me)))

    if weight.pieces:
        shapes = (sds((16, 192, 384), bf16),) * 2
        specs = [
            pl.BlockSpec((16, 96, 384), lambda j, me: (0, jnp.minimum(j, 1), 0)),
            pl.BlockSpec((16, 96, 384), lambda j, me: (0, jnp.clip(j - 2, 0, 1), 0)),
        ]
    else:
        shapes = (sds((FF, D), bf16),)
        specs = [pl.BlockSpec((D, D), lambda j, me: (block(j, me), 0))]
    return call(
        functools.partial(up_back_kernel, images, weight),
        (sds((n, D), f32), sds((8, FF), f32)) + shapes,
        (me, *weight.arrays, slope, m, hidden, col),
        weight.specs + [cols(n), whole((n, D)), cols(16), whole((n, 128))],
        [pl.BlockSpec((SPLIT, D), lambda j, me: (jnp.maximum(j - blocks, 0), 0)), cols(8)] + specs,
        grid=(blocks + steps,),
        vmem=40,
        scratch=weight.scratch + [pltpu.VMEM((steps * SPLIT, FF), bf16)],
        flops=4 * n * D * FF,
        prefetch=1,
    )


def middle_back_kernel(images, weight, me_ref, *refs):
    count = len(weight.arrays)
    h_ref, dm_ref, col_ref, spread_ref, o_ref, vec_ref = refs[count : count + 6]
    dh_ref, do_ref, dw_ref, dvec_ref, w_ref, sems, dat_ref = refs[count + 6 :]
    i = pl.program_id(0)

    @pl.when(i == 0)
    def _():
        weight.start(me_ref, refs[:count], w_ref, sems)

    @pl.when(i < images)
    def _():
        hat, inverse = normalized(h_ref[...])
        dm = dm_ref[...]
        part = norm_back(dm, hat, inverse, vec_ref[2:3, :])
        here = spread_ref[pl.ds(i, 1), :]
        dh = col_ref[:, 0:1] * here + part
        dh_ref[...] = dh
        dat = dh.astype(bf16)
        dat_ref[pl.ds(pl.multiple_of(i * ROWS, 16), ROWS), :] = dat
        sums = jnp.concatenate(
            [
                column_sum(dm * hat),
                column_sum(dm),
                column_sum(dat.astype(f32)),
                column_sum(col_ref[:, 0:1]) * here.astype(bf16).astype(f32),
                jnp.zeros((4, D), f32),
            ],
            axis=0,
        )
        accumulate(i, dvec_ref, sums)

    @pl.when(i == images)
    def _():
        dw = tn(dat_ref[...], o_ref[...]).astype(bf16)
        if weight.pieces:
            for half in range(2):
                weave(dw_ref.at[half], dw[half * 384 : half * 384 + 384])
        else:
            dw_ref[...] = dw
        weight.wait(me_ref, refs[:count], w_ref, sems)
        do_ref[...] = nn(dat_ref[...], w_ref[...].reshape(D, D)).astype(bf16)


def middle_backward(images, h, dm, col, spread, o, weight, vec, me):
    n = images * ROWS
    dw_shape = (2, 16, 48, 384) if weight.pieces else (D, D)

    def rows(cols):
        return pl.BlockSpec((ROWS, cols), lambda i, me: (jnp.minimum(i, images - 1), 0))

    return call(
        functools.partial(middle_back_kernel, images, weight),
        (sds((n, D), f32), sds((n, D), bf16), sds(dw_shape, bf16), sds((8, D), f32)),
        (me, *weight.arrays, h, dm, col, spread, o, vec),
        weight.specs + [rows(D), rows(D), rows(128), whole((16, D)), whole((n, D)), whole((16, D))],
        [rows(D), whole((n, D)), whole(dw_shape), whole((8, D))],
        grid=(images + 1,),
        scratch=weight.scratch + [pltpu.VMEM((n, D), bf16)],
        flops=4 * n * D * D,
        prefetch=1,
    )


def attention_again_kernel(qkv_ref, lse_ref, col_ref, p_ref):
    low_half = lax.broadcasted_iota(jnp.int32, (ROWS, 2 * HEAD), 1) < HEAD
    valid = jnp.broadcast_to(col_ref[:, 0:1], (ROWS, ROWS)) > 0.0
    for pair in range(HEADS // 2):
        at = pair * 2 * HEAD
        q = qkv_ref[:, at : at + 2 * HEAD]
        k = qkv_ref[:, D + at : D + at + 2 * HEAD]
        for half in range(2):
            keep = low_half if half == 0 else jnp.logical_not(low_half)
            head = 2 * pair + half
            s = jnp.where(valid, nt(jnp.where(keep, k, jnp.zeros_like(k)), q), masked_score)
            p_ref[0, head] = jnp.exp(s - lse_ref[0, head : head + 1, :]).astype(bf16)


def attention_again(images, qkv, lse, col):
    n = images * ROWS
    return call(
        attention_again_kernel,
        (sds((images, HEADS, ROWS, ROWS), bf16),),
        (qkv, lse, col),
        [rows_at(ROWS, 3 * D), pl.BlockSpec((1, 16, ROWS), lambda i: (i, 0, 0)), rows_at(ROWS, 128)],
        [pl.BlockSpec((1, HEADS, ROWS, ROWS), lambda i: (i, 0, 0, 0))],
        grid=(images,),
        flops=2 * n * ROWS * D,
    )[0]


def attention_back_kernel(qkv_ref, do_ref, p_ref, dqkv_ref, db_ref):
    i = pl.program_id(0)
    low_half = lax.broadcasted_iota(jnp.int32, (ROWS, 2 * HEAD), 1) < HEAD
    for pair in range(HEADS // 2):
        at = pair * 2 * HEAD
        q = qkv_ref[:, at : at + 2 * HEAD]
        k = qkv_ref[:, D + at : D + at + 2 * HEAD]
        v = qkv_ref[:, 2 * D + at : 2 * D + at + 2 * HEAD]
        do = do_ref[:, at : at + 2 * HEAD]
        dv, dk, dq = [], [], []
        for half in range(2):
            keep = low_half if half == 0 else jnp.logical_not(low_half)
            only_k = jnp.where(keep, k, jnp.zeros_like(k))
            only_v = jnp.where(keep, v, jnp.zeros_like(v))
            head = 2 * pair + half
            rounded = p_ref[0, head]
            p = rounded.astype(f32)
            dp = nt(only_v, do)
            share = jnp.sum(p * dp, axis=0, keepdims=True)
            ds = (p * (dp - share)).astype(bf16)
            dv.append(nn(rounded, do))
            dk.append(nn(ds, q))
            dq.append(tn(ds, only_k))
        dqkv_ref[:, at : at + 2 * HEAD] = ((dq[0] + dq[1]) * (HEAD**-0.5)).astype(bf16)
        dqkv_ref[:, D + at : D + at + 2 * HEAD] = jnp.where(low_half, dk[0], dk[1]).astype(bf16)
        dqkv_ref[:, 2 * D + at : 2 * D + at + 2 * HEAD] = jnp.where(low_half, dv[0], dv[1]).astype(bf16)
    accumulate(i, db_ref, nn(jnp.ones((16, ROWS), bf16), dqkv_ref[...]))


def attention_backward(images, qkv, do, p):
    n = images * ROWS
    return call(
        attention_back_kernel,
        (sds((n, 3 * D), bf16), sds((16, 3 * D), f32)),
        (qkv, do, p),
        [
            rows_at(ROWS, 3 * D),
            rows_at(ROWS, D),
            pl.BlockSpec((1, HEADS, ROWS, ROWS), lambda i: (i, 0, 0, 0)),
        ],
        [rows_at(ROWS, 3 * D), whole((16, 3 * D))],
        grid=(images,),
        flops=10 * n * ROWS * D,
    )


def qkv_grad_kernel(dqkv_ref, a_ref, dw_ref):
    dw_ref[...] = tn(dqkv_ref[...], a_ref[...]).astype(bf16)


def qkv_weight_grad(images, dqkv, a):
    n = images * ROWS
    return call(
        qkv_grad_kernel,
        (sds((3 * D, D), bf16),),
        (dqkv, a),
        [cols_at(n, D), whole((n, D))],
        [rows_at(D, D)],
        grid=(3,),
        flops=6 * n * D * D,
    )[0]


def qkv_grad_fast_kernel(_, dqkv_ref, a_ref, out_ref, pieces_ref):
    j = pl.program_id(0)

    @pl.when(j < 3)
    def _():
        weave(pieces_ref, tn(dqkv_ref[...], a_ref[...]).astype(bf16))

    @pl.when(j == 3)
    def _():
        pieces_ref[...] = out_ref[0]


def qkv_weight_grad_fast(images, dqkv, a, dw_out, me, other):
    n = images * ROWS

    def half(me):
        return 1 - me[CORE] if other else me[CORE]

    return call(
        qkv_grad_fast_kernel,
        (sds((16, 192, 384), bf16),),
        (me, dqkv, a, dw_out),
        [
            pl.BlockSpec((n, 384), lambda j, me: (0, half(me) * 3 + jnp.minimum(j, 2))),
            whole((n, D)),
            pl.BlockSpec((1, 16, 48, 384), lambda j, me: (half(me), 0, 0, 0)),
        ],
        [pl.BlockSpec((16, 48, 384), lambda j, me: (0, j, 0))],
        grid=(4,),
        flops=3 * n * D * D,
        prefetch=1,
    )[0]


def input_back_kernel(weight, me_ref, *refs):
    count = len(weight.arrays)
    x_ref, dqkv_ref, dh_ref, vec_ref, two_ref, bias_ref, up_ref, out_ref, dvec_ref, w_ref, sems, sum_ref = refs[count:]
    i = pl.program_id(0)
    weight.load(me_ref, refs[:count], w_ref, sems)
    da = nn(dqkv_ref[...], w_ref[...].reshape(3 * D, D))
    hat, inverse = normalized(x_ref[...].astype(f32))
    out = dh_ref[...] + norm_back(da, hat, inverse, vec_ref[0:1, :])
    out_ref[0] = out[0:PATCHES, :]
    sums = jnp.concatenate([column_sum(da * hat), column_sum(da), jnp.zeros((6, D), f32)], axis=0)
    accumulate(i, sum_ref, sums)

    @pl.when(i == pl.num_programs(0) - 1)
    def _():
        dvec_ref[...] = jnp.zeros_like(dvec_ref)
        dvec_ref[0:2, :] = sum_ref[0:2, :]
        dvec_ref[2:4, :] = two_ref[0:2, :]
        dvec_ref[4:5, :] = bias_ref[0:1, 0:D]
        dvec_ref[5:6, :] = bias_ref[0:1, 2 * D : 3 * D]
        dvec_ref[6:7, :] = two_ref[2:3, :]
        for b in range(FF // D):
            dvec_ref[7 + b : 8 + b, :] = up_ref[0:1, b * D : (b + 1) * D]
        dvec_ref[7 + FF // D : 8 + FF // D, :] = two_ref[3:4, :]


def input_backward(images, x, dqkv, weight, dh, vec, g_two, g_bias, g_bias_up, me):
    n = images * ROWS
    return call(
        functools.partial(input_back_kernel, weight),
        (sds((images, PATCHES, D), f32), sds((16, D), f32)),
        (me, *weight.arrays, x, dqkv, dh, vec, g_two, g_bias, g_bias_up),
        weight.specs
        + [rows_at(ROWS, D), rows_at(ROWS, 3 * D), rows_at(ROWS, D)]
        + [whole(a.shape) for a in (vec, g_two, g_bias, g_bias_up)],
        [pl.BlockSpec((1, PATCHES, D), lambda i, *_: (i, 0, 0)), whole((16, D))],
        grid=(images,),
        scratch=weight.scratch + [pltpu.VMEM((8, D), f32)],
        flops=6 * n * D * D,
        prefetch=1,
    )


SUMMED, DOWN, PROJ, NONE, VEC = 0, 1, 2, 3, 4


def adam_kernel(part_rows, fast, each, kind_ref, row_ref, *refs):
    master_ref, first_ref, second_ref, summed_ref, down_ref, proj_ref, vec_ref = refs[:7]
    new_master_ref, new_first_ref, new_second_ref, grad_ref, woven_ref = refs[7:]
    wide = FF // D
    for k in range(each):
        slot = pl.program_id(0) * each + k
        kind = kind_ref[slot]

        @pl.when(kind == SUMMED)
        def _():
            if fast:
                for z in range(4):
                    for y in range(2):
                        grad_ref[16 * z : 16 * z + 16, 384 * y : 384 * y + 384] = summed_ref[2 * z + y, k].astype(f32)
            else:
                grad_ref[...] = summed_ref[k].astype(f32)

        @pl.when(kind == VEC)
        def _():
            grad_ref[...] = jnp.zeros_like(grad_ref)
            grad_ref[0 : vec_ref.shape[0], :] = vec_ref[...]

        @pl.when(kind == DOWN)
        def _():
            for c in range(D // 128):
                for b in range(wide):
                    lanes = slice(b * D + c * 128, b * D + c * 128 + 128)
                    woven_ref[c, pl.ds(b, part_rows // wide, stride=wide), :] = down_ref[k, 0 : part_rows // wide, lanes]
                grad_ref[:, c * 128 : (c + 1) * 128] = woven_ref[c]

        @pl.when(kind == PROJ)
        def _():
            at = pl.multiple_of(row_ref[slot], part_rows)
            grad_ref[...] = proj_ref[pl.ds(at, part_rows), :]

        @pl.when(kind == NONE)
        def _():
            grad_ref[...] = jnp.zeros_like(grad_ref)

        grad = grad_ref[...]
        master = master_ref[0, k]
        first = beta_one * first_ref[0, k] + (1.0 - beta_one) * grad
        second = beta_two * second_ref[0, k] + (1.0 - beta_two) * grad * grad
        new_first_ref[0, k] = first
        new_second_ref[0, k] = second
        direction = first / (1.0 - beta_one**STEP)
        size = jnp.sqrt(second / (1.0 - beta_two**STEP)) + adam_eps
        new_master_ref[0, k] = master - learn_rate * (direction / size + decay_rate * master)


def adam(kind, row, master, first, second, summed, down, proj, vec, fast):
    slots, part_rows = master.shape[1:3]
    each = 2
    block = pl.BlockSpec((1, each, part_rows, D), lambda s, *_: (0, s, 0, 0))
    if fast:
        summed_spec = pl.BlockSpec((8, each, 16, 384), lambda s, *_: (0, s, 0, 0))
    else:
        summed_spec = pl.BlockSpec((each, part_rows, D), lambda s, *_: (s, 0, 0))
    return call(
        functools.partial(adam_kernel, part_rows, fast, each),
        (sds(master.shape, f32),) * 3,
        (kind, row, master, first, second, summed, down, proj, vec),
        [
            block,
            block,
            block,
            summed_spec,
            pl.BlockSpec((each,) + down.shape[1:], lambda s, *_: (s, 0, 0)),
            whole(proj.shape),
            whole(vec.shape),
        ],
        [block] * 3,
        grid=(slots // each,),
        scratch=[pltpu.VMEM((part_rows, D), f32), pltpu.VMEM((D // 128, part_rows, 128), f32)],
        flops=20 * slots * part_rows * D,
        in_hbm=(2, 3, 4),
        prefetch=2,
    )


def rank_grad_kernel(images, kind_ref, row_ref, *refs):
    dz_ref, pooled_ref, down_ref, proj_ref = refs[-4:]
    held = jnp.concatenate([ref[...].reshape(64, PACK) for ref in refs[:-4]], axis=0)
    row = lax.broadcasted_iota(jnp.int32, (D, 128), 0)
    col = lax.broadcasted_iota(jnp.int32, (D, 128), 1)
    wanted = jnp.full((D, 128), -1, jnp.int32)
    for s in range(8):
        first = jnp.where(kind_ref[s] == DOWN, row_ref[s], -D)
        wanted = jnp.where(col // 16 == s, first + col % 16, wanted)
    mine = nn(held[:, 0:D], jnp.where(row == wanted, 1.0, 0.0).astype(bf16)).astype(bf16)
    shape = (512, 512)
    row = lax.broadcasted_iota(jnp.int32, shape, 0)
    col = lax.broadcasted_iota(jnp.int32, shape, 1)
    first = 0
    for segment in range(3):
        here = (row - col == segment * images) & (row // 16 == col // 16) & (col % 16 < images)
        rank = nn(jnp.where(here, 1.0, 0.0).astype(bf16), mine).astype(bf16)
        part = held[:, D:PACK] if segment == 0 else held
        down_ref[:, first : first + part.shape[1]] = tn(rank, part)
        first += part.shape[1]
    proj_ref[...] = tn(dz_ref[...], pooled_ref[...])


def rank_grads(images, kind, row, arrays, dz, pooled):
    return call(
        functools.partial(rank_grad_kernel, images),
        (sds((128, FF), f32), sds((EMB, D), f32)),
        (kind, row, *arrays, dz, pooled),
        [whole(a.shape) for a in arrays] + [whole(dz.shape), whole(pooled.shape)],
        [whole((128, FF)), whole((EMB, D))],
        flops=256 * D * FF,
        prefetch=2,
    )


def slot_place(owner_list, slot_count):
    tile_count = owner_list.shape[0]
    earlier = jnp.tril(jnp.ones((tile_count, tile_count), jnp.int32), -1)
    same_owner = (owner_list[:, None] == owner_list[None, :]).astype(jnp.int32)
    return owner_list * slot_count + jnp.sum(same_owner * earlier, axis=1)


def gather_weights(master, placed):
    n_dp, n_rep = lax.axis_size("dp"), lax.axis_size("rep")
    slots, part_rows = master.shape[1:3]
    gathered = lax.all_gather(master.astype(bf16), AXES, axis=0, tiled=True)
    gathered = gathered.reshape(n_dp, n_rep * slots, part_rows, D)
    return jnp.transpose(jnp.take(gathered, placed, axis=1), (1, 0, 2, 3)).reshape(-1, D)


def scatter_grads(tiles, tile_of_slot, slots, part_rows):
    n_dp, n_rep = lax.axis_size("dp"), lax.axis_size("rep")
    count = tiles.shape[0]
    tiles = jnp.concatenate([tiles, jnp.zeros((1, TR, D), tiles.dtype)], axis=0)
    index = jnp.where(tile_of_slot < count, tile_of_slot, count)
    buffer = jnp.take(tiles, index, axis=0).reshape(n_rep * slots, n_dp, part_rows, D)
    buffer = jnp.transpose(buffer, (1, 0, 2, 3)).reshape(n_dp * n_rep, slots, part_rows, D)
    return lax.psum_scatter(buffer, AXES, scatter_dimension=0, tiled=True)[0]


def pairs(move):
    def number(x, z, y, c):
        return x * 16 + z * 4 + y * 2 + c

    return [(number(x, z, y, c), number(*move(x, z, y, c))) for x, z, y in PIECES for c in range(2)]


SWAP_CORE = pairs(lambda x, z, y, c: (x, z, y, 1 - c))
SWAP_X = pairs(lambda x, z, y, c: (1 - x, z, y, c))
SWAP_Y = pairs(lambda x, z, y, c: (x, z, 1 - y, c))
SWAP_Z = pairs(lambda x, z, y, c: (x, z ^ 1, y, c))
SWAP_ZZ = pairs(lambda x, z, y, c: (x, z ^ 2, y, c))
SWAP_XY = pairs(lambda x, z, y, c: (1 - x, z, 1 - y, c))
ACROSS_Z = [pairs(lambda x, z, y, c, k=k: (x, z ^ k, y, c)) for k in (1, 2, 3)]
CROSS_ONE = pairs(lambda x, z, y, c: (1 - x, z, y, c) if c == 0 else (x, z, 1 - y, c))
CROSS_TWO = pairs(lambda x, z, y, c: (x, z, 1 - y, c) if c == 0 else (1 - x, z, y, c))


def send(value, permutation):
    return lax.ppermute(value, AXES, permutation)


def add_kernel(count, pieces, outputs, _, *refs):
    for p in range(pieces):
        total = refs[p * count][0].astype(f32)
        for k in range(1, count):
            total += refs[p * count + k][0].astype(f32)
        outs = refs[pieces * count :]
        if outputs == 1:
            outs[0][p] = total.astype(outs[0].dtype)
        else:
            outs[p][...] = total.astype(outs[p].dtype)


def add_pieces(sources, me, pieces, steps=1, dtypes=(bf16,), near=()):
    rows = sources[0][0].shape[1]
    each = pieces // steps
    arrays, specs = [], []
    for p in range(each):
        for array, at in sources:
            arrays.append(array)
            specs.append(pl.BlockSpec((1, rows, 384), lambda i, me, p=p, at=at: (at(i * each + p, me), 0, 0)))
    if len(dtypes) == 1:
        shapes = (sds((pieces, rows, 384), dtypes[0]),)
        outs = [pl.BlockSpec((each, rows, 384), lambda i, me: (i, 0, 0))]
    else:
        shapes = tuple(sds((rows, 384), dtype) for dtype in dtypes)
        outs = [whole((rows, 384))] * pieces
    in_hbm = [k + 1 for k in range(len(arrays)) if k % len(sources) not in near]
    results = call(
        functools.partial(add_kernel, len(sources), each, len(dtypes)),
        shapes,
        (me, *arrays),
        specs,
        outs,
        grid=(steps,),
        flops=pieces * rows * D,
        in_hbm=in_hbm,
        prefetch=1,
    )
    return results[0] if len(dtypes) == 1 else results


class PieceSum:
    def __init__(self, other, me):
        self.me = me
        self.one = send(other, SWAP_CORE)

    def first_send(self, i, me):
        return jnp.where(me[CORE] == 0, (1 - me[X]) * 8 + i, i * 2 + 1 - me[Y])

    def kept(self, i, me):
        return jnp.where(me[CORE] == 0, me[X] * 8 + i, i * 2 + me[Y])

    def second_send(self, i, me):
        return jnp.where(me[CORE] == 0, 2 * i + 1 - me[Y], (1 - me[X]) * 4 + i)

    def second_keep(self, i, me):
        return jnp.where(me[CORE] == 0, 2 * i + me[Y], me[X] * 4 + i)

    def cross_one(self):
        parts = [(self.mine, self.first_send), (self.one, self.first_send)]
        self.two = send(add_pieces(parts, self.me, 8, 2), CROSS_ONE)

    def cross_two(self):
        def own(i, me):
            return self.kept(self.second_send(i, me), me)

        parts = [(self.mine, own), (self.one, own), (self.two, self.second_send)]
        self.three = send(add_pieces(parts, self.me, 4), CROSS_TWO)

    def partial(self):
        def crossed(i, me):
            return self.second_keep(me[Z] ^ i, me)

        def own(i, me):
            return self.kept(crossed(i, me), me)

        parts = [(self.mine, own), (self.one, own), (self.two, crossed)]
        self.sums = add_pieces(parts, self.me, 4, dtypes=(f32,))

    def cross_z(self):
        parts = [(self.sums, lambda i, me: i), (self.three, lambda i, me: me[Z] ^ i)]
        self.own, *parts = add_pieces(parts, self.me, 4, dtypes=(f32, bf16, bf16, bf16), near=(0, 1))
        self.last = [send(part, move) for part, move in zip(parts, ACROSS_Z, strict=True)]

    def total(self):
        parts = [(part[None], lambda i, me: 0) for part in (self.own, *self.last)]
        return add_pieces(parts, self.me, 1, near=(0, 1, 2, 3))[0]


def place_kernel(index_ref, *refs):
    out_ref = refs[-1]
    for k in range(out_ref.shape[0]):
        at = index_ref[k]
        for q in range(4):

            @pl.when((at >= 12 * q) & (at < 12 * q + 12))
            def _():
                out_ref[k] = refs[q][pl.ds(pl.multiple_of((at - 12 * q) * 16, 16), 16), :]

        @pl.when(at >= 48)
        def _():
            out_ref[k] = jnp.zeros((16, 384), bf16)


def return_to_owners(sums, place):
    placed = call(
        place_kernel,
        (sds((64, 16, 384), bf16),),
        (place, *sums),
        [whole((192, 384))] * 4,
        [whole((64, 16, 384))],
        prefetch=1,
    )[0]
    return lax.all_to_all(placed.reshape(8, 8, 16, 384), "rep", 0, 0, axis_index_groups=SAME_CORE)


def plan_kernel(owner_ref, me_ref, pick_ref, place_ref, kind_ref, row_ref, counts, placed, tile_of):
    x, c = me_ref[X], me_ref[CORE]
    rep = me_ref[Z] * 4 + me_ref[Y] * 2 + c

    @pl.loop(0, 16)
    def _(r):
        counts[r] = 0

    @pl.loop(0, 128)
    def _(k):
        tile_of[k] = 1 << 20

    @pl.loop(0, VEC_TILE + 1)
    def _(t):
        owner = owner_ref[t]
        at = owner * 8 + counts[owner]
        counts[owner] = counts[owner] + 1
        placed[t] = at
        tile_of[at] = t

    def slab(t):
        at = placed[t]
        owner = at // 8
        return jnp.where(owner % 2 == c, 0, 64) + owner // 2 * 8 + at % 8

    def fill(first, count, tile):
        @pl.loop(0, count)
        def _(k):
            pick_ref[first + k] = slab(tile + k)

    base = 0
    for tiles, tile in CHUNK_TILES:
        fill(base, tiles, tile + tiles * c)
        base += tiles
    pick_ref[base] = slab(VEC_TILE)

    @pl.loop(0, 64)
    def _(k):
        t = tile_of[k // 8 * 16 + c * 8 + k % 8]
        u = t - QKV_TILES
        v = u - OUT_TILES
        half = jnp.where(t < QKV_TILES, t // 9, jnp.where(u < OUT_TILES, u // 3, v // 12))
        place = jnp.where(t < QKV_TILES, t % 9, jnp.where(u < OUT_TILES, 9 + u % 3, 12 + v % 12))
        place_ref[k] = jnp.where(t < DOWN_FIRST, jnp.where(half == c, place, 24 + place), 48)

    @pl.loop(0, 8)
    def _(k):
        t = tile_of[rep * 8 + k]
        is_down = (t >= DOWN_FIRST) & (t < PROJ_FIRST)
        is_proj = (t >= PROJ_FIRST) & (t < VEC_TILE)
        kind = jnp.where(t < DOWN_FIRST, SUMMED, jnp.where(is_down, DOWN, jnp.where(is_proj, PROJ, NONE)))
        kind_ref[k] = jnp.where((t == VEC_TILE) & (x == 0), VEC, kind)
        row_ref[k] = jnp.where(
            is_down, ((t - DOWN_FIRST) * TR + x * 64) // 4, jnp.where(is_proj, (t - PROJ_FIRST) * TR + x * 64, 0)
        )


def plan(owner_list, me):
    smem = pl.BlockSpec(memory_space=pltpu.SMEM)
    sizes = (sum(tiles for tiles, _ in CHUNK_TILES) + 1, 64, 8, 8)
    return pl.pallas_call(
        plan_kernel,
        out_shape=tuple(sds((size,), jnp.int32) for size in sizes),
        in_specs=[smem, smem],
        out_specs=(smem,) * 4,
        scratch_shapes=[pltpu.SMEM((16,), jnp.int32), pltpu.SMEM((128,), jnp.int32), pltpu.SMEM((128,), jnp.int32)],
    )(owner_list, me)


def prepare_kernel(owner_ref, me_ref, master_ref, out_ref, lanes_ref, tile_ref):
    rep = me_ref[Z] * 4 + me_ref[Y] * 2 + me_ref[CORE]
    for s in range(9):
        tile_ref[s] = 0

    def note(t, held):
        here = owner_ref[t] == rep

        @pl.when(here)
        def _():
            tile_ref[held] = t

        return held + jnp.where(here, 1, 0)

    lax.fori_loop(DOWN_FIRST, PROJ_FIRST, note, lax.fori_loop(0, DOWN_FIRST, note, 0))
    for s in range(8):
        down = (tile_ref[s] >= DOWN_FIRST) & (tile_ref[s] < PROJ_FIRST)

        @pl.when(jnp.logical_not(down))
        def _():
            for z in range(4):
                for y in range(2):
                    out_ref[2 * z + y, s] = master_ref[0, s, 16 * z : 16 * z + 16, 384 * y : 384 * y + 384].astype(bf16)

        @pl.when(down)
        def _():
            for k in range(6):
                lanes_ref[k] = master_ref[0, s, :, 128 * k : 128 * k + 128]
            for z in range(4):
                for k in range(6):
                    part = lanes_ref[k, pl.ds(z, 16, stride=4), :]
                    out_ref[2 * z + k // 3, s, :, k % 3 * 128 : k % 3 * 128 + 128] = part.astype(bf16)


def pick_kernel(index_ref, mine_ref, theirs_ref, text_ref, one_ref, two_ref, three_ref):
    def slab(k, ref, j):
        at = index_ref[k]

        @pl.when(at < 64)
        def _():
            ref[j] = mine_ref[at]

        @pl.when(at >= 64)
        def _():
            ref[j] = theirs_ref[at - 64]

    k = 0
    for (tiles, _), (chunk, first) in zip(CHUNK_TILES, CHUNK_AT, strict=True):
        for j in range(tiles):
            slab(k, (one_ref, two_ref, three_ref)[chunk], first + j)
            k += 1
    slab(k, one_ref, 12)
    text = text_ref[...].astype(f32)
    count = text.shape[0]
    text = (text * lax.rsqrt(jnp.sum(text * text, axis=-1, keepdims=True) + unit_eps)).astype(bf16)
    three_ref[14] = jnp.zeros((16, 384), bf16)
    three_ref[14, 0:count, :] = text[:, 0:384]
    three_ref[14, 8 : 8 + count, 0:128] = text[:, 384:512]


class Spread:
    def __init__(self, block):
        self.parts = [block] + [send(block, move) for move in ACROSS_Z]

    def cross_one(self):
        self.ring = jnp.stack(self.parts)
        self.one = send(self.ring, CROSS_ONE)
        self.two = send(self.ring, CROSS_TWO)

    def cross_two(self):
        self.both = send(self.one, CROSS_TWO)
        self.near = [send(v, SWAP_CORE) for v in (self.ring, self.one, self.two)]

    def finish(self):
        self.near.append(send(self.both, SWAP_CORE))

    def arrays(self):
        return (self.ring, self.one, self.two, self.both, *self.near)


def meet(*values):
    return lax.optimization_barrier(values)


def sources(me):
    for other in range(2):
        c = me[CORE] if other == 0 else 1 - me[CORE]
        for crossed in range(4):
            one, two = crossed % 2, crossed // 2
            flip_x = jnp.where(c == 0, one, two)
            flip_y = jnp.where(c == 0, two, one)
            yield c, me[X] + flip_x - 2 * me[X] * flip_x, me[Y] + flip_y - 2 * me[Y] * flip_y


def pick_slabs(master, text_emb, owner_list, me):
    prepared = call(
        prepare_kernel,
        (sds((8, 8, 16, 384), bf16),),
        (owner_list, me, master),
        [whole(master.shape)],
        [whole((8, 8, 16, 384))],
        scratch=[pltpu.VMEM((6, 64, 128), f32), pltpu.SMEM((16,), jnp.int32)],
        in_hbm=(2,),
        prefetch=2,
    )[0]
    pick, place, kind, row = plan(owner_list, me)
    mine = lax.all_to_all(prepared, "rep", 0, 0, axis_index_groups=SAME_CORE).reshape(64, 16, 384)
    blocks = call(
        pick_kernel,
        tuple(sds((slabs, 16, 384), bf16) for slabs in (13, 12, 15)),
        (pick, mine, send(mine, SWAP_CORE), text_emb),
        [whole((64, 16, 384)), whole((64, 16, 384)), whole(text_emb.shape)],
        [whole((slabs, 16, 384)) for slabs in (13, 12, 15)],
        prefetch=1,
    )
    return blocks, place, kind, row


def shards(block_in, tissue, text_emb, text_order, owner_list, master, first_moment, second_moment):
    n_dp = lax.axis_size("dp")
    n_rep = lax.axis_size("rep")
    images = block_in.shape[0]
    slots, part_rows = master.shape[1:3]
    image_total = text_order.shape[0]
    n = images * ROWS
    dp_at, rep_at = lax.axis_index("dp"), lax.axis_index("rep")
    first_image = lax.axis_index(AXES) * images

    x = jnp.pad(block_in, ((0, 0), (0, ROWS - PATCHES), (0, 0))).reshape(n, D)
    valid = jnp.pad((tissue > 0).astype(f32), ((0, 0), (0, ROWS - PATCHES)))
    mask_row = valid[:, None, :]
    col = jnp.broadcast_to(valid.reshape(n, 1), (n, 128))
    numbers = jnp.arange(images, dtype=jnp.int32)
    sel = jnp.where(
        numbers[:, None, None] == jnp.arange(16, dtype=jnp.int32)[None, :, None], valid[:, None, :], 0.0
    ).astype(bf16)
    inv_count = jnp.pad(1.0 / jnp.sum(valid, axis=1), (0, 16 - images))
    inv_count = jnp.broadcast_to(inv_count[:, None], (16, 128))
    order = jnp.broadcast_to(text_order[:, None], (image_total, 128))
    first_image = first_image.astype(jnp.int32)[None]

    fast = (n_dp, n_rep, slots, part_rows) == (2, 16, 8, 64)
    if fast:
        me = jnp.stack([dp_at, rep_at // 4, rep_at // 2 % 2, rep_at % 2]).astype(jnp.int32)
        (block_one, block_two, block_three), place, kind, row = pick_slabs(master, text_emb, owner_list, me)
        x, col, sel, inv_count, order, first_image, block_one = lax.optimization_barrier(
            (x, col, sel, inv_count, order, first_image, block_one)
        )
        one = Spread(block_one)
        *one.parts, block_two, block_three = meet(*one.parts, block_two, block_three)
        one.cross_one()
        two = Spread(block_two)
        one.ring, one.one, one.two = meet(one.ring, one.one, one.two)
        one.cross_two()
        *two.parts, block_three = meet(*two.parts, block_three)
        three = Spread(block_three)
        one.both, *two.parts = meet(one.both, *two.parts)
        one.finish()
        two.cross_one()
        w_qkv = Weight(one.arrays(), QKV_TILES)
        w_out = Weight(one.arrays(), OUT_TILES, 9)
        a, qkv, vec = qkv_forward(images, x, jnp.zeros((16, D), f32), w_qkv, me)
        qkv, two.ring, two.one, two.two, *three.parts = meet(qkv, two.ring, two.one, two.two, *three.parts)
        two.cross_two()
        three.ring = jnp.stack(three.parts)
        three.one = send(three.ring, CROSS_ONE)
        o, lse = attention_forward(images, qkv, mask_row)
        o, two.both, three.ring, *two.near = meet(o, two.both, three.ring, *two.near)
        two.finish()
        three.two = send(three.ring, CROSS_TWO)
        w_up = Weight(two.arrays(), UP_TILES)
        h, m = middle_forward(images, x, o, vec, w_out, me)
        h, m, two.near[3], three.ring, three.one, three.two = meet(h, m, two.near[3], three.ring, three.one, three.two)
        three.cross_two()
        bias_up = vec[7 : 7 + FF // D].reshape(FF // D, 1, D)
        w_up = Weight(two.arrays(), UP_TILES)
        act, slope = up_forward(images, m, w_up, bias_up, me)
        act, three.both, *three.near = meet(act, three.both, *three.near)
        three.finish()
        w_down = Weight(three.arrays(), DOWN_TILES, quarters=True)
        w_proj = Weight(three.arrays(), PROJ_TILES, 12)
        all_text = jnp.zeros((16, 128), bf16)
    else:
        me = jnp.zeros((4,), jnp.int32)
        placed = slot_place(owner_list, slots)
        hits = placed[None, :] == jnp.arange(n_rep * slots, dtype=jnp.int32)[:, None]
        tile_ids = jnp.arange(owner_list.shape[0], dtype=jnp.int32)[None, :]
        tile_of_slot = jnp.where(jnp.any(hits, axis=1), jnp.sum(jnp.where(hits, tile_ids, 0), axis=1), 1 << 20)
        text = text_emb.astype(f32)
        own_text = (text * lax.rsqrt(jnp.sum(text * text, axis=-1, keepdims=True) + unit_eps)).astype(bf16)
        all_text = lax.all_gather(own_text, AXES, axis=0, tiled=True)
        tiles = gather_weights(master, placed).reshape(-1, TR, D)
        w_qkv = Weight([tiles[:QKV_TILES]], QKV_TILES)
        w_out = Weight([tiles[QKV_TILES : QKV_TILES + OUT_TILES]], OUT_TILES)
        w_up = Weight([tiles[QKV_TILES + OUT_TILES : DOWN_FIRST]], UP_TILES)
        w_down = Weight([tiles[DOWN_FIRST:PROJ_FIRST].reshape(DOWN_TILES, TR // 4, FF)], DOWN_TILES, quarters=True)
        w_proj = Weight([tiles[PROJ_FIRST:VEC_TILE]], PROJ_TILES)
        a, qkv, vec = qkv_forward(images, x, tiles[VEC_TILE, :16].astype(f32), w_qkv, me)
        bias_up = vec[7 : 7 + FF // D].reshape(FF // D, 1, D)
        o, lse = attention_forward(images, qkv, mask_row)
        h, m = middle_forward(images, x, o, vec, w_out, me)
        act, slope = up_forward(images, m, w_up, bias_up, me)
    block_out, pooled = down_forward(images, act, w_down, h, vec, sel, inv_count, me)

    pooled_all = lax.all_to_all(jnp.broadcast_to(pooled[None, :images], (n_dp * n_rep, images, D)), AXES, 0, 0)
    act_sum = act_sums(images, act, sel)
    probabilities = attention_again(images, qkv, lse, col)
    if fast:
        pooled_all, act_sum, probabilities = meet(pooled_all, act_sum, probabilities)
    dz_all, rank, spread, hidden, pooled_all = loss_backward(
        me, first_image, pooled_all, all_text, order, w_proj, w_down, inv_count
    )

    both = jnp.concatenate([rank[:images], act_sum[:images]], axis=1)
    if fast:
        packed = jnp.concatenate([both[:, at * PACK : (at + 1) * PACK] for at in range(3)], axis=0)
        ranks = Spread(jnp.pad(packed, ((0, 16 - 3 * images), (0, 0))))
        dm, g_bias_up, other, mine = up_backward(images, slope, m, w_up, hidden, col, me)
        dm, other, mine, *ranks.parts = meet(dm, other, mine, *ranks.parts)
        up_sum = PieceSum(other, me)
        ranks.cross_one()
        dh, do, g_out, g_two = middle_backward(images, h, dm, col, spread, o, w_out, vec, me)
        dh, do, up_sum.mine, up_sum.one, ranks.ring, ranks.one, ranks.two = meet(
            dh, do, mine, up_sum.one, ranks.ring, ranks.one, ranks.two
        )
        up_sum.cross_one()
        ranks.cross_two()
        dqkv, g_bias = attention_backward(images, qkv, do, probabilities)
        dqkv, up_sum.two, ranks.both, *ranks.near = meet(dqkv, up_sum.two, ranks.both, *ranks.near)
        up_sum.cross_two()
        ranks.finish()
        other = qkv_weight_grad_fast(images, dqkv, a, g_out, me, True)
        other, dqkv = meet(other, dqkv)
        qkv_sum = PieceSum(other, me)
        mine = qkv_weight_grad_fast(images, dqkv, a, g_out, me, False)
        up_sum.partial()
        dqkv, up_sum.sums, up_sum.three, qkv_sum.mine, qkv_sum.one, ranks.near[3] = meet(
            dqkv, up_sum.sums, up_sum.three, mine, qkv_sum.one, ranks.near[3]
        )
        qkv_sum.cross_one()
        up_sum.cross_z()
        input_grad, vec_sum = input_backward(images, x, dqkv, w_qkv, dh, vec, g_two, g_bias, g_bias_up, me)
        vec_sum, qkv_sum.two, *up_sum.last = meet(vec_sum, qkv_sum.two, *up_sum.last)
        qkv_sum.cross_two()
        near_vec = send(vec_sum, SWAP_CORE)
        up_total = up_sum.total()
        near_up = send(up_total, SWAP_CORE)
        qkv_sum.partial()
        vec_sum, near_vec, qkv_sum.sums, near_up = meet(vec_sum, near_vec, qkv_sum.sums, near_up)
        vec_sum += near_vec
        across = [send(vec_sum, move) for move in (SWAP_X, SWAP_Y, SWAP_XY)]
        g_down, g_proj = rank_grads(images, kind, row, ranks.arrays(), dz_all, pooled_all)
        vec_sum, qkv_sum.three, g_down, g_proj, *across = meet(vec_sum, qkv_sum.three, g_down, g_proj, *across)
        qkv_sum.cross_z()
        vec_sum += across[0] + across[1] + across[2]
        vec_sum += send(vec_sum, SWAP_Z)
        vec_sum += send(vec_sum, SWAP_ZZ)
        vec_total, g_down, *qkv_sum.last = meet(vec_sum, g_down.reshape(8, 16, FF), *qkv_sum.last)
        qkv_total = qkv_sum.total()
        summed = return_to_owners((qkv_total, up_total, send(qkv_total, SWAP_CORE), near_up), place)
    else:
        both_all = lax.all_gather(both, AXES, axis=0, tiled=True)
        dm, g_bias_up, g_up = up_backward(images, slope, m, w_up, hidden, col, me)
        dh, do, g_out, g_two = middle_backward(images, h, dm, col, spread, o, w_out, vec, me)
        dqkv, g_bias = attention_backward(images, qkv, do, probabilities)
        g_qkv = qkv_weight_grad(images, dqkv, a)
        input_grad, vec_total = input_backward(images, x, dqkv, w_qkv, dh, vec, g_two, g_bias, g_bias_up, me)
        mine = lax.dynamic_slice_in_dim(tile_of_slot, rep_at * slots, slots)
        first_row = dp_at * part_rows
        is_down = (mine >= DOWN_FIRST) & (mine < PROJ_FIRST)
        is_proj = (mine >= PROJ_FIRST) & (mine < VEC_TILE)
        kind = jnp.where(is_down, DOWN, jnp.where(is_proj, PROJ, jnp.where(mine <= VEC_TILE, SUMMED, NONE)))
        kind = kind.astype(jnp.int32)
        each = part_rows * D // FF
        row = jnp.where(is_proj, (mine - PROJ_FIRST) * TR + first_row, 0)
        down_rows = jnp.clip(((mine - DOWN_FIRST) * TR + first_row) * D // FF, 0, D - each)
        g_down = tn(both_all[:, :D], both_all[:, D:])
        g_down = jnp.stack([lax.dynamic_slice_in_dim(g_down, at, each) for at in down_rows])
        g_down = jnp.pad(g_down, ((0, 0), (0, max(0, 8 - each)), (0, 0)))
        g_proj = tn(dz_all, pooled_all)
        last = jnp.pad(vec_total, ((0, TR - 16), (0, 0))).astype(bf16)
        tiles = jnp.concatenate([g_qkv, g_out, g_up, last], axis=0).reshape(-1, TR, D)
        index = jnp.where(tile_of_slot == VEC_TILE, DOWN_FIRST, jnp.where(tile_of_slot < DOWN_FIRST, tile_of_slot, 1 << 20))
        summed = scatter_grads(tiles, index, slots, part_rows)
    new_master, new_first, new_second = adam(
        kind, row, master, first_moment, second_moment, summed, g_down, g_proj, vec_total, fast
    )
    return block_out, input_grad, new_master, new_first, new_second


def solution(mesh):
    in_specs = (
        P(("dp", "rep"), None, None),
        P(("dp", "rep"), None),
        P(("dp", "rep"), None),
        P(),
        P(),
        P("rep", None, "dp", None),
        P("rep", None, "dp", None),
        P("rep", None, "dp", None),
    )
    out_specs = (
        P(("dp", "rep"), None, None),
        P(("dp", "rep"), None, None),
        P("rep", None, "dp", None),
        P("rep", None, "dp", None),
        P("rep", None, "dp", None),
    )
    return jax.shard_map(shards, mesh=mesh, in_specs=in_specs, out_specs=out_specs, check_vma=False)
```

```python
import functools

import jax
import jax.numpy as jnp
from jax import lax
from jax.experimental import pallas as pl
from jax.experimental.pallas import tpu as pltpu
from jax.sharding import PartitionSpec as P

D = 768
HEADS = 12
HEAD = 64
FF = 3072
EMB = 512
PATCHES = 196
STEP = 10
ROWS = 208
TR = 128

logit_scale = 50.0
learn_rate = 0.03
beta_one = 0.9
beta_two = 0.999
adam_eps = 1e-08
decay_rate = 0.05
norm_eps = 1e-05
unit_eps = 1e-06
masked_score = -1000000000.0

bf16 = jnp.bfloat16
f32 = jnp.float32
AXES = ("dp", "rep")
MIB = 1 << 20

X, Z, Y, CORE = range(4)
PIECES = [(x, z, y) for x in range(2) for z in range(4) for y in range(2)]

QKV_TILES = 3 * D // TR
OUT_TILES = D // TR
UP_TILES = FF // TR
DOWN_TILES = FF // TR
PROJ_TILES = EMB // TR
DOWN_FIRST = QKV_TILES + OUT_TILES + UP_TILES
PROJ_FIRST = DOWN_FIRST + DOWN_TILES
VEC_TILE = PROJ_FIRST + PROJ_TILES
PACK = (D + FF) // 3
CHUNK_TILES = (
    (QKV_TILES // 2, 0),
    (OUT_TILES // 2, QKV_TILES),
    (UP_TILES // 2, QKV_TILES + OUT_TILES),
    (DOWN_TILES // 2, DOWN_FIRST),
    (PROJ_TILES // 2, PROJ_FIRST),
)
CHUNK_AT = ((0, 0), (1, 0), (1, 3), (2, 0), (2, 12))
SLABS = (10, 15, 15)
SAME_CORE = [[i * 2 + c for i in range(8)] for c in range(2)]


def nn(a, b):
    return lax.dot_general(a, b, (((1,), (0,)), ((), ())), preferred_element_type=f32)


def nt(a, b):
    return lax.dot_general(a, b, (((1,), (1,)), ((), ())), preferred_element_type=f32)


def tn(a, b):
    return lax.dot_general(a, b, (((0,), (0,)), ((), ())), preferred_element_type=f32)


def call(kernel, outs, ins, in_specs, out_specs, grid=None, scratch=(), flops=0, vmem=24, prefetch=0, in_hbm=(), out_hbm=(), vmem_in=(), vmem_out=()):
    ins = [
        pltpu.with_memory_space_constraint(a, pltpu.HBM) if k >= prefetch and (s.memory_space is pltpu.HBM or k in in_hbm) else a
        for k, (a, s) in enumerate(zip(ins, [None] * prefetch + list(in_specs), strict=True))
    ]
    ins = [pltpu.with_memory_space_constraint(a, pltpu.VMEM) if k in vmem_in else a for k, a in enumerate(ins)]
    moved = sum(a.size * a.dtype.itemsize for a in ins) + sum(o.size * o.dtype.itemsize for o in outs)
    spaces = {k: pltpu.HBM for k in out_hbm} | {k: pltpu.VMEM for k in vmem_out}
    outs = [spaces[k](o.shape, o.dtype) if k in spaces else o for k, o in enumerate(outs)]
    params = pltpu.CompilerParams(
        vmem_limit_bytes=vmem * MIB,
        dimension_semantics=("arbitrary",) * len(grid or ()) or None,
    )
    return pl.pallas_call(
        kernel,
        out_shape=tuple(outs),
        grid_spec=pltpu.PrefetchScalarGridSpec(
            num_scalar_prefetch=prefetch,
            grid=grid or (1,),
            in_specs=in_specs,
            out_specs=tuple(out_specs),
            scratch_shapes=list(scratch),
        ),
        compiler_params=params,
        cost_estimate=pl.CostEstimate(flops=1, bytes_accessed=1, transcendentals=0),
    )(*ins)


def whole(shape):
    return pl.BlockSpec(shape, lambda *_: (0,) * len(shape))


def rows_at(rows, cols):
    return pl.BlockSpec((rows, cols), lambda i, *_: (i, 0))


def cols_at(rows, cols):
    return pl.BlockSpec((rows, cols), lambda i, *_: (0, i))


def sds(shape, dtype):
    return jax.ShapeDtypeStruct(shape, dtype)


class Weight:
    def __init__(self, arrays, tiles, first=0, quarters=False):
        self.arrays, self.tiles, self.first, self.quarters = tuple(arrays), tiles, first, quarters
        self.pieces = len(arrays) > 1
        self.specs = [pl.BlockSpec(memory_space=pltpu.HBM)] * len(arrays)
        shape = (tiles, TR // 4, FF) if quarters else (tiles, TR, D)
        self.scratch = [pltpu.VMEM(shape, bf16), pltpu.SemaphoreType.DMA((32 if self.pieces else 1,))]

    def copies(self, me, refs, out, sems):
        if not self.pieces:
            return [lambda: pltpu.make_async_copy(refs[0], out, sems.at[0])]
        copies = []
        half = self.tiles // 2
        for at, (c, x, y) in enumerate(sources(me)):
            for back in range(4):
                z = me[Z] ^ back
                if self.quarters:
                    row, col = x * 16, z * D + y * 384
                else:
                    row, col = x * 64 + z * 16, y * 384
                rows = pl.ds(pl.multiple_of(row, 16), 16)
                cols = pl.ds(pl.multiple_of(col, 128), 384)
                source = refs[at].at[back, pl.ds(self.first, half)]
                place = out.at[pl.ds(half * c, half), rows, cols]
                copies.append(functools.partial(pltpu.make_async_copy, source, place, sems.at[len(copies)]))
        return copies

    def start(self, me, refs, out, sems):
        for copy in self.copies(me, refs, out, sems):
            copy().start()

    def wait(self, me, refs, out, sems, part=None, parts=1):
        copies = self.copies(me, refs, out, sems)
        if part is not None and not self.pieces:
            copies = copies if part == 0 else []
        elif part is not None:
            copies = copies[16 * part : 16 * part + 16] if parts == 2 else copies[part::4]
        for copy in copies:
            copy().wait()

    def load(self, me, refs, out, sems):
        @pl.when(pl.program_id(0) == 0)
        def _():
            self.start(me, refs, out, sems)
            self.wait(me, refs, out, sems)


def normalized(x):
    center = x - jnp.mean(x, axis=-1, keepdims=True)
    spread = jnp.mean(center * center, axis=-1, keepdims=True)
    inverse = lax.rsqrt(spread + norm_eps)
    return center * inverse, inverse


def norm_back(grad, hat, inverse, gain):
    scaled = grad * gain
    first = jnp.mean(scaled, axis=-1, keepdims=True)
    second = jnp.mean(scaled * hat, axis=-1, keepdims=True)
    return inverse * (scaled - first - hat * second)


def accumulate(i, ref, value):
    @pl.when(i == 0)
    def _():
        ref[...] = value

    @pl.when(i > 0)
    def _():
        ref[...] += value


def column_sum(x):
    return jnp.sum(x, axis=0, keepdims=True)


def qkv_block(j, me):
    return jnp.where(me[CORE] == 0, j, 2 - j)


def qkv_kernel(images, weight, me_ref, *refs):
    count = len(weight.arrays)
    pieces = refs[:count]
    x_ref, vec_in_ref, a_ref, qkv_ref, vec_ref, w_ref, sems, vec_half, vec_sems = refs[count:]
    j = pl.program_id(0)

    @pl.when(j == 0)
    def _():
        weight.start(me_ref, pieces, w_ref, sems)
        if weight.pieces:
            parts = []
            for at, (_, x, y) in list(enumerate(sources(me_ref)))[:4]:
                for back in range(4):
                    copy = pltpu.make_async_copy(pieces[at].at[back, 9], vec_half.at[y], vec_sems.at[len(parts)])
                    parts.append(((x == 0) & ((me_ref[Z] ^ back) == 0), copy))
            for here, copy in parts:
                pl.when(here)(copy.start)
            for here, copy in parts:
                pl.when(here)(copy.wait)
            vec_ref[...] = jnp.concatenate([vec_half[0], vec_half[1]], axis=1).astype(f32)
        else:
            vec_ref[...] = vec_in_ref[...]
        for i in range(images):
            hat, _ = normalized(x_ref[pl.ds(i * ROWS, ROWS), :].astype(f32))
            a_ref[pl.ds(i * ROWS, ROWS), :] = (hat * vec_ref[0:1, :] + vec_ref[1:2, :]).astype(bf16)
        weight.wait(me_ref, pieces, w_ref, sems, 0, 2)

    @pl.when(j == 1)
    def _():
        weight.wait(me_ref, pieces, w_ref, sems, 1, 2)

    j = qkv_block(j, me_ref)
    bias = jnp.where(j == 0, vec_ref[4:5, :], jnp.where(j == 2, vec_ref[5:6, :], 0.0))
    scale = jnp.where(j == 0, f32(HEAD**-0.5), f32(1.0))
    w = w_ref[pl.ds(6 * j, 6)].reshape(D, D)
    qkv_ref[...] = ((nt(a_ref[...], w) + bias) * scale).astype(bf16)


def qkv_forward(images, x, vec, weight, me):
    n = images * ROWS
    return call(
        functools.partial(qkv_kernel, images, weight),
        (sds((n, D), bf16), sds((n, 3 * D), bf16), sds((16, D), f32)),
        (me, *weight.arrays, x, vec),
        weight.specs + [whole((n, D)), whole((16, D))],
        [whole((n, D)), pl.BlockSpec((n, D), lambda j, me: (0, qkv_block(j, me))), whole((16, D))],
        grid=(3,),
        out_hbm=(0,),
        scratch=weight.scratch + [pltpu.VMEM((2, 16, 384), bf16), pltpu.SemaphoreType.DMA((16,))],
        flops=2 * n * D * 3 * D,
        prefetch=1,
    )


def attention_kernel(qkv_ref, mask_ref, o_ref, lse_ref):
    lane = lax.broadcasted_iota(jnp.int32, (ROWS, 2 * HEAD), 1)
    low_half = lane < HEAD
    valid = mask_ref[0] > 0.0
    lse_all = jnp.zeros((ROWS, 128), f32)
    for pair in range(HEADS // 2):
        at = pair * 2 * HEAD
        q = qkv_ref[:, at : at + 2 * HEAD]
        k = qkv_ref[:, D + at : D + at + 2 * HEAD]
        v = qkv_ref[:, 2 * D + at : 2 * D + at + 2 * HEAD]
        mixed = []
        for half in range(2):
            keep = low_half if half == 0 else jnp.logical_not(low_half)
            s = nt(q, jnp.where(keep, k, jnp.zeros_like(k)))
            s = jnp.where(valid, s, masked_score)
            top = jnp.max(s, axis=-1, keepdims=True)
            e = jnp.exp(s - top)
            total = jnp.sum(e, axis=-1, keepdims=True)
            p = e * (1.0 / total)
            mixed.append(nn(p.astype(bf16), v))
            lse_all = jnp.where(lane == 2 * pair + half, top + jnp.log(total), lse_all)
        o_ref[:, at : at + 2 * HEAD] = jnp.where(low_half, mixed[0], mixed[1]).astype(bf16)
    lse_ref[0] = jnp.transpose(lse_all)[0:16, :]


def attention_forward(images, qkv, mask_row):
    n = images * ROWS
    return call(
        attention_kernel,
        (sds((n, D), bf16), sds((images, 16, ROWS), f32)),
        (qkv, mask_row),
        [rows_at(ROWS, 3 * D), pl.BlockSpec((1, 1, ROWS), lambda i: (i, 0, 0))],
        [rows_at(ROWS, D), pl.BlockSpec((1, 16, ROWS), lambda i: (i, 0, 0))],
        grid=(images,),
        flops=4 * n * ROWS * D,
    )


def middle_kernel(weight, me_ref, *refs):
    count = len(weight.arrays)
    x_ref, o_ref, vec_ref, h_ref, m_ref, w_ref, sems = refs[count:]
    weight.load(me_ref, refs[:count], w_ref, sems)
    part = nt(o_ref[...], w_ref[...].reshape(D, D)) + vec_ref[6:7, :]
    middle = x_ref[...].astype(f32) + part
    h_ref[...] = middle
    hat, _ = normalized(middle)
    m_ref[...] = (hat * vec_ref[2:3, :] + vec_ref[3:4, :]).astype(bf16)


def middle_forward(images, x, o, vec, weight, me):
    n = images * ROWS
    return call(
        functools.partial(middle_kernel, weight),
        (sds((n, D), f32), sds((n, D), bf16)),
        (me, *weight.arrays, x, o, vec),
        weight.specs + [rows_at(ROWS, D), rows_at(ROWS, D), whole((16, D))],
        [rows_at(ROWS, D), rows_at(ROWS, D)],
        grid=(images,),
        scratch=weight.scratch,
        flops=2 * n * D * D,
        prefetch=1,
    )


def gelu_parts(u):
    size = jnp.abs(u)
    t = 1.0 / (1.0 + 0.23164189 * size)
    poly = t * (0.127414796 + t * (-0.142248368 + t * (0.7107068705 + t * (-0.7265760135 + t * 0.5307027145))))
    e = jnp.exp2(u * u * -0.7213475204444817)
    act = jnp.maximum(u, 0.0) - size * (poly * e)
    w = e * (poly - 0.3989422804014327 * size)
    return act, jnp.where(u >= 0.0, 1.0 - w, w)


def own_block(j, me):
    return (j // 2 + me[CORE]) % 2 * 2 + j % 2


def up_kernel(images, weight, me_ref, *refs):
    count = len(weight.arrays)
    m_ref, bias_ref, act_ref, slope_ref, w_ref, sems = refs[count:]
    j = pl.program_id(0)

    @pl.when(j == 0)
    def _():
        weight.start(me_ref, refs[:count], w_ref, sems)
        weight.wait(me_ref, refs[:count], w_ref, sems, 0, 2)

    @pl.when(j == 2)
    def _():
        weight.wait(me_ref, refs[:count], w_ref, sems, 1, 2)

    w = w_ref[pl.ds(6 * own_block(j, me_ref), 6)].reshape(D, D)
    for i in range(images):
        at = pl.ds(i * ROWS, ROWS)
        act, slope = gelu_parts(nt(m_ref[at, :], w) + bias_ref[0])
        act_ref[at, :] = act.astype(bf16)
        slope_ref[at, :] = slope.astype(bf16)


def up_forward(images, m, weight, bias, me):
    n = images * ROWS
    cols = pl.BlockSpec((n, D), lambda j, me: (0, own_block(j, me)))
    return call(
        functools.partial(up_kernel, images, weight),
        (sds((n, FF), bf16), sds((n, FF), bf16)),
        (me, *weight.arrays, m, bias),
        weight.specs + [whole((n, D)), pl.BlockSpec((1, 1, D), lambda j, me: (own_block(j, me), 0, 0))],
        [cols, cols],
        grid=(FF // D,),
        out_hbm=(1,),
        scratch=weight.scratch,
        flops=2 * n * D * FF,
        prefetch=1,
    )


def act_sum_kernel(images, act_ref, sel_ref, sum_ref):
    total = jnp.zeros(sum_ref.shape, f32)
    for i in range(images):
        total += nn(sel_ref[i], act_ref[pl.ds(i * ROWS, ROWS), :])
    sum_ref[...] = total.astype(bf16)


def act_sums(images, act, sel):
    n = images * ROWS
    return call(
        functools.partial(act_sum_kernel, images),
        (sds((16, FF), bf16),),
        (act, sel),
        [cols_at(n, D), whole((images, 16, ROWS))],
        [cols_at(16, D)],
        grid=(FF // D,),
        flops=32 * n * FF,
    )[0]


def down_kernel(images, weight, me_ref, *refs):
    count = len(weight.arrays)
    act_ref, h_ref, vec_ref, sel_ref, inv_ref, out_ref, pooled_ref, w_ref, sems, sum_ref, y_ref = refs[count:]
    k = pl.program_id(0)
    quarters = FF // D

    @pl.when(k == 0)
    def _():
        weight.start(me_ref, refs[:count], w_ref, sems)

    for part in range(quarters):

        @pl.when(k == part)
        def _():
            weight.wait(me_ref, refs[:count], w_ref, sems, part, quarters)

    @pl.when(k < quarters)
    def _():
        cols = pl.ds(pl.multiple_of((me_ref[Z] ^ k) * D, 128), D)
        accumulate(k, y_ref, nt(act_ref[...], w_ref[:, :, cols].reshape(D, D)))

    @pl.when(k >= quarters)
    def _():
        i = k - quarters
        y = y_ref[pl.ds(pl.multiple_of(i * ROWS, 16), ROWS), :] + vec_ref[11:12, :]
        out = (h_ref[...] + y).astype(bf16)
        out_ref[0] = out[0:PATCHES, :]
        accumulate(i, sum_ref, nn(sel_ref[i], out))
        pooled_ref[...] = (sum_ref[...] * inv_ref[:, 0:1]).astype(bf16)


def down_forward(images, act, weight, h, vec, sel, inv_count, me):
    n = images * ROWS
    quarters = FF // D

    def image(k):
        return jnp.maximum(k - quarters, 0)

    def quarter(k, me):
        return me[Z] ^ jnp.minimum(k, quarters - 1)

    return call(
        functools.partial(down_kernel, images, weight),
        (sds((images, PATCHES, D), bf16), sds((16, D), bf16)),
        (me, *weight.arrays, act, h, vec, sel, inv_count),
        weight.specs[:-1]
        + [
            pl.BlockSpec(memory_space=pl.ANY),
            pl.BlockSpec((n, D), lambda k, me: (0, quarter(k, me))),
            pl.BlockSpec((ROWS, D), lambda k, me: (image(k), 0)),
            whole((16, D)),
            whole((images, 16, ROWS)),
            whole((16, 128)),
        ],
        [
            pl.BlockSpec((1, PATCHES, D), lambda k, me: (image(k), 0, 0)),
            whole((16, D)),
        ],
        grid=(quarters + images,),
        scratch=weight.scratch + [pltpu.VMEM((16, D), f32), pltpu.VMEM((n, D), f32)],
        flops=2 * n * D * FF,
        prefetch=1,
    )


def loss_kernel(total_images, proj, down, me_ref, first_ref, *refs):
    count = len(proj.arrays)
    pieces = refs[:count]
    if proj.pieces:
        down_pieces, rest = pieces, refs[count:]
    else:
        down_pieces, rest = refs[count : count + 1], refs[count + 1 :]
    text_ref, pooled_ref, order_ref, inv_ref, dz_ref, rank_ref, spread_ref, hidden_ref, all_ref = rest[:9]
    proj_ref, proj_sems, down_ref, down_sems, rows_ref = rest[9:14]
    down_copies = down.copies(me_ref, down_pieces, down_ref, down_sems)
    proj_copies = proj.copies(me_ref, pieces, proj_ref, proj_sems)
    if proj.pieces:
        slab_ref, slab_sems = rest[14:]
        for at, (c, x, y) in enumerate(sources(me_ref)):
            for back in range(4):
                device = x * 16 + (me_ref[Z] ^ back) * 4 + y * 2 + c
                out = slab_ref.at[pl.ds(pl.multiple_of(device * 16, 16), 16)]
                source = pieces[at].at[back, 14]
                proj_copies.append(
                    functools.partial(pltpu.make_async_copy, source, out, slab_sems.at[at * 4 + back])
                )
    for copy in proj_copies + down_copies:
        copy().start()
    for copy in proj_copies:
        copy().wait()
    if proj.pieces:
        images = total_images // 32
        shape = (total_images, 512)
        row = lax.broadcasted_iota(jnp.int32, shape, 0)
        col = lax.broadcasted_iota(jnp.int32, shape, 1)
        start = row // images * 16 + row % images
        held = slab_ref[...]
        left = nn(jnp.where(col == start, 1.0, 0.0).astype(bf16), held)
        right = nn(jnp.where(col == start + 8, 1.0, 0.0).astype(bf16), held[:, 0:128])
        text = jnp.concatenate([left, right], axis=1).astype(bf16)
    else:
        text = text_ref[...]
    proj_w = proj_ref[...].reshape(EMB, D)
    each = total_images // pooled_ref.shape[0]
    for d in range(pooled_ref.shape[0]):
        rows_ref[d * each : d * each + each, :] = pooled_ref[d].astype(f32)
    pooled = rows_ref[...].astype(bf16)
    all_ref[...] = pooled
    z = nt(pooled, proj_w)
    square = jnp.sum(z * z, axis=-1, keepdims=True) + unit_eps
    inverse = lax.rsqrt(square)
    image = (z * inverse).astype(bf16)
    s = logit_scale * nt(image, text)
    shape = (total_images, total_images)
    hit = jnp.where(order_ref[:, 0:1] == lax.broadcasted_iota(jnp.int32, shape, 1), 1.0, 0.0)
    part = 1.0 / (2.0 * total_images)

    def grad_of(axis):
        top = jnp.max(s, axis=axis, keepdims=True)
        lse = top + jnp.log(jnp.sum(jnp.exp(s - top), axis=axis, keepdims=True))
        return ((jnp.exp(s - lse) - hit) * part).astype(bf16)

    de = logit_scale * (nn(grad_of(1), text) + nn(grad_of(0), text))
    dz = inverse * de - z * (inverse * inverse * inverse * jnp.sum(z * de, axis=-1, keepdims=True))
    dz = dz.astype(bf16)
    dz_ref[...] = dz
    pick = lax.broadcasted_iota(jnp.int32, (16, total_images), 1) == (
        first_ref[0] + lax.broadcasted_iota(jnp.int32, (16, total_images), 0)
    )
    own = nn(jnp.where(pick, 1.0, 0.0).astype(bf16), dz).astype(bf16)
    spread = nn(own, proj_w) * inv_ref[:, 0:1]
    spread_ref[...] = spread
    rank = spread.astype(bf16)
    rank_ref[...] = rank
    for copy in down_copies:
        copy().wait()
    hidden_ref[...] = nn(rank, down_ref[...].reshape(D, FF))


def loss_backward(me, first, pooled, text, order, proj, down, inv_count):
    total = pooled.shape[0] * pooled.shape[1]
    if proj.pieces:
        arrays, extra = proj.arrays, [pltpu.VMEM((512, 384), bf16), pltpu.SemaphoreType.DMA((32,))]
    else:
        arrays, extra = proj.arrays + down.arrays, []
    return call(
        functools.partial(loss_kernel, total, proj, down),
        (sds((total, EMB), bf16), sds((16, D), bf16), sds((16, D), f32), sds((16, FF), f32), sds((total, D), bf16)),
        (me, first, *arrays, text, pooled, order, inv_count),
        [pl.BlockSpec(memory_space=pltpu.HBM)] * len(arrays)
        + [whole(text.shape), whole(pooled.shape), whole((total, 128)), whole((16, 128))],
        [whole((total, EMB)), whole((16, D)), whole((16, D)), whole((16, FF)), whole((total, D))],
        scratch=proj.scratch + down.scratch + [pltpu.VMEM((total, D), f32)] + extra,
        flops=6 * total * total * EMB + 2 * total * D * EMB + 32 * D * FF,
        vmem=32,
        prefetch=2,
    )


def weave(ref, value):
    for t in range(value.shape[0] // TR):
        for x, z, y in PIECES:
            row = t * TR + x * 64 + z * 16
            ref[x * 8 + z * 2 + y, pl.ds(t * 16, 16), :] = value[row : row + 16, y * 384 : y * 384 + 384]


def half_block(j, me):
    return (j // 2 + 1 - me[CORE]) % 2 * 2 + j % 2


SPLIT = 528


def up_back_kernel(images, weight, me_ref, *refs):
    count = len(weight.arrays)
    slope_ref, m_ref, hidden_ref, col_ref, dm_ref, db_ref = refs[count : count + 6]
    w_ref, sems, du_ref = refs[-3:]
    j = pl.program_id(0)
    blocks = FF // D

    @pl.when(j == 0)
    def _():
        weight.start(me_ref, refs[:count], w_ref, sems)

    @pl.when(j < blocks)
    def _():
        cols = pl.ds(pl.multiple_of(half_block(j, me_ref) * D, 128), D)
        total = jnp.zeros((1, D), f32)
        for i in range(images):
            at = pl.ds(i * ROWS, ROWS)
            du = (slope_ref[at, :].astype(f32) * (col_ref[at, 0:1] * hidden_ref[i : i + 1, :])).astype(bf16)
            du_ref[at, cols] = du
            total += column_sum(du.astype(f32))
        db_ref[...] = jnp.broadcast_to(total, db_ref.shape)
        dw = tn(du_ref[pl.ds(0, images * ROWS), cols], m_ref[...]).astype(bf16)
        if not weight.pieces:
            refs[count + 6][...] = dw
            return
        send_ref, keep_ref = refs[count + 6 : count + 8]

        @pl.when(j < 2)
        def _():
            weave(send_ref, dw)

        @pl.when(j >= 2)
        def _():
            weave(keep_ref, dw)

    @pl.when(j == blocks)
    def _():
        weight.wait(me_ref, refs[:count], w_ref, sems)

    @pl.when(j >= blocks)
    def _():
        rows = pl.ds(pl.multiple_of((j - blocks) * SPLIT, 16), SPLIT)
        dm_ref[...] = nn(du_ref[rows, :], w_ref[...].reshape(FF, D))


def up_backward(images, slope, m, weight, hidden, col, me):
    n = images * ROWS
    blocks = FF // D
    steps = -(-n // SPLIT)

    def block(j, me):
        return half_block(jnp.minimum(j, blocks - 1), me)

    def cols(rows):
        return pl.BlockSpec((rows, D), lambda j, me: (0, block(j, me)))

    if weight.pieces:
        shapes = (sds((16, 192, 384), bf16),) * 2
        specs = [
            pl.BlockSpec((16, 96, 384), lambda j, me: (0, jnp.minimum(j, 1), 0)),
            pl.BlockSpec((16, 96, 384), lambda j, me: (0, jnp.clip(j - 2, 0, 1), 0)),
        ]
    else:
        shapes = (sds((FF, D), bf16),)
        specs = [pl.BlockSpec((D, D), lambda j, me: (block(j, me), 0))]
    return call(
        functools.partial(up_back_kernel, images, weight),
        (sds((n, D), f32), sds((8, FF), f32)) + shapes,
        (me, *weight.arrays, slope, m, hidden, col),
        weight.specs + [cols(n), whole((n, D)), cols(16), whole((n, 128))],
        [pl.BlockSpec((SPLIT, D), lambda j, me: (jnp.maximum(j - blocks, 0), 0)), cols(8)] + specs,
        grid=(blocks + steps,),
        vmem=40,
        scratch=weight.scratch + [pltpu.VMEM((steps * SPLIT, FF), bf16)],
        flops=4 * n * D * FF,
        prefetch=1,
    )


def middle_back_kernel(images, weight, me_ref, *refs):
    count = len(weight.arrays)
    h_ref, dm_ref, col_ref, spread_ref, o_ref, vec_ref = refs[count : count + 6]
    dh_ref, do_ref, dw_ref, dvec_ref, w_ref, sems, dat_ref = refs[count + 6 :]
    i = pl.program_id(0)

    @pl.when(i == 0)
    def _():
        weight.start(me_ref, refs[:count], w_ref, sems)

    @pl.when(i < images)
    def _():
        hat, inverse = normalized(h_ref[...])
        dm = dm_ref[...]
        part = norm_back(dm, hat, inverse, vec_ref[2:3, :])
        here = spread_ref[pl.ds(i, 1), :]
        dh = col_ref[:, 0:1] * here + part
        dh_ref[...] = dh
        dat = dh.astype(bf16)
        dat_ref[pl.ds(pl.multiple_of(i * ROWS, 16), ROWS), :] = dat
        sums = jnp.concatenate(
            [
                column_sum(dm * hat),
                column_sum(dm),
                column_sum(dat.astype(f32)),
                column_sum(col_ref[:, 0:1]) * here.astype(bf16).astype(f32),
                jnp.zeros((4, D), f32),
            ],
            axis=0,
        )
        accumulate(i, dvec_ref, sums)

    @pl.when(i == images)
    def _():
        dw = tn(dat_ref[...], o_ref[...]).astype(bf16)
        if weight.pieces:
            for half in range(2):
                weave(dw_ref.at[half], dw[half * 384 : half * 384 + 384])
        else:
            dw_ref[...] = dw
        weight.wait(me_ref, refs[:count], w_ref, sems)
        do_ref[...] = nn(dat_ref[...], w_ref[...].reshape(D, D)).astype(bf16)


def middle_backward(images, h, dm, col, spread, o, weight, vec, me):
    n = images * ROWS
    dw_shape = (2, 16, 48, 384) if weight.pieces else (D, D)

    def rows(cols):
        return pl.BlockSpec((ROWS, cols), lambda i, me: (jnp.minimum(i, images - 1), 0))

    return call(
        functools.partial(middle_back_kernel, images, weight),
        (sds((n, D), f32), sds((n, D), bf16), sds(dw_shape, bf16), sds((8, D), f32)),
        (me, *weight.arrays, h, dm, col, spread, o, vec),
        weight.specs + [rows(D), rows(D), rows(128), whole((16, D)), whole((n, D)), whole((16, D))],
        [rows(D), whole((n, D)), whole(dw_shape), whole((8, D))],
        grid=(images + 1,),
        in_hbm=(1 + len(weight.arrays),),
        vmem_in=(2 + len(weight.arrays),) if weight.pieces else (),
        scratch=weight.scratch + [pltpu.VMEM((n, D), bf16)],
        flops=4 * n * D * D,
        prefetch=1,
    )


def attention_again_kernel(qkv_ref, lse_ref, col_ref, p_ref):
    low_half = lax.broadcasted_iota(jnp.int32, (ROWS, 2 * HEAD), 1) < HEAD
    valid = jnp.broadcast_to(col_ref[:, 0:1], (ROWS, ROWS)) > 0.0
    for pair in range(HEADS // 2):
        at = pair * 2 * HEAD
        q = qkv_ref[:, at : at + 2 * HEAD]
        k = qkv_ref[:, D + at : D + at + 2 * HEAD]
        for half in range(2):
            keep = low_half if half == 0 else jnp.logical_not(low_half)
            head = 2 * pair + half
            s = jnp.where(valid, nt(jnp.where(keep, k, jnp.zeros_like(k)), q), masked_score)
            p_ref[0, head] = jnp.exp(s - lse_ref[0, head : head + 1, :]).astype(bf16)


def attention_again(images, qkv, lse, col):
    n = images * ROWS
    return call(
        attention_again_kernel,
        (sds((images, HEADS, ROWS, ROWS), bf16),),
        (qkv, lse, col),
        [rows_at(ROWS, 3 * D), pl.BlockSpec((1, 16, ROWS), lambda i: (i, 0, 0)), rows_at(ROWS, 128)],
        [pl.BlockSpec((1, HEADS, ROWS, ROWS), lambda i: (i, 0, 0, 0))],
        grid=(images,),
        vmem_out=(0,),
        flops=2 * n * ROWS * D,
    )[0]


def attention_back_kernel(qkv_ref, do_ref, p_ref, dqkv_ref, db_ref):
    i = pl.program_id(0)
    low_half = lax.broadcasted_iota(jnp.int32, (ROWS, 2 * HEAD), 1) < HEAD
    for pair in range(HEADS // 2):
        at = pair * 2 * HEAD
        q = qkv_ref[:, at : at + 2 * HEAD]
        k = qkv_ref[:, D + at : D + at + 2 * HEAD]
        v = qkv_ref[:, 2 * D + at : 2 * D + at + 2 * HEAD]
        do = do_ref[:, at : at + 2 * HEAD]
        dv, dk, dq = [], [], []
        for half in range(2):
            keep = low_half if half == 0 else jnp.logical_not(low_half)
            only_k = jnp.where(keep, k, jnp.zeros_like(k))
            only_v = jnp.where(keep, v, jnp.zeros_like(v))
            head = 2 * pair + half
            rounded = p_ref[0, head]
            p = rounded.astype(f32)
            dp = nt(only_v, do)
            share = jnp.sum(p * dp, axis=0, keepdims=True)
            ds = (p * (dp - share)).astype(bf16)
            dv.append(nn(rounded, do))
            dk.append(nn(ds, q))
            dq.append(tn(ds, only_k))
        dqkv_ref[:, at : at + 2 * HEAD] = ((dq[0] + dq[1]) * (HEAD**-0.5)).astype(bf16)
        dqkv_ref[:, D + at : D + at + 2 * HEAD] = jnp.where(low_half, dk[0], dk[1]).astype(bf16)
        dqkv_ref[:, 2 * D + at : 2 * D + at + 2 * HEAD] = jnp.where(low_half, dv[0], dv[1]).astype(bf16)
    accumulate(i, db_ref, nn(jnp.ones((16, ROWS), bf16), dqkv_ref[...]))


def attention_backward(images, qkv, do, p):
    n = images * ROWS
    return call(
        attention_back_kernel,
        (sds((n, 3 * D), bf16), sds((16, 3 * D), f32)),
        (qkv, do, p),
        [
            rows_at(ROWS, 3 * D),
            rows_at(ROWS, D),
            pl.BlockSpec((1, HEADS, ROWS, ROWS), lambda i: (i, 0, 0, 0)),
        ],
        [rows_at(ROWS, 3 * D), whole((16, 3 * D))],
        grid=(images,),
        vmem_in=(2,),
        flops=10 * n * ROWS * D,
    )


def qkv_grad_kernel(dqkv_ref, a_ref, dw_ref):
    dw_ref[...] = tn(dqkv_ref[...], a_ref[...]).astype(bf16)


def qkv_weight_grad(images, dqkv, a):
    n = images * ROWS
    return call(
        qkv_grad_kernel,
        (sds((3 * D, D), bf16),),
        (dqkv, a),
        [cols_at(n, D), whole((n, D))],
        [rows_at(D, D)],
        grid=(3,),
        flops=6 * n * D * D,
    )[0]


def qkv_grad_fast_kernel(_, dqkv_ref, a_ref, out_ref, pieces_ref):
    j = pl.program_id(0)

    @pl.when(j < 3)
    def _():
        weave(pieces_ref, tn(dqkv_ref[...], a_ref[...]).astype(bf16))

    @pl.when(j == 3)
    def _():
        pieces_ref[...] = out_ref[0]


def qkv_weight_grad_fast(images, dqkv, a, dw_out, me, other):
    n = images * ROWS

    def half(me):
        return 1 - me[CORE] if other else me[CORE]

    return call(
        qkv_grad_fast_kernel,
        (sds((16, 192, 384), bf16),),
        (me, dqkv, a, dw_out),
        [
            pl.BlockSpec((n, 384), lambda j, me: (0, half(me) * 3 + jnp.minimum(j, 2))),
            whole((n, D)),
            pl.BlockSpec((1, 16, 48, 384), lambda j, me: (half(me), 0, 0, 0)),
        ],
        [pl.BlockSpec((16, 48, 384), lambda j, me: (0, j, 0))],
        grid=(4,),
        out_hbm=(0,),
        flops=3 * n * D * D,
        prefetch=1,
    )[0]


def input_back_kernel(weight, me_ref, *refs):
    count = len(weight.arrays)
    x_ref, dqkv_ref, dh_ref, vec_ref, two_ref, bias_ref, up_ref, out_ref, dvec_ref, w_ref, sems, sum_ref = refs[count:]
    i = pl.program_id(0)
    weight.load(me_ref, refs[:count], w_ref, sems)
    da = nn(dqkv_ref[...], w_ref[...].reshape(3 * D, D))
    hat, inverse = normalized(x_ref[...].astype(f32))
    out = dh_ref[...] + norm_back(da, hat, inverse, vec_ref[0:1, :])
    out_ref[0] = out[0:PATCHES, :]
    sums = jnp.concatenate([column_sum(da * hat), column_sum(da), jnp.zeros((6, D), f32)], axis=0)
    accumulate(i, sum_ref, sums)

    @pl.when(i == pl.num_programs(0) - 1)
    def _():
        dvec_ref[...] = jnp.zeros_like(dvec_ref)
        dvec_ref[0:2, :] = sum_ref[0:2, :]
        dvec_ref[2:4, :] = two_ref[0:2, :]
        dvec_ref[4:5, :] = bias_ref[0:1, 0:D]
        dvec_ref[5:6, :] = bias_ref[0:1, 2 * D : 3 * D]
        dvec_ref[6:7, :] = two_ref[2:3, :]
        for b in range(FF // D):
            dvec_ref[7 + b : 8 + b, :] = up_ref[0:1, b * D : (b + 1) * D]
        dvec_ref[7 + FF // D : 8 + FF // D, :] = two_ref[3:4, :]


def input_backward(images, x, dqkv, weight, dh, vec, g_two, g_bias, g_bias_up, me):
    n = images * ROWS
    return call(
        functools.partial(input_back_kernel, weight),
        (sds((images, PATCHES, D), f32), sds((16, D), f32)),
        (me, *weight.arrays, x, dqkv, dh, vec, g_two, g_bias, g_bias_up),
        weight.specs
        + [rows_at(ROWS, D), rows_at(ROWS, 3 * D), rows_at(ROWS, D)]
        + [whole(a.shape) for a in (vec, g_two, g_bias, g_bias_up)],
        [pl.BlockSpec((1, PATCHES, D), lambda i, *_: (i, 0, 0)), whole((16, D))],
        grid=(images,),
        scratch=weight.scratch + [pltpu.VMEM((8, D), f32)],
        flops=6 * n * D * D,
        prefetch=1,
    )


SUMMED, DOWN, PROJ, NONE, VEC = 0, 1, 2, 3, 4


def adam_kernel(part_rows, fast, each, kind_ref, row_ref, *refs):
    master_ref, first_ref, second_ref, summed_ref, down_ref, proj_ref, vec_ref = refs[:7]
    new_master_ref, new_first_ref, new_second_ref, grad_ref, woven_ref = refs[7:]
    wide = FF // D
    for k in range(each):
        slot = pl.program_id(0) * each + k
        kind = kind_ref[slot]

        @pl.when(kind == SUMMED)
        def _():
            if fast:
                for z in range(4):
                    for y in range(2):
                        grad_ref[16 * z : 16 * z + 16, 384 * y : 384 * y + 384] = summed_ref[2 * z + y, k].astype(f32)
            else:
                grad_ref[...] = summed_ref[k].astype(f32)

        @pl.when(kind == VEC)
        def _():
            grad_ref[...] = jnp.zeros_like(grad_ref)
            grad_ref[0 : vec_ref.shape[0], :] = vec_ref[...]

        @pl.when(kind == DOWN)
        def _():
            for c in range(D // 128):
                for b in range(wide):
                    lanes = slice(b * D + c * 128, b * D + c * 128 + 128)
                    woven_ref[c, pl.ds(b, part_rows // wide, stride=wide), :] = down_ref[k, 0 : part_rows // wide, lanes]
                grad_ref[:, c * 128 : (c + 1) * 128] = woven_ref[c]

        @pl.when(kind == PROJ)
        def _():
            at = pl.multiple_of(row_ref[slot], part_rows)
            grad_ref[...] = proj_ref[pl.ds(at, part_rows), :]

        @pl.when(kind == NONE)
        def _():
            grad_ref[...] = jnp.zeros_like(grad_ref)

        grad = grad_ref[...]
        master = master_ref[0, k]
        first = beta_one * first_ref[0, k] + (1.0 - beta_one) * grad
        second = beta_two * second_ref[0, k] + (1.0 - beta_two) * grad * grad
        new_first_ref[0, k] = first
        new_second_ref[0, k] = second
        direction = first / (1.0 - beta_one**STEP)
        size = jnp.sqrt(second / (1.0 - beta_two**STEP)) + adam_eps
        new_master_ref[0, k] = master - learn_rate * (direction / size + decay_rate * master)


def adam(kind, row, master, first, second, summed, down, proj, vec, fast):
    slots, part_rows = master.shape[1:3]
    each = slots // 2
    block = pl.BlockSpec((1, each, part_rows, D), lambda s, *_: (0, s, 0, 0))
    if fast:
        summed_spec = pl.BlockSpec((8, each, 16, 384), lambda s, *_: (0, s, 0, 0))
    else:
        summed_spec = pl.BlockSpec((each, part_rows, D), lambda s, *_: (s, 0, 0))
    return call(
        functools.partial(adam_kernel, part_rows, fast, each),
        (sds(master.shape, f32),) * 3,
        (kind, row, master, first, second, summed, down, proj, vec),
        [
            block,
            block,
            block,
            summed_spec,
            pl.BlockSpec((each,) + down.shape[1:], lambda s, *_: (s, 0, 0)),
            whole(proj.shape),
            whole(vec.shape),
        ],
        [block] * 3,
        grid=(slots // each,),
        scratch=[pltpu.VMEM((part_rows, D), f32), pltpu.VMEM((D // 128, part_rows, 128), f32)],
        flops=20 * slots * part_rows * D,
        in_hbm=(2, 3, 4, 6, 7),
        prefetch=2,
    )


def rank_grad_kernel(images, kind_ref, row_ref, *refs):
    dz_ref, pooled_ref, down_ref, proj_ref = refs[-4:]
    held = jnp.concatenate([ref[...].reshape(64, PACK) for ref in refs[:-4]], axis=0)
    row = lax.broadcasted_iota(jnp.int32, (D, 128), 0)
    col = lax.broadcasted_iota(jnp.int32, (D, 128), 1)
    wanted = jnp.full((D, 128), -1, jnp.int32)
    for s in range(8):
        first = jnp.where(kind_ref[s] == DOWN, row_ref[s], -D)
        wanted = jnp.where(col // 16 == s, first + col % 16, wanted)
    mine = nn(held[:, 0:D], jnp.where(row == wanted, 1.0, 0.0).astype(bf16)).astype(bf16)
    shape = (512, 512)
    row = lax.broadcasted_iota(jnp.int32, shape, 0)
    col = lax.broadcasted_iota(jnp.int32, shape, 1)
    first = 0
    for segment in range(3):
        here = (row - col == segment * images) & (row // 16 == col // 16) & (col % 16 < images)
        rank = nn(jnp.where(here, 1.0, 0.0).astype(bf16), mine).astype(bf16)
        part = held[:, D:PACK] if segment == 0 else held
        down_ref[:, first : first + part.shape[1]] = tn(rank, part)
        first += part.shape[1]
    proj_ref[...] = tn(dz_ref[...], pooled_ref[...])


def rank_grads(images, kind, row, arrays, dz, pooled):
    return call(
        functools.partial(rank_grad_kernel, images),
        (sds((128, FF), f32), sds((EMB, D), f32)),
        (kind, row, *arrays, dz, pooled),
        [whole(a.shape) for a in arrays] + [whole(dz.shape), whole(pooled.shape)],
        [whole((128, FF)), whole((EMB, D))],
        out_hbm=(0, 1),
        flops=256 * D * FF,
        prefetch=2,
    )


def slot_place(owner_list, slot_count):
    tile_count = owner_list.shape[0]
    earlier = jnp.tril(jnp.ones((tile_count, tile_count), jnp.int32), -1)
    same_owner = (owner_list[:, None] == owner_list[None, :]).astype(jnp.int32)
    return owner_list * slot_count + jnp.sum(same_owner * earlier, axis=1)


def gather_weights(master, placed):
    n_dp, n_rep = lax.axis_size("dp"), lax.axis_size("rep")
    slots, part_rows = master.shape[1:3]
    gathered = lax.all_gather(master.astype(bf16), AXES, axis=0, tiled=True)
    gathered = gathered.reshape(n_dp, n_rep * slots, part_rows, D)
    return jnp.transpose(jnp.take(gathered, placed, axis=1), (1, 0, 2, 3)).reshape(-1, D)


def scatter_grads(tiles, tile_of_slot, slots, part_rows):
    n_dp, n_rep = lax.axis_size("dp"), lax.axis_size("rep")
    count = tiles.shape[0]
    tiles = jnp.concatenate([tiles, jnp.zeros((1, TR, D), tiles.dtype)], axis=0)
    index = jnp.where(tile_of_slot < count, tile_of_slot, count)
    buffer = jnp.take(tiles, index, axis=0).reshape(n_rep * slots, n_dp, part_rows, D)
    buffer = jnp.transpose(buffer, (1, 0, 2, 3)).reshape(n_dp * n_rep, slots, part_rows, D)
    return lax.psum_scatter(buffer, AXES, scatter_dimension=0, tiled=True)[0]


def pairs(move):
    def number(x, z, y, c):
        return x * 16 + z * 4 + y * 2 + c

    return [(number(x, z, y, c), number(*move(x, z, y, c))) for x, z, y in PIECES for c in range(2)]


SWAP_CORE = pairs(lambda x, z, y, c: (x, z, y, 1 - c))
SWAP_X = pairs(lambda x, z, y, c: (1 - x, z, y, c))
SWAP_Y = pairs(lambda x, z, y, c: (x, z, 1 - y, c))
SWAP_Z = pairs(lambda x, z, y, c: (x, z ^ 1, y, c))
SWAP_ZZ = pairs(lambda x, z, y, c: (x, z ^ 2, y, c))
SWAP_XY = pairs(lambda x, z, y, c: (1 - x, z, 1 - y, c))
ACROSS_Z = [pairs(lambda x, z, y, c, k=k: (x, z ^ k, y, c)) for k in (1, 2, 3)]
CROSS_ONE = pairs(lambda x, z, y, c: (1 - x, z, y, c) if c == 0 else (x, z, 1 - y, c))
CROSS_TWO = pairs(lambda x, z, y, c: (x, z, 1 - y, c) if c == 0 else (1 - x, z, y, c))


def send(value, permutation):
    return lax.ppermute(value, AXES, permutation)


def add_kernel(count, pieces, outputs, _, *refs):
    for p in range(pieces):
        total = refs[p * count][0].astype(f32)
        for k in range(1, count):
            total += refs[p * count + k][0].astype(f32)
        outs = refs[pieces * count :]
        if outputs == 1:
            outs[0][p] = total.astype(outs[0].dtype)
        else:
            outs[p][...] = total.astype(outs[p].dtype)


def add_pieces(sources, me, pieces, steps=1, dtypes=(bf16,), near=()):
    rows = sources[0][0].shape[1]
    each = pieces // steps
    arrays, specs = [], []
    for p in range(each):
        for array, at in sources:
            arrays.append(array)
            specs.append(pl.BlockSpec((1, rows, 384), lambda i, me, p=p, at=at: (at(i * each + p, me), 0, 0)))
    if len(dtypes) == 1:
        shapes = (sds((pieces, rows, 384), dtypes[0]),)
        outs = [pl.BlockSpec((each, rows, 384), lambda i, me: (i, 0, 0))]
    else:
        shapes = tuple(sds((rows, 384), dtype) for dtype in dtypes)
        outs = [whole((rows, 384))] * pieces
    in_hbm = [k + 1 for k in range(len(arrays)) if k % len(sources) not in near]
    results = call(
        functools.partial(add_kernel, len(sources), each, len(dtypes)),
        shapes,
        (me, *arrays),
        specs,
        outs,
        grid=(steps,),
        flops=pieces * rows * D,
        in_hbm=in_hbm,
        prefetch=1,
    )
    return results[0] if len(dtypes) == 1 else results


class PieceSum:
    def __init__(self, other, me):
        self.me = me
        self.one = send(other, SWAP_CORE)

    def first_send(self, i, me):
        return jnp.where(me[CORE] == 0, (1 - me[X]) * 8 + i, i * 2 + 1 - me[Y])

    def kept(self, i, me):
        return jnp.where(me[CORE] == 0, me[X] * 8 + i, i * 2 + me[Y])

    def second_send(self, i, me):
        return jnp.where(me[CORE] == 0, 2 * i + 1 - me[Y], (1 - me[X]) * 4 + i)

    def second_keep(self, i, me):
        return jnp.where(me[CORE] == 0, 2 * i + me[Y], me[X] * 4 + i)

    def cross_one(self):
        parts = [(self.mine, self.first_send), (self.one, self.first_send)]
        self.two = send(add_pieces(parts, self.me, 8, 2, near=(1,)), CROSS_ONE)

    def cross_two(self):
        def own(i, me):
            return self.kept(self.second_send(i, me), me)

        parts = [(self.mine, own), (self.one, own), (self.two, self.second_send)]
        self.three = send(add_pieces(parts, self.me, 4, near=(2,)), CROSS_TWO)

    def partial(self):
        def crossed(i, me):
            return self.second_keep(me[Z] ^ i, me)

        def own(i, me):
            return self.kept(crossed(i, me), me)

        parts = [(self.mine, own), (self.one, own), (self.two, crossed)]
        self.sums = add_pieces(parts, self.me, 4, dtypes=(f32,))

    def cross_z(self):
        parts = [(self.sums, lambda i, me: i), (self.three, lambda i, me: me[Z] ^ i)]
        self.own, *parts = add_pieces(parts, self.me, 4, dtypes=(f32, bf16, bf16, bf16), near=(0, 1))
        self.last = [send(part, move) for part, move in zip(parts, ACROSS_Z, strict=True)]

    def total(self):
        parts = [(part[None], lambda i, me: 0) for part in (self.own, *self.last)]
        return add_pieces(parts, self.me, 1, near=(0, 1, 2, 3))[0]


def place_kernel(index_ref, *refs):
    out_ref = refs[-1]
    for k in range(out_ref.shape[0]):
        at = index_ref[k]
        for q in range(4):

            @pl.when((at >= 12 * q) & (at < 12 * q + 12))
            def _():
                out_ref[k] = refs[q][pl.ds(pl.multiple_of((at - 12 * q) * 16, 16), 16), :]

        @pl.when(at >= 48)
        def _():
            out_ref[k] = jnp.zeros((16, 384), bf16)


def return_to_owners(sums, place):
    placed = call(
        place_kernel,
        (sds((64, 16, 384), bf16),),
        (place, *sums),
        [whole((192, 384))] * 4,
        [whole((64, 16, 384))],
        prefetch=1,
    )[0]
    return lax.all_to_all(placed.reshape(8, 8, 16, 384), "rep", 0, 0, axis_index_groups=SAME_CORE)


def plan_kernel(owner_ref, me_ref, pick_ref, place_ref, kind_ref, row_ref, counts, placed, tile_of):
    x, c = me_ref[X], me_ref[CORE]
    rep = me_ref[Z] * 4 + me_ref[Y] * 2 + c

    @pl.loop(0, 16)
    def _(r):
        counts[r] = 0

    @pl.loop(0, 128)
    def _(k):
        tile_of[k] = 1 << 20

    @pl.loop(0, VEC_TILE + 1)
    def _(t):
        owner = owner_ref[t]
        at = owner * 8 + counts[owner]
        counts[owner] = counts[owner] + 1
        placed[t] = at
        tile_of[at] = t

    def slab(t):
        at = placed[t]
        owner = at // 8
        return jnp.where(owner % 2 == c, 0, 64) + owner // 2 * 8 + at % 8

    def fill(first, count, tile):
        @pl.loop(0, count)
        def _(k):
            pick_ref[first + k] = slab(tile + k)

    base = 0
    for tiles, tile in CHUNK_TILES:
        fill(base, tiles, tile + tiles * c)
        base += tiles
    pick_ref[base] = slab(VEC_TILE)

    @pl.loop(0, 64)
    def _(k):
        t = tile_of[k // 8 * 16 + c * 8 + k % 8]
        u = t - QKV_TILES
        v = u - OUT_TILES
        half = jnp.where(t < QKV_TILES, t // 9, jnp.where(u < OUT_TILES, u // 3, v // 12))
        place = jnp.where(t < QKV_TILES, t % 9, jnp.where(u < OUT_TILES, 9 + u % 3, 12 + v % 12))
        place_ref[k] = jnp.where(t < DOWN_FIRST, jnp.where(half == c, place, 24 + place), 48)

    @pl.loop(0, 8)
    def _(k):
        t = tile_of[rep * 8 + k]
        is_down = (t >= DOWN_FIRST) & (t < PROJ_FIRST)
        is_proj = (t >= PROJ_FIRST) & (t < VEC_TILE)
        kind = jnp.where(t < DOWN_FIRST, SUMMED, jnp.where(is_down, DOWN, jnp.where(is_proj, PROJ, NONE)))
        kind_ref[k] = jnp.where((t == VEC_TILE) & (x == 0), VEC, kind)
        row_ref[k] = jnp.where(
            is_down, ((t - DOWN_FIRST) * TR + x * 64) // 4, jnp.where(is_proj, (t - PROJ_FIRST) * TR + x * 64, 0)
        )


def plan(owner_list, me):
    smem = pl.BlockSpec(memory_space=pltpu.SMEM)
    sizes = (sum(tiles for tiles, _ in CHUNK_TILES) + 1, 64, 8, 8)
    return pl.pallas_call(
        plan_kernel,
        out_shape=tuple(sds((size,), jnp.int32) for size in sizes),
        in_specs=[smem, smem],
        out_specs=(smem,) * 4,
        scratch_shapes=[pltpu.SMEM((16,), jnp.int32), pltpu.SMEM((128,), jnp.int32), pltpu.SMEM((128,), jnp.int32)],
    )(owner_list, me)


def prepare_kernel(owner_ref, me_ref, master_ref, out_ref, lanes_ref, tile_ref):
    rep = me_ref[Z] * 4 + me_ref[Y] * 2 + me_ref[CORE]
    for s in range(9):
        tile_ref[s] = 0

    def note(t, held):
        here = owner_ref[t] == rep

        @pl.when(here)
        def _():
            tile_ref[held] = t

        return held + jnp.where(here, 1, 0)

    lax.fori_loop(DOWN_FIRST, PROJ_FIRST, note, lax.fori_loop(0, DOWN_FIRST, note, 0))
    for s in range(8):
        down = (tile_ref[s] >= DOWN_FIRST) & (tile_ref[s] < PROJ_FIRST)

        @pl.when(jnp.logical_not(down))
        def _():
            for z in range(4):
                for y in range(2):
                    out_ref[2 * z + y, s] = master_ref[0, s, 16 * z : 16 * z + 16, 384 * y : 384 * y + 384].astype(bf16)

        @pl.when(down)
        def _():
            for k in range(6):
                lanes_ref[k] = master_ref[0, s, :, 128 * k : 128 * k + 128]
            for z in range(4):
                for k in range(6):
                    part = lanes_ref[k, pl.ds(z, 16, stride=4), :]
                    out_ref[2 * z + k // 3, s, :, k % 3 * 128 : k % 3 * 128 + 128] = part.astype(bf16)


def pick_kernel(index_ref, mine_ref, theirs_ref, text_ref, one_ref, two_ref, three_ref):
    def slab(k, ref, j):
        at = index_ref[k]

        @pl.when(at < 64)
        def _():
            ref[j] = mine_ref[at]

        @pl.when(at >= 64)
        def _():
            ref[j] = theirs_ref[at - 64]

    k = 0
    for (tiles, _), (chunk, first) in zip(CHUNK_TILES, CHUNK_AT, strict=True):
        for j in range(tiles):
            slab(k, (one_ref, two_ref, three_ref)[chunk], first + j)
            k += 1
    slab(k, one_ref, 9)
    text = text_ref[...].astype(f32)
    count = text.shape[0]
    text = (text * lax.rsqrt(jnp.sum(text * text, axis=-1, keepdims=True) + unit_eps)).astype(bf16)
    three_ref[14] = jnp.zeros((16, 384), bf16)
    three_ref[14, 0:count, :] = text[:, 0:384]
    three_ref[14, 8 : 8 + count, 0:128] = text[:, 384:512]


class Spread:
    def __init__(self, block):
        self.parts = [block] + [send(block, move) for move in ACROSS_Z]

    def cross_one(self):
        self.ring = jnp.stack(self.parts)
        self.one = send(self.ring, CROSS_ONE)
        self.two = None
        self.near = []

    def cross_two(self):
        if self.two is None:
            self.two = send(self.ring, CROSS_TWO)
        self.both = send(self.one, CROSS_TWO)

    def send_near(self, *which):
        for k in which:
            self.near.append(send(getattr(self, ("ring", "one", "two", "both")[k]), SWAP_CORE))

    def finish(self):
        self.send_near(*range(len(self.near), 4))

    def arrays(self):
        return (self.ring, self.one, self.two, self.both, *self.near)


def meet(*values):
    return lax.optimization_barrier(values)


def sources(me):
    for other in range(2):
        c = me[CORE] if other == 0 else 1 - me[CORE]
        for crossed in range(4):
            one, two = crossed % 2, crossed // 2
            flip_x = jnp.where(c == 0, one, two)
            flip_y = jnp.where(c == 0, two, one)
            yield c, me[X] + flip_x - 2 * me[X] * flip_x, me[Y] + flip_y - 2 * me[Y] * flip_y


def pick_slabs(master, text_emb, owner_list, me, *others):
    prepared = call(
        prepare_kernel,
        (sds((8, 8, 16, 384), bf16),),
        (owner_list, me, master),
        [whole(master.shape)],
        [whole((8, 8, 16, 384))],
        scratch=[pltpu.VMEM((6, 64, 128), f32), pltpu.SMEM((16,), jnp.int32)],
        in_hbm=(2,),
        prefetch=2,
    )[0]
    pick, place, kind, row = plan(owner_list, me)
    mine = lax.all_to_all(prepared, "rep", 0, 0, axis_index_groups=SAME_CORE).reshape(64, 16, 384)
    mine, pick, *others = meet(mine, pick, *others)
    blocks = call(
        pick_kernel,
        tuple(sds((slabs, 16, 384), bf16) for slabs in SLABS),
        (pick, mine, send(mine, SWAP_CORE), text_emb),
        [whole((64, 16, 384)), whole((64, 16, 384)), whole(text_emb.shape)],
        [whole((slabs, 16, 384)) for slabs in SLABS],
        prefetch=1,
    )
    return blocks, (place, kind, row), others


def shards(block_in, tissue, text_emb, text_order, owner_list, master, first_moment, second_moment):
    n_dp = lax.axis_size("dp")
    n_rep = lax.axis_size("rep")
    images = block_in.shape[0]
    slots, part_rows = master.shape[1:3]
    image_total = text_order.shape[0]
    n = images * ROWS
    dp_at, rep_at = lax.axis_index("dp"), lax.axis_index("rep")
    first_image = lax.axis_index(AXES) * images

    x = jnp.pad(block_in, ((0, 0), (0, ROWS - PATCHES), (0, 0))).reshape(n, D)
    valid = jnp.pad((tissue > 0).astype(f32), ((0, 0), (0, ROWS - PATCHES)))
    mask_row = valid[:, None, :]
    col = jnp.broadcast_to(valid.reshape(n, 1), (n, 128))
    numbers = jnp.arange(images, dtype=jnp.int32)
    sel = jnp.where(
        numbers[:, None, None] == jnp.arange(16, dtype=jnp.int32)[None, :, None], valid[:, None, :], 0.0
    ).astype(bf16)
    inv_count = jnp.pad(1.0 / jnp.sum(valid, axis=1), (0, 16 - images))
    inv_count = jnp.broadcast_to(inv_count[:, None], (16, 128))
    order = jnp.broadcast_to(text_order[:, None], (image_total, 128))
    first_image = first_image.astype(jnp.int32)[None]

    fast = (n_dp, n_rep, slots, part_rows) == (2, 16, 8, 64)
    if fast:
        me = jnp.stack([dp_at, rep_at // 4, rep_at // 2 % 2, rep_at % 2]).astype(jnp.int32)
        (block_one, block_two, block_three), (place, kind, row), others = pick_slabs(
            master, text_emb, owner_list, me, x, mask_row, col, sel, inv_count, order, first_image
        )
        x, mask_row, col, sel, inv_count, order, first_image = others
        one = Spread(block_one)
        *one.parts, block_two = meet(*one.parts, block_two)
        one.cross_one()
        one.two = send(one.ring, CROSS_TWO)
        two = Spread(block_two)
        one.ring, one.one, one.two = meet(one.ring, one.one, one.two)
        one.cross_two()
        one.send_near(0, 1)
        one.two, *two.parts = meet(one.two, *two.parts)
        one.send_near(2)
        one.both, block_three = meet(one.both, block_three)
        one.finish()
        two.cross_one()
        two.send_near(0)
        w_qkv = Weight(one.arrays(), QKV_TILES)
        a, qkv, vec = qkv_forward(images, x, jnp.zeros((16, D), f32), w_qkv, me)
        qkv, two.ring, two.one, two.near[0], block_three = meet(qkv, two.ring, two.one, two.near[0], block_three)
        two.cross_two()
        three = Spread(block_three)
        o, lse = attention_forward(images, qkv, mask_row)
        o, two.two, two.both, *three.parts = meet(o, two.two, two.both, *three.parts)
        two.finish()
        three.cross_one()
        w_out = Weight(two.arrays(), OUT_TILES)
        h, m = middle_forward(images, x, o, vec, w_out, me)
        h, m, three.ring, three.one = meet(h, m, three.ring, three.one)
        three.cross_two()
        three.send_near(0, 1)
        bias_up = vec[7 : 7 + FF // D].reshape(FF // D, 1, D)
        w_up = Weight(two.arrays(), UP_TILES, 3)
        act, slope = up_forward(images, m, w_up, bias_up, me)
        act, three.two, three.both, *three.near = meet(act, three.two, three.both, *three.near)
        three.finish()
        w_down = Weight(three.arrays(), DOWN_TILES, quarters=True)
        w_proj = Weight(three.arrays(), PROJ_TILES, 12)
        all_text = jnp.zeros((16, 128), bf16)
    else:
        me = jnp.zeros((4,), jnp.int32)
        placed = slot_place(owner_list, slots)
        hits = placed[None, :] == jnp.arange(n_rep * slots, dtype=jnp.int32)[:, None]
        tile_ids = jnp.arange(owner_list.shape[0], dtype=jnp.int32)[None, :]
        tile_of_slot = jnp.where(jnp.any(hits, axis=1), jnp.sum(jnp.where(hits, tile_ids, 0), axis=1), 1 << 20)
        text = text_emb.astype(f32)
        own_text = (text * lax.rsqrt(jnp.sum(text * text, axis=-1, keepdims=True) + unit_eps)).astype(bf16)
        all_text = lax.all_gather(own_text, AXES, axis=0, tiled=True)
        tiles = gather_weights(master, placed).reshape(-1, TR, D)
        w_qkv = Weight([tiles[:QKV_TILES]], QKV_TILES)
        w_out = Weight([tiles[QKV_TILES : QKV_TILES + OUT_TILES]], OUT_TILES)
        w_up = Weight([tiles[QKV_TILES + OUT_TILES : DOWN_FIRST]], UP_TILES)
        w_down = Weight([tiles[DOWN_FIRST:PROJ_FIRST].reshape(DOWN_TILES, TR // 4, FF)], DOWN_TILES, quarters=True)
        w_proj = Weight([tiles[PROJ_FIRST:VEC_TILE]], PROJ_TILES)
        a, qkv, vec = qkv_forward(images, x, tiles[VEC_TILE, :16].astype(f32), w_qkv, me)
        bias_up = vec[7 : 7 + FF // D].reshape(FF // D, 1, D)
        o, lse = attention_forward(images, qkv, mask_row)
        h, m = middle_forward(images, x, o, vec, w_out, me)
        act, slope = up_forward(images, m, w_up, bias_up, me)
    block_out, pooled = down_forward(images, act, w_down, h, vec, sel, inv_count, me)

    pooled_all = lax.all_to_all(jnp.broadcast_to(pooled[None, :images], (n_dp * n_rep, images, D)), AXES, 0, 0)
    act_sum = act_sums(images, act, sel)
    probabilities = attention_again(images, qkv, lse, col)
    if fast:
        pooled_all, act_sum, probabilities = meet(pooled_all, act_sum, probabilities)
    dz_all, rank, spread, hidden, pooled_all = loss_backward(
        me, first_image, pooled_all, all_text, order, w_proj, w_down, inv_count
    )

    both = jnp.concatenate([rank[:images], act_sum[:images]], axis=1)
    if fast:
        packed = jnp.concatenate([both[:, at * PACK : (at + 1) * PACK] for at in range(3)], axis=0)
        ranks = Spread(jnp.pad(packed, ((0, 16 - 3 * images), (0, 0))))
        dm, g_bias_up, other, mine = up_backward(images, slope, m, w_up, hidden, col, me)
        dm, other, mine, *ranks.parts = meet(dm, other, mine, *ranks.parts)
        up_sum = PieceSum(other, me)
        ranks.cross_one()
        ranks.two = send(ranks.ring, CROSS_TWO)
        dh, do, g_out, g_two = middle_backward(images, h, dm, col, spread, o, w_out, vec, me)
        dh, do, up_sum.mine, up_sum.one, ranks.ring, ranks.one, ranks.two = meet(
            dh, do, mine, up_sum.one, ranks.ring, ranks.one, ranks.two
        )
        up_sum.cross_one()
        ranks.cross_two()
        ranks.send_near(0, 1, 2)
        dqkv, g_bias = attention_backward(images, qkv, do, probabilities)
        dqkv, up_sum.two, ranks.both, *ranks.near = meet(dqkv, up_sum.two, ranks.both, *ranks.near)
        ranks.finish()
        up_sum.cross_two()
        other = qkv_weight_grad_fast(images, dqkv, a, g_out, me, True)
        other, dqkv = meet(other, dqkv)
        qkv_sum = PieceSum(other, me)
        mine = qkv_weight_grad_fast(images, dqkv, a, g_out, me, False)
        up_sum.partial()
        dqkv, up_sum.sums, up_sum.three, qkv_sum.mine, qkv_sum.one, ranks.near[3] = meet(
            dqkv, up_sum.sums, up_sum.three, mine, qkv_sum.one, ranks.near[3]
        )
        qkv_sum.cross_one()
        up_sum.cross_z()
        input_grad, vec_sum = input_backward(images, x, dqkv, w_qkv, dh, vec, g_two, g_bias, g_bias_up, me)
        vec_sum, qkv_sum.two, *up_sum.last = meet(vec_sum, qkv_sum.two, *up_sum.last)
        qkv_sum.cross_two()
        near_vec = send(vec_sum, SWAP_CORE)
        up_total = up_sum.total()
        vec_sum, near_vec, up_total = meet(vec_sum, near_vec, up_total)
        vec_sum += near_vec
        vec_sum += send(vec_sum, SWAP_ZZ)
        qkv_sum.partial()
        vec_sum, qkv_sum.sums, qkv_sum.three, up_total = meet(vec_sum, qkv_sum.sums, qkv_sum.three, up_total)
        qkv_sum.cross_z()
        near_up = send(up_total, SWAP_CORE)
        vec_sum += send(vec_sum, SWAP_Y)
        vec_sum += send(vec_sum, SWAP_Z)
        near_up, vec_sum, *qkv_sum.last = meet(near_up, vec_sum, *qkv_sum.last)
        qkv_total = qkv_sum.total()
        near_qkv = send(qkv_total, SWAP_CORE)
        near_qkv, vec_sum = meet(near_qkv, vec_sum)
        summed = return_to_owners((qkv_total, up_total, near_qkv, near_up), place)
        vec_total = vec_sum + send(vec_sum, SWAP_X)
        g_down, g_proj = rank_grads(images, kind, row, ranks.arrays(), dz_all, pooled_all)
        summed, g_down, g_proj, vec_total = meet(summed, g_down.reshape(8, 16, FF), g_proj, vec_total)
    else:
        both_all = lax.all_gather(both, AXES, axis=0, tiled=True)
        dm, g_bias_up, g_up = up_backward(images, slope, m, w_up, hidden, col, me)
        dh, do, g_out, g_two = middle_backward(images, h, dm, col, spread, o, w_out, vec, me)
        dqkv, g_bias = attention_backward(images, qkv, do, probabilities)
        g_qkv = qkv_weight_grad(images, dqkv, a)
        input_grad, vec_total = input_backward(images, x, dqkv, w_qkv, dh, vec, g_two, g_bias, g_bias_up, me)
        mine = lax.dynamic_slice_in_dim(tile_of_slot, rep_at * slots, slots)
        first_row = dp_at * part_rows
        is_down = (mine >= DOWN_FIRST) & (mine < PROJ_FIRST)
        is_proj = (mine >= PROJ_FIRST) & (mine < VEC_TILE)
        kind = jnp.where(is_down, DOWN, jnp.where(is_proj, PROJ, jnp.where(mine <= VEC_TILE, SUMMED, NONE)))
        kind = kind.astype(jnp.int32)
        each = part_rows * D // FF
        row = jnp.where(is_proj, (mine - PROJ_FIRST) * TR + first_row, 0)
        down_rows = jnp.clip(((mine - DOWN_FIRST) * TR + first_row) * D // FF, 0, D - each)
        g_down = tn(both_all[:, :D], both_all[:, D:])
        g_down = jnp.stack([lax.dynamic_slice_in_dim(g_down, at, each) for at in down_rows])
        g_down = jnp.pad(g_down, ((0, 0), (0, max(0, 8 - each)), (0, 0)))
        g_proj = tn(dz_all, pooled_all)
        last = jnp.pad(vec_total, ((0, TR - 16), (0, 0))).astype(bf16)
        tiles = jnp.concatenate([g_qkv, g_out, g_up, last], axis=0).reshape(-1, TR, D)
        index = jnp.where(tile_of_slot == VEC_TILE, DOWN_FIRST, jnp.where(tile_of_slot < DOWN_FIRST, tile_of_slot, 1 << 20))
        summed = scatter_grads(tiles, index, slots, part_rows)
    new_master, new_first, new_second = adam(
        kind, row, master, first_moment, second_moment, summed, g_down, g_proj, vec_total, fast
    )
    return block_out, input_grad, new_master, new_first, new_second


def solution(mesh):
    in_specs = (
        P(("dp", "rep"), None, None),
        P(("dp", "rep"), None),
        P(("dp", "rep"), None),
        P(),
        P(),
        P("rep", None, "dp", None),
        P("rep", None, "dp", None),
        P("rep", None, "dp", None),
    )
    out_specs = (
        P(("dp", "rep"), None, None),
        P(("dp", "rep"), None, None),
        P("rep", None, "dp", None),
        P("rep", None, "dp", None),
        P("rep", None, "dp", None),
    )
    return jax.shard_map(shards, mesh=mesh, in_specs=in_specs, out_specs=out_specs, check_vma=False)
```

```python
import functools

import jax
import jax.numpy as jnp
from jax import lax
from jax.experimental import pallas as pl
from jax.experimental.pallas import tpu as pltpu
from jax.sharding import PartitionSpec as P

D = 768
HEADS = 12
HEAD = 64
FF = 3072
EMB = 512
PATCHES = 196
STEP = 10
ROWS = 208
TR = 128

logit_scale = 50.0
learn_rate = 0.03
beta_one = 0.9
beta_two = 0.999
adam_eps = 1e-08
decay_rate = 0.05
norm_eps = 1e-05
unit_eps = 1e-06
masked_score = -1000000000.0

bf16 = jnp.bfloat16
f32 = jnp.float32
AXES = ("dp", "rep")
MIB = 1 << 20

X, Z, Y, CORE = range(4)
PIECES = [(x, z, y) for x in range(2) for z in range(4) for y in range(2)]

QKV_TILES = 3 * D // TR
OUT_TILES = D // TR
UP_TILES = FF // TR
DOWN_TILES = FF // TR
PROJ_TILES = EMB // TR
DOWN_FIRST = QKV_TILES + OUT_TILES + UP_TILES
PROJ_FIRST = DOWN_FIRST + DOWN_TILES
VEC_TILE = PROJ_FIRST + PROJ_TILES
PACK = (D + FF) // 3
CHUNK_TILES = (
    (QKV_TILES // 2, 0),
    (OUT_TILES // 2, QKV_TILES),
    (UP_TILES // 2, QKV_TILES + OUT_TILES),
    (DOWN_TILES // 2, DOWN_FIRST),
    (PROJ_TILES // 2, PROJ_FIRST),
)
CHUNK_AT = ((0, 0), (1, 0), (1, 3), (2, 0), (2, 12))
SLABS = (10, 15, 15)
CHIPS = [(dz, dy) for dz in range(4) for dy in range(2)]


def nn(a, b):
    return lax.dot_general(a, b, (((1,), (0,)), ((), ())), preferred_element_type=f32)


def nt(a, b):
    return lax.dot_general(a, b, (((1,), (1,)), ((), ())), preferred_element_type=f32)


def tn(a, b):
    return lax.dot_general(a, b, (((0,), (0,)), ((), ())), preferred_element_type=f32)


def call(kernel, outs, ins, in_specs, out_specs, grid=None, scratch=(), flops=0, vmem=24, prefetch=0, in_hbm=(), out_hbm=(), vmem_in=(), vmem_out=()):
    ins = [
        pltpu.with_memory_space_constraint(a, pltpu.HBM) if k >= prefetch and (s.memory_space is pltpu.HBM or k in in_hbm) else a
        for k, (a, s) in enumerate(zip(ins, [None] * prefetch + list(in_specs), strict=True))
    ]
    ins = [pltpu.with_memory_space_constraint(a, pltpu.VMEM) if k in vmem_in else a for k, a in enumerate(ins)]
    moved = sum(a.size * a.dtype.itemsize for a in ins) + sum(o.size * o.dtype.itemsize for o in outs)
    spaces = {k: pltpu.HBM for k in out_hbm} | {k: pltpu.VMEM for k in vmem_out}
    outs = [spaces[k](o.shape, o.dtype) if k in spaces else o for k, o in enumerate(outs)]
    params = pltpu.CompilerParams(
        vmem_limit_bytes=vmem * MIB,
        dimension_semantics=("arbitrary",) * len(grid or ()) or None,
    )
    return pl.pallas_call(
        kernel,
        out_shape=tuple(outs),
        grid_spec=pltpu.PrefetchScalarGridSpec(
            num_scalar_prefetch=prefetch,
            grid=grid or (1,),
            in_specs=in_specs,
            out_specs=tuple(out_specs),
            scratch_shapes=list(scratch),
        ),
        compiler_params=params,
        cost_estimate=pl.CostEstimate(flops=1, bytes_accessed=1, transcendentals=0),
    )(*ins)


def whole(shape):
    return pl.BlockSpec(shape, lambda *_: (0,) * len(shape))


def rows_at(rows, cols):
    return pl.BlockSpec((rows, cols), lambda i, *_: (i, 0))


def cols_at(rows, cols):
    return pl.BlockSpec((rows, cols), lambda i, *_: (0, i))


def sds(shape, dtype):
    return jax.ShapeDtypeStruct(shape, dtype)


class Weight:
    def __init__(self, arrays, tiles, first=0, quarters=False):
        self.arrays, self.tiles, self.first, self.quarters = tuple(arrays), tiles, first, quarters
        self.pieces = len(arrays) > 1
        self.specs = [pl.BlockSpec(memory_space=pltpu.HBM)] * len(arrays)
        shape = (tiles, TR // 4, FF) if quarters else (tiles, TR, D)
        self.scratch = [pltpu.VMEM(shape, bf16), pltpu.SemaphoreType.DMA((32 if self.pieces else 1,))]

    def copies(self, me, refs, out, sems):
        if not self.pieces:
            return [lambda: pltpu.make_async_copy(refs[0], out, sems.at[0])]
        copies = []
        half = self.tiles // 2
        for at, (c, x, y) in enumerate(sources(me)):
            for back in range(4):
                z = me[Z] ^ back
                if self.quarters:
                    row, col = x * 16, z * D + y * 384
                else:
                    row, col = x * 64 + z * 16, y * 384
                rows = pl.ds(pl.multiple_of(row, 16), 16)
                cols = pl.ds(pl.multiple_of(col, 128), 384)
                source = refs[at].at[back, pl.ds(self.first, half)]
                place = out.at[pl.ds(half * c, half), rows, cols]
                copies.append(functools.partial(pltpu.make_async_copy, source, place, sems.at[len(copies)]))
        return copies

    def start(self, me, refs, out, sems):
        for copy in self.copies(me, refs, out, sems):
            copy().start()

    def wait(self, me, refs, out, sems, part=None, parts=1):
        copies = self.copies(me, refs, out, sems)
        if part is not None and not self.pieces:
            copies = copies if part == 0 else []
        elif part is not None:
            copies = copies[16 * part : 16 * part + 16] if parts == 2 else copies[part::4]
        for copy in copies:
            copy().wait()

    def load(self, me, refs, out, sems):
        @pl.when(pl.program_id(0) == 0)
        def _():
            self.start(me, refs, out, sems)
            self.wait(me, refs, out, sems)


def normalized(x):
    center = x - jnp.mean(x, axis=-1, keepdims=True)
    spread = jnp.mean(center * center, axis=-1, keepdims=True)
    inverse = lax.rsqrt(spread + norm_eps)
    return center * inverse, inverse


def norm_back(grad, hat, inverse, gain):
    scaled = grad * gain
    first = jnp.mean(scaled, axis=-1, keepdims=True)
    second = jnp.mean(scaled * hat, axis=-1, keepdims=True)
    return inverse * (scaled - first - hat * second)


def accumulate(i, ref, value):
    @pl.when(i == 0)
    def _():
        ref[...] = value

    @pl.when(i > 0)
    def _():
        ref[...] += value


def column_sum(x):
    return jnp.sum(x, axis=0, keepdims=True)


def third(j, me):
    return jnp.where(me[CORE] == 0, j, 2 - j)


def qkv_kernel(images, weight, me_ref, *refs):
    count = len(weight.arrays)
    pieces = refs[:count]
    x_ref, vec_in_ref, a_ref, qkv_ref, vec_ref, w_ref, sems, vec_half, vec_sems = refs[count:]
    j = pl.program_id(0)

    @pl.when(j == 0)
    def _():
        weight.start(me_ref, pieces, w_ref, sems)
        if weight.pieces:
            parts = []
            for at, (_, x, y) in list(enumerate(sources(me_ref)))[:4]:
                for back in range(4):
                    copy = pltpu.make_async_copy(pieces[at].at[back, 9], vec_half.at[y], vec_sems.at[len(parts)])
                    parts.append(((x == 0) & ((me_ref[Z] ^ back) == 0), copy))
            for here, copy in parts:
                pl.when(here)(copy.start)
            for here, copy in parts:
                pl.when(here)(copy.wait)
            vec_ref[...] = jnp.concatenate([vec_half[0], vec_half[1]], axis=1).astype(f32)
        else:
            vec_ref[...] = vec_in_ref[...]
        for i in range(images):
            hat, _ = normalized(x_ref[pl.ds(i * ROWS, ROWS), :].astype(f32))
            a_ref[pl.ds(i * ROWS, ROWS), :] = (hat * vec_ref[0:1, :] + vec_ref[1:2, :]).astype(bf16)
        weight.wait(me_ref, pieces, w_ref, sems, 0, 2)

    @pl.when(j == 1)
    def _():
        weight.wait(me_ref, pieces, w_ref, sems, 1, 2)

    j = third(j, me_ref)
    bias = jnp.where(j == 0, vec_ref[4:5, :], jnp.where(j == 2, vec_ref[5:6, :], 0.0))
    scale = jnp.where(j == 0, f32(HEAD**-0.5), f32(1.0))
    w = w_ref[pl.ds(6 * j, 6)].reshape(D, D)
    qkv_ref[...] = ((nt(a_ref[...], w) + bias) * scale).astype(bf16)


def qkv_forward(images, x, vec, weight, me):
    n = images * ROWS
    return call(
        functools.partial(qkv_kernel, images, weight),
        (sds((n, D), bf16), sds((n, 3 * D), bf16), sds((16, D), f32)),
        (me, *weight.arrays, x, vec),
        weight.specs + [whole((n, D)), whole((16, D))],
        [whole((n, D)), pl.BlockSpec((n, D), lambda j, me: (0, third(j, me))), whole((16, D))],
        grid=(3,),
        out_hbm=(0,),
        scratch=weight.scratch + [pltpu.VMEM((2, 16, 384), bf16), pltpu.SemaphoreType.DMA((16,))],
        flops=2 * n * D * 3 * D,
        prefetch=1,
    )


def attention_kernel(qkv_ref, mask_ref, o_ref, lse_ref):
    lane = lax.broadcasted_iota(jnp.int32, (ROWS, 2 * HEAD), 1)
    low_half = lane < HEAD
    valid = mask_ref[0] > 0.0
    lse_all = jnp.zeros((ROWS, 128), f32)
    for pair in range(HEADS // 2):
        at = pair * 2 * HEAD
        q = qkv_ref[:, at : at + 2 * HEAD]
        k = qkv_ref[:, D + at : D + at + 2 * HEAD]
        v = qkv_ref[:, 2 * D + at : 2 * D + at + 2 * HEAD]
        mixed = []
        for half in range(2):
            keep = low_half if half == 0 else jnp.logical_not(low_half)
            s = nt(q, jnp.where(keep, k, jnp.zeros_like(k)))
            s = jnp.where(valid, s, masked_score)
            top = jnp.max(s, axis=-1, keepdims=True)
            e = jnp.exp(s - top)
            total = jnp.sum(e, axis=-1, keepdims=True)
            p = e * (1.0 / total)
            mixed.append(nn(p.astype(bf16), v))
            lse_all = jnp.where(lane == 2 * pair + half, top + jnp.log(total), lse_all)
        o_ref[:, at : at + 2 * HEAD] = jnp.where(low_half, mixed[0], mixed[1]).astype(bf16)
    lse_ref[0] = jnp.transpose(lse_all)[0:16, :]


def attention_forward(images, qkv, mask_row):
    n = images * ROWS
    return call(
        attention_kernel,
        (sds((n, D), bf16), sds((images, 16, ROWS), f32)),
        (qkv, mask_row),
        [rows_at(ROWS, 3 * D), pl.BlockSpec((1, 1, ROWS), lambda i: (i, 0, 0))],
        [rows_at(ROWS, D), pl.BlockSpec((1, 16, ROWS), lambda i: (i, 0, 0))],
        grid=(images,),
        flops=4 * n * ROWS * D,
    )


def middle_kernel(weight, me_ref, *refs):
    count = len(weight.arrays)
    x_ref, o_ref, vec_ref, h_ref, m_ref, w_ref, sems = refs[count:]
    weight.load(me_ref, refs[:count], w_ref, sems)
    part = nt(o_ref[...], w_ref[...].reshape(D, D)) + vec_ref[6:7, :]
    middle = x_ref[...].astype(f32) + part
    h_ref[...] = middle
    hat, _ = normalized(middle)
    m_ref[...] = (hat * vec_ref[2:3, :] + vec_ref[3:4, :]).astype(bf16)


def middle_forward(images, x, o, vec, weight, me):
    n = images * ROWS
    return call(
        functools.partial(middle_kernel, weight),
        (sds((n, D), f32), sds((n, D), bf16)),
        (me, *weight.arrays, x, o, vec),
        weight.specs + [rows_at(ROWS, D), rows_at(ROWS, D), whole((16, D))],
        [rows_at(ROWS, D), rows_at(ROWS, D)],
        grid=(images,),
        scratch=weight.scratch,
        flops=2 * n * D * D,
        prefetch=1,
    )


def gelu_parts(u):
    phi = 0.5 + 0.5 * lax.erf(u * 0.7071067811865476)
    density = jnp.exp2(u * u * -0.7213475204444817) * 0.3989422804014327
    return u * phi, phi + u * density


def own_block(j, me):
    return (j // 2 + me[CORE]) % 2 * 2 + j % 2


def up_kernel(images, weight, me_ref, *refs):
    count = len(weight.arrays)
    m_ref, bias_ref, act_ref, slope_ref, w_ref, sems = refs[count:]
    j = pl.program_id(0)

    @pl.when(j == 0)
    def _():
        weight.start(me_ref, refs[:count], w_ref, sems)
        weight.wait(me_ref, refs[:count], w_ref, sems, 0, 2)

    @pl.when(j == 2)
    def _():
        weight.wait(me_ref, refs[:count], w_ref, sems, 1, 2)

    w = w_ref[pl.ds(6 * own_block(j, me_ref), 6)].reshape(D, D)
    for i in range(images):
        at = pl.ds(i * ROWS, ROWS)
        act, slope = gelu_parts(nt(m_ref[at, :], w) + bias_ref[0])
        act_ref[at, :] = act.astype(bf16)
        slope_ref[at, :] = slope.astype(bf16)


def up_forward(images, m, weight, bias, me):
    n = images * ROWS
    cols = pl.BlockSpec((n, D), lambda j, me: (0, own_block(j, me)))
    return call(
        functools.partial(up_kernel, images, weight),
        (sds((n, FF), bf16), sds((n, FF), bf16)),
        (me, *weight.arrays, m, bias),
        weight.specs + [whole((n, D)), pl.BlockSpec((1, 1, D), lambda j, me: (own_block(j, me), 0, 0))],
        [cols, cols],
        grid=(FF // D,),
        vmem_out=(0,),
        out_hbm=(1,),
        scratch=weight.scratch,
        flops=2 * n * D * FF,
        prefetch=1,
    )


def act_sum_kernel(images, act_ref, sel_ref, sum_ref):
    total = jnp.zeros(sum_ref.shape, f32)
    for i in range(images):
        total += nn(sel_ref[i], act_ref[pl.ds(i * ROWS, ROWS), :])
    sum_ref[...] = total.astype(bf16)


def act_sums(images, act, sel):
    n = images * ROWS
    return call(
        functools.partial(act_sum_kernel, images),
        (sds((16, FF), bf16),),
        (act, sel),
        [cols_at(n, D), whole((images, 16, ROWS))],
        [cols_at(16, D)],
        grid=(FF // D,),
        flops=32 * n * FF,
    )[0]


def down_kernel(images, weight, me_ref, *refs):
    count = len(weight.arrays)
    act_ref, h_ref, vec_ref, sel_ref, inv_ref, out_ref, pooled_ref, w_ref, sems = refs[count:]
    j = pl.program_id(0)

    @pl.when(j == 0)
    def _():
        weight.start(me_ref, refs[:count], w_ref, sems)
        weight.wait(me_ref, refs[:count], w_ref, sems, 0, 2)

    @pl.when(j == 1)
    def _():
        weight.wait(me_ref, refs[:count], w_ref, sems, 1, 2)

    tiles = DOWN_TILES // 3
    w = w_ref[pl.ds(tiles * third(j, me_ref), tiles)].reshape(D // 3, FF)
    y = nt(act_ref[...], w)
    total = jnp.zeros((16, D // 3), f32)
    for i in range(images):
        rows = slice(i * ROWS, i * ROWS + ROWS)
        out = (h_ref[rows, :] + (y[rows] + vec_ref[11:12, :])).astype(bf16)
        out_ref[i] = out[0:PATCHES, :]
        total += nn(sel_ref[i], out)
    pooled_ref[...] = (total * inv_ref[:, 0:1]).astype(bf16)


def down_forward(images, act, weight, h, vec, sel, inv_count, me):
    n = images * ROWS

    def cols(rows):
        return pl.BlockSpec((rows, D // 3), lambda j, me: (0, third(j, me)))

    return call(
        functools.partial(down_kernel, images, weight),
        (sds((images, PATCHES, D), bf16), sds((16, D), bf16)),
        (me, *weight.arrays, act, h, vec, sel, inv_count),
        weight.specs[:-1]
        + [
            pl.BlockSpec(memory_space=pl.ANY),
            pl.BlockSpec(memory_space=pltpu.VMEM),
            cols(n),
            cols(16),
            whole((images, 16, ROWS)),
            whole((16, 128)),
        ],
        [pl.BlockSpec((images, PATCHES, D // 3), lambda j, me: (0, 0, third(j, me))), cols(16)],
        grid=(3,),
        vmem_in=(1 + len(weight.arrays),),
        scratch=weight.scratch,
        flops=2 * n * D * FF,
        prefetch=1,
    )


def loss_kernel(total_images, proj, down, me_ref, first_ref, *refs):
    count = len(proj.arrays)
    pieces = refs[:count]
    if proj.pieces:
        down_pieces, rest = pieces, refs[count:]
    else:
        down_pieces, rest = refs[count : count + 1], refs[count + 1 :]
    text_ref, pooled_ref, order_ref, inv_ref, dz_ref, rank_ref, spread_ref, hidden_ref, all_ref = rest[:9]
    proj_ref, proj_sems, down_ref, down_sems, rows_ref = rest[9:14]
    down_copies = down.copies(me_ref, down_pieces, down_ref, down_sems)
    proj_copies = proj.copies(me_ref, pieces, proj_ref, proj_sems)
    if proj.pieces:
        slab_ref, slab_sems = rest[14:]
        for at, (c, x, y) in enumerate(sources(me_ref)):
            for back in range(4):
                device = x * 16 + (me_ref[Z] ^ back) * 4 + y * 2 + c
                out = slab_ref.at[pl.ds(pl.multiple_of(device * 16, 16), 16)]
                source = pieces[at].at[back, 14]
                proj_copies.append(
                    functools.partial(pltpu.make_async_copy, source, out, slab_sems.at[at * 4 + back])
                )
    for copy in proj_copies + down_copies:
        copy().start()
    for copy in proj_copies:
        copy().wait()
    if proj.pieces:
        images = total_images // 32
        shape = (total_images, 512)
        row = lax.broadcasted_iota(jnp.int32, shape, 0)
        col = lax.broadcasted_iota(jnp.int32, shape, 1)
        start = row // images * 16 + row % images
        held = slab_ref[...]
        left = nn(jnp.where(col == start, 1.0, 0.0).astype(bf16), held)
        right = nn(jnp.where(col == start + 8, 1.0, 0.0).astype(bf16), held[:, 0:128])
        text = jnp.concatenate([left, right], axis=1).astype(bf16)
    else:
        text = text_ref[...]
    proj_w = proj_ref[...].reshape(EMB, D)
    each = total_images // pooled_ref.shape[0]
    for d in range(pooled_ref.shape[0]):
        rows_ref[d * each : d * each + each, :] = pooled_ref[d].astype(f32)
    pooled = rows_ref[...].astype(bf16)
    all_ref[...] = pooled
    z = nt(pooled, proj_w)
    square = jnp.sum(z * z, axis=-1, keepdims=True) + unit_eps
    inverse = lax.rsqrt(square)
    image = (z * inverse).astype(bf16)
    s = logit_scale * nt(image, text)
    shape = (total_images, total_images)
    hit = jnp.where(order_ref[:, 0:1] == lax.broadcasted_iota(jnp.int32, shape, 1), 1.0, 0.0)
    part = 1.0 / (2.0 * total_images)

    def grad_of(axis):
        top = jnp.max(s, axis=axis, keepdims=True)
        lse = top + jnp.log(jnp.sum(jnp.exp(s - top), axis=axis, keepdims=True))
        return ((jnp.exp(s - lse) - hit) * part).astype(bf16)

    de = logit_scale * (nn(grad_of(1), text) + nn(grad_of(0), text))
    dz = inverse * de - z * (inverse * inverse * inverse * jnp.sum(z * de, axis=-1, keepdims=True))
    dz = dz.astype(bf16)
    dz_ref[...] = dz
    pick = lax.broadcasted_iota(jnp.int32, (16, total_images), 1) == (
        first_ref[0] + lax.broadcasted_iota(jnp.int32, (16, total_images), 0)
    )
    own = nn(jnp.where(pick, 1.0, 0.0).astype(bf16), dz).astype(bf16)
    spread = nn(own, proj_w) * inv_ref[:, 0:1]
    spread_ref[...] = spread
    rank = spread.astype(bf16)
    rank_ref[...] = rank
    for copy in down_copies:
        copy().wait()
    hidden_ref[...] = nn(rank, down_ref[...].reshape(D, FF))


def loss_backward(me, first, pooled, text, order, proj, down, inv_count):
    total = pooled.shape[0] * pooled.shape[1]
    if proj.pieces:
        arrays, extra = proj.arrays, [pltpu.VMEM((512, 384), bf16), pltpu.SemaphoreType.DMA((32,))]
    else:
        arrays, extra = proj.arrays + down.arrays, []
    return call(
        functools.partial(loss_kernel, total, proj, down),
        (sds((total, EMB), bf16), sds((16, D), bf16), sds((16, D), f32), sds((16, FF), f32), sds((total, D), bf16)),
        (me, first, *arrays, text, pooled, order, inv_count),
        [pl.BlockSpec(memory_space=pltpu.HBM)] * len(arrays)
        + [whole(text.shape), whole(pooled.shape), whole((total, 128)), whole((16, 128))],
        [whole((total, EMB)), whole((16, D)), whole((16, D)), whole((16, FF)), whole((total, D))],
        scratch=proj.scratch + down.scratch + [pltpu.VMEM((total, D), f32)] + extra,
        flops=6 * total * total * EMB + 2 * total * D * EMB + 32 * D * FF,
        vmem=32,
        prefetch=2,
    )


def weave(ref, value):
    for t in range(value.shape[0] // TR):
        for x, z, y in PIECES:
            row = t * TR + x * 64 + z * 16
            ref[x * 8 + z * 2 + y, pl.ds(t * 16, 16), :] = value[row : row + 16, y * 384 : y * 384 + 384]


def half_block(j, me):
    return (j // 2 + 1 - me[CORE]) % 2 * 2 + j % 2


DM_COLS = 256


def up_back_kernel(images, weight, me_ref, *refs):
    count = len(weight.arrays)
    slope_ref, m_ref, hidden_ref, col_ref, dm_ref, db_ref = refs[count : count + 6]
    w_ref, sems, du_ref = refs[-3:]
    j = pl.program_id(0)
    blocks = FF // D

    @pl.when(j == 0)
    def _():
        weight.start(me_ref, refs[:count], w_ref, sems)

    @pl.when(j < blocks)
    def _():
        cols = pl.ds(pl.multiple_of(half_block(j, me_ref) * D, 128), D)
        total = jnp.zeros((1, D), f32)
        for i in range(images):
            at = pl.ds(i * ROWS, ROWS)
            du = (slope_ref[at, :].astype(f32) * (col_ref[at, 0:1] * hidden_ref[i : i + 1, :])).astype(bf16)
            du_ref[at, cols] = du
            total += column_sum(du.astype(f32))
        db_ref[...] = jnp.broadcast_to(total, db_ref.shape)
        dw = tn(du_ref[:, cols], m_ref[...]).astype(bf16)
        if not weight.pieces:
            refs[count + 6][...] = dw
            return
        send_ref, keep_ref = refs[count + 6 : count + 8]

        @pl.when(j < 2)
        def _():
            weave(send_ref, dw)

        @pl.when(j >= 2)
        def _():
            weave(keep_ref, dw)

    @pl.when(j == blocks)
    def _():
        weight.wait(me_ref, refs[:count], w_ref, sems)

    @pl.when(j >= blocks)
    def _():
        for k in range(D // DM_COLS):

            @pl.when(j == blocks + k)
            def _():
                dm_ref[...] = nn(du_ref[...], w_ref[:, :, k * DM_COLS : (k + 1) * DM_COLS].reshape(FF, DM_COLS))


def up_backward(images, slope, m, weight, hidden, col, me):
    n = images * ROWS
    blocks = FF // D
    steps = D // DM_COLS

    def block(j, me):
        return half_block(jnp.minimum(j, blocks - 1), me)

    def cols(rows):
        return pl.BlockSpec((rows, D), lambda j, me: (0, block(j, me)))

    if weight.pieces:
        shapes = (sds((16, 192, 384), bf16),) * 2
        specs = [
            pl.BlockSpec((16, 96, 384), lambda j, me: (0, jnp.minimum(j, 1), 0)),
            pl.BlockSpec((16, 96, 384), lambda j, me: (0, jnp.clip(j - 2, 0, 1), 0)),
        ]
    else:
        shapes = (sds((FF, D), bf16),)
        specs = [pl.BlockSpec((D, D), lambda j, me: (block(j, me), 0))]
    return call(
        functools.partial(up_back_kernel, images, weight),
        (sds((n, D), f32), sds((8, FF), f32)) + shapes,
        (me, *weight.arrays, slope, m, hidden, col),
        weight.specs + [cols(n), whole((n, D)), cols(16), whole((n, 128))],
        [pl.BlockSpec((n, DM_COLS), lambda j, me: (0, jnp.maximum(j - blocks, 0))), cols(8)] + specs,
        grid=(blocks + steps,),
        vmem=40,
        scratch=weight.scratch + [pltpu.VMEM((n, FF), bf16)],
        flops=4 * n * D * FF,
        prefetch=1,
    )


def middle_back_kernel(images, weight, me_ref, *refs):
    count = len(weight.arrays)
    h_ref, dm_ref, col_ref, spread_ref, o_ref, vec_ref = refs[count : count + 6]
    dh_ref, do_ref, dw_ref, dvec_ref, w_ref, sems, dat_ref = refs[count + 6 :]
    i = pl.program_id(0)

    @pl.when(i == 0)
    def _():
        weight.start(me_ref, refs[:count], w_ref, sems)

    @pl.when(i < images)
    def _():
        hat, inverse = normalized(h_ref[...])
        dm = dm_ref[...]
        part = norm_back(dm, hat, inverse, vec_ref[2:3, :])
        here = spread_ref[pl.ds(i, 1), :]
        dh = col_ref[:, 0:1] * here + part
        dh_ref[...] = dh
        dat = dh.astype(bf16)
        dat_ref[pl.ds(pl.multiple_of(i * ROWS, 16), ROWS), :] = dat
        sums = jnp.concatenate(
            [
                column_sum(dm * hat),
                column_sum(dm),
                column_sum(dat.astype(f32)),
                column_sum(col_ref[:, 0:1]) * here.astype(bf16).astype(f32),
                jnp.zeros((4, D), f32),
            ],
            axis=0,
        )
        accumulate(i, dvec_ref, sums)

    @pl.when(i == images)
    def _():
        dw = tn(dat_ref[...], o_ref[...]).astype(bf16)
        if weight.pieces:
            for half in range(2):
                weave(dw_ref.at[half], dw[half * 384 : half * 384 + 384])
        else:
            dw_ref[...] = dw
        weight.wait(me_ref, refs[:count], w_ref, sems)
        do_ref[...] = nn(dat_ref[...], w_ref[...].reshape(D, D)).astype(bf16)


def middle_backward(images, h, dm, col, spread, o, weight, vec, me):
    n = images * ROWS
    dw_shape = (2, 16, 48, 384) if weight.pieces else (D, D)

    def rows(cols):
        return pl.BlockSpec((ROWS, cols), lambda i, me: (jnp.minimum(i, images - 1), 0))

    return call(
        functools.partial(middle_back_kernel, images, weight),
        (sds((n, D), f32), sds((n, D), bf16), sds(dw_shape, bf16), sds((8, D), f32)),
        (me, *weight.arrays, h, dm, col, spread, o, vec),
        weight.specs + [rows(D), rows(D), rows(128), whole((16, D)), whole((n, D)), whole((16, D))],
        [rows(D), whole((n, D)), whole(dw_shape), whole((8, D))],
        grid=(images + 1,),
        in_hbm=(1 + len(weight.arrays),),
        vmem_in=(2 + len(weight.arrays),) if weight.pieces else (),
        scratch=weight.scratch + [pltpu.VMEM((n, D), bf16)],
        flops=4 * n * D * D,
        prefetch=1,
    )


def attention_again_kernel(qkv_ref, lse_ref, col_ref, p_ref):
    low_half = lax.broadcasted_iota(jnp.int32, (ROWS, 2 * HEAD), 1) < HEAD
    valid = jnp.broadcast_to(col_ref[:, 0:1], (ROWS, ROWS)) > 0.0
    for pair in range(HEADS // 2):
        at = pair * 2 * HEAD
        q = qkv_ref[:, at : at + 2 * HEAD]
        k = qkv_ref[:, D + at : D + at + 2 * HEAD]
        for half in range(2):
            keep = low_half if half == 0 else jnp.logical_not(low_half)
            head = 2 * pair + half
            s = jnp.where(valid, nt(jnp.where(keep, k, jnp.zeros_like(k)), q), masked_score)
            p_ref[0, head] = jnp.exp(s - lse_ref[0, head : head + 1, :]).astype(bf16)


def attention_again(images, qkv, lse, col):
    n = images * ROWS
    return call(
        attention_again_kernel,
        (sds((images, HEADS, ROWS, ROWS), bf16),),
        (qkv, lse, col),
        [rows_at(ROWS, 3 * D), pl.BlockSpec((1, 16, ROWS), lambda i: (i, 0, 0)), rows_at(ROWS, 128)],
        [pl.BlockSpec((1, HEADS, ROWS, ROWS), lambda i: (i, 0, 0, 0))],
        grid=(images,),
        vmem_out=(0,),
        flops=2 * n * ROWS * D,
    )[0]


def attention_back_kernel(qkv_ref, do_ref, p_ref, dqkv_ref, db_ref):
    i = pl.program_id(0)
    low_half = lax.broadcasted_iota(jnp.int32, (ROWS, 2 * HEAD), 1) < HEAD
    for pair in range(HEADS // 2):
        at = pair * 2 * HEAD
        q = qkv_ref[:, at : at + 2 * HEAD]
        k = qkv_ref[:, D + at : D + at + 2 * HEAD]
        v = qkv_ref[:, 2 * D + at : 2 * D + at + 2 * HEAD]
        do = do_ref[:, at : at + 2 * HEAD]
        dv, dk, dq = [], [], []
        for half in range(2):
            keep = low_half if half == 0 else jnp.logical_not(low_half)
            only_k = jnp.where(keep, k, jnp.zeros_like(k))
            only_v = jnp.where(keep, v, jnp.zeros_like(v))
            head = 2 * pair + half
            rounded = p_ref[0, head]
            p = rounded.astype(f32)
            dp = nt(only_v, do)
            share = jnp.sum(p * dp, axis=0, keepdims=True)
            ds = (p * (dp - share)).astype(bf16)
            dv.append(nn(rounded, do))
            dk.append(nn(ds, q))
            dq.append(tn(ds, only_k))
        dqkv_ref[:, at : at + 2 * HEAD] = ((dq[0] + dq[1]) * (HEAD**-0.5)).astype(bf16)
        dqkv_ref[:, D + at : D + at + 2 * HEAD] = jnp.where(low_half, dk[0], dk[1]).astype(bf16)
        dqkv_ref[:, 2 * D + at : 2 * D + at + 2 * HEAD] = jnp.where(low_half, dv[0], dv[1]).astype(bf16)
    accumulate(i, db_ref, nn(jnp.ones((16, ROWS), bf16), dqkv_ref[...]))


def attention_backward(images, qkv, do, p):
    n = images * ROWS
    return call(
        attention_back_kernel,
        (sds((n, 3 * D), bf16), sds((16, 3 * D), f32)),
        (qkv, do, p),
        [
            rows_at(ROWS, 3 * D),
            rows_at(ROWS, D),
            pl.BlockSpec((1, HEADS, ROWS, ROWS), lambda i: (i, 0, 0, 0)),
        ],
        [rows_at(ROWS, 3 * D), whole((16, 3 * D))],
        grid=(images,),
        vmem_in=(2,),
        flops=10 * n * ROWS * D,
    )


def qkv_grad_kernel(dqkv_ref, a_ref, dw_ref):
    dw_ref[...] = tn(dqkv_ref[...], a_ref[...]).astype(bf16)


def qkv_weight_grad(images, dqkv, a):
    n = images * ROWS
    return call(
        qkv_grad_kernel,
        (sds((3 * D, D), bf16),),
        (dqkv, a),
        [cols_at(n, D), whole((n, D))],
        [rows_at(D, D)],
        grid=(3,),
        flops=6 * n * D * D,
    )[0]


def qkv_grad_fast_kernel(_, dqkv_ref, a_ref, out_ref, pieces_ref):
    j = pl.program_id(0)

    @pl.when(j < 3)
    def _():
        weave(pieces_ref, tn(dqkv_ref[...], a_ref[...]).astype(bf16))

    @pl.when(j == 3)
    def _():
        pieces_ref[...] = out_ref[0]


def qkv_weight_grad_fast(images, dqkv, a, dw_out, me, other):
    n = images * ROWS

    def half(me):
        return 1 - me[CORE] if other else me[CORE]

    return call(
        qkv_grad_fast_kernel,
        (sds((16, 192, 384), bf16),),
        (me, dqkv, a, dw_out),
        [
            pl.BlockSpec((n, 384), lambda j, me: (0, half(me) * 3 + jnp.minimum(j, 2))),
            whole((n, D)),
            pl.BlockSpec((1, 16, 48, 384), lambda j, me: (half(me), 0, 0, 0)),
        ],
        [pl.BlockSpec((16, 48, 384), lambda j, me: (0, j, 0))],
        grid=(4,),
        out_hbm=(0,),
        flops=3 * n * D * D,
        prefetch=1,
    )[0]


def input_back_kernel(weight, me_ref, *refs):
    count = len(weight.arrays)
    x_ref, dqkv_ref, dh_ref, vec_ref, two_ref, bias_ref, up_ref, out_ref, dvec_ref, w_ref, sems, sum_ref = refs[count:]
    i = pl.program_id(0)
    weight.load(me_ref, refs[:count], w_ref, sems)
    da = nn(dqkv_ref[...], w_ref[...].reshape(3 * D, D))
    hat, inverse = normalized(x_ref[...].astype(f32))
    out = dh_ref[...] + norm_back(da, hat, inverse, vec_ref[0:1, :])
    out_ref[0] = out[0:PATCHES, :]
    sums = jnp.concatenate([column_sum(da * hat), column_sum(da), jnp.zeros((6, D), f32)], axis=0)
    accumulate(i, sum_ref, sums)

    @pl.when(i == pl.num_programs(0) - 1)
    def _():
        dvec_ref[...] = jnp.zeros_like(dvec_ref)
        dvec_ref[0:2, :] = sum_ref[0:2, :]
        dvec_ref[2:4, :] = two_ref[0:2, :]
        dvec_ref[4:5, :] = bias_ref[0:1, 0:D]
        dvec_ref[5:6, :] = bias_ref[0:1, 2 * D : 3 * D]
        dvec_ref[6:7, :] = two_ref[2:3, :]
        for b in range(FF // D):
            dvec_ref[7 + b : 8 + b, :] = up_ref[0:1, b * D : (b + 1) * D]
        dvec_ref[7 + FF // D : 8 + FF // D, :] = two_ref[3:4, :]


def input_backward(images, x, dqkv, weight, dh, vec, g_two, g_bias, g_bias_up, me):
    n = images * ROWS
    return call(
        functools.partial(input_back_kernel, weight),
        (sds((images, PATCHES, D), f32), sds((16, D), f32)),
        (me, *weight.arrays, x, dqkv, dh, vec, g_two, g_bias, g_bias_up),
        weight.specs
        + [rows_at(ROWS, D), rows_at(ROWS, 3 * D), rows_at(ROWS, D)]
        + [whole(a.shape) for a in (vec, g_two, g_bias, g_bias_up)],
        [pl.BlockSpec((1, PATCHES, D), lambda i, *_: (i, 0, 0)), whole((16, D))],
        grid=(images,),
        scratch=weight.scratch + [pltpu.VMEM((8, D), f32)],
        flops=6 * n * D * D,
        prefetch=1,
    )


SUMMED, DOWN, PROJ, NONE, VEC = 0, 1, 2, 3, 4


def adam_kernel(part_rows, fast, each, kind_ref, row_ref, me_ref, *refs):
    master_ref, first_ref, second_ref, down_ref, proj_ref, vec_ref = refs[:6]
    summed_refs = refs[6:-5]
    new_master_ref, new_first_ref, new_second_ref, grad_ref, woven_ref = refs[-5:]
    wide = FF // D
    for k in range(each):
        slot = pl.program_id(0) * each + k
        kind = kind_ref[slot]

        @pl.when(kind == SUMMED)
        def _():
            if fast:
                for summed_ref, (dz, dy) in zip(summed_refs, CHIPS, strict=True):
                    rows = pl.ds(pl.multiple_of((me_ref[Z] ^ dz) * 16, 16), 16)
                    cols = pl.ds(pl.multiple_of((me_ref[Y] ^ dy) * 384, 128), 384)
                    grad_ref[rows, cols] = summed_ref[k].astype(f32)
            else:
                grad_ref[...] = summed_refs[0][k].astype(f32)

        @pl.when(kind == VEC)
        def _():
            grad_ref[...] = jnp.zeros_like(grad_ref)
            grad_ref[0 : vec_ref.shape[0], :] = vec_ref[...]

        @pl.when(kind == DOWN)
        def _():
            for c in range(D // 128):
                for b in range(wide):
                    lanes = slice(b * D + c * 128, b * D + c * 128 + 128)
                    woven_ref[c, pl.ds(b, part_rows // wide, stride=wide), :] = down_ref[k, 0 : part_rows // wide, lanes]
                grad_ref[:, c * 128 : (c + 1) * 128] = woven_ref[c]

        @pl.when(kind == PROJ)
        def _():
            at = pl.multiple_of(row_ref[slot], part_rows)
            grad_ref[...] = proj_ref[pl.ds(at, part_rows), :]

        @pl.when(kind == NONE)
        def _():
            grad_ref[...] = jnp.zeros_like(grad_ref)

        grad = grad_ref[...]
        master = master_ref[0, k]
        first = beta_one * first_ref[0, k] + (1.0 - beta_one) * grad
        second = beta_two * second_ref[0, k] + (1.0 - beta_two) * grad * grad
        new_first_ref[0, k] = first
        new_second_ref[0, k] = second
        direction = first / (1.0 - beta_one**STEP)
        size = jnp.sqrt(second / (1.0 - beta_two**STEP)) + adam_eps
        new_master_ref[0, k] = master - learn_rate * (direction / size + decay_rate * master)


def adam(kind, row, me, master, first, second, summed, down, proj, vec):
    slots, part_rows = master.shape[1:3]
    each = slots // 2
    block = pl.BlockSpec((1, each, part_rows, D), lambda s, *_: (0, s, 0, 0))
    fast = len(summed) > 1
    return call(
        functools.partial(adam_kernel, part_rows, fast, each),
        (sds(master.shape, f32),) * 3,
        (kind, row, me, master, first, second, down, proj, vec, *summed),
        [
            block,
            block,
            block,
            pl.BlockSpec((each,) + down.shape[1:], lambda s, *_: (s, 0, 0)),
            whole(proj.shape),
            whole(vec.shape),
        ]
        + [pl.BlockSpec((each,) + a.shape[1:], lambda s, *_: (s, 0, 0)) for a in summed],
        [block] * 3,
        grid=(slots // each,),
        scratch=[pltpu.VMEM((part_rows, D), f32), pltpu.VMEM((D // 128, part_rows, 128), f32)],
        flops=20 * slots * part_rows * D,
        in_hbm=(3, 4, 5, 6, 7),
        prefetch=3,
    )


def rank_grad_kernel(images, kind_ref, row_ref, *refs):
    dz_ref, pooled_ref, down_ref, proj_ref = refs[-4:]
    held = jnp.concatenate([ref[...].reshape(64, PACK) for ref in refs[:-4]], axis=0)
    row = lax.broadcasted_iota(jnp.int32, (D, 128), 0)
    col = lax.broadcasted_iota(jnp.int32, (D, 128), 1)
    wanted = jnp.full((D, 128), -1, jnp.int32)
    for s in range(8):
        first = jnp.where(kind_ref[s] == DOWN, row_ref[s], -D)
        wanted = jnp.where(col // 16 == s, first + col % 16, wanted)
    mine = nn(held[:, 0:D], jnp.where(row == wanted, 1.0, 0.0).astype(bf16)).astype(bf16)
    shape = (512, 512)
    row = lax.broadcasted_iota(jnp.int32, shape, 0)
    col = lax.broadcasted_iota(jnp.int32, shape, 1)
    first = 0
    for segment in range(3):
        here = (row - col == segment * images) & (row // 16 == col // 16) & (col % 16 < images)
        rank = nn(jnp.where(here, 1.0, 0.0).astype(bf16), mine).astype(bf16)
        part = held[:, D:PACK] if segment == 0 else held
        down_ref[:, first : first + part.shape[1]] = tn(rank, part)
        first += part.shape[1]
    proj_ref[...] = tn(dz_ref[...], pooled_ref[...])


def rank_grads(images, kind, row, arrays, dz, pooled):
    return call(
        functools.partial(rank_grad_kernel, images),
        (sds((128, FF), f32), sds((EMB, D), f32)),
        (kind, row, *arrays, dz, pooled),
        [whole(a.shape) for a in arrays] + [whole(dz.shape), whole(pooled.shape)],
        [whole((128, FF)), whole((EMB, D))],
        out_hbm=(0, 1),
        flops=256 * D * FF,
        prefetch=2,
    )


def slot_place(owner_list, slot_count):
    tile_count = owner_list.shape[0]
    earlier = jnp.tril(jnp.ones((tile_count, tile_count), jnp.int32), -1)
    same_owner = (owner_list[:, None] == owner_list[None, :]).astype(jnp.int32)
    return owner_list * slot_count + jnp.sum(same_owner * earlier, axis=1)


def gather_weights(master, placed):
    n_dp, n_rep = lax.axis_size("dp"), lax.axis_size("rep")
    slots, part_rows = master.shape[1:3]
    gathered = lax.all_gather(master.astype(bf16), AXES, axis=0, tiled=True)
    gathered = gathered.reshape(n_dp, n_rep * slots, part_rows, D)
    return jnp.transpose(jnp.take(gathered, placed, axis=1), (1, 0, 2, 3)).reshape(-1, D)


def scatter_grads(tiles, tile_of_slot, slots, part_rows):
    n_dp, n_rep = lax.axis_size("dp"), lax.axis_size("rep")
    count = tiles.shape[0]
    tiles = jnp.concatenate([tiles, jnp.zeros((1, TR, D), tiles.dtype)], axis=0)
    index = jnp.where(tile_of_slot < count, tile_of_slot, count)
    buffer = jnp.take(tiles, index, axis=0).reshape(n_rep * slots, n_dp, part_rows, D)
    buffer = jnp.transpose(buffer, (1, 0, 2, 3)).reshape(n_dp * n_rep, slots, part_rows, D)
    return lax.psum_scatter(buffer, AXES, scatter_dimension=0, tiled=True)[0]


def pairs(move):
    def number(x, z, y, c):
        return x * 16 + z * 4 + y * 2 + c

    return [(number(x, z, y, c), number(*move(x, z, y, c))) for x, z, y in PIECES for c in range(2)]


SWAP_CORE = pairs(lambda x, z, y, c: (x, z, y, 1 - c))
SWAP_X = pairs(lambda x, z, y, c: (1 - x, z, y, c))
SWAP_Y = pairs(lambda x, z, y, c: (x, z, 1 - y, c))
SWAP_Z = pairs(lambda x, z, y, c: (x, z ^ 1, y, c))
SWAP_ZZ = pairs(lambda x, z, y, c: (x, z ^ 2, y, c))
SWAP_XY = pairs(lambda x, z, y, c: (1 - x, z, 1 - y, c))
ACROSS_Z = [pairs(lambda x, z, y, c, k=k: (x, z ^ k, y, c)) for k in (1, 2, 3)]
CROSS_ONE = pairs(lambda x, z, y, c: (1 - x, z, y, c) if c == 0 else (x, z, 1 - y, c))
CROSS_TWO = pairs(lambda x, z, y, c: (x, z, 1 - y, c) if c == 0 else (1 - x, z, y, c))


def send(value, permutation):
    return lax.ppermute(value, AXES, permutation)


def add_kernel(count, pieces, outputs, _, *refs):
    for p in range(pieces):
        total = refs[p * count][0].astype(f32)
        for k in range(1, count):
            total += refs[p * count + k][0].astype(f32)
        outs = refs[pieces * count :]
        if outputs == 1:
            outs[0][p] = total.astype(outs[0].dtype)
        else:
            outs[p][...] = total.astype(outs[p].dtype)


def add_pieces(sources, me, pieces, steps=1, dtypes=(bf16,), near=()):
    rows = sources[0][0].shape[1]
    each = pieces // steps
    arrays, specs = [], []
    for p in range(each):
        for array, at in sources:
            arrays.append(array)
            specs.append(pl.BlockSpec((1, rows, 384), lambda i, me, p=p, at=at: (at(i * each + p, me), 0, 0)))
    if len(dtypes) == 1:
        shapes = (sds((pieces, rows, 384), dtypes[0]),)
        outs = [pl.BlockSpec((each, rows, 384), lambda i, me: (i, 0, 0))]
    else:
        shapes = tuple(sds((rows, 384), dtype) for dtype in dtypes)
        outs = [whole((rows, 384))] * pieces
    in_hbm = [k + 1 for k in range(len(arrays)) if k % len(sources) not in near]
    results = call(
        functools.partial(add_kernel, len(sources), each, len(dtypes)),
        shapes,
        (me, *arrays),
        specs,
        outs,
        grid=(steps,),
        flops=pieces * rows * D,
        in_hbm=in_hbm,
        prefetch=1,
    )
    return results[0] if len(dtypes) == 1 else results


class PieceSum:
    def __init__(self, other, me):
        self.me = me
        self.one = send(other, SWAP_CORE)

    def first_send(self, i, me):
        return jnp.where(me[CORE] == 0, (1 - me[X]) * 8 + i, i * 2 + 1 - me[Y])

    def kept(self, i, me):
        return jnp.where(me[CORE] == 0, me[X] * 8 + i, i * 2 + me[Y])

    def second_send(self, i, me):
        return jnp.where(me[CORE] == 0, 2 * i + 1 - me[Y], (1 - me[X]) * 4 + i)

    def second_keep(self, i, me):
        return jnp.where(me[CORE] == 0, 2 * i + me[Y], me[X] * 4 + i)

    def cross_one(self):
        parts = [(self.mine, self.first_send), (self.one, self.first_send)]
        self.two = send(add_pieces(parts, self.me, 8, 2, near=(1,)), CROSS_ONE)

    def cross_two(self):
        def own(i, me):
            return self.kept(self.second_send(i, me), me)

        parts = [(self.mine, own), (self.one, own), (self.two, self.second_send)]
        self.three = send(add_pieces(parts, self.me, 4, near=(2,)), CROSS_TWO)

    def partial(self):
        def crossed(i, me):
            return self.second_keep(me[Z] ^ i, me)

        def own(i, me):
            return self.kept(crossed(i, me), me)

        parts = [(self.mine, own), (self.one, own), (self.two, crossed)]
        self.sums = add_pieces(parts, self.me, 4, dtypes=(f32,))

    def cross_z(self):
        parts = [(self.sums, lambda i, me: i), (self.three, lambda i, me: me[Z] ^ i)]
        self.own, *parts = add_pieces(parts, self.me, 4, dtypes=(f32, bf16, bf16, bf16), near=(0, 1))
        self.last = [send(part, move) for part, move in zip(parts, ACROSS_Z, strict=True)]

    def total(self):
        parts = [(part[None], lambda i, me: 0) for part in (self.own, *self.last)]
        return add_pieces(parts, self.me, 1, near=(0, 1, 2, 3))[0]


def place_kernel(index_ref, *refs):
    for k in range(64):
        at = index_ref[k]
        out_ref = refs[4 + k // 8]
        for q in range(4):

            @pl.when((at >= 12 * q) & (at < 12 * q + 12))
            def _():
                out_ref[k % 8] = refs[q][pl.ds(pl.multiple_of((at - 12 * q) * 16, 16), 16), :]

        @pl.when(at >= 48)
        def _():
            out_ref[k % 8] = jnp.zeros((16, 384), bf16)


def return_to_owners(sums, place):
    placed = call(
        place_kernel,
        (sds((8, 16, 384), bf16),) * 8,
        (place, *sums),
        [whole((192, 384))] * 4,
        [whole((8, 16, 384))] * 8,
        prefetch=1,
    )
    return exchange(placed)


def plan_kernel(owner_ref, me_ref, pick_ref, place_ref, kind_ref, row_ref, counts, placed, tile_of):
    x, c = me_ref[X], me_ref[CORE]
    rep = me_ref[Z] * 4 + me_ref[Y] * 2 + c

    @pl.loop(0, 16)
    def _(r):
        counts[r] = 0

    @pl.loop(0, 128)
    def _(k):
        tile_of[k] = 1 << 20

    @pl.loop(0, VEC_TILE + 1)
    def _(t):
        owner = owner_ref[t]
        at = owner * 8 + counts[owner]
        counts[owner] = counts[owner] + 1
        placed[t] = at
        tile_of[at] = t

    def slab(t):
        at = placed[t]
        owner = at // 8
        chip = (owner // 4 ^ me_ref[Z]) * 2 + (owner // 2 % 2 ^ me_ref[Y])
        return jnp.where(owner % 2 == c, 0, 64) + chip * 8 + at % 8

    def fill(first, count, tile):
        @pl.loop(0, count)
        def _(k):
            pick_ref[first + k] = slab(tile + k)

    base = 0
    for tiles, tile in CHUNK_TILES:
        fill(base, tiles, tile + tiles * c)
        base += tiles
    pick_ref[base] = slab(VEC_TILE)

    @pl.loop(0, 64)
    def _(k):
        chip = k // 8
        owner = (chip // 2 ^ me_ref[Z]) * 4 + (chip % 2 ^ me_ref[Y]) * 2 + c
        t = tile_of[owner * 8 + k % 8]
        u = t - QKV_TILES
        v = u - OUT_TILES
        half = jnp.where(t < QKV_TILES, t // 9, jnp.where(u < OUT_TILES, u // 3, v // 12))
        place = jnp.where(t < QKV_TILES, t % 9, jnp.where(u < OUT_TILES, 9 + u % 3, 12 + v % 12))
        place_ref[k] = jnp.where(t < DOWN_FIRST, jnp.where(half == c, place, 24 + place), 48)

    @pl.loop(0, 8)
    def _(k):
        t = tile_of[rep * 8 + k]
        is_down = (t >= DOWN_FIRST) & (t < PROJ_FIRST)
        is_proj = (t >= PROJ_FIRST) & (t < VEC_TILE)
        kind = jnp.where(t < DOWN_FIRST, SUMMED, jnp.where(is_down, DOWN, jnp.where(is_proj, PROJ, NONE)))
        kind_ref[k] = jnp.where((t == VEC_TILE) & (x == 0), VEC, kind)
        row_ref[k] = jnp.where(
            is_down, ((t - DOWN_FIRST) * TR + x * 64) // 4, jnp.where(is_proj, (t - PROJ_FIRST) * TR + x * 64, 0)
        )


def plan(owner_list, me):
    smem = pl.BlockSpec(memory_space=pltpu.SMEM)
    sizes = (sum(tiles for tiles, _ in CHUNK_TILES) + 1, 64, 8, 8)
    return pl.pallas_call(
        plan_kernel,
        out_shape=tuple(sds((size,), jnp.int32) for size in sizes),
        in_specs=[smem, smem],
        out_specs=(smem,) * 4,
        scratch_shapes=[pltpu.SMEM((16,), jnp.int32), pltpu.SMEM((128,), jnp.int32), pltpu.SMEM((128,), jnp.int32)],
    )(owner_list, me)


def prepare_kernel(owner_ref, me_ref, master_ref, *refs):
    out_refs, (lanes_ref, tile_ref) = refs[:8], refs[8:]
    rep = me_ref[Z] * 4 + me_ref[Y] * 2 + me_ref[CORE]
    for s in range(9):
        tile_ref[s] = 0

    def note(t, held):
        here = owner_ref[t] == rep

        @pl.when(here)
        def _():
            tile_ref[held] = t

        return held + jnp.where(here, 1, 0)

    lax.fori_loop(DOWN_FIRST, PROJ_FIRST, note, lax.fori_loop(0, DOWN_FIRST, note, 0))
    for s in range(8):
        down = (tile_ref[s] >= DOWN_FIRST) & (tile_ref[s] < PROJ_FIRST)

        @pl.when(jnp.logical_not(down))
        def _():
            for k, (dz, dy) in enumerate(CHIPS):
                rows = pl.ds(pl.multiple_of((me_ref[Z] ^ dz) * 16, 16), 16)
                cols = pl.ds(pl.multiple_of((me_ref[Y] ^ dy) * 384, 128), 384)
                out_refs[k][s] = master_ref[0, s, rows, cols].astype(bf16)

        @pl.when(down)
        def _():
            for k in range(6):
                lanes_ref[k] = master_ref[0, s, :, 128 * k : 128 * k + 128]
            for k, (dz, dy) in enumerate(CHIPS):
                for q in range(3):
                    part = lanes_ref[(me_ref[Y] ^ dy) * 3 + q, pl.ds(me_ref[Z] ^ dz, 16, stride=4), :]
                    out_refs[k][s, :, 128 * q : 128 * q + 128] = part.astype(bf16)


def pick_kernel(index_ref, mine_ref, theirs_ref, text_ref, one_ref, two_ref, three_ref):
    def slab(k, ref, j):
        at = index_ref[k]

        @pl.when(at < 64)
        def _():
            ref[j] = mine_ref[at]

        @pl.when(at >= 64)
        def _():
            ref[j] = theirs_ref[at - 64]

    k = 0
    for (tiles, _), (chunk, first) in zip(CHUNK_TILES, CHUNK_AT, strict=True):
        for j in range(tiles):
            slab(k, (one_ref, two_ref, three_ref)[chunk], first + j)
            k += 1
    slab(k, one_ref, 9)
    text = text_ref[...].astype(f32)
    count = text.shape[0]
    text = (text * lax.rsqrt(jnp.sum(text * text, axis=-1, keepdims=True) + unit_eps)).astype(bf16)
    three_ref[14] = jnp.zeros((16, 384), bf16)
    three_ref[14, 0:count, :] = text[:, 0:384]
    three_ref[14, 8 : 8 + count, 0:128] = text[:, 384:512]


class Spread:
    def __init__(self, block=None):
        if block is not None:
            self.parts = [block] + [send(block, move) for move in ACROSS_Z]

    def cross_one(self, ring=None):
        self.ring = jnp.stack(self.parts) if ring is None else ring
        self.one = send(self.ring, CROSS_ONE)
        self.two = None
        self.near = []

    def cross_two(self):
        if self.two is None:
            self.two = send(self.ring, CROSS_TWO)
        self.both = send(self.one, CROSS_TWO)

    def send_near(self, *which):
        for k in which:
            self.near.append(send(getattr(self, ("ring", "one", "two", "both")[k]), SWAP_CORE))

    def finish(self):
        self.send_near(*range(len(self.near), 4))

    def arrays(self):
        return (self.ring, self.one, self.two, self.both, *self.near)


def meet(*values):
    return lax.optimization_barrier(values)


def sources(me):
    for other in range(2):
        c = me[CORE] if other == 0 else 1 - me[CORE]
        for crossed in range(4):
            one, two = crossed % 2, crossed // 2
            flip_x = jnp.where(c == 0, one, two)
            flip_y = jnp.where(c == 0, two, one)
            yield c, me[X] + flip_x - 2 * me[X] * flip_x, me[Y] + flip_y - 2 * me[Y] * flip_y


def exchange(blocks):
    return [blocks[0]] + [
        send(blocks[k], pairs(lambda x, z, y, c, k=k: (x, z ^ CHIPS[k][0], y ^ CHIPS[k][1], c))) for k in range(1, 8)
    ]


def pick_slabs(master, text_emb, owner_list, me, *others):
    prepared = call(
        prepare_kernel,
        (sds((8, 16, 384), bf16),) * 8,
        (owner_list, me, master),
        [whole(master.shape)],
        [whole((8, 16, 384))] * 8,
        scratch=[pltpu.VMEM((6, 64, 128), f32), pltpu.SMEM((16,), jnp.int32)],
        in_hbm=(2,),
        prefetch=2,
    )
    pick, place, kind, row = plan(owner_list, me)
    *mine, pick = meet(*exchange(prepared), pick)
    mine = jnp.concatenate(mine)
    mine, *others = meet(mine, *others)
    blocks = call(
        pick_kernel,
        tuple(sds((slabs, 16, 384), bf16) for slabs in SLABS),
        (pick, mine, send(mine, SWAP_CORE), text_emb),
        [whole((64, 16, 384)), whole((64, 16, 384)), whole(text_emb.shape)],
        [whole((slabs, 16, 384)) for slabs in SLABS],
        prefetch=1,
    )
    return blocks, (place, kind, row), others


def shards(block_in, tissue, text_emb, text_order, owner_list, master, first_moment, second_moment):
    n_dp = lax.axis_size("dp")
    n_rep = lax.axis_size("rep")
    images = block_in.shape[0]
    slots, part_rows = master.shape[1:3]
    image_total = text_order.shape[0]
    n = images * ROWS
    dp_at, rep_at = lax.axis_index("dp"), lax.axis_index("rep")
    first_image = lax.axis_index(AXES) * images

    x = jnp.pad(block_in, ((0, 0), (0, ROWS - PATCHES), (0, 0))).reshape(n, D)
    valid = jnp.pad((tissue > 0).astype(f32), ((0, 0), (0, ROWS - PATCHES)))
    mask_row = valid[:, None, :]
    col = jnp.broadcast_to(valid.reshape(n, 1), (n, 128))
    numbers = jnp.arange(images, dtype=jnp.int32)
    sel = jnp.where(
        numbers[:, None, None] == jnp.arange(16, dtype=jnp.int32)[None, :, None], valid[:, None, :], 0.0
    ).astype(bf16)
    inv_count = jnp.pad(1.0 / jnp.sum(valid, axis=1), (0, 16 - images))
    inv_count = jnp.broadcast_to(inv_count[:, None], (16, 128))
    order = jnp.broadcast_to(text_order[:, None], (image_total, 128))
    first_image = first_image.astype(jnp.int32)[None]

    fast = (n_dp, n_rep, slots, part_rows) == (2, 16, 8, 64)
    if fast:
        me = jnp.stack([dp_at, rep_at // 4, rep_at // 2 % 2, rep_at % 2]).astype(jnp.int32)
        (block_one, block_two, block_three), (place, kind, row), others = pick_slabs(
            master, text_emb, owner_list, me, x, mask_row, col, sel, inv_count, order, first_image
        )
        x, mask_row, col, sel, inv_count, order, first_image = others
        one = Spread(block_one)
        *one.parts, block_two = meet(*one.parts, block_two)
        one.cross_one()
        one.two = send(one.ring, CROSS_TWO)
        two = Spread(block_two)
        one.ring, one.one, one.two = meet(one.ring, one.one, one.two)
        one.cross_two()
        one.send_near(0, 1)
        one.two, *two.parts = meet(one.two, *two.parts)
        one.send_near(2)
        one.both, block_three = meet(one.both, block_three)
        one.finish()
        two.cross_one()
        two.send_near(0)
        w_qkv = Weight(one.arrays(), QKV_TILES)
        a, qkv, vec = qkv_forward(images, x, jnp.zeros((16, D), f32), w_qkv, me)
        qkv, two.ring, two.one, two.near[0], block_three = meet(qkv, two.ring, two.one, two.near[0], block_three)
        two.cross_two()
        three = Spread(block_three)
        o, lse = attention_forward(images, qkv, mask_row)
        o, two.two, two.both, *three.parts = meet(o, two.two, two.both, *three.parts)
        two.finish()
        three.cross_one()
        w_out = Weight(two.arrays(), OUT_TILES)
        h, m = middle_forward(images, x, o, vec, w_out, me)
        h, m, three.ring, three.one = meet(h, m, three.ring, three.one)
        three.cross_two()
        three.send_near(0, 1)
        bias_up = vec[7 : 7 + FF // D].reshape(FF // D, 1, D)
        w_up = Weight(two.arrays(), UP_TILES, 3)
        act, slope = up_forward(images, m, w_up, bias_up, me)
        act, three.two, three.both, *three.near = meet(act, three.two, three.both, *three.near)
        three.finish()
        w_down = Weight(three.arrays(), DOWN_TILES, quarters=True)
        w_proj = Weight(three.arrays(), PROJ_TILES, 12)
        all_text = jnp.zeros((16, 128), bf16)
    else:
        me = jnp.zeros((4,), jnp.int32)
        placed = slot_place(owner_list, slots)
        hits = placed[None, :] == jnp.arange(n_rep * slots, dtype=jnp.int32)[:, None]
        tile_ids = jnp.arange(owner_list.shape[0], dtype=jnp.int32)[None, :]
        tile_of_slot = jnp.where(jnp.any(hits, axis=1), jnp.sum(jnp.where(hits, tile_ids, 0), axis=1), 1 << 20)
        text = text_emb.astype(f32)
        own_text = (text * lax.rsqrt(jnp.sum(text * text, axis=-1, keepdims=True) + unit_eps)).astype(bf16)
        all_text = lax.all_gather(own_text, AXES, axis=0, tiled=True)
        tiles = gather_weights(master, placed).reshape(-1, TR, D)
        w_qkv = Weight([tiles[:QKV_TILES]], QKV_TILES)
        w_out = Weight([tiles[QKV_TILES : QKV_TILES + OUT_TILES]], OUT_TILES)
        w_up = Weight([tiles[QKV_TILES + OUT_TILES : DOWN_FIRST]], UP_TILES)
        w_down = Weight([tiles[DOWN_FIRST:PROJ_FIRST].reshape(DOWN_TILES, TR // 4, FF)], DOWN_TILES, quarters=True)
        w_proj = Weight([tiles[PROJ_FIRST:VEC_TILE]], PROJ_TILES)
        a, qkv, vec = qkv_forward(images, x, tiles[VEC_TILE, :16].astype(f32), w_qkv, me)
        bias_up = vec[7 : 7 + FF // D].reshape(FF // D, 1, D)
        o, lse = attention_forward(images, qkv, mask_row)
        h, m = middle_forward(images, x, o, vec, w_out, me)
        act, slope = up_forward(images, m, w_up, bias_up, me)
    block_out, pooled = down_forward(images, act, w_down, h, vec, sel, inv_count, me)

    pooled_all = lax.all_to_all(jnp.broadcast_to(pooled[None, :images], (n_dp * n_rep, images, D)), AXES, 0, 0)
    act_sum = act_sums(images, act, sel)
    probabilities = attention_again(images, qkv, lse, col)
    if fast:
        pooled_all, act_sum, probabilities = meet(pooled_all, act_sum, probabilities)
    dz_all, rank, spread, hidden, pooled_all = loss_backward(
        me, first_image, pooled_all, all_text, order, w_proj, w_down, inv_count
    )

    both = jnp.concatenate([rank[:images], act_sum[:images]], axis=1)
    if fast:
        packed = jnp.concatenate([both[:, at * PACK : (at + 1) * PACK] for at in range(3)], axis=0)
        ranks = Spread()
        packed = jnp.pad(packed, ((0, 16 - 3 * images), (0, 0)))
        beside = send(packed, SWAP_Z)
        dm, g_bias_up, other, mine = up_backward(images, slope, m, w_up, hidden, col, me)
        dm, other, mine, packed, beside = meet(dm, other, mine, packed, beside)
        up_sum = PieceSum(other, me)
        pair = jnp.stack([packed, beside])
        far = send(pair, SWAP_ZZ)
        dh, do, g_out, g_two = middle_backward(images, h, dm, col, spread, o, w_out, vec, me)
        dh, do, up_sum.mine, up_sum.one, pair, far = meet(dh, do, mine, up_sum.one, pair, far)
        up_sum.cross_one()
        dqkv, g_bias = attention_backward(images, qkv, do, probabilities)
        dqkv, up_sum.two, pair, far = meet(dqkv, up_sum.two, pair, far)
        up_sum.cross_two()
        ranks.cross_one(jnp.concatenate([pair, far]))
        ranks.two = send(ranks.ring, CROSS_TWO)
        other = qkv_weight_grad_fast(images, dqkv, a, g_out, me, True)
        other, dqkv = meet(other, dqkv)
        qkv_sum = PieceSum(other, me)
        mine = qkv_weight_grad_fast(images, dqkv, a, g_out, me, False)
        up_sum.partial()
        dqkv, up_sum.sums, up_sum.three, qkv_sum.mine, qkv_sum.one, ranks.ring, ranks.one, ranks.two = meet(
            dqkv, up_sum.sums, up_sum.three, mine, qkv_sum.one, ranks.ring, ranks.one, ranks.two
        )
        qkv_sum.cross_one()
        up_sum.cross_z()
        ranks.cross_two()
        input_grad, vec_sum = input_backward(images, x, dqkv, w_qkv, dh, vec, g_two, g_bias, g_bias_up, me)
        vec_sum, qkv_sum.two, ranks.ring, ranks.one, ranks.two, ranks.both, *up_sum.last = meet(
            vec_sum, qkv_sum.two, ranks.ring, ranks.one, ranks.two, ranks.both, *up_sum.last
        )
        qkv_sum.cross_two()
        near_vec = send(vec_sum, SWAP_CORE)
        ranks.send_near(0, 1)
        up_total = up_sum.total()
        vec_sum, near_vec, up_total = meet(vec_sum, near_vec, up_total)
        vec_sum += near_vec
        vec_sum += send(vec_sum, SWAP_ZZ)
        qkv_sum.partial()
        vec_sum, qkv_sum.sums, qkv_sum.three, up_total, ranks.two, ranks.both, *ranks.near = meet(
            vec_sum, qkv_sum.sums, qkv_sum.three, up_total, ranks.two, ranks.both, *ranks.near
        )
        qkv_sum.cross_z()
        near_up = send(up_total, SWAP_CORE)
        vec_sum += send(vec_sum, SWAP_Y)
        vec_sum += send(vec_sum, SWAP_Z)
        near_up, vec_sum, ranks.two, ranks.both, *qkv_sum.last = meet(
            near_up, vec_sum, ranks.two, ranks.both, *qkv_sum.last
        )
        qkv_total = qkv_sum.total()
        near_qkv = send(qkv_total, SWAP_CORE)
        ranks.finish()
        across = send(vec_sum, SWAP_X)
        near_qkv, across, *ranks.near = meet(near_qkv, across, *ranks.near)
        vec_total = vec_sum + across
        summed = return_to_owners((qkv_total, up_total, near_qkv, near_up), place)
        g_down, g_proj = rank_grads(images, kind, row, ranks.arrays(), dz_all, pooled_all)
        g_down, g_proj, vec_total, *summed = meet(g_down.reshape(8, 16, FF), g_proj, vec_total, *summed)
    else:
        both_all = lax.all_gather(both, AXES, axis=0, tiled=True)
        dm, g_bias_up, g_up = up_backward(images, slope, m, w_up, hidden, col, me)
        dh, do, g_out, g_two = middle_backward(images, h, dm, col, spread, o, w_out, vec, me)
        dqkv, g_bias = attention_backward(images, qkv, do, probabilities)
        g_qkv = qkv_weight_grad(images, dqkv, a)
        input_grad, vec_total = input_backward(images, x, dqkv, w_qkv, dh, vec, g_two, g_bias, g_bias_up, me)
        mine = lax.dynamic_slice_in_dim(tile_of_slot, rep_at * slots, slots)
        first_row = dp_at * part_rows
        is_down = (mine >= DOWN_FIRST) & (mine < PROJ_FIRST)
        is_proj = (mine >= PROJ_FIRST) & (mine < VEC_TILE)
        kind = jnp.where(is_down, DOWN, jnp.where(is_proj, PROJ, jnp.where(mine <= VEC_TILE, SUMMED, NONE)))
        kind = kind.astype(jnp.int32)
        each = part_rows * D // FF
        row = jnp.where(is_proj, (mine - PROJ_FIRST) * TR + first_row, 0)
        down_rows = jnp.clip(((mine - DOWN_FIRST) * TR + first_row) * D // FF, 0, D - each)
        g_down = tn(both_all[:, :D], both_all[:, D:])
        g_down = jnp.stack([lax.dynamic_slice_in_dim(g_down, at, each) for at in down_rows])
        g_down = jnp.pad(g_down, ((0, 0), (0, max(0, 8 - each)), (0, 0)))
        g_proj = tn(dz_all, pooled_all)
        last = jnp.pad(vec_total, ((0, TR - 16), (0, 0))).astype(bf16)
        tiles = jnp.concatenate([g_qkv, g_out, g_up, last], axis=0).reshape(-1, TR, D)
        index = jnp.where(tile_of_slot == VEC_TILE, DOWN_FIRST, jnp.where(tile_of_slot < DOWN_FIRST, tile_of_slot, 1 << 20))
        summed = [scatter_grads(tiles, index, slots, part_rows)]
    new_master, new_first, new_second = adam(
        kind, row, me, master, first_moment, second_moment, summed, g_down, g_proj, vec_total
    )
    return block_out, input_grad, new_master, new_first, new_second


def solution(mesh):
    in_specs = (
        P(("dp", "rep"), None, None),
        P(("dp", "rep"), None),
        P(("dp", "rep"), None),
        P(),
        P(),
        P("rep", None, "dp", None),
        P("rep", None, "dp", None),
        P("rep", None, "dp", None),
    )
    out_specs = (
        P(("dp", "rep"), None, None),
        P(("dp", "rep"), None, None),
        P("rep", None, "dp", None),
        P("rep", None, "dp", None),
        P("rep", None, "dp", None),
    )
    return jax.shard_map(shards, mesh=mesh, in_specs=in_specs, out_specs=out_specs, check_vma=False)
```

```python
import functools

import jax
import jax.numpy as jnp
from jax import lax
from jax.experimental import pallas as pl
from jax.experimental.pallas import tpu as pltpu
from jax.sharding import PartitionSpec as P

D = 768
HEADS = 12
HEAD = 64
FF = 3072
EMB = 512
PATCHES = 196
STEP = 10
ROWS = 208
TR = 128

logit_scale = 50.0
learn_rate = 0.03
beta_one = 0.9
beta_two = 0.999
adam_eps = 1e-08
decay_rate = 0.05
norm_eps = 1e-05
unit_eps = 1e-06
masked_score = -1000000000.0

bf16 = jnp.bfloat16
f32 = jnp.float32
AXES = ("dp", "rep")
MIB = 1 << 20

X, Z, Y, CORE = range(4)
PIECES = [(x, z, y) for x in range(2) for z in range(4) for y in range(2)]

QKV_TILES = 3 * D // TR
OUT_TILES = D // TR
UP_TILES = FF // TR
DOWN_TILES = FF // TR
PROJ_TILES = EMB // TR
DOWN_FIRST = QKV_TILES + OUT_TILES + UP_TILES
PROJ_FIRST = DOWN_FIRST + DOWN_TILES
VEC_TILE = PROJ_FIRST + PROJ_TILES
PACK = (D + FF) // 3
CHUNK_TILES = (
    (QKV_TILES // 2, 0),
    (OUT_TILES // 2, QKV_TILES),
    (UP_TILES // 2, QKV_TILES + OUT_TILES),
    (DOWN_TILES // 2, DOWN_FIRST),
    (PROJ_TILES // 2, PROJ_FIRST),
)
CHUNK_AT = ((0, 0), (1, 0), (1, 3), (2, 0), (2, 12))
SLABS = (10, 15, 15)
CHIPS = [(dz, dy) for dz in range(4) for dy in range(2)]


def nn(a, b):
    return lax.dot_general(a, b, (((1,), (0,)), ((), ())), preferred_element_type=f32)


def nt(a, b):
    return lax.dot_general(a, b, (((1,), (1,)), ((), ())), preferred_element_type=f32)


def tn(a, b):
    return lax.dot_general(a, b, (((0,), (0,)), ((), ())), preferred_element_type=f32)


def call(kernel, outs, ins, in_specs, out_specs, grid=None, scratch=(), flops=0, vmem=24, prefetch=0, in_hbm=(), out_hbm=(), vmem_in=(), vmem_out=()):
    ins = [
        pltpu.with_memory_space_constraint(a, pltpu.HBM) if k >= prefetch and (s.memory_space is pltpu.HBM or k in in_hbm) else a
        for k, (a, s) in enumerate(zip(ins, [None] * prefetch + list(in_specs), strict=True))
    ]
    ins = [pltpu.with_memory_space_constraint(a, pltpu.VMEM) if k in vmem_in else a for k, a in enumerate(ins)]
    moved = sum(a.size * a.dtype.itemsize for a in ins) + sum(o.size * o.dtype.itemsize for o in outs)
    spaces = {k: pltpu.HBM for k in out_hbm} | {k: pltpu.VMEM for k in vmem_out}
    outs = [spaces[k](o.shape, o.dtype) if k in spaces else o for k, o in enumerate(outs)]
    params = pltpu.CompilerParams(
        vmem_limit_bytes=vmem * MIB,
        dimension_semantics=("arbitrary",) * len(grid or ()) or None,
    )
    return pl.pallas_call(
        kernel,
        out_shape=tuple(outs),
        grid_spec=pltpu.PrefetchScalarGridSpec(
            num_scalar_prefetch=prefetch,
            grid=grid or (1,),
            in_specs=in_specs,
            out_specs=tuple(out_specs),
            scratch_shapes=list(scratch),
        ),
        compiler_params=params,
        cost_estimate=pl.CostEstimate(flops=1, bytes_accessed=1, transcendentals=0),
    )(*ins)


def whole(shape):
    return pl.BlockSpec(shape, lambda *_: (0,) * len(shape))


def rows_at(rows, cols):
    return pl.BlockSpec((rows, cols), lambda i, *_: (i, 0))


def cols_at(rows, cols):
    return pl.BlockSpec((rows, cols), lambda i, *_: (0, i))


def sds(shape, dtype):
    return jax.ShapeDtypeStruct(shape, dtype)


class Weight:
    def __init__(self, arrays, tiles, first=0, quarters=False):
        self.arrays, self.tiles, self.first, self.quarters = tuple(arrays), tiles, first, quarters
        self.pieces = len(arrays) > 1
        self.specs = [pl.BlockSpec(memory_space=pltpu.HBM)] * len(arrays)
        shape = (tiles, TR // 4, FF) if quarters else (tiles, TR, D)
        self.scratch = [pltpu.VMEM(shape, bf16), pltpu.SemaphoreType.DMA((32 if self.pieces else 1,))]

    def copies(self, me, refs, out, sems):
        if not self.pieces:
            return [lambda: pltpu.make_async_copy(refs[0], out, sems.at[0])]
        copies = []
        half = self.tiles // 2
        for at, (c, x, y) in enumerate(sources(me)):
            for back in range(4):
                z = me[Z] ^ back
                if self.quarters:
                    row, col = x * 16, z * D + y * 384
                else:
                    row, col = x * 64 + z * 16, y * 384
                rows = pl.ds(pl.multiple_of(row, 16), 16)
                cols = pl.ds(pl.multiple_of(col, 128), 384)
                source = refs[at].at[back, pl.ds(self.first, half)]
                place = out.at[pl.ds(half * c, half), rows, cols]
                copies.append(functools.partial(pltpu.make_async_copy, source, place, sems.at[len(copies)]))
        return copies

    def start(self, me, refs, out, sems):
        for copy in self.copies(me, refs, out, sems):
            copy().start()

    def wait(self, me, refs, out, sems, part=None, parts=1):
        copies = self.copies(me, refs, out, sems)
        if part is not None and not self.pieces:
            copies = copies if part == 0 else []
        elif part is not None:
            copies = copies[16 * part : 16 * part + 16] if parts == 2 else copies[part::4]
        for copy in copies:
            copy().wait()

    def load(self, me, refs, out, sems):
        @pl.when(pl.program_id(0) == 0)
        def _():
            self.start(me, refs, out, sems)
            self.wait(me, refs, out, sems)


def normalized(x):
    center = x - jnp.mean(x, axis=-1, keepdims=True)
    spread = jnp.mean(center * center, axis=-1, keepdims=True)
    inverse = lax.rsqrt(spread + norm_eps)
    return center * inverse, inverse


def norm_back(grad, hat, inverse, gain):
    scaled = grad * gain
    first = jnp.mean(scaled, axis=-1, keepdims=True)
    second = jnp.mean(scaled * hat, axis=-1, keepdims=True)
    return inverse * (scaled - first - hat * second)


def accumulate(i, ref, value):
    @pl.when(i == 0)
    def _():
        ref[...] = value

    @pl.when(i > 0)
    def _():
        ref[...] += value


def column_sum(x):
    return jnp.sum(x, axis=0, keepdims=True)


def third(j, me):
    return jnp.where(me[CORE] == 0, j, 2 - j)


def qkv_kernel(images, weight, me_ref, *refs):
    count = len(weight.arrays)
    pieces = refs[:count]
    x_ref, vec_in_ref, a_ref, qkv_ref, vec_ref, w_ref, sems, vec_half, vec_sems = refs[count:]
    j = pl.program_id(0)

    @pl.when(j == 0)
    def _():
        weight.start(me_ref, pieces, w_ref, sems)
        if weight.pieces:
            parts = []
            for at, (_, x, y) in list(enumerate(sources(me_ref)))[:4]:
                for back in range(4):
                    copy = pltpu.make_async_copy(pieces[at].at[back, 9], vec_half.at[y], vec_sems.at[len(parts)])
                    parts.append(((x == 0) & ((me_ref[Z] ^ back) == 0), copy))
            for here, copy in parts:
                pl.when(here)(copy.start)
            for here, copy in parts:
                pl.when(here)(copy.wait)
            vec_ref[...] = jnp.concatenate([vec_half[0], vec_half[1]], axis=1).astype(f32)
        else:
            vec_ref[...] = vec_in_ref[...]
        for i in range(images):
            hat, _ = normalized(x_ref[pl.ds(i * ROWS, ROWS), :].astype(f32))
            a_ref[pl.ds(i * ROWS, ROWS), :] = (hat * vec_ref[0:1, :] + vec_ref[1:2, :]).astype(bf16)
        weight.wait(me_ref, pieces, w_ref, sems, 0, 2)

    @pl.when(j == 1)
    def _():
        weight.wait(me_ref, pieces, w_ref, sems, 1, 2)

    j = third(j, me_ref)
    bias = jnp.where(j == 0, vec_ref[4:5, :], jnp.where(j == 2, vec_ref[5:6, :], 0.0))
    scale = jnp.where(j == 0, f32(HEAD**-0.5), f32(1.0))
    w = w_ref[pl.ds(6 * j, 6)].reshape(D, D)
    qkv_ref[...] = ((nt(a_ref[...], w) + bias) * scale).astype(bf16)


def qkv_forward(images, x, vec, weight, me):
    n = images * ROWS
    return call(
        functools.partial(qkv_kernel, images, weight),
        (sds((n, D), bf16), sds((n, 3 * D), bf16), sds((16, D), f32)),
        (me, *weight.arrays, x, vec),
        weight.specs + [whole((n, D)), whole((16, D))],
        [whole((n, D)), pl.BlockSpec((n, D), lambda j, me: (0, third(j, me))), whole((16, D))],
        grid=(3,),
        out_hbm=(0,),
        scratch=weight.scratch + [pltpu.VMEM((2, 16, 384), bf16), pltpu.SemaphoreType.DMA((16,))],
        flops=2 * n * D * 3 * D,
        prefetch=1,
    )


def attention_kernel(qkv_ref, mask_ref, o_ref, lse_ref):
    lane = lax.broadcasted_iota(jnp.int32, (ROWS, 2 * HEAD), 1)
    low_half = lane < HEAD
    valid = mask_ref[0] > 0.0
    lse_all = jnp.zeros((ROWS, 128), f32)
    for pair in range(HEADS // 2):
        at = pair * 2 * HEAD
        q = qkv_ref[:, at : at + 2 * HEAD]
        k = qkv_ref[:, D + at : D + at + 2 * HEAD]
        v = qkv_ref[:, 2 * D + at : 2 * D + at + 2 * HEAD]
        mixed = []
        for half in range(2):
            keep = low_half if half == 0 else jnp.logical_not(low_half)
            s = nt(q, jnp.where(keep, k, jnp.zeros_like(k)))
            s = jnp.where(valid, s, masked_score)
            top = jnp.max(s, axis=-1, keepdims=True)
            e = jnp.exp(s - top)
            total = jnp.sum(e, axis=-1, keepdims=True)
            p = e * (1.0 / total)
            mixed.append(nn(p.astype(bf16), v))
            lse_all = jnp.where(lane == 2 * pair + half, top + jnp.log(total), lse_all)
        o_ref[:, at : at + 2 * HEAD] = jnp.where(low_half, mixed[0], mixed[1]).astype(bf16)
    lse_ref[0] = jnp.transpose(lse_all)[0:16, :]


def attention_forward(images, qkv, mask_row):
    n = images * ROWS
    return call(
        attention_kernel,
        (sds((n, D), bf16), sds((images, 16, ROWS), f32)),
        (qkv, mask_row),
        [rows_at(ROWS, 3 * D), pl.BlockSpec((1, 1, ROWS), lambda i: (i, 0, 0))],
        [rows_at(ROWS, D), pl.BlockSpec((1, 16, ROWS), lambda i: (i, 0, 0))],
        grid=(images,),
        flops=4 * n * ROWS * D,
    )


def middle_kernel(weight, me_ref, *refs):
    count = len(weight.arrays)
    x_ref, o_ref, vec_ref, h_ref, m_ref, w_ref, sems = refs[count:]
    weight.load(me_ref, refs[:count], w_ref, sems)
    part = nt(o_ref[...], w_ref[...].reshape(D, D)) + vec_ref[6:7, :]
    middle = x_ref[...].astype(f32) + part
    h_ref[...] = middle
    hat, _ = normalized(middle)
    m_ref[...] = (hat * vec_ref[2:3, :] + vec_ref[3:4, :]).astype(bf16)


def middle_forward(images, x, o, vec, weight, me):
    n = images * ROWS
    return call(
        functools.partial(middle_kernel, weight),
        (sds((n, D), f32), sds((n, D), bf16)),
        (me, *weight.arrays, x, o, vec),
        weight.specs + [rows_at(ROWS, D), rows_at(ROWS, D), whole((16, D))],
        [rows_at(ROWS, D), rows_at(ROWS, D)],
        grid=(images,),
        scratch=weight.scratch,
        flops=2 * n * D * D,
        prefetch=1,
    )


def gelu_parts(u):
    phi = 0.5 + 0.5 * lax.erf(u * 0.7071067811865476)
    density = jnp.exp2(u * u * -0.7213475204444817) * 0.3989422804014327
    return u * phi, phi + u * density


def own_block(j, me):
    return (j // 2 + me[CORE]) % 2 * 2 + j % 2


def up_kernel(images, weight, me_ref, *refs):
    count = len(weight.arrays)
    m_ref, bias_ref, act_ref, slope_ref, w_ref, sems = refs[count:]
    j = pl.program_id(0)

    @pl.when(j == 0)
    def _():
        weight.start(me_ref, refs[:count], w_ref, sems)
        weight.wait(me_ref, refs[:count], w_ref, sems, 0, 2)

    @pl.when(j == 2)
    def _():
        weight.wait(me_ref, refs[:count], w_ref, sems, 1, 2)

    w = w_ref[pl.ds(6 * own_block(j, me_ref), 6)].reshape(D, D)
    for i in range(images):
        at = pl.ds(i * ROWS, ROWS)
        act, slope = gelu_parts(nt(m_ref[at, :], w) + bias_ref[0])
        act_ref[at, :] = act.astype(bf16)
        slope_ref[at, :] = slope.astype(bf16)


def up_forward(images, m, weight, bias, me):
    n = images * ROWS
    cols = pl.BlockSpec((n, D), lambda j, me: (0, own_block(j, me)))
    return call(
        functools.partial(up_kernel, images, weight),
        (sds((n, FF), bf16), sds((n, FF), bf16)),
        (me, *weight.arrays, m, bias),
        weight.specs + [whole((n, D)), pl.BlockSpec((1, 1, D), lambda j, me: (own_block(j, me), 0, 0))],
        [cols, cols],
        grid=(FF // D,),
        vmem_out=(0,),
        out_hbm=(1,),
        scratch=weight.scratch,
        flops=2 * n * D * FF,
        prefetch=1,
    )


def act_sum_kernel(images, act_ref, sel_ref, sum_ref):
    total = jnp.zeros(sum_ref.shape, f32)
    for i in range(images):
        total += nn(sel_ref[i], act_ref[pl.ds(i * ROWS, ROWS), :])
    sum_ref[...] = total.astype(bf16)


def act_sums(images, act, sel):
    n = images * ROWS
    return call(
        functools.partial(act_sum_kernel, images),
        (sds((16, FF), bf16),),
        (act, sel),
        [cols_at(n, D), whole((images, 16, ROWS))],
        [cols_at(16, D)],
        grid=(FF // D,),
        flops=32 * n * FF,
    )[0]


def down_kernel(images, weight, me_ref, *refs):
    count = len(weight.arrays)
    act_ref, h_ref, vec_ref, sel_ref, inv_ref, out_ref, pooled_ref, w_ref, sems = refs[count:]
    j = pl.program_id(0)

    @pl.when(j == 0)
    def _():
        weight.start(me_ref, refs[:count], w_ref, sems)
        weight.wait(me_ref, refs[:count], w_ref, sems, 0, 2)

    @pl.when(j == 1)
    def _():
        weight.wait(me_ref, refs[:count], w_ref, sems, 1, 2)

    tiles = DOWN_TILES // 3
    w = w_ref[pl.ds(tiles * third(j, me_ref), tiles)].reshape(D // 3, FF)
    y = nt(act_ref[...], w)
    total = jnp.zeros((16, D // 3), f32)
    for i in range(images):
        rows = slice(i * ROWS, i * ROWS + ROWS)
        out = (h_ref[rows, :] + (y[rows] + vec_ref[11:12, :])).astype(bf16)
        out_ref[i] = out[0:PATCHES, :]
        total += nn(sel_ref[i], out)
    pooled_ref[...] = (total * inv_ref[:, 0:1]).astype(bf16)


def down_forward(images, act, weight, h, vec, sel, inv_count, me):
    n = images * ROWS

    def cols(rows):
        return pl.BlockSpec((rows, D // 3), lambda j, me: (0, third(j, me)))

    return call(
        functools.partial(down_kernel, images, weight),
        (sds((images, PATCHES, D), bf16), sds((16, D), bf16)),
        (me, *weight.arrays, act, h, vec, sel, inv_count),
        weight.specs[:-1]
        + [
            pl.BlockSpec(memory_space=pl.ANY),
            pl.BlockSpec(memory_space=pltpu.VMEM),
            cols(n),
            cols(16),
            whole((images, 16, ROWS)),
            whole((16, 128)),
        ],
        [pl.BlockSpec((images, PATCHES, D // 3), lambda j, me: (0, 0, third(j, me))), cols(16)],
        grid=(3,),
        vmem_in=(1 + len(weight.arrays),),
        scratch=weight.scratch,
        flops=2 * n * D * FF,
        prefetch=1,
    )


def loss_kernel(total_images, proj, down, me_ref, first_ref, *refs):
    count = len(proj.arrays)
    pieces = refs[:count]
    if proj.pieces:
        down_pieces, rest = pieces, refs[count:]
    else:
        down_pieces, rest = refs[count : count + 1], refs[count + 1 :]
    text_ref, pooled_ref, order_ref, inv_ref, dz_ref, rank_ref, spread_ref, hidden_ref, all_ref = rest[:9]
    proj_ref, proj_sems, down_ref, down_sems, rows_ref = rest[9:14]
    down_copies = down.copies(me_ref, down_pieces, down_ref, down_sems)
    proj_copies = proj.copies(me_ref, pieces, proj_ref, proj_sems)
    if proj.pieces:
        slab_ref, slab_sems = rest[14:]
        for at, (c, x, y) in enumerate(sources(me_ref)):
            for back in range(4):
                device = x * 16 + (me_ref[Z] ^ back) * 4 + y * 2 + c
                out = slab_ref.at[pl.ds(pl.multiple_of(device * 16, 16), 16)]
                source = pieces[at].at[back, 14]
                proj_copies.append(
                    functools.partial(pltpu.make_async_copy, source, out, slab_sems.at[at * 4 + back])
                )
    for copy in proj_copies + down_copies:
        copy().start()
    for copy in proj_copies:
        copy().wait()
    if proj.pieces:
        images = total_images // 32
        shape = (total_images, 512)
        row = lax.broadcasted_iota(jnp.int32, shape, 0)
        col = lax.broadcasted_iota(jnp.int32, shape, 1)
        start = row // images * 16 + row % images
        held = slab_ref[...]
        left = nn(jnp.where(col == start, 1.0, 0.0).astype(bf16), held)
        right = nn(jnp.where(col == start + 8, 1.0, 0.0).astype(bf16), held[:, 0:128])
        text = jnp.concatenate([left, right], axis=1).astype(bf16)
    else:
        text = text_ref[...]
    proj_w = proj_ref[...].reshape(EMB, D)
    each = total_images // pooled_ref.shape[0]
    for d in range(pooled_ref.shape[0]):
        rows_ref[d * each : d * each + each, :] = pooled_ref[d].astype(f32)
    pooled = rows_ref[...].astype(bf16)
    all_ref[...] = pooled
    z = nt(pooled, proj_w)
    square = jnp.sum(z * z, axis=-1, keepdims=True) + unit_eps
    inverse = lax.rsqrt(square)
    image = (z * inverse).astype(bf16)
    s = logit_scale * nt(image, text)
    shape = (total_images, total_images)
    hit = jnp.where(order_ref[:, 0:1] == lax.broadcasted_iota(jnp.int32, shape, 1), 1.0, 0.0)
    part = 1.0 / (2.0 * total_images)

    def grad_of(axis):
        top = jnp.max(s, axis=axis, keepdims=True)
        lse = top + jnp.log(jnp.sum(jnp.exp(s - top), axis=axis, keepdims=True))
        return ((jnp.exp(s - lse) - hit) * part).astype(bf16)

    de = logit_scale * (nn(grad_of(1), text) + nn(grad_of(0), text))
    dz = inverse * de - z * (inverse * inverse * inverse * jnp.sum(z * de, axis=-1, keepdims=True))
    dz = dz.astype(bf16)
    dz_ref[...] = dz
    pick = lax.broadcasted_iota(jnp.int32, (16, total_images), 1) == (
        first_ref[0] + lax.broadcasted_iota(jnp.int32, (16, total_images), 0)
    )
    own = nn(jnp.where(pick, 1.0, 0.0).astype(bf16), dz).astype(bf16)
    spread = nn(own, proj_w) * inv_ref[:, 0:1]
    spread_ref[...] = spread
    rank = spread.astype(bf16)
    rank_ref[...] = rank
    for copy in down_copies:
        copy().wait()
    hidden_ref[...] = nn(rank, down_ref[...].reshape(D, FF))


def loss_backward(me, first, pooled, text, order, proj, down, inv_count):
    total = pooled.shape[0] * pooled.shape[1]
    if proj.pieces:
        arrays, extra = proj.arrays, [pltpu.VMEM((512, 384), bf16), pltpu.SemaphoreType.DMA((32,))]
    else:
        arrays, extra = proj.arrays + down.arrays, []
    return call(
        functools.partial(loss_kernel, total, proj, down),
        (sds((total, EMB), bf16), sds((16, D), bf16), sds((16, D), f32), sds((16, FF), f32), sds((total, D), bf16)),
        (me, first, *arrays, text, pooled, order, inv_count),
        [pl.BlockSpec(memory_space=pltpu.HBM)] * len(arrays)
        + [whole(text.shape), whole(pooled.shape), whole((total, 128)), whole((16, 128))],
        [whole((total, EMB)), whole((16, D)), whole((16, D)), whole((16, FF)), whole((total, D))],
        scratch=proj.scratch + down.scratch + [pltpu.VMEM((total, D), f32)] + extra,
        flops=6 * total * total * EMB + 2 * total * D * EMB + 32 * D * FF,
        vmem=32,
        prefetch=2,
    )


def weave(ref, value):
    for t in range(value.shape[0] // TR):
        for x, z, y in PIECES:
            row = t * TR + x * 64 + z * 16
            ref[x * 8 + z * 2 + y, pl.ds(t * 16, 16), :] = value[row : row + 16, y * 384 : y * 384 + 384]


def half_block(j, me):
    return (j // 2 + 1 - me[CORE]) % 2 * 2 + j % 2


DM_COLS = 256


def up_back_kernel(images, weight, me_ref, *refs):
    count = len(weight.arrays)
    slope_ref, m_ref, hidden_ref, col_ref, dm_ref, db_ref = refs[count : count + 6]
    w_ref, sems, du_ref = refs[-3:]
    j = pl.program_id(0)
    blocks = FF // D

    @pl.when(j == 0)
    def _():
        weight.start(me_ref, refs[:count], w_ref, sems)

    @pl.when(j < blocks)
    def _():
        cols = pl.ds(pl.multiple_of(half_block(j, me_ref) * D, 128), D)
        total = jnp.zeros((1, D), f32)
        for i in range(images):
            at = pl.ds(i * ROWS, ROWS)
            du = (slope_ref[at, :].astype(f32) * (col_ref[at, 0:1] * hidden_ref[i : i + 1, :])).astype(bf16)
            du_ref[at, cols] = du
            total += column_sum(du.astype(f32))
        db_ref[...] = jnp.broadcast_to(total, db_ref.shape)
        dw = tn(du_ref[:, cols], m_ref[...]).astype(bf16)
        if not weight.pieces:
            refs[count + 6][...] = dw
            return
        send_ref, keep_ref = refs[count + 6 : count + 8]

        @pl.when(j < 2)
        def _():
            weave(send_ref, dw)

        @pl.when(j >= 2)
        def _():
            weave(keep_ref, dw)

    @pl.when(j == blocks)
    def _():
        weight.wait(me_ref, refs[:count], w_ref, sems)

    @pl.when(j >= blocks)
    def _():
        for k in range(D // DM_COLS):

            @pl.when(j == blocks + k)
            def _():
                dm_ref[...] = nn(du_ref[...], w_ref[:, :, k * DM_COLS : (k + 1) * DM_COLS].reshape(FF, DM_COLS))


def up_backward(images, slope, m, weight, hidden, col, me):
    n = images * ROWS
    blocks = FF // D
    steps = D // DM_COLS

    def block(j, me):
        return half_block(jnp.minimum(j, blocks - 1), me)

    def cols(rows):
        return pl.BlockSpec((rows, D), lambda j, me: (0, block(j, me)))

    if weight.pieces:
        shapes = (sds((16, 192, 384), bf16),) * 2
        specs = [
            pl.BlockSpec((16, 96, 384), lambda j, me: (0, jnp.minimum(j, 1), 0)),
            pl.BlockSpec((16, 96, 384), lambda j, me: (0, jnp.clip(j - 2, 0, 1), 0)),
        ]
    else:
        shapes = (sds((FF, D), bf16),)
        specs = [pl.BlockSpec((D, D), lambda j, me: (block(j, me), 0))]
    return call(
        functools.partial(up_back_kernel, images, weight),
        (sds((n, D), f32), sds((8, FF), f32)) + shapes,
        (me, *weight.arrays, slope, m, hidden, col),
        weight.specs + [cols(n), whole((n, D)), cols(16), whole((n, 128))],
        [pl.BlockSpec((n, DM_COLS), lambda j, me: (0, jnp.maximum(j - blocks, 0))), cols(8)] + specs,
        grid=(blocks + steps,),
        vmem=40,
        scratch=weight.scratch + [pltpu.VMEM((n, FF), bf16)],
        flops=4 * n * D * FF,
        prefetch=1,
    )


def middle_back_kernel(images, weight, me_ref, *refs):
    count = len(weight.arrays)
    h_ref, dm_ref, col_ref, spread_ref, o_ref, vec_ref = refs[count : count + 6]
    dh_ref, do_ref, dw_ref, dvec_ref, w_ref, sems, dat_ref = refs[count + 6 :]
    i = pl.program_id(0)

    @pl.when(i == 0)
    def _():
        weight.start(me_ref, refs[:count], w_ref, sems)

    @pl.when(i < images)
    def _():
        hat, inverse = normalized(h_ref[...])
        dm = dm_ref[...]
        part = norm_back(dm, hat, inverse, vec_ref[2:3, :])
        here = spread_ref[pl.ds(i, 1), :]
        dh = col_ref[:, 0:1] * here + part
        dh_ref[...] = dh
        dat = dh.astype(bf16)
        dat_ref[pl.ds(pl.multiple_of(i * ROWS, 16), ROWS), :] = dat
        sums = jnp.concatenate(
            [
                column_sum(dm * hat),
                column_sum(dm),
                column_sum(dat.astype(f32)),
                column_sum(col_ref[:, 0:1]) * here.astype(bf16).astype(f32),
                jnp.zeros((4, D), f32),
            ],
            axis=0,
        )
        accumulate(i, dvec_ref, sums)

    @pl.when(i == images)
    def _():
        dw = tn(dat_ref[...], o_ref[...]).astype(bf16)
        if weight.pieces:
            for half in range(2):
                weave(dw_ref.at[half], dw[half * 384 : half * 384 + 384])
        else:
            dw_ref[...] = dw
        weight.wait(me_ref, refs[:count], w_ref, sems)
        do_ref[...] = nn(dat_ref[...], w_ref[...].reshape(D, D)).astype(bf16)


def middle_backward(images, h, dm, col, spread, o, weight, vec, me):
    n = images * ROWS
    dw_shape = (2, 16, 48, 384) if weight.pieces else (D, D)

    def rows(cols):
        return pl.BlockSpec((ROWS, cols), lambda i, me: (jnp.minimum(i, images - 1), 0))

    return call(
        functools.partial(middle_back_kernel, images, weight),
        (sds((n, D), f32), sds((n, D), bf16), sds(dw_shape, bf16), sds((8, D), f32)),
        (me, *weight.arrays, h, dm, col, spread, o, vec),
        weight.specs + [rows(D), rows(D), rows(128), whole((16, D)), whole((n, D)), whole((16, D))],
        [rows(D), whole((n, D)), whole(dw_shape), whole((8, D))],
        grid=(images + 1,),
        in_hbm=(1 + len(weight.arrays),),
        vmem_in=(2 + len(weight.arrays),) if weight.pieces else (),
        scratch=weight.scratch + [pltpu.VMEM((n, D), bf16)],
        flops=4 * n * D * D,
        prefetch=1,
    )


def attention_again_kernel(qkv_ref, lse_ref, col_ref, p_ref):
    low_half = lax.broadcasted_iota(jnp.int32, (ROWS, 2 * HEAD), 1) < HEAD
    valid = jnp.broadcast_to(col_ref[:, 0:1], (ROWS, ROWS)) > 0.0
    for pair in range(HEADS // 2):
        at = pair * 2 * HEAD
        q = qkv_ref[:, at : at + 2 * HEAD]
        k = qkv_ref[:, D + at : D + at + 2 * HEAD]
        for half in range(2):
            keep = low_half if half == 0 else jnp.logical_not(low_half)
            head = 2 * pair + half
            s = jnp.where(valid, nt(jnp.where(keep, k, jnp.zeros_like(k)), q), masked_score)
            p_ref[0, head] = jnp.exp(s - lse_ref[0, head : head + 1, :]).astype(bf16)


def attention_again(images, qkv, lse, col):
    n = images * ROWS
    return call(
        attention_again_kernel,
        (sds((images, HEADS, ROWS, ROWS), bf16),),
        (qkv, lse, col),
        [rows_at(ROWS, 3 * D), pl.BlockSpec((1, 16, ROWS), lambda i: (i, 0, 0)), rows_at(ROWS, 128)],
        [pl.BlockSpec((1, HEADS, ROWS, ROWS), lambda i: (i, 0, 0, 0))],
        grid=(images,),
        vmem_out=(0,),
        flops=2 * n * ROWS * D,
    )[0]


def attention_back_kernel(qkv_ref, do_ref, p_ref, dqkv_ref, db_ref):
    i = pl.program_id(0)
    low_half = lax.broadcasted_iota(jnp.int32, (ROWS, 2 * HEAD), 1) < HEAD
    for pair in range(HEADS // 2):
        at = pair * 2 * HEAD
        q = qkv_ref[:, at : at + 2 * HEAD]
        k = qkv_ref[:, D + at : D + at + 2 * HEAD]
        v = qkv_ref[:, 2 * D + at : 2 * D + at + 2 * HEAD]
        do = do_ref[:, at : at + 2 * HEAD]
        dv, dk, dq = [], [], []
        for half in range(2):
            keep = low_half if half == 0 else jnp.logical_not(low_half)
            only_k = jnp.where(keep, k, jnp.zeros_like(k))
            only_v = jnp.where(keep, v, jnp.zeros_like(v))
            head = 2 * pair + half
            rounded = p_ref[0, head]
            p = rounded.astype(f32)
            dp = nt(only_v, do)
            share = jnp.sum(p * dp, axis=0, keepdims=True)
            ds = (p * (dp - share)).astype(bf16)
            dv.append(nn(rounded, do))
            dk.append(nn(ds, q))
            dq.append(tn(ds, only_k))
        dqkv_ref[:, at : at + 2 * HEAD] = ((dq[0] + dq[1]) * (HEAD**-0.5)).astype(bf16)
        dqkv_ref[:, D + at : D + at + 2 * HEAD] = jnp.where(low_half, dk[0], dk[1]).astype(bf16)
        dqkv_ref[:, 2 * D + at : 2 * D + at + 2 * HEAD] = jnp.where(low_half, dv[0], dv[1]).astype(bf16)
    accumulate(i, db_ref, nn(jnp.ones((16, ROWS), bf16), dqkv_ref[...]))


def attention_backward(images, qkv, do, p):
    n = images * ROWS
    return call(
        attention_back_kernel,
        (sds((n, 3 * D), bf16), sds((16, 3 * D), f32)),
        (qkv, do, p),
        [
            rows_at(ROWS, 3 * D),
            rows_at(ROWS, D),
            pl.BlockSpec((1, HEADS, ROWS, ROWS), lambda i: (i, 0, 0, 0)),
        ],
        [rows_at(ROWS, 3 * D), whole((16, 3 * D))],
        grid=(images,),
        vmem_in=(2,),
        flops=10 * n * ROWS * D,
    )


def qkv_grad_kernel(dqkv_ref, a_ref, dw_ref):
    dw_ref[...] = tn(dqkv_ref[...], a_ref[...]).astype(bf16)


def qkv_weight_grad(images, dqkv, a):
    n = images * ROWS
    return call(
        qkv_grad_kernel,
        (sds((3 * D, D), bf16),),
        (dqkv, a),
        [cols_at(n, D), whole((n, D))],
        [rows_at(D, D)],
        grid=(3,),
        flops=6 * n * D * D,
    )[0]


def qkv_grad_fast_kernel(_, dqkv_ref, a_ref, out_ref, pieces_ref):
    j = pl.program_id(0)

    @pl.when(j < 3)
    def _():
        weave(pieces_ref, tn(dqkv_ref[...], a_ref[...]).astype(bf16))

    @pl.when(j == 3)
    def _():
        pieces_ref[...] = out_ref[0]


def qkv_weight_grad_fast(images, dqkv, a, dw_out, me, other):
    n = images * ROWS

    def half(me):
        return 1 - me[CORE] if other else me[CORE]

    return call(
        qkv_grad_fast_kernel,
        (sds((16, 192, 384), bf16),),
        (me, dqkv, a, dw_out),
        [
            pl.BlockSpec((n, 384), lambda j, me: (0, half(me) * 3 + jnp.minimum(j, 2))),
            whole((n, D)),
            pl.BlockSpec((1, 16, 48, 384), lambda j, me: (half(me), 0, 0, 0)),
        ],
        [pl.BlockSpec((16, 48, 384), lambda j, me: (0, j, 0))],
        grid=(4,),
        out_hbm=(0,),
        flops=3 * n * D * D,
        prefetch=1,
    )[0]


def input_back_kernel(weight, me_ref, *refs):
    count = len(weight.arrays)
    x_ref, dqkv_ref, dh_ref, vec_ref, two_ref, bias_ref, up_ref, out_ref, dvec_ref, w_ref, sems, sum_ref = refs[count:]
    i = pl.program_id(0)
    weight.load(me_ref, refs[:count], w_ref, sems)
    da = nn(dqkv_ref[...], w_ref[...].reshape(3 * D, D))
    hat, inverse = normalized(x_ref[...].astype(f32))
    out = dh_ref[...] + norm_back(da, hat, inverse, vec_ref[0:1, :])
    out_ref[0] = out[0:PATCHES, :]
    sums = jnp.concatenate([column_sum(da * hat), column_sum(da), jnp.zeros((6, D), f32)], axis=0)
    accumulate(i, sum_ref, sums)

    @pl.when(i == pl.num_programs(0) - 1)
    def _():
        dvec_ref[...] = jnp.zeros_like(dvec_ref)
        dvec_ref[0:2, :] = sum_ref[0:2, :]
        dvec_ref[2:4, :] = two_ref[0:2, :]
        dvec_ref[4:5, :] = bias_ref[0:1, 0:D]
        dvec_ref[5:6, :] = bias_ref[0:1, 2 * D : 3 * D]
        dvec_ref[6:7, :] = two_ref[2:3, :]
        for b in range(FF // D):
            dvec_ref[7 + b : 8 + b, :] = up_ref[0:1, b * D : (b + 1) * D]
        dvec_ref[7 + FF // D : 8 + FF // D, :] = two_ref[3:4, :]


def input_backward(images, x, dqkv, weight, dh, vec, g_two, g_bias, g_bias_up, me):
    n = images * ROWS
    return call(
        functools.partial(input_back_kernel, weight),
        (sds((images, PATCHES, D), f32), sds((16, D), f32)),
        (me, *weight.arrays, x, dqkv, dh, vec, g_two, g_bias, g_bias_up),
        weight.specs
        + [rows_at(ROWS, D), rows_at(ROWS, 3 * D), rows_at(ROWS, D)]
        + [whole(a.shape) for a in (vec, g_two, g_bias, g_bias_up)],
        [pl.BlockSpec((1, PATCHES, D), lambda i, *_: (i, 0, 0)), whole((16, D))],
        grid=(images,),
        scratch=weight.scratch + [pltpu.VMEM((8, D), f32)],
        flops=6 * n * D * D,
        prefetch=1,
    )


SUMMED, DOWN, PROJ, NONE, VEC = 0, 1, 2, 3, 4


def adam_kernel(part_rows, fast, each, kind_ref, row_ref, me_ref, *refs):
    master_ref, first_ref, second_ref, down_ref, proj_ref, vec_ref = refs[:6]
    summed_refs = refs[6:-5]
    new_master_ref, new_first_ref, new_second_ref, grad_ref, woven_ref = refs[-5:]
    wide = FF // D
    for k in range(each):
        slot = pl.program_id(0) * each + k
        kind = kind_ref[slot]

        @pl.when(kind == SUMMED)
        def _():
            if fast:
                for summed_ref, (dz, dy) in zip(summed_refs, CHIPS, strict=True):
                    rows = pl.ds(pl.multiple_of((me_ref[Z] ^ dz) * 16, 16), 16)
                    cols = pl.ds(pl.multiple_of((me_ref[Y] ^ dy) * 384, 128), 384)
                    grad_ref[rows, cols] = summed_ref[k].astype(f32)
            else:
                grad_ref[...] = summed_refs[0][k].astype(f32)

        @pl.when(kind == VEC)
        def _():
            grad_ref[...] = jnp.zeros_like(grad_ref)
            grad_ref[0 : vec_ref.shape[0], :] = vec_ref[...]

        @pl.when(kind == DOWN)
        def _():
            for c in range(D // 128):
                for b in range(wide):
                    lanes = slice(b * D + c * 128, b * D + c * 128 + 128)
                    woven_ref[c, pl.ds(b, part_rows // wide, stride=wide), :] = down_ref[k, 0 : part_rows // wide, lanes]
                grad_ref[:, c * 128 : (c + 1) * 128] = woven_ref[c]

        @pl.when(kind == PROJ)
        def _():
            at = pl.multiple_of(row_ref[slot], part_rows)
            grad_ref[...] = proj_ref[pl.ds(at, part_rows), :]

        @pl.when(kind == NONE)
        def _():
            grad_ref[...] = jnp.zeros_like(grad_ref)

        grad = grad_ref[...]
        master = master_ref[0, k]
        first = beta_one * first_ref[0, k] + (1.0 - beta_one) * grad
        second = beta_two * second_ref[0, k] + (1.0 - beta_two) * grad * grad
        new_first_ref[0, k] = first
        new_second_ref[0, k] = second
        direction = first / (1.0 - beta_one**STEP)
        size = jnp.sqrt(second / (1.0 - beta_two**STEP)) + adam_eps
        new_master_ref[0, k] = master - learn_rate * (direction / size + decay_rate * master)


def adam(kind, row, me, master, first, second, summed, down, proj, vec):
    slots, part_rows = master.shape[1:3]
    each = slots // 2
    block = pl.BlockSpec((1, each, part_rows, D), lambda s, *_: (0, s, 0, 0))
    fast = len(summed) > 1
    return call(
        functools.partial(adam_kernel, part_rows, fast, each),
        (sds(master.shape, f32),) * 3,
        (kind, row, me, master, first, second, down, proj, vec, *summed),
        [
            block,
            block,
            block,
            pl.BlockSpec((each,) + down.shape[1:], lambda s, *_: (s, 0, 0)),
            whole(proj.shape),
            whole(vec.shape),
        ]
        + [pl.BlockSpec((each,) + a.shape[1:], lambda s, *_: (s, 0, 0)) for a in summed],
        [block] * 3,
        grid=(slots // each,),
        scratch=[pltpu.VMEM((part_rows, D), f32), pltpu.VMEM((D // 128, part_rows, 128), f32)],
        flops=20 * slots * part_rows * D,
        in_hbm=(3, 4, 5, 6, 7),
        prefetch=3,
    )


def rank_grad_kernel(images, kind_ref, row_ref, *refs):
    dz_ref, pooled_ref, down_ref, proj_ref = refs[-4:]
    held = jnp.concatenate([ref[...].reshape(64, PACK) for ref in refs[:-4]], axis=0)
    row = lax.broadcasted_iota(jnp.int32, (D, 128), 0)
    col = lax.broadcasted_iota(jnp.int32, (D, 128), 1)
    wanted = jnp.full((D, 128), -1, jnp.int32)
    for s in range(8):
        first = jnp.where(kind_ref[s] == DOWN, row_ref[s], -D)
        wanted = jnp.where(col // 16 == s, first + col % 16, wanted)
    mine = nn(held[:, 0:D], jnp.where(row == wanted, 1.0, 0.0).astype(bf16)).astype(bf16)
    shape = (512, 512)
    row = lax.broadcasted_iota(jnp.int32, shape, 0)
    col = lax.broadcasted_iota(jnp.int32, shape, 1)
    first = 0
    for segment in range(3):
        here = (row - col == segment * images) & (row // 16 == col // 16) & (col % 16 < images)
        rank = nn(jnp.where(here, 1.0, 0.0).astype(bf16), mine).astype(bf16)
        part = held[:, D:PACK] if segment == 0 else held
        down_ref[:, first : first + part.shape[1]] = tn(rank, part)
        first += part.shape[1]
    proj_ref[...] = tn(dz_ref[...], pooled_ref[...])


def rank_grads(images, kind, row, arrays, dz, pooled):
    return call(
        functools.partial(rank_grad_kernel, images),
        (sds((128, FF), f32), sds((EMB, D), f32)),
        (kind, row, *arrays, dz, pooled),
        [whole(a.shape) for a in arrays] + [whole(dz.shape), whole(pooled.shape)],
        [whole((128, FF)), whole((EMB, D))],
        out_hbm=(0, 1),
        flops=256 * D * FF,
        prefetch=2,
    )


def slot_place(owner_list, slot_count):
    tile_count = owner_list.shape[0]
    earlier = jnp.tril(jnp.ones((tile_count, tile_count), jnp.int32), -1)
    same_owner = (owner_list[:, None] == owner_list[None, :]).astype(jnp.int32)
    return owner_list * slot_count + jnp.sum(same_owner * earlier, axis=1)


def gather_weights(master, placed):
    n_dp, n_rep = lax.axis_size("dp"), lax.axis_size("rep")
    slots, part_rows = master.shape[1:3]
    gathered = lax.all_gather(master.astype(bf16), AXES, axis=0, tiled=True)
    gathered = gathered.reshape(n_dp, n_rep * slots, part_rows, D)
    return jnp.transpose(jnp.take(gathered, placed, axis=1), (1, 0, 2, 3)).reshape(-1, D)


def scatter_grads(tiles, tile_of_slot, slots, part_rows):
    n_dp, n_rep = lax.axis_size("dp"), lax.axis_size("rep")
    count = tiles.shape[0]
    tiles = jnp.concatenate([tiles, jnp.zeros((1, TR, D), tiles.dtype)], axis=0)
    index = jnp.where(tile_of_slot < count, tile_of_slot, count)
    buffer = jnp.take(tiles, index, axis=0).reshape(n_rep * slots, n_dp, part_rows, D)
    buffer = jnp.transpose(buffer, (1, 0, 2, 3)).reshape(n_dp * n_rep, slots, part_rows, D)
    return lax.psum_scatter(buffer, AXES, scatter_dimension=0, tiled=True)[0]


def pairs(move):
    def number(x, z, y, c):
        return x * 16 + z * 4 + y * 2 + c

    return [(number(x, z, y, c), number(*move(x, z, y, c))) for x, z, y in PIECES for c in range(2)]


SWAP_CORE = pairs(lambda x, z, y, c: (x, z, y, 1 - c))
SWAP_X = pairs(lambda x, z, y, c: (1 - x, z, y, c))
SWAP_Y = pairs(lambda x, z, y, c: (x, z, 1 - y, c))
SWAP_Z = pairs(lambda x, z, y, c: (x, z ^ 1, y, c))
SWAP_ZZ = pairs(lambda x, z, y, c: (x, z ^ 2, y, c))
SWAP_XY = pairs(lambda x, z, y, c: (1 - x, z, 1 - y, c))
ACROSS_Z = [pairs(lambda x, z, y, c, k=k: (x, z ^ k, y, c)) for k in (1, 2, 3)]
CROSS_ONE = pairs(lambda x, z, y, c: (1 - x, z, y, c) if c == 0 else (x, z, 1 - y, c))
CROSS_TWO = pairs(lambda x, z, y, c: (x, z, 1 - y, c) if c == 0 else (1 - x, z, y, c))


def send(value, permutation):
    return lax.ppermute(value, AXES, permutation)


def add_kernel(count, pieces, outputs, _, *refs):
    for p in range(pieces):
        total = refs[p * count][0].astype(f32)
        for k in range(1, count):
            total += refs[p * count + k][0].astype(f32)
        outs = refs[pieces * count :]
        if outputs == 1:
            outs[0][p] = total.astype(outs[0].dtype)
        else:
            outs[p][...] = total.astype(outs[p].dtype)


def add_pieces(sources, me, pieces, steps=1, dtypes=(bf16,), near=()):
    rows = sources[0][0].shape[1]
    each = pieces // steps
    arrays, specs = [], []
    for p in range(each):
        for array, at in sources:
            arrays.append(array)
            specs.append(pl.BlockSpec((1, rows, 384), lambda i, me, p=p, at=at: (at(i * each + p, me), 0, 0)))
    if len(dtypes) == 1:
        shapes = (sds((pieces, rows, 384), dtypes[0]),)
        outs = [pl.BlockSpec((each, rows, 384), lambda i, me: (i, 0, 0))]
    else:
        shapes = tuple(sds((rows, 384), dtype) for dtype in dtypes)
        outs = [whole((rows, 384))] * pieces
    in_hbm = [k + 1 for k in range(len(arrays)) if k % len(sources) not in near]
    results = call(
        functools.partial(add_kernel, len(sources), each, len(dtypes)),
        shapes,
        (me, *arrays),
        specs,
        outs,
        grid=(steps,),
        flops=pieces * rows * D,
        in_hbm=in_hbm,
        prefetch=1,
    )
    return results[0] if len(dtypes) == 1 else results


class PieceSum:
    def __init__(self, other, me):
        self.me = me
        self.one = send(other, SWAP_CORE)

    def first_send(self, i, me):
        return jnp.where(me[CORE] == 0, (1 - me[X]) * 8 + i, i * 2 + 1 - me[Y])

    def kept(self, i, me):
        return jnp.where(me[CORE] == 0, me[X] * 8 + i, i * 2 + me[Y])

    def second_send(self, i, me):
        return jnp.where(me[CORE] == 0, 2 * i + 1 - me[Y], (1 - me[X]) * 4 + i)

    def second_keep(self, i, me):
        return jnp.where(me[CORE] == 0, 2 * i + me[Y], me[X] * 4 + i)

    def cross_one(self):
        parts = [(self.mine, self.first_send), (self.one, self.first_send)]
        self.two = send(add_pieces(parts, self.me, 8, 2, near=(1,)), CROSS_ONE)

    def cross_two(self):
        def own(i, me):
            return self.kept(self.second_send(i, me), me)

        parts = [(self.mine, own), (self.one, own), (self.two, self.second_send)]
        self.three = send(add_pieces(parts, self.me, 4, near=(2,)), CROSS_TWO)

    def partial(self):
        def crossed(i, me):
            return self.second_keep(me[Z] ^ i, me)

        def own(i, me):
            return self.kept(crossed(i, me), me)

        parts = [(self.mine, own), (self.one, own), (self.two, crossed)]
        self.sums = add_pieces(parts, self.me, 4, dtypes=(f32,))

    def cross_z(self):
        parts = [(self.sums, lambda i, me: i), (self.three, lambda i, me: me[Z] ^ i)]
        self.own, *parts = add_pieces(parts, self.me, 4, dtypes=(f32, bf16, bf16, bf16), near=(0, 1))
        self.last = [send(part, move) for part, move in zip(parts, ACROSS_Z, strict=True)]

    def total(self):
        parts = [(part[None], lambda i, me: 0) for part in (self.own, *self.last)]
        return add_pieces(parts, self.me, 1, near=(0, 1, 2, 3))[0]


def place_kernel(index_ref, *refs):
    for k in range(64):
        at = index_ref[k]
        out_ref = refs[4 + k // 8]
        for q in range(4):

            @pl.when((at >= 12 * q) & (at < 12 * q + 12))
            def _():
                out_ref[k % 8] = refs[q][pl.ds(pl.multiple_of((at - 12 * q) * 16, 16), 16), :]

        @pl.when(at >= 48)
        def _():
            out_ref[k % 8] = jnp.zeros((16, 384), bf16)


def return_to_owners(sums, place):
    placed = call(
        place_kernel,
        (sds((8, 16, 384), bf16),) * 8,
        (place, *sums),
        [whole((192, 384))] * 4,
        [whole((8, 16, 384))] * 8,
        prefetch=1,
    )
    return exchange(placed)


def plan_kernel(owner_ref, me_ref, pick_ref, place_ref, kind_ref, row_ref, counts, placed, tile_of):
    x, c = me_ref[X], me_ref[CORE]
    rep = me_ref[Z] * 4 + me_ref[Y] * 2 + c

    @pl.loop(0, 16)
    def _(r):
        counts[r] = 0

    @pl.loop(0, 128)
    def _(k):
        tile_of[k] = 1 << 20

    @pl.loop(0, VEC_TILE + 1)
    def _(t):
        owner = owner_ref[t]
        at = owner * 8 + counts[owner]
        counts[owner] = counts[owner] + 1
        placed[t] = at
        tile_of[at] = t

    def slab(t):
        at = placed[t]
        owner = at // 8
        chip = (owner // 4 ^ me_ref[Z]) * 2 + (owner // 2 % 2 ^ me_ref[Y])
        return jnp.where(owner % 2 == c, 0, 64) + chip * 8 + at % 8

    def fill(first, count, tile):
        @pl.loop(0, count)
        def _(k):
            pick_ref[first + k] = slab(tile + k)

    base = 0
    for tiles, tile in CHUNK_TILES:
        fill(base, tiles, tile + tiles * c)
        base += tiles
    pick_ref[base] = slab(VEC_TILE)

    @pl.loop(0, 64)
    def _(k):
        chip = k // 8
        owner = (chip // 2 ^ me_ref[Z]) * 4 + (chip % 2 ^ me_ref[Y]) * 2 + c
        t = tile_of[owner * 8 + k % 8]
        u = t - QKV_TILES
        v = u - OUT_TILES
        half = jnp.where(t < QKV_TILES, t // 9, jnp.where(u < OUT_TILES, u // 3, v // 12))
        place = jnp.where(t < QKV_TILES, t % 9, jnp.where(u < OUT_TILES, 9 + u % 3, 12 + v % 12))
        place_ref[k] = jnp.where(t < DOWN_FIRST, jnp.where(half == c, place, 24 + place), 48)

    @pl.loop(0, 8)
    def _(k):
        t = tile_of[rep * 8 + k]
        is_down = (t >= DOWN_FIRST) & (t < PROJ_FIRST)
        is_proj = (t >= PROJ_FIRST) & (t < VEC_TILE)
        kind = jnp.where(t < DOWN_FIRST, SUMMED, jnp.where(is_down, DOWN, jnp.where(is_proj, PROJ, NONE)))
        kind_ref[k] = jnp.where((t == VEC_TILE) & (x == 0), VEC, kind)
        row_ref[k] = jnp.where(
            is_down, ((t - DOWN_FIRST) * TR + x * 64) // 4, jnp.where(is_proj, (t - PROJ_FIRST) * TR + x * 64, 0)
        )


def plan(owner_list, me):
    smem = pl.BlockSpec(memory_space=pltpu.SMEM)
    sizes = (sum(tiles for tiles, _ in CHUNK_TILES) + 1, 64, 8, 8)
    return pl.pallas_call(
        plan_kernel,
        out_shape=tuple(sds((size,), jnp.int32) for size in sizes),
        in_specs=[smem, smem],
        out_specs=(smem,) * 4,
        scratch_shapes=[pltpu.SMEM((16,), jnp.int32), pltpu.SMEM((128,), jnp.int32), pltpu.SMEM((128,), jnp.int32)],
    )(owner_list, me)


def prepare_kernel(owner_ref, me_ref, master_ref, *refs):
    out_refs, (lanes_ref, tile_ref) = refs[:8], refs[8:]
    rep = me_ref[Z] * 4 + me_ref[Y] * 2 + me_ref[CORE]
    for s in range(9):
        tile_ref[s] = 0

    def note(t, held):
        here = owner_ref[t] == rep

        @pl.when(here)
        def _():
            tile_ref[held] = t

        return held + jnp.where(here, 1, 0)

    lax.fori_loop(DOWN_FIRST, PROJ_FIRST, note, lax.fori_loop(0, DOWN_FIRST, note, 0))
    for s in range(8):
        down = (tile_ref[s] >= DOWN_FIRST) & (tile_ref[s] < PROJ_FIRST)

        @pl.when(jnp.logical_not(down))
        def _():
            for k, (dz, dy) in enumerate(CHIPS):
                rows = pl.ds(pl.multiple_of((me_ref[Z] ^ dz) * 16, 16), 16)
                cols = pl.ds(pl.multiple_of((me_ref[Y] ^ dy) * 384, 128), 384)
                out_refs[k][s] = master_ref[0, s, rows, cols].astype(bf16)

        @pl.when(down)
        def _():
            for k in range(6):
                lanes_ref[k] = master_ref[0, s, :, 128 * k : 128 * k + 128]
            for k, (dz, dy) in enumerate(CHIPS):
                for q in range(3):
                    part = lanes_ref[(me_ref[Y] ^ dy) * 3 + q, pl.ds(me_ref[Z] ^ dz, 16, stride=4), :]
                    out_refs[k][s, :, 128 * q : 128 * q + 128] = part.astype(bf16)


def pick_kernel(index_ref, mine_ref, theirs_ref, text_ref, one_ref, two_ref, three_ref):
    def slab(k, ref, j):
        at = index_ref[k]

        @pl.when(at < 64)
        def _():
            ref[j] = mine_ref[at]

        @pl.when(at >= 64)
        def _():
            ref[j] = theirs_ref[at - 64]

    k = 0
    for (tiles, _), (chunk, first) in zip(CHUNK_TILES, CHUNK_AT, strict=True):
        for j in range(tiles):
            slab(k, (one_ref, two_ref, three_ref)[chunk], first + j)
            k += 1
    slab(k, one_ref, 9)
    text = text_ref[...].astype(f32)
    count = text.shape[0]
    text = (text * lax.rsqrt(jnp.sum(text * text, axis=-1, keepdims=True) + unit_eps)).astype(bf16)
    three_ref[14] = jnp.zeros((16, 384), bf16)
    three_ref[14, 0:count, :] = text[:, 0:384]
    three_ref[14, 8 : 8 + count, 0:128] = text[:, 384:512]


class Spread:
    def __init__(self, block=None):
        if block is not None:
            self.parts = [block] + [send(block, move) for move in ACROSS_Z]

    def cross_one(self, ring=None):
        self.ring = jnp.stack(self.parts) if ring is None else ring
        self.one = send(self.ring, CROSS_ONE)
        self.two = None
        self.near = []

    def cross_two(self):
        if self.two is None:
            self.two = send(self.ring, CROSS_TWO)
        self.both = send(self.one, CROSS_TWO)

    def send_near(self, *which):
        for k in which:
            self.near.append(send(getattr(self, ("ring", "one", "two", "both")[k]), SWAP_CORE))

    def finish(self):
        self.send_near(*range(len(self.near), 4))

    def arrays(self):
        return (self.ring, self.one, self.two, self.both, *self.near)


def meet(*values):
    return lax.optimization_barrier(values)


def sources(me):
    for other in range(2):
        c = me[CORE] if other == 0 else 1 - me[CORE]
        for crossed in range(4):
            one, two = crossed % 2, crossed // 2
            flip_x = jnp.where(c == 0, one, two)
            flip_y = jnp.where(c == 0, two, one)
            yield c, me[X] + flip_x - 2 * me[X] * flip_x, me[Y] + flip_y - 2 * me[Y] * flip_y


def exchange(blocks):
    return [blocks[0]] + [
        send(blocks[k], pairs(lambda x, z, y, c, k=k: (x, z ^ CHIPS[k][0], y ^ CHIPS[k][1], c))) for k in range(1, 8)
    ]


def pick_slabs(master, text_emb, owner_list, me, *others):
    prepared = call(
        prepare_kernel,
        (sds((8, 16, 384), bf16),) * 8,
        (owner_list, me, master),
        [whole(master.shape)],
        [whole((8, 16, 384))] * 8,
        scratch=[pltpu.VMEM((6, 64, 128), f32), pltpu.SMEM((16,), jnp.int32)],
        in_hbm=(2,),
        prefetch=2,
    )
    pick, place, kind, row = plan(owner_list, me)
    *mine, pick = meet(*exchange(prepared), pick)
    mine = jnp.concatenate(mine)
    mine, *others = meet(mine, *others)
    blocks = call(
        pick_kernel,
        tuple(sds((slabs, 16, 384), bf16) for slabs in SLABS),
        (pick, mine, send(mine, SWAP_CORE), text_emb),
        [whole((64, 16, 384)), whole((64, 16, 384)), whole(text_emb.shape)],
        [whole((slabs, 16, 384)) for slabs in SLABS],
        prefetch=1,
    )
    return blocks, (place, kind, row), others


def shards(block_in, tissue, text_emb, text_order, owner_list, master, first_moment, second_moment):
    n_dp = lax.axis_size("dp")
    n_rep = lax.axis_size("rep")
    images = block_in.shape[0]
    slots, part_rows = master.shape[1:3]
    image_total = text_order.shape[0]
    n = images * ROWS
    dp_at, rep_at = lax.axis_index("dp"), lax.axis_index("rep")
    first_image = lax.axis_index(AXES) * images

    x = jnp.pad(block_in, ((0, 0), (0, ROWS - PATCHES), (0, 0))).reshape(n, D)
    valid = jnp.pad((tissue > 0).astype(f32), ((0, 0), (0, ROWS - PATCHES)))
    mask_row = valid[:, None, :]
    col = jnp.broadcast_to(valid.reshape(n, 1), (n, 128))
    numbers = jnp.arange(images, dtype=jnp.int32)
    sel = jnp.where(
        numbers[:, None, None] == jnp.arange(16, dtype=jnp.int32)[None, :, None], valid[:, None, :], 0.0
    ).astype(bf16)
    inv_count = jnp.pad(1.0 / jnp.sum(valid, axis=1), (0, 16 - images))
    inv_count = jnp.broadcast_to(inv_count[:, None], (16, 128))
    order = jnp.broadcast_to(text_order[:, None], (image_total, 128))
    first_image = first_image.astype(jnp.int32)[None]

    fast = (n_dp, n_rep, slots, part_rows) == (2, 16, 8, 64)
    if fast:
        me = jnp.stack([dp_at, rep_at // 4, rep_at // 2 % 2, rep_at % 2]).astype(jnp.int32)
        (block_one, block_two, block_three), (place, kind, row), others = pick_slabs(
            master, text_emb, owner_list, me, x, mask_row, col, sel, inv_count, order, first_image
        )
        x, mask_row, col, sel, inv_count, order, first_image = others
        one = Spread(block_one)
        *one.parts, block_two = meet(*one.parts, block_two)
        one.cross_one()
        one.two = send(one.ring, CROSS_TWO)
        two = Spread(block_two)
        one.ring, one.one, one.two = meet(one.ring, one.one, one.two)
        one.cross_two()
        one.ring, one.one, one.two, *two.parts = meet(one.ring, one.one, one.two, *two.parts)
        one.send_near(0, 1, 2)
        one.both, block_three = meet(one.both, block_three)
        one.finish()
        two.cross_one()
        two.two = send(two.ring, CROSS_TWO)
        three = Spread(block_three)
        w_qkv = Weight(one.arrays(), QKV_TILES)
        a, qkv, vec = qkv_forward(images, x, jnp.zeros((16, D), f32), w_qkv, me)
        qkv, two.ring, two.one, two.two, *three.parts = meet(qkv, two.ring, two.one, two.two, *three.parts)
        two.cross_two()
        two.send_near(0, 1, 2)
        o, lse = attention_forward(images, qkv, mask_row)
        o, two.both, *two.near = meet(o, two.both, *two.near)
        two.finish()
        three.cross_one()
        w_out = Weight(two.arrays(), OUT_TILES)
        h, m = middle_forward(images, x, o, vec, w_out, me)
        h, m, three.ring, three.one = meet(h, m, three.ring, three.one)
        three.cross_two()
        three.send_near(0, 1)
        bias_up = vec[7 : 7 + FF // D].reshape(FF // D, 1, D)
        w_up = Weight(two.arrays(), UP_TILES, 3)
        act, slope = up_forward(images, m, w_up, bias_up, me)
        act, three.two, three.both, *three.near = meet(act, three.two, three.both, *three.near)
        three.finish()
        w_down = Weight(three.arrays(), DOWN_TILES, quarters=True)
        w_proj = Weight(three.arrays(), PROJ_TILES, 12)
        all_text = jnp.zeros((16, 128), bf16)
    else:
        me = jnp.zeros((4,), jnp.int32)
        placed = slot_place(owner_list, slots)
        hits = placed[None, :] == jnp.arange(n_rep * slots, dtype=jnp.int32)[:, None]
        tile_ids = jnp.arange(owner_list.shape[0], dtype=jnp.int32)[None, :]
        tile_of_slot = jnp.where(jnp.any(hits, axis=1), jnp.sum(jnp.where(hits, tile_ids, 0), axis=1), 1 << 20)
        text = text_emb.astype(f32)
        own_text = (text * lax.rsqrt(jnp.sum(text * text, axis=-1, keepdims=True) + unit_eps)).astype(bf16)
        all_text = lax.all_gather(own_text, AXES, axis=0, tiled=True)
        tiles = gather_weights(master, placed).reshape(-1, TR, D)
        w_qkv = Weight([tiles[:QKV_TILES]], QKV_TILES)
        w_out = Weight([tiles[QKV_TILES : QKV_TILES + OUT_TILES]], OUT_TILES)
        w_up = Weight([tiles[QKV_TILES + OUT_TILES : DOWN_FIRST]], UP_TILES)
        w_down = Weight([tiles[DOWN_FIRST:PROJ_FIRST].reshape(DOWN_TILES, TR // 4, FF)], DOWN_TILES, quarters=True)
        w_proj = Weight([tiles[PROJ_FIRST:VEC_TILE]], PROJ_TILES)
        a, qkv, vec = qkv_forward(images, x, tiles[VEC_TILE, :16].astype(f32), w_qkv, me)
        bias_up = vec[7 : 7 + FF // D].reshape(FF // D, 1, D)
        o, lse = attention_forward(images, qkv, mask_row)
        h, m = middle_forward(images, x, o, vec, w_out, me)
        act, slope = up_forward(images, m, w_up, bias_up, me)
    block_out, pooled = down_forward(images, act, w_down, h, vec, sel, inv_count, me)

    pooled_all = lax.all_to_all(jnp.broadcast_to(pooled[None, :images], (n_dp * n_rep, images, D)), AXES, 0, 0)
    act_sum = act_sums(images, act, sel)
    probabilities = attention_again(images, qkv, lse, col)
    if fast:
        pooled_all, act_sum, probabilities = meet(pooled_all, act_sum, probabilities)
    dz_all, rank, spread, hidden, pooled_all = loss_backward(
        me, first_image, pooled_all, all_text, order, w_proj, w_down, inv_count
    )

    both = jnp.concatenate([rank[:images], act_sum[:images]], axis=1)
    if fast:
        packed = jnp.concatenate([both[:, at * PACK : (at + 1) * PACK] for at in range(3)], axis=0)
        ranks = Spread()
        packed = jnp.pad(packed, ((0, 16 - 3 * images), (0, 0)))
        beside = send(packed, SWAP_Z)
        dm, g_bias_up, other, mine = up_backward(images, slope, m, w_up, hidden, col, me)
        dm, other, mine, packed, beside = meet(dm, other, mine, packed, beside)
        up_sum = PieceSum(other, me)
        pair = jnp.stack([packed, beside])
        far = send(pair, SWAP_ZZ)
        dh, do, g_out, g_two = middle_backward(images, h, dm, col, spread, o, w_out, vec, me)
        dh, do, up_sum.mine, up_sum.one, pair, far = meet(dh, do, mine, up_sum.one, pair, far)
        up_sum.cross_one()
        dqkv, g_bias = attention_backward(images, qkv, do, probabilities)
        dqkv, up_sum.two, pair, far = meet(dqkv, up_sum.two, pair, far)
        up_sum.cross_two()
        ranks.cross_one(jnp.concatenate([pair, far]))
        ranks.two = send(ranks.ring, CROSS_TWO)
        other = qkv_weight_grad_fast(images, dqkv, a, g_out, me, True)
        other, dqkv = meet(other, dqkv)
        qkv_sum = PieceSum(other, me)
        mine = qkv_weight_grad_fast(images, dqkv, a, g_out, me, False)
        up_sum.partial()
        dqkv, up_sum.sums, up_sum.three, qkv_sum.mine, qkv_sum.one, ranks.ring, ranks.one, ranks.two = meet(
            dqkv, up_sum.sums, up_sum.three, mine, qkv_sum.one, ranks.ring, ranks.one, ranks.two
        )
        qkv_sum.cross_one()
        up_sum.cross_z()
        ranks.cross_two()
        input_grad, vec_sum = input_backward(images, x, dqkv, w_qkv, dh, vec, g_two, g_bias, g_bias_up, me)
        vec_sum, qkv_sum.two, ranks.ring, ranks.one, ranks.two, ranks.both, *up_sum.last = meet(
            vec_sum, qkv_sum.two, ranks.ring, ranks.one, ranks.two, ranks.both, *up_sum.last
        )
        qkv_sum.cross_two()
        near_vec = send(vec_sum, SWAP_CORE)
        ranks.send_near(0, 1)
        up_total = up_sum.total()
        vec_sum, near_vec, up_total = meet(vec_sum, near_vec, up_total)
        vec_sum += near_vec
        vec_sum += send(vec_sum, SWAP_ZZ)
        qkv_sum.partial()
        vec_sum, qkv_sum.sums, qkv_sum.three, up_total, ranks.two, ranks.both, *ranks.near = meet(
            vec_sum, qkv_sum.sums, qkv_sum.three, up_total, ranks.two, ranks.both, *ranks.near
        )
        qkv_sum.cross_z()
        near_up = send(up_total, SWAP_CORE)
        vec_sum += send(vec_sum, SWAP_Y)
        vec_sum += send(vec_sum, SWAP_Z)
        near_up, vec_sum, ranks.two, ranks.both, *qkv_sum.last = meet(
            near_up, vec_sum, ranks.two, ranks.both, *qkv_sum.last
        )
        qkv_total = qkv_sum.total()
        near_qkv = send(qkv_total, SWAP_CORE)
        ranks.finish()
        across = send(vec_sum, SWAP_X)
        near_qkv, across, *ranks.near = meet(near_qkv, across, *ranks.near)
        vec_total = vec_sum + across
        summed = return_to_owners((qkv_total, up_total, near_qkv, near_up), place)
        g_down, g_proj = rank_grads(images, kind, row, ranks.arrays(), dz_all, pooled_all)
        g_down, g_proj, vec_total, *summed = meet(g_down.reshape(8, 16, FF), g_proj, vec_total, *summed)
    else:
        both_all = lax.all_gather(both, AXES, axis=0, tiled=True)
        dm, g_bias_up, g_up = up_backward(images, slope, m, w_up, hidden, col, me)
        dh, do, g_out, g_two = middle_backward(images, h, dm, col, spread, o, w_out, vec, me)
        dqkv, g_bias = attention_backward(images, qkv, do, probabilities)
        g_qkv = qkv_weight_grad(images, dqkv, a)
        input_grad, vec_total = input_backward(images, x, dqkv, w_qkv, dh, vec, g_two, g_bias, g_bias_up, me)
        mine = lax.dynamic_slice_in_dim(tile_of_slot, rep_at * slots, slots)
        first_row = dp_at * part_rows
        is_down = (mine >= DOWN_FIRST) & (mine < PROJ_FIRST)
        is_proj = (mine >= PROJ_FIRST) & (mine < VEC_TILE)
        kind = jnp.where(is_down, DOWN, jnp.where(is_proj, PROJ, jnp.where(mine <= VEC_TILE, SUMMED, NONE)))
        kind = kind.astype(jnp.int32)
        each = part_rows * D // FF
        row = jnp.where(is_proj, (mine - PROJ_FIRST) * TR + first_row, 0)
        down_rows = jnp.clip(((mine - DOWN_FIRST) * TR + first_row) * D // FF, 0, D - each)
        g_down = tn(both_all[:, :D], both_all[:, D:])
        g_down = jnp.stack([lax.dynamic_slice_in_dim(g_down, at, each) for at in down_rows])
        g_down = jnp.pad(g_down, ((0, 0), (0, max(0, 8 - each)), (0, 0)))
        g_proj = tn(dz_all, pooled_all)
        last = jnp.pad(vec_total, ((0, TR - 16), (0, 0))).astype(bf16)
        tiles = jnp.concatenate([g_qkv, g_out, g_up, last], axis=0).reshape(-1, TR, D)
        index = jnp.where(tile_of_slot == VEC_TILE, DOWN_FIRST, jnp.where(tile_of_slot < DOWN_FIRST, tile_of_slot, 1 << 20))
        summed = [scatter_grads(tiles, index, slots, part_rows)]
    new_master, new_first, new_second = adam(
        kind, row, me, master, first_moment, second_moment, summed, g_down, g_proj, vec_total
    )
    return block_out, input_grad, new_master, new_first, new_second


def solution(mesh):
    in_specs = (
        P(("dp", "rep"), None, None),
        P(("dp", "rep"), None),
        P(("dp", "rep"), None),
        P(),
        P(),
        P("rep", None, "dp", None),
        P("rep", None, "dp", None),
        P("rep", None, "dp", None),
    )
    out_specs = (
        P(("dp", "rep"), None, None),
        P(("dp", "rep"), None, None),
        P("rep", None, "dp", None),
        P("rep", None, "dp", None),
        P("rep", None, "dp", None),
    )
    return jax.shard_map(shards, mesh=mesh, in_specs=in_specs, out_specs=out_specs, check_vma=False)
```

```python
import functools

import jax
import jax.numpy as jnp
from jax import lax
from jax.experimental import pallas as pl
from jax.experimental.pallas import tpu as pltpu
from jax.sharding import PartitionSpec as P

D = 768
HEADS = 12
HEAD = 64
FF = 3072
EMB = 512
PATCHES = 196
STEP = 10
ROWS = 208
TR = 128

logit_scale = 50.0
learn_rate = 0.03
beta_one = 0.9
beta_two = 0.999
adam_eps = 1e-08
decay_rate = 0.05
norm_eps = 1e-05
unit_eps = 1e-06
masked_score = -1000000000.0

bf16 = jnp.bfloat16
f32 = jnp.float32
AXES = ("dp", "rep")
MIB = 1 << 20

X, Z, Y, CORE = range(4)
PIECES = [(x, z, y) for x in range(2) for z in range(4) for y in range(2)]

QKV_TILES = 3 * D // TR
OUT_TILES = D // TR
UP_TILES = FF // TR
DOWN_TILES = FF // TR
PROJ_TILES = EMB // TR
DOWN_FIRST = QKV_TILES + OUT_TILES + UP_TILES
PROJ_FIRST = DOWN_FIRST + DOWN_TILES
VEC_TILE = PROJ_FIRST + PROJ_TILES
PACK = (D + FF) // 3
CHUNK_TILES = (
    (QKV_TILES // 2, 0),
    (OUT_TILES // 2, QKV_TILES),
    (UP_TILES // 2, QKV_TILES + OUT_TILES),
    (DOWN_TILES // 2, DOWN_FIRST),
    (PROJ_TILES // 2, PROJ_FIRST),
)
CHUNK_AT = ((0, 0), (1, 0), (1, 3), (2, 0), (2, 12))
SLABS = (10, 15, 15)
CHIPS = [(dz, dy) for dz in range(4) for dy in range(2)]


def nn(a, b):
    return lax.dot_general(a, b, (((1,), (0,)), ((), ())), preferred_element_type=f32)


def nt(a, b):
    return lax.dot_general(a, b, (((1,), (1,)), ((), ())), preferred_element_type=f32)


def tn(a, b):
    return lax.dot_general(a, b, (((0,), (0,)), ((), ())), preferred_element_type=f32)


def call(kernel, outs, ins, in_specs, out_specs, grid=None, scratch=(), flops=0, vmem=24, prefetch=0, in_hbm=(), out_hbm=(), vmem_in=(), vmem_out=()):
    ins = [
        pltpu.with_memory_space_constraint(a, pltpu.HBM) if k >= prefetch and (s.memory_space is pltpu.HBM or k in in_hbm) else a
        for k, (a, s) in enumerate(zip(ins, [None] * prefetch + list(in_specs), strict=True))
    ]
    ins = [pltpu.with_memory_space_constraint(a, pltpu.VMEM) if k in vmem_in else a for k, a in enumerate(ins)]
    moved = sum(a.size * a.dtype.itemsize for a in ins) + sum(o.size * o.dtype.itemsize for o in outs)
    spaces = {k: pltpu.HBM for k in out_hbm} | {k: pltpu.VMEM for k in vmem_out}
    outs = [spaces[k](o.shape, o.dtype) if k in spaces else o for k, o in enumerate(outs)]
    params = pltpu.CompilerParams(
        vmem_limit_bytes=vmem * MIB,
        dimension_semantics=("arbitrary",) * len(grid or ()) or None,
    )
    return pl.pallas_call(
        kernel,
        out_shape=tuple(outs),
        grid_spec=pltpu.PrefetchScalarGridSpec(
            num_scalar_prefetch=prefetch,
            grid=grid or (1,),
            in_specs=in_specs,
            out_specs=tuple(out_specs),
            scratch_shapes=list(scratch),
        ),
        compiler_params=params,
        cost_estimate=pl.CostEstimate(flops=1, bytes_accessed=1, transcendentals=0),
    )(*ins)


def whole(shape):
    return pl.BlockSpec(shape, lambda *_: (0,) * len(shape))


def rows_at(rows, cols):
    return pl.BlockSpec((rows, cols), lambda i, *_: (i, 0))


def cols_at(rows, cols):
    return pl.BlockSpec((rows, cols), lambda i, *_: (0, i))


def sds(shape, dtype):
    return jax.ShapeDtypeStruct(shape, dtype)


class Weight:
    def __init__(self, arrays, tiles, first=0, quarters=False):
        self.arrays, self.tiles, self.first, self.quarters = tuple(arrays), tiles, first, quarters
        self.pieces = len(arrays) > 1
        self.specs = [pl.BlockSpec(memory_space=pltpu.HBM)] * len(arrays)
        shape = (tiles, TR // 4, FF) if quarters else (tiles, TR, D)
        self.scratch = [pltpu.VMEM(shape, bf16), pltpu.SemaphoreType.DMA((32 if self.pieces else 1,))]

    def copies(self, me, refs, out, sems):
        if not self.pieces:
            return [lambda: pltpu.make_async_copy(refs[0], out, sems.at[0])]
        copies = []
        half = self.tiles // 2
        for at, (c, x, y) in enumerate(sources(me)):
            for back in range(4):
                z = me[Z] ^ back
                if self.quarters:
                    row, col = x * 16, z * D + y * 384
                else:
                    row, col = x * 64 + z * 16, y * 384
                rows = pl.ds(pl.multiple_of(row, 16), 16)
                cols = pl.ds(pl.multiple_of(col, 128), 384)
                source = refs[at].at[back, pl.ds(self.first, half)]
                place = out.at[pl.ds(half * c, half), rows, cols]
                copies.append(functools.partial(pltpu.make_async_copy, source, place, sems.at[len(copies)]))
        return copies

    def start(self, me, refs, out, sems):
        for copy in self.copies(me, refs, out, sems):
            copy().start()

    def wait(self, me, refs, out, sems, part=None, parts=1):
        copies = self.copies(me, refs, out, sems)
        if part is not None and not self.pieces:
            copies = copies if part == 0 else []
        elif part is not None:
            copies = copies[16 * part : 16 * part + 16] if parts == 2 else copies[part::4]
        for copy in copies:
            copy().wait()

    def load(self, me, refs, out, sems):
        @pl.when(pl.program_id(0) == 0)
        def _():
            self.start(me, refs, out, sems)
            self.wait(me, refs, out, sems)


def normalized(x):
    center = x - jnp.mean(x, axis=-1, keepdims=True)
    spread = jnp.mean(center * center, axis=-1, keepdims=True)
    inverse = lax.rsqrt(spread + norm_eps)
    return center * inverse, inverse


def norm_back(grad, hat, inverse, gain):
    scaled = grad * gain
    first = jnp.mean(scaled, axis=-1, keepdims=True)
    second = jnp.mean(scaled * hat, axis=-1, keepdims=True)
    return inverse * (scaled - first - hat * second)


def accumulate(i, ref, value):
    @pl.when(i == 0)
    def _():
        ref[...] = value

    @pl.when(i > 0)
    def _():
        ref[...] += value


def column_sum(x):
    return jnp.sum(x, axis=0, keepdims=True)


def third(j, me):
    return jnp.where(me[CORE] == 0, j, 2 - j)


def qkv_kernel(images, weight, me_ref, *refs):
    count = len(weight.arrays)
    pieces = refs[:count]
    x_ref, vec_in_ref, a_ref, qkv_ref, vec_ref, w_ref, sems, vec_half, vec_sems = refs[count:]
    j = pl.program_id(0)

    @pl.when(j == 0)
    def _():
        weight.start(me_ref, pieces, w_ref, sems)
        if weight.pieces:
            parts = []
            for at, (_, x, y) in list(enumerate(sources(me_ref)))[:4]:
                for back in range(4):
                    copy = pltpu.make_async_copy(pieces[at].at[back, 9], vec_half.at[y], vec_sems.at[len(parts)])
                    parts.append(((x == 0) & ((me_ref[Z] ^ back) == 0), copy))
            for here, copy in parts:
                pl.when(here)(copy.start)
            for here, copy in parts:
                pl.when(here)(copy.wait)
            vec_ref[...] = jnp.concatenate([vec_half[0], vec_half[1]], axis=1).astype(f32)
        else:
            vec_ref[...] = vec_in_ref[...]
        for i in range(images):
            hat, _ = normalized(x_ref[pl.ds(i * ROWS, ROWS), :].astype(f32))
            a_ref[pl.ds(i * ROWS, ROWS), :] = (hat * vec_ref[0:1, :] + vec_ref[1:2, :]).astype(bf16)
        weight.wait(me_ref, pieces, w_ref, sems, 0, 2)

    @pl.when(j == 1)
    def _():
        weight.wait(me_ref, pieces, w_ref, sems, 1, 2)

    j = third(j, me_ref)
    bias = jnp.where(j == 0, vec_ref[4:5, :], jnp.where(j == 2, vec_ref[5:6, :], 0.0))
    scale = jnp.where(j == 0, f32(HEAD**-0.5), f32(1.0))
    w = w_ref[pl.ds(6 * j, 6)].reshape(D, D)
    qkv_ref[...] = ((nt(a_ref[...], w) + bias) * scale).astype(bf16)


def qkv_forward(images, x, vec, weight, me):
    n = images * ROWS
    return call(
        functools.partial(qkv_kernel, images, weight),
        (sds((n, D), bf16), sds((n, 3 * D), bf16), sds((16, D), f32)),
        (me, *weight.arrays, x, vec),
        weight.specs + [whole((n, D)), whole((16, D))],
        [whole((n, D)), pl.BlockSpec((n, D), lambda j, me: (0, third(j, me))), whole((16, D))],
        grid=(3,),
        out_hbm=(0,),
        scratch=weight.scratch + [pltpu.VMEM((2, 16, 384), bf16), pltpu.SemaphoreType.DMA((16,))],
        flops=2 * n * D * 3 * D,
        prefetch=1,
    )


def attention_kernel(qkv_ref, mask_ref, o_ref, lse_ref):
    lane = lax.broadcasted_iota(jnp.int32, (ROWS, 2 * HEAD), 1)
    low_half = lane < HEAD
    valid = mask_ref[0] > 0.0
    lse_all = jnp.zeros((ROWS, 128), f32)
    for pair in range(HEADS // 2):
        at = pair * 2 * HEAD
        q = qkv_ref[:, at : at + 2 * HEAD]
        k = qkv_ref[:, D + at : D + at + 2 * HEAD]
        v = qkv_ref[:, 2 * D + at : 2 * D + at + 2 * HEAD]
        mixed = []
        for half in range(2):
            keep = low_half if half == 0 else jnp.logical_not(low_half)
            s = nt(q, jnp.where(keep, k, jnp.zeros_like(k)))
            s = jnp.where(valid, s, masked_score)
            top = jnp.max(s, axis=-1, keepdims=True)
            e = jnp.exp(s - top)
            total = jnp.sum(e, axis=-1, keepdims=True)
            p = e * (1.0 / total)
            mixed.append(nn(p.astype(bf16), v))
            lse_all = jnp.where(lane == 2 * pair + half, top + jnp.log(total), lse_all)
        o_ref[:, at : at + 2 * HEAD] = jnp.where(low_half, mixed[0], mixed[1]).astype(bf16)
    lse_ref[0] = jnp.transpose(lse_all)[0:16, :]


def attention_forward(images, qkv, mask_row):
    n = images * ROWS
    return call(
        attention_kernel,
        (sds((n, D), bf16), sds((images, 16, ROWS), f32)),
        (qkv, mask_row),
        [rows_at(ROWS, 3 * D), pl.BlockSpec((1, 1, ROWS), lambda i: (i, 0, 0))],
        [rows_at(ROWS, D), pl.BlockSpec((1, 16, ROWS), lambda i: (i, 0, 0))],
        grid=(images,),
        flops=4 * n * ROWS * D,
    )


def middle_kernel(weight, me_ref, *refs):
    count = len(weight.arrays)
    x_ref, o_ref, vec_ref, h_ref, m_ref, w_ref, sems = refs[count:]
    weight.load(me_ref, refs[:count], w_ref, sems)
    part = nt(o_ref[...], w_ref[...].reshape(D, D)) + vec_ref[6:7, :]
    middle = x_ref[...].astype(f32) + part
    h_ref[...] = middle
    hat, _ = normalized(middle)
    m_ref[...] = (hat * vec_ref[2:3, :] + vec_ref[3:4, :]).astype(bf16)


def middle_forward(images, x, o, vec, weight, me):
    n = images * ROWS
    return call(
        functools.partial(middle_kernel, weight),
        (sds((n, D), f32), sds((n, D), bf16)),
        (me, *weight.arrays, x, o, vec),
        weight.specs + [rows_at(ROWS, D), rows_at(ROWS, D), whole((16, D))],
        [rows_at(ROWS, D), rows_at(ROWS, D)],
        grid=(images,),
        scratch=weight.scratch,
        flops=2 * n * D * D,
        prefetch=1,
    )


def gelu_parts(u):
    phi = 0.5 + 0.5 * lax.erf(u * 0.7071067811865476)
    density = jnp.exp2(u * u * -0.7213475204444817) * 0.3989422804014327
    return u * phi, phi + u * density


def own_block(j, me):
    return (j // 2 + me[CORE]) % 2 * 2 + j % 2


def up_kernel(images, weight, me_ref, *refs):
    count = len(weight.arrays)
    m_ref, bias_ref, act_ref, slope_ref, w_ref, sems = refs[count:]
    j = pl.program_id(0)

    @pl.when(j == 0)
    def _():
        weight.start(me_ref, refs[:count], w_ref, sems)
        weight.wait(me_ref, refs[:count], w_ref, sems, 0, 2)

    @pl.when(j == 2)
    def _():
        weight.wait(me_ref, refs[:count], w_ref, sems, 1, 2)

    w = w_ref[pl.ds(6 * own_block(j, me_ref), 6)].reshape(D, D)
    for i in range(images):
        at = pl.ds(i * ROWS, ROWS)
        act, slope = gelu_parts(nt(m_ref[at, :], w) + bias_ref[0])
        act_ref[at, :] = act.astype(bf16)
        slope_ref[at, :] = slope.astype(bf16)


def up_forward(images, m, weight, bias, me):
    n = images * ROWS
    cols = pl.BlockSpec((n, D), lambda j, me: (0, own_block(j, me)))
    return call(
        functools.partial(up_kernel, images, weight),
        (sds((n, FF), bf16), sds((n, FF), bf16)),
        (me, *weight.arrays, m, bias),
        weight.specs + [whole((n, D)), pl.BlockSpec((1, 1, D), lambda j, me: (own_block(j, me), 0, 0))],
        [cols, cols],
        grid=(FF // D,),
        vmem_out=(0,),
        out_hbm=(1,),
        scratch=weight.scratch,
        flops=2 * n * D * FF,
        prefetch=1,
    )


def act_sum_kernel(images, act_ref, sel_ref, sum_ref):
    total = jnp.zeros(sum_ref.shape, f32)
    for i in range(images):
        total += nn(sel_ref[i], act_ref[pl.ds(i * ROWS, ROWS), :])
    sum_ref[...] = total.astype(bf16)


def act_sums(images, act, sel):
    n = images * ROWS
    return call(
        functools.partial(act_sum_kernel, images),
        (sds((16, FF), bf16),),
        (act, sel),
        [cols_at(n, D), whole((images, 16, ROWS))],
        [cols_at(16, D)],
        grid=(FF // D,),
        flops=32 * n * FF,
    )[0]


def down_kernel(images, weight, me_ref, *refs):
    count = len(weight.arrays)
    act_ref, h_ref, vec_ref, sel_ref, inv_ref, out_ref, pooled_ref, w_ref, sems = refs[count:]
    j = pl.program_id(0)

    @pl.when(j == 0)
    def _():
        weight.start(me_ref, refs[:count], w_ref, sems)
        weight.wait(me_ref, refs[:count], w_ref, sems, 0, 2)

    @pl.when(j == 1)
    def _():
        weight.wait(me_ref, refs[:count], w_ref, sems, 1, 2)

    tiles = DOWN_TILES // 3
    w = w_ref[pl.ds(tiles * third(j, me_ref), tiles)].reshape(D // 3, FF)
    y = nt(act_ref[...], w)
    total = jnp.zeros((16, D // 3), f32)
    for i in range(images):
        rows = slice(i * ROWS, i * ROWS + ROWS)
        out = (h_ref[rows, :] + (y[rows] + vec_ref[11:12, :])).astype(bf16)
        out_ref[i] = out[0:PATCHES, :]
        total += nn(sel_ref[i], out)
    pooled_ref[...] = (total * inv_ref[:, 0:1]).astype(bf16)


def down_forward(images, act, weight, h, vec, sel, inv_count, me):
    n = images * ROWS

    def cols(rows):
        return pl.BlockSpec((rows, D // 3), lambda j, me: (0, third(j, me)))

    return call(
        functools.partial(down_kernel, images, weight),
        (sds((images, PATCHES, D), bf16), sds((16, D), bf16)),
        (me, *weight.arrays, act, h, vec, sel, inv_count),
        weight.specs[:-1]
        + [
            pl.BlockSpec(memory_space=pl.ANY),
            pl.BlockSpec(memory_space=pltpu.VMEM),
            cols(n),
            cols(16),
            whole((images, 16, ROWS)),
            whole((16, 128)),
        ],
        [pl.BlockSpec((images, PATCHES, D // 3), lambda j, me: (0, 0, third(j, me))), cols(16)],
        grid=(3,),
        vmem_in=(1 + len(weight.arrays),),
        scratch=weight.scratch,
        flops=2 * n * D * FF,
        prefetch=1,
    )


def loss_kernel(total_images, proj, down, me_ref, first_ref, *refs):
    count = len(proj.arrays)
    pieces = refs[:count]
    if proj.pieces:
        down_pieces, rest = pieces, refs[count:]
    else:
        down_pieces, rest = refs[count : count + 1], refs[count + 1 :]
    text_ref, pooled_ref, order_ref, inv_ref, dz_ref, rank_ref, spread_ref, hidden_ref, all_ref = rest[:9]
    proj_ref, proj_sems, down_ref, down_sems, rows_ref = rest[9:14]
    down_copies = down.copies(me_ref, down_pieces, down_ref, down_sems)
    proj_copies = proj.copies(me_ref, pieces, proj_ref, proj_sems)
    if proj.pieces:
        slab_ref, slab_sems = rest[14:]
        for at, (c, x, y) in enumerate(sources(me_ref)):
            for back in range(4):
                device = x * 16 + (me_ref[Z] ^ back) * 4 + y * 2 + c
                out = slab_ref.at[pl.ds(pl.multiple_of(device * 16, 16), 16)]
                source = pieces[at].at[back, 14]
                proj_copies.append(
                    functools.partial(pltpu.make_async_copy, source, out, slab_sems.at[at * 4 + back])
                )
    for copy in proj_copies + down_copies:
        copy().start()
    for copy in proj_copies:
        copy().wait()
    if proj.pieces:
        images = total_images // 32
        shape = (total_images, 512)
        row = lax.broadcasted_iota(jnp.int32, shape, 0)
        col = lax.broadcasted_iota(jnp.int32, shape, 1)
        start = row // images * 16 + row % images
        held = slab_ref[...]
        left = nn(jnp.where(col == start, 1.0, 0.0).astype(bf16), held)
        right = nn(jnp.where(col == start + 8, 1.0, 0.0).astype(bf16), held[:, 0:128])
        text = jnp.concatenate([left, right], axis=1).astype(bf16)
    else:
        text = text_ref[...]
    proj_w = proj_ref[...].reshape(EMB, D)
    each = total_images // pooled_ref.shape[0]
    for d in range(pooled_ref.shape[0]):
        rows_ref[d * each : d * each + each, :] = pooled_ref[d].astype(f32)
    pooled = rows_ref[...].astype(bf16)
    all_ref[...] = pooled
    z = nt(pooled, proj_w)
    square = jnp.sum(z * z, axis=-1, keepdims=True) + unit_eps
    inverse = lax.rsqrt(square)
    image = (z * inverse).astype(bf16)
    s = logit_scale * nt(image, text)
    shape = (total_images, total_images)
    hit = jnp.where(order_ref[:, 0:1] == lax.broadcasted_iota(jnp.int32, shape, 1), 1.0, 0.0)
    part = 1.0 / (2.0 * total_images)

    def grad_of(axis):
        top = jnp.max(s, axis=axis, keepdims=True)
        lse = top + jnp.log(jnp.sum(jnp.exp(s - top), axis=axis, keepdims=True))
        return ((jnp.exp(s - lse) - hit) * part).astype(bf16)

    de = logit_scale * (nn(grad_of(1), text) + nn(grad_of(0), text))
    dz = inverse * de - z * (inverse * inverse * inverse * jnp.sum(z * de, axis=-1, keepdims=True))
    dz = dz.astype(bf16)
    dz_ref[...] = dz
    pick = lax.broadcasted_iota(jnp.int32, (16, total_images), 1) == (
        first_ref[0] + lax.broadcasted_iota(jnp.int32, (16, total_images), 0)
    )
    own = nn(jnp.where(pick, 1.0, 0.0).astype(bf16), dz).astype(bf16)
    spread = nn(own, proj_w) * inv_ref[:, 0:1]
    spread_ref[...] = spread
    rank = spread.astype(bf16)
    rank_ref[...] = rank
    for copy in down_copies:
        copy().wait()
    hidden_ref[...] = nn(rank, down_ref[...].reshape(D, FF))


def loss_backward(me, first, pooled, text, order, proj, down, inv_count):
    total = pooled.shape[0] * pooled.shape[1]
    if proj.pieces:
        arrays, extra = proj.arrays, [pltpu.VMEM((512, 384), bf16), pltpu.SemaphoreType.DMA((32,))]
    else:
        arrays, extra = proj.arrays + down.arrays, []
    return call(
        functools.partial(loss_kernel, total, proj, down),
        (sds((total, EMB), bf16), sds((16, D), bf16), sds((16, D), f32), sds((16, FF), f32), sds((total, D), bf16)),
        (me, first, *arrays, text, pooled, order, inv_count),
        [pl.BlockSpec(memory_space=pltpu.HBM)] * len(arrays)
        + [whole(text.shape), whole(pooled.shape), whole((total, 128)), whole((16, 128))],
        [whole((total, EMB)), whole((16, D)), whole((16, D)), whole((16, FF)), whole((total, D))],
        scratch=proj.scratch + down.scratch + [pltpu.VMEM((total, D), f32)] + extra,
        flops=6 * total * total * EMB + 2 * total * D * EMB + 32 * D * FF,
        vmem=32,
        prefetch=2,
    )


def weave(ref, value):
    for t in range(value.shape[0] // TR):
        for x, z, y in PIECES:
            row = t * TR + x * 64 + z * 16
            ref[x * 8 + z * 2 + y, pl.ds(t * 16, 16), :] = value[row : row + 16, y * 384 : y * 384 + 384]


def half_block(j, me):
    return (j // 2 + 1 - me[CORE]) % 2 * 2 + j % 2


DM_COLS = 256


def up_back_kernel(images, weight, me_ref, *refs):
    count = len(weight.arrays)
    slope_ref, m_ref, hidden_ref, col_ref, dm_ref, db_ref = refs[count : count + 6]
    w_ref, sems, du_ref = refs[-3:]
    j = pl.program_id(0)
    blocks = FF // D

    @pl.when(j == 0)
    def _():
        weight.start(me_ref, refs[:count], w_ref, sems)

    @pl.when(j < blocks)
    def _():
        cols = pl.ds(pl.multiple_of(half_block(j, me_ref) * D, 128), D)
        total = jnp.zeros((1, D), f32)
        for i in range(images):
            at = pl.ds(i * ROWS, ROWS)
            du = (slope_ref[at, :].astype(f32) * (col_ref[at, 0:1] * hidden_ref[i : i + 1, :])).astype(bf16)
            du_ref[at, cols] = du
            total += column_sum(du.astype(f32))
        db_ref[...] = jnp.broadcast_to(total, db_ref.shape)
        dw = tn(du_ref[:, cols], m_ref[...]).astype(bf16)
        if not weight.pieces:
            refs[count + 6][...] = dw
            return
        send_ref, keep_ref = refs[count + 6 : count + 8]

        @pl.when(j < 2)
        def _():
            weave(send_ref, dw)

        @pl.when(j >= 2)
        def _():
            weave(keep_ref, dw)

    @pl.when(j == blocks)
    def _():
        weight.wait(me_ref, refs[:count], w_ref, sems)

    @pl.when(j >= blocks)
    def _():
        for k in range(D // DM_COLS):

            @pl.when(j == blocks + k)
            def _():
                dm_ref[...] = nn(du_ref[...], w_ref[:, :, k * DM_COLS : (k + 1) * DM_COLS].reshape(FF, DM_COLS))


def up_backward(images, slope, m, weight, hidden, col, me):
    n = images * ROWS
    blocks = FF // D
    steps = D // DM_COLS

    def block(j, me):
        return half_block(jnp.minimum(j, blocks - 1), me)

    def cols(rows):
        return pl.BlockSpec((rows, D), lambda j, me: (0, block(j, me)))

    if weight.pieces:
        shapes = (sds((16, 192, 384), bf16),) * 2
        specs = [
            pl.BlockSpec((16, 96, 384), lambda j, me: (0, jnp.minimum(j, 1), 0)),
            pl.BlockSpec((16, 96, 384), lambda j, me: (0, jnp.clip(j - 2, 0, 1), 0)),
        ]
    else:
        shapes = (sds((FF, D), bf16),)
        specs = [pl.BlockSpec((D, D), lambda j, me: (block(j, me), 0))]
    return call(
        functools.partial(up_back_kernel, images, weight),
        (sds((n, D), f32), sds((8, FF), f32)) + shapes,
        (me, *weight.arrays, slope, m, hidden, col),
        weight.specs + [cols(n), whole((n, D)), cols(16), whole((n, 128))],
        [pl.BlockSpec((n, DM_COLS), lambda j, me: (0, jnp.maximum(j - blocks, 0))), cols(8)] + specs,
        grid=(blocks + steps,),
        vmem=40,
        scratch=weight.scratch + [pltpu.VMEM((n, FF), bf16)],
        flops=4 * n * D * FF,
        prefetch=1,
    )


def middle_back_kernel(images, weight, me_ref, *refs):
    count = len(weight.arrays)
    h_ref, dm_ref, col_ref, spread_ref, o_ref, vec_ref = refs[count : count + 6]
    dh_ref, do_ref, dw_ref, dvec_ref, w_ref, sems, dat_ref = refs[count + 6 :]
    i = pl.program_id(0)

    @pl.when(i == 0)
    def _():
        weight.start(me_ref, refs[:count], w_ref, sems)

    @pl.when(i < images)
    def _():
        hat, inverse = normalized(h_ref[...])
        dm = dm_ref[...]
        part = norm_back(dm, hat, inverse, vec_ref[2:3, :])
        here = spread_ref[pl.ds(i, 1), :]
        dh = col_ref[:, 0:1] * here + part
        dh_ref[...] = dh
        dat = dh.astype(bf16)
        dat_ref[pl.ds(pl.multiple_of(i * ROWS, 16), ROWS), :] = dat
        sums = jnp.concatenate(
            [
                column_sum(dm * hat),
                column_sum(dm),
                column_sum(dat.astype(f32)),
                column_sum(col_ref[:, 0:1]) * here.astype(bf16).astype(f32),
                jnp.zeros((4, D), f32),
            ],
            axis=0,
        )
        accumulate(i, dvec_ref, sums)

    @pl.when(i == images)
    def _():
        dw = tn(dat_ref[...], o_ref[...]).astype(bf16)
        if weight.pieces:
            for half in range(2):
                weave(dw_ref.at[half], dw[half * 384 : half * 384 + 384])
        else:
            dw_ref[...] = dw
        weight.wait(me_ref, refs[:count], w_ref, sems)
        do_ref[...] = nn(dat_ref[...], w_ref[...].reshape(D, D)).astype(bf16)


def middle_backward(images, h, dm, col, spread, o, weight, vec, me):
    n = images * ROWS
    dw_shape = (2, 16, 48, 384) if weight.pieces else (D, D)

    def rows(cols):
        return pl.BlockSpec((ROWS, cols), lambda i, me: (jnp.minimum(i, images - 1), 0))

    return call(
        functools.partial(middle_back_kernel, images, weight),
        (sds((n, D), f32), sds((n, D), bf16), sds(dw_shape, bf16), sds((8, D), f32)),
        (me, *weight.arrays, h, dm, col, spread, o, vec),
        weight.specs + [rows(D), rows(D), rows(128), whole((16, D)), whole((n, D)), whole((16, D))],
        [rows(D), whole((n, D)), whole(dw_shape), whole((8, D))],
        grid=(images + 1,),
        in_hbm=(1 + len(weight.arrays),),
        vmem_in=(2 + len(weight.arrays),) if weight.pieces else (),
        scratch=weight.scratch + [pltpu.VMEM((n, D), bf16)],
        flops=4 * n * D * D,
        prefetch=1,
    )


def attention_again_kernel(qkv_ref, lse_ref, col_ref, p_ref):
    low_half = lax.broadcasted_iota(jnp.int32, (ROWS, 2 * HEAD), 1) < HEAD
    valid = jnp.broadcast_to(col_ref[:, 0:1], (ROWS, ROWS)) > 0.0
    for pair in range(HEADS // 2):
        at = pair * 2 * HEAD
        q = qkv_ref[:, at : at + 2 * HEAD]
        k = qkv_ref[:, D + at : D + at + 2 * HEAD]
        for half in range(2):
            keep = low_half if half == 0 else jnp.logical_not(low_half)
            head = 2 * pair + half
            s = jnp.where(valid, nt(jnp.where(keep, k, jnp.zeros_like(k)), q), masked_score)
            p_ref[0, head] = jnp.exp(s - lse_ref[0, head : head + 1, :]).astype(bf16)


def attention_again(images, qkv, lse, col):
    n = images * ROWS
    return call(
        attention_again_kernel,
        (sds((images, HEADS, ROWS, ROWS), bf16),),
        (qkv, lse, col),
        [rows_at(ROWS, 3 * D), pl.BlockSpec((1, 16, ROWS), lambda i: (i, 0, 0)), rows_at(ROWS, 128)],
        [pl.BlockSpec((1, HEADS, ROWS, ROWS), lambda i: (i, 0, 0, 0))],
        grid=(images,),
        vmem_out=(0,),
        flops=2 * n * ROWS * D,
    )[0]


def attention_back_kernel(qkv_ref, do_ref, p_ref, dqkv_ref, db_ref):
    i = pl.program_id(0)
    low_half = lax.broadcasted_iota(jnp.int32, (ROWS, 2 * HEAD), 1) < HEAD
    for pair in range(HEADS // 2):
        at = pair * 2 * HEAD
        q = qkv_ref[:, at : at + 2 * HEAD]
        k = qkv_ref[:, D + at : D + at + 2 * HEAD]
        v = qkv_ref[:, 2 * D + at : 2 * D + at + 2 * HEAD]
        do = do_ref[:, at : at + 2 * HEAD]
        dv, dk, dq = [], [], []
        for half in range(2):
            keep = low_half if half == 0 else jnp.logical_not(low_half)
            only_k = jnp.where(keep, k, jnp.zeros_like(k))
            only_v = jnp.where(keep, v, jnp.zeros_like(v))
            head = 2 * pair + half
            rounded = p_ref[0, head]
            p = rounded.astype(f32)
            dp = nt(only_v, do)
            share = jnp.sum(p * dp, axis=0, keepdims=True)
            ds = (p * (dp - share)).astype(bf16)
            dv.append(nn(rounded, do))
            dk.append(nn(ds, q))
            dq.append(tn(ds, only_k))
        dqkv_ref[:, at : at + 2 * HEAD] = ((dq[0] + dq[1]) * (HEAD**-0.5)).astype(bf16)
        dqkv_ref[:, D + at : D + at + 2 * HEAD] = jnp.where(low_half, dk[0], dk[1]).astype(bf16)
        dqkv_ref[:, 2 * D + at : 2 * D + at + 2 * HEAD] = jnp.where(low_half, dv[0], dv[1]).astype(bf16)
    accumulate(i, db_ref, nn(jnp.ones((16, ROWS), bf16), dqkv_ref[...]))


def attention_backward(images, qkv, do, p):
    n = images * ROWS
    return call(
        attention_back_kernel,
        (sds((n, 3 * D), bf16), sds((16, 3 * D), f32)),
        (qkv, do, p),
        [
            rows_at(ROWS, 3 * D),
            rows_at(ROWS, D),
            pl.BlockSpec((1, HEADS, ROWS, ROWS), lambda i: (i, 0, 0, 0)),
        ],
        [rows_at(ROWS, 3 * D), whole((16, 3 * D))],
        grid=(images,),
        vmem_in=(2,),
        flops=10 * n * ROWS * D,
    )


def qkv_grad_kernel(dqkv_ref, a_ref, dw_ref):
    dw_ref[...] = tn(dqkv_ref[...], a_ref[...]).astype(bf16)


def qkv_weight_grad(images, dqkv, a):
    n = images * ROWS
    return call(
        qkv_grad_kernel,
        (sds((3 * D, D), bf16),),
        (dqkv, a),
        [cols_at(n, D), whole((n, D))],
        [rows_at(D, D)],
        grid=(3,),
        flops=6 * n * D * D,
    )[0]


def qkv_grad_fast_kernel(_, dqkv_ref, a_ref, out_ref, pieces_ref):
    j = pl.program_id(0)

    @pl.when(j < 3)
    def _():
        weave(pieces_ref, tn(dqkv_ref[...], a_ref[...]).astype(bf16))

    @pl.when(j == 3)
    def _():
        pieces_ref[...] = out_ref[0]


def qkv_weight_grad_fast(images, dqkv, a, dw_out, me, other):
    n = images * ROWS

    def half(me):
        return 1 - me[CORE] if other else me[CORE]

    return call(
        qkv_grad_fast_kernel,
        (sds((16, 192, 384), bf16),),
        (me, dqkv, a, dw_out),
        [
            pl.BlockSpec((n, 384), lambda j, me: (0, half(me) * 3 + jnp.minimum(j, 2))),
            whole((n, D)),
            pl.BlockSpec((1, 16, 48, 384), lambda j, me: (half(me), 0, 0, 0)),
        ],
        [pl.BlockSpec((16, 48, 384), lambda j, me: (0, j, 0))],
        grid=(4,),
        out_hbm=(0,),
        flops=3 * n * D * D,
        prefetch=1,
    )[0]


def input_back_kernel(weight, me_ref, *refs):
    count = len(weight.arrays)
    x_ref, dqkv_ref, dh_ref, vec_ref, two_ref, bias_ref, up_ref, out_ref, dvec_ref, w_ref, sems, sum_ref = refs[count:]
    i = pl.program_id(0)
    weight.load(me_ref, refs[:count], w_ref, sems)
    da = nn(dqkv_ref[...], w_ref[...].reshape(3 * D, D))
    hat, inverse = normalized(x_ref[...].astype(f32))
    out = dh_ref[...] + norm_back(da, hat, inverse, vec_ref[0:1, :])
    out_ref[0] = out[0:PATCHES, :]
    sums = jnp.concatenate([column_sum(da * hat), column_sum(da), jnp.zeros((6, D), f32)], axis=0)
    accumulate(i, sum_ref, sums)

    @pl.when(i == pl.num_programs(0) - 1)
    def _():
        dvec_ref[...] = jnp.zeros_like(dvec_ref)
        dvec_ref[0:2, :] = sum_ref[0:2, :]
        dvec_ref[2:4, :] = two_ref[0:2, :]
        dvec_ref[4:5, :] = bias_ref[0:1, 0:D]
        dvec_ref[5:6, :] = bias_ref[0:1, 2 * D : 3 * D]
        dvec_ref[6:7, :] = two_ref[2:3, :]
        for b in range(FF // D):
            dvec_ref[7 + b : 8 + b, :] = up_ref[0:1, b * D : (b + 1) * D]
        dvec_ref[7 + FF // D : 8 + FF // D, :] = two_ref[3:4, :]


def input_backward(images, x, dqkv, weight, dh, vec, g_two, g_bias, g_bias_up, me):
    n = images * ROWS
    return call(
        functools.partial(input_back_kernel, weight),
        (sds((images, PATCHES, D), f32), sds((16, D), f32)),
        (me, *weight.arrays, x, dqkv, dh, vec, g_two, g_bias, g_bias_up),
        weight.specs
        + [rows_at(ROWS, D), rows_at(ROWS, 3 * D), rows_at(ROWS, D)]
        + [whole(a.shape) for a in (vec, g_two, g_bias, g_bias_up)],
        [pl.BlockSpec((1, PATCHES, D), lambda i, *_: (i, 0, 0)), whole((16, D))],
        grid=(images,),
        scratch=weight.scratch + [pltpu.VMEM((8, D), f32)],
        flops=6 * n * D * D,
        prefetch=1,
    )


SUMMED, DOWN, PROJ, NONE, VEC = 0, 1, 2, 3, 4


def adam_kernel(part_rows, fast, each, kind_ref, row_ref, me_ref, *refs):
    master_ref, first_ref, second_ref, down_ref, proj_ref, vec_ref = refs[:6]
    summed_refs = refs[6:-5]
    new_master_ref, new_first_ref, new_second_ref, grad_ref, woven_ref = refs[-5:]
    wide = FF // D
    for k in range(each):
        slot = pl.program_id(0) * each + k
        kind = kind_ref[slot]

        @pl.when(kind == SUMMED)
        def _():
            if fast:
                for summed_ref, (dz, dy) in zip(summed_refs, CHIPS, strict=True):
                    rows = pl.ds(pl.multiple_of((me_ref[Z] ^ dz) * 16, 16), 16)
                    cols = pl.ds(pl.multiple_of((me_ref[Y] ^ dy) * 384, 128), 384)
                    grad_ref[rows, cols] = summed_ref[k].astype(f32)
            else:
                grad_ref[...] = summed_refs[0][k].astype(f32)

        @pl.when(kind == VEC)
        def _():
            grad_ref[...] = jnp.zeros_like(grad_ref)
            grad_ref[0 : vec_ref.shape[0], :] = vec_ref[...]

        @pl.when(kind == DOWN)
        def _():
            for c in range(D // 128):
                for b in range(wide):
                    lanes = slice(b * D + c * 128, b * D + c * 128 + 128)
                    woven_ref[c, pl.ds(b, part_rows // wide, stride=wide), :] = down_ref[k, 0 : part_rows // wide, lanes]
                grad_ref[:, c * 128 : (c + 1) * 128] = woven_ref[c]

        @pl.when(kind == PROJ)
        def _():
            at = pl.multiple_of(row_ref[slot], part_rows)
            grad_ref[...] = proj_ref[pl.ds(at, part_rows), :]

        @pl.when(kind == NONE)
        def _():
            grad_ref[...] = jnp.zeros_like(grad_ref)

        grad = grad_ref[...]
        master = master_ref[0, k]
        first = beta_one * first_ref[0, k] + (1.0 - beta_one) * grad
        second = beta_two * second_ref[0, k] + (1.0 - beta_two) * grad * grad
        new_first_ref[0, k] = first
        new_second_ref[0, k] = second
        direction = first / (1.0 - beta_one**STEP)
        size = jnp.sqrt(second / (1.0 - beta_two**STEP)) + adam_eps
        new_master_ref[0, k] = master - learn_rate * (direction / size + decay_rate * master)


def adam(kind, row, me, master, first, second, summed, down, proj, vec):
    slots, part_rows = master.shape[1:3]
    each = slots // 2
    block = pl.BlockSpec((1, each, part_rows, D), lambda s, *_: (0, s, 0, 0))
    fast = len(summed) > 1
    return call(
        functools.partial(adam_kernel, part_rows, fast, each),
        (sds(master.shape, f32),) * 3,
        (kind, row, me, master, first, second, down, proj, vec, *summed),
        [
            block,
            block,
            block,
            pl.BlockSpec((each,) + down.shape[1:], lambda s, *_: (s, 0, 0)),
            whole(proj.shape),
            whole(vec.shape),
        ]
        + [pl.BlockSpec((each,) + a.shape[1:], lambda s, *_: (s, 0, 0)) for a in summed],
        [block] * 3,
        grid=(slots // each,),
        scratch=[pltpu.VMEM((part_rows, D), f32), pltpu.VMEM((D // 128, part_rows, 128), f32)],
        flops=20 * slots * part_rows * D,
        in_hbm=(3, 4, 5),
        vmem_in=(6, 7) if fast else (),
        prefetch=3,
    )


def rank_grad_kernel(images, kind_ref, row_ref, *refs):
    dz_ref, pooled_ref, down_ref, proj_ref = refs[-4:]
    held = jnp.concatenate([ref[...].reshape(64, PACK) for ref in refs[:-4]], axis=0)
    row = lax.broadcasted_iota(jnp.int32, (D, 128), 0)
    col = lax.broadcasted_iota(jnp.int32, (D, 128), 1)
    wanted = jnp.full((D, 128), -1, jnp.int32)
    for s in range(8):
        first = jnp.where(kind_ref[s] == DOWN, row_ref[s], -D)
        wanted = jnp.where(col // 16 == s, first + col % 16, wanted)
    mine = nn(held[:, 0:D], jnp.where(row == wanted, 1.0, 0.0).astype(bf16)).astype(bf16)
    shape = (512, 512)
    row = lax.broadcasted_iota(jnp.int32, shape, 0)
    col = lax.broadcasted_iota(jnp.int32, shape, 1)
    first = 0
    for segment in range(3):
        here = (row - col == segment * images) & (row // 16 == col // 16) & (col % 16 < images)
        rank = nn(jnp.where(here, 1.0, 0.0).astype(bf16), mine).astype(bf16)
        part = held[:, D:PACK] if segment == 0 else held
        down_ref[:, :, first : first + part.shape[1]] = tn(rank, part).reshape(8, 16, part.shape[1])
        first += part.shape[1]
    proj_ref[...] = tn(dz_ref[...], pooled_ref[...])


def rank_grads(images, kind, row, arrays, dz, pooled):
    return call(
        functools.partial(rank_grad_kernel, images),
        (sds((8, 16, FF), f32), sds((EMB, D), f32)),
        (kind, row, *arrays, dz, pooled),
        [whole(a.shape) for a in arrays] + [whole(dz.shape), whole(pooled.shape)],
        [whole((8, 16, FF)), whole((EMB, D))],
        vmem_out=(0, 1),
        flops=256 * D * FF,
        prefetch=2,
    )


def slot_place(owner_list, slot_count):
    tile_count = owner_list.shape[0]
    earlier = jnp.tril(jnp.ones((tile_count, tile_count), jnp.int32), -1)
    same_owner = (owner_list[:, None] == owner_list[None, :]).astype(jnp.int32)
    return owner_list * slot_count + jnp.sum(same_owner * earlier, axis=1)


def gather_weights(master, placed):
    n_dp, n_rep = lax.axis_size("dp"), lax.axis_size("rep")
    slots, part_rows = master.shape[1:3]
    gathered = lax.all_gather(master.astype(bf16), AXES, axis=0, tiled=True)
    gathered = gathered.reshape(n_dp, n_rep * slots, part_rows, D)
    return jnp.transpose(jnp.take(gathered, placed, axis=1), (1, 0, 2, 3)).reshape(-1, D)


def scatter_grads(tiles, tile_of_slot, slots, part_rows):
    n_dp, n_rep = lax.axis_size("dp"), lax.axis_size("rep")
    count = tiles.shape[0]
    tiles = jnp.concatenate([tiles, jnp.zeros((1, TR, D), tiles.dtype)], axis=0)
    index = jnp.where(tile_of_slot < count, tile_of_slot, count)
    buffer = jnp.take(tiles, index, axis=0).reshape(n_rep * slots, n_dp, part_rows, D)
    buffer = jnp.transpose(buffer, (1, 0, 2, 3)).reshape(n_dp * n_rep, slots, part_rows, D)
    return lax.psum_scatter(buffer, AXES, scatter_dimension=0, tiled=True)[0]


def pairs(move):
    def number(x, z, y, c):
        return x * 16 + z * 4 + y * 2 + c

    return [(number(x, z, y, c), number(*move(x, z, y, c))) for x, z, y in PIECES for c in range(2)]


SWAP_CORE = pairs(lambda x, z, y, c: (x, z, y, 1 - c))
SWAP_X = pairs(lambda x, z, y, c: (1 - x, z, y, c))
SWAP_Y = pairs(lambda x, z, y, c: (x, z, 1 - y, c))
SWAP_Z = pairs(lambda x, z, y, c: (x, z ^ 1, y, c))
SWAP_ZZ = pairs(lambda x, z, y, c: (x, z ^ 2, y, c))
SWAP_XY = pairs(lambda x, z, y, c: (1 - x, z, 1 - y, c))
ACROSS_Z = [pairs(lambda x, z, y, c, k=k: (x, z ^ k, y, c)) for k in (1, 2, 3)]
CROSS_ONE = pairs(lambda x, z, y, c: (1 - x, z, y, c) if c == 0 else (x, z, 1 - y, c))
CROSS_TWO = pairs(lambda x, z, y, c: (x, z, 1 - y, c) if c == 0 else (1 - x, z, y, c))


def send(value, permutation):
    return lax.ppermute(value, AXES, permutation)


def add_kernel(count, pieces, outputs, _, *refs):
    for p in range(pieces):
        total = refs[p * count][0].astype(f32)
        for k in range(1, count):
            total += refs[p * count + k][0].astype(f32)
        outs = refs[pieces * count :]
        if outputs == 1:
            outs[0][p] = total.astype(outs[0].dtype)
        else:
            outs[p][...] = total.astype(outs[p].dtype)


def add_pieces(sources, me, pieces, steps=1, dtypes=(bf16,), near=()):
    rows = sources[0][0].shape[1]
    each = pieces // steps
    arrays, specs = [], []
    for p in range(each):
        for array, at in sources:
            arrays.append(array)
            specs.append(pl.BlockSpec((1, rows, 384), lambda i, me, p=p, at=at: (at(i * each + p, me), 0, 0)))
    if len(dtypes) == 1:
        shapes = (sds((pieces, rows, 384), dtypes[0]),)
        outs = [pl.BlockSpec((each, rows, 384), lambda i, me: (i, 0, 0))]
    else:
        shapes = tuple(sds((rows, 384), dtype) for dtype in dtypes)
        outs = [whole((rows, 384))] * pieces
    in_hbm = [k + 1 for k in range(len(arrays)) if k % len(sources) not in near]
    results = call(
        functools.partial(add_kernel, len(sources), each, len(dtypes)),
        shapes,
        (me, *arrays),
        specs,
        outs,
        grid=(steps,),
        flops=pieces * rows * D,
        in_hbm=in_hbm,
        prefetch=1,
    )
    return results[0] if len(dtypes) == 1 else results


class PieceSum:
    def __init__(self, other, me):
        self.me = me
        self.one = send(other, SWAP_CORE)

    def first_send(self, i, me):
        return jnp.where(me[CORE] == 0, (1 - me[X]) * 8 + i, i * 2 + 1 - me[Y])

    def kept(self, i, me):
        return jnp.where(me[CORE] == 0, me[X] * 8 + i, i * 2 + me[Y])

    def second_send(self, i, me):
        return jnp.where(me[CORE] == 0, 2 * i + 1 - me[Y], (1 - me[X]) * 4 + i)

    def second_keep(self, i, me):
        return jnp.where(me[CORE] == 0, 2 * i + me[Y], me[X] * 4 + i)

    def cross_one(self):
        parts = [(self.mine, self.first_send), (self.one, self.first_send)]
        self.two = send(add_pieces(parts, self.me, 8, 2, near=(1,)), CROSS_ONE)

    def cross_two(self):
        def own(i, me):
            return self.kept(self.second_send(i, me), me)

        parts = [(self.mine, own), (self.one, own), (self.two, self.second_send)]
        self.part = add_pieces(parts, self.me, 4, near=(2,))
        self.three = send(self.part, CROSS_TWO)

    def partial(self):
        def crossed(i, me):
            return self.second_keep(me[Z] ^ i, me)

        def own(i, me):
            return self.kept(crossed(i, me), me)

        parts = [(self.mine, own), (self.one, own), (self.two, crossed)]
        self.sums = add_pieces(parts, self.me, 4, dtypes=(f32,))

    def cross_z(self):
        parts = [(self.sums, lambda i, me: i), (self.three, lambda i, me: me[Z] ^ i)]
        self.own, *parts = add_pieces(parts, self.me, 4, dtypes=(f32, bf16, bf16, bf16), near=(0, 1))
        self.last = [send(part, move) for part, move in zip(parts, ACROSS_Z, strict=True)]

    def total(self):
        parts = [(part[None], lambda i, me: 0) for part in (self.own, *self.last)]
        return add_pieces(parts, self.me, 1, near=(0, 1, 2, 3))[0]


def place_kernel(index_ref, *refs):
    for k in range(64):
        at = index_ref[k]
        out_ref = refs[4 + k // 8]
        for q in range(4):

            @pl.when((at >= 12 * q) & (at < 12 * q + 12))
            def _():
                out_ref[k % 8] = refs[q][pl.ds(pl.multiple_of((at - 12 * q) * 16, 16), 16), :]

        @pl.when(at >= 48)
        def _():
            out_ref[k % 8] = jnp.zeros((16, 384), bf16)


def return_to_owners(sums, place):
    placed = call(
        place_kernel,
        (sds((8, 16, 384), bf16),) * 8,
        (place, *sums),
        [whole((192, 384))] * 4,
        [whole((8, 16, 384))] * 8,
        prefetch=1,
    )
    return exchange(placed)


def plan_kernel(owner_ref, me_ref, pick_ref, place_ref, kind_ref, row_ref, counts, placed, tile_of):
    x, c = me_ref[X], me_ref[CORE]
    rep = me_ref[Z] * 4 + me_ref[Y] * 2 + c

    @pl.loop(0, 16)
    def _(r):
        counts[r] = 0

    @pl.loop(0, 128)
    def _(k):
        tile_of[k] = 1 << 20

    @pl.loop(0, VEC_TILE + 1)
    def _(t):
        owner = owner_ref[t]
        at = owner * 8 + counts[owner]
        counts[owner] = counts[owner] + 1
        placed[t] = at
        tile_of[at] = t

    def slab(t):
        at = placed[t]
        owner = at // 8
        chip = (owner // 4 ^ me_ref[Z]) * 2 + (owner // 2 % 2 ^ me_ref[Y])
        return jnp.where(owner % 2 == c, 0, 64) + chip * 8 + at % 8

    def fill(first, count, tile):
        @pl.loop(0, count)
        def _(k):
            pick_ref[first + k] = slab(tile + k)

    base = 0
    for tiles, tile in CHUNK_TILES:
        fill(base, tiles, tile + tiles * c)
        base += tiles
    pick_ref[base] = slab(VEC_TILE)

    @pl.loop(0, 64)
    def _(k):
        chip = k // 8
        owner = (chip // 2 ^ me_ref[Z]) * 4 + (chip % 2 ^ me_ref[Y]) * 2 + c
        t = tile_of[owner * 8 + k % 8]
        u = t - QKV_TILES
        v = u - OUT_TILES
        half = jnp.where(t < QKV_TILES, t // 9, jnp.where(u < OUT_TILES, u // 3, v // 12))
        place = jnp.where(t < QKV_TILES, t % 9, jnp.where(u < OUT_TILES, 9 + u % 3, 12 + v % 12))
        place_ref[k] = jnp.where(t < DOWN_FIRST, jnp.where(half == c, place, 24 + place), 48)

    @pl.loop(0, 8)
    def _(k):
        t = tile_of[rep * 8 + k]
        is_down = (t >= DOWN_FIRST) & (t < PROJ_FIRST)
        is_proj = (t >= PROJ_FIRST) & (t < VEC_TILE)
        kind = jnp.where(t < DOWN_FIRST, SUMMED, jnp.where(is_down, DOWN, jnp.where(is_proj, PROJ, NONE)))
        kind_ref[k] = jnp.where((t == VEC_TILE) & (x == 0), VEC, kind)
        row_ref[k] = jnp.where(
            is_down, ((t - DOWN_FIRST) * TR + x * 64) // 4, jnp.where(is_proj, (t - PROJ_FIRST) * TR + x * 64, 0)
        )


def plan(owner_list, me):
    smem = pl.BlockSpec(memory_space=pltpu.SMEM)
    sizes = (sum(tiles for tiles, _ in CHUNK_TILES) + 1, 64, 8, 8)
    return pl.pallas_call(
        plan_kernel,
        out_shape=tuple(sds((size,), jnp.int32) for size in sizes),
        in_specs=[smem, smem],
        out_specs=(smem,) * 4,
        scratch_shapes=[pltpu.SMEM((16,), jnp.int32), pltpu.SMEM((128,), jnp.int32), pltpu.SMEM((128,), jnp.int32)],
    )(owner_list, me)


def prepare_kernel(owner_ref, me_ref, master_ref, *refs):
    out_refs, (lanes_ref, tile_ref) = refs[:8], refs[8:]
    rep = me_ref[Z] * 4 + me_ref[Y] * 2 + me_ref[CORE]
    for s in range(9):
        tile_ref[s] = 0

    def note(t, held):
        here = owner_ref[t] == rep

        @pl.when(here)
        def _():
            tile_ref[held] = t

        return held + jnp.where(here, 1, 0)

    lax.fori_loop(DOWN_FIRST, PROJ_FIRST, note, lax.fori_loop(0, DOWN_FIRST, note, 0))
    for s in range(8):
        down = (tile_ref[s] >= DOWN_FIRST) & (tile_ref[s] < PROJ_FIRST)

        @pl.when(jnp.logical_not(down))
        def _():
            for k, (dz, dy) in enumerate(CHIPS):
                rows = pl.ds(pl.multiple_of((me_ref[Z] ^ dz) * 16, 16), 16)
                cols = pl.ds(pl.multiple_of((me_ref[Y] ^ dy) * 384, 128), 384)
                out_refs[k][s] = master_ref[0, s, rows, cols].astype(bf16)

        @pl.when(down)
        def _():
            for k in range(6):
                lanes_ref[k] = master_ref[0, s, :, 128 * k : 128 * k + 128]
            for k, (dz, dy) in enumerate(CHIPS):
                for q in range(3):
                    part = lanes_ref[(me_ref[Y] ^ dy) * 3 + q, pl.ds(me_ref[Z] ^ dz, 16, stride=4), :]
                    out_refs[k][s, :, 128 * q : 128 * q + 128] = part.astype(bf16)


def pick_kernel(index_ref, mine_ref, theirs_ref, text_ref, one_ref, two_ref, three_ref):
    def slab(k, ref, j):
        at = index_ref[k]

        @pl.when(at < 64)
        def _():
            ref[j] = mine_ref[at]

        @pl.when(at >= 64)
        def _():
            ref[j] = theirs_ref[at - 64]

    k = 0
    for (tiles, _), (chunk, first) in zip(CHUNK_TILES, CHUNK_AT, strict=True):
        for j in range(tiles):
            slab(k, (one_ref, two_ref, three_ref)[chunk], first + j)
            k += 1
    slab(k, one_ref, 9)
    text = text_ref[...].astype(f32)
    count = text.shape[0]
    text = (text * lax.rsqrt(jnp.sum(text * text, axis=-1, keepdims=True) + unit_eps)).astype(bf16)
    three_ref[14] = jnp.zeros((16, 384), bf16)
    three_ref[14, 0:count, :] = text[:, 0:384]
    three_ref[14, 8 : 8 + count, 0:128] = text[:, 384:512]


class Spread:
    def __init__(self, block=None):
        if block is not None:
            self.parts = [block] + [send(block, move) for move in ACROSS_Z]

    def cross_one(self, ring=None):
        self.ring = jnp.stack(self.parts) if ring is None else ring
        self.one = send(self.ring, CROSS_ONE)
        self.two = None
        self.near = []

    def cross_two(self):
        if self.two is None:
            self.two = send(self.ring, CROSS_TWO)
        self.both = send(self.one, CROSS_TWO)

    def send_near(self, *which):
        for k in which:
            self.near.append(send(getattr(self, ("ring", "one", "two", "both")[k]), SWAP_CORE))

    def finish(self):
        self.send_near(*range(len(self.near), 4))

    def arrays(self):
        return (self.ring, self.one, self.two, self.both, *self.near)


def meet(*values):
    return lax.optimization_barrier(values)


def sources(me):
    for other in range(2):
        c = me[CORE] if other == 0 else 1 - me[CORE]
        for crossed in range(4):
            one, two = crossed % 2, crossed // 2
            flip_x = jnp.where(c == 0, one, two)
            flip_y = jnp.where(c == 0, two, one)
            yield c, me[X] + flip_x - 2 * me[X] * flip_x, me[Y] + flip_y - 2 * me[Y] * flip_y


def exchange(blocks):
    return [blocks[0]] + [
        send(blocks[k], pairs(lambda x, z, y, c, k=k: (x, z ^ CHIPS[k][0], y ^ CHIPS[k][1], c))) for k in range(1, 8)
    ]


def pick_slabs(master, text_emb, owner_list, me, *others):
    prepared = call(
        prepare_kernel,
        (sds((8, 16, 384), bf16),) * 8,
        (owner_list, me, master),
        [whole(master.shape)],
        [whole((8, 16, 384))] * 8,
        scratch=[pltpu.VMEM((6, 64, 128), f32), pltpu.SMEM((16,), jnp.int32)],
        in_hbm=(2,),
        prefetch=2,
    )
    pick, place, kind, row = plan(owner_list, me)
    *mine, pick = meet(*exchange(prepared), pick)
    mine = jnp.concatenate(mine)
    mine, *others = meet(mine, *others)
    blocks = call(
        pick_kernel,
        tuple(sds((slabs, 16, 384), bf16) for slabs in SLABS),
        (pick, mine, send(mine, SWAP_CORE), text_emb),
        [whole((64, 16, 384)), whole((64, 16, 384)), whole(text_emb.shape)],
        [whole((slabs, 16, 384)) for slabs in SLABS],
        prefetch=1,
    )
    return blocks, (place, kind, row), others


def shards(block_in, tissue, text_emb, text_order, owner_list, master, first_moment, second_moment):
    n_dp = lax.axis_size("dp")
    n_rep = lax.axis_size("rep")
    images = block_in.shape[0]
    slots, part_rows = master.shape[1:3]
    image_total = text_order.shape[0]
    n = images * ROWS
    dp_at, rep_at = lax.axis_index("dp"), lax.axis_index("rep")
    first_image = lax.axis_index(AXES) * images

    x = jnp.pad(block_in, ((0, 0), (0, ROWS - PATCHES), (0, 0))).reshape(n, D)
    valid = jnp.pad((tissue > 0).astype(f32), ((0, 0), (0, ROWS - PATCHES)))
    mask_row = valid[:, None, :]
    col = jnp.broadcast_to(valid.reshape(n, 1), (n, 128))
    numbers = jnp.arange(images, dtype=jnp.int32)
    sel = jnp.where(
        numbers[:, None, None] == jnp.arange(16, dtype=jnp.int32)[None, :, None], valid[:, None, :], 0.0
    ).astype(bf16)
    inv_count = jnp.pad(1.0 / jnp.sum(valid, axis=1), (0, 16 - images))
    inv_count = jnp.broadcast_to(inv_count[:, None], (16, 128))
    order = jnp.broadcast_to(text_order[:, None], (image_total, 128))
    first_image = first_image.astype(jnp.int32)[None]

    fast = (n_dp, n_rep, slots, part_rows) == (2, 16, 8, 64)
    if fast:
        me = jnp.stack([dp_at, rep_at // 4, rep_at // 2 % 2, rep_at % 2]).astype(jnp.int32)
        (block_one, block_two, block_three), (place, kind, row), others = pick_slabs(
            master, text_emb, owner_list, me, x, mask_row, col, sel, inv_count, order, first_image
        )
        x, mask_row, col, sel, inv_count, order, first_image = others
        one = Spread(block_one)
        *one.parts, block_two = meet(*one.parts, block_two)
        one.cross_one()
        one.two = send(one.ring, CROSS_TWO)
        two = Spread(block_two)
        one.ring, one.one, one.two = meet(one.ring, one.one, one.two)
        one.cross_two()
        one.ring, one.one, one.two, *two.parts = meet(one.ring, one.one, one.two, *two.parts)
        one.send_near(0, 1, 2)
        one.both, block_three = meet(one.both, block_three)
        one.finish()
        two.cross_one()
        two.two = send(two.ring, CROSS_TWO)
        three = Spread(block_three)
        w_qkv = Weight(one.arrays(), QKV_TILES)
        a, qkv, vec = qkv_forward(images, x, jnp.zeros((16, D), f32), w_qkv, me)
        qkv, two.ring, two.one, two.two, *three.parts = meet(qkv, two.ring, two.one, two.two, *three.parts)
        two.cross_two()
        two.send_near(0, 1, 2)
        o, lse = attention_forward(images, qkv, mask_row)
        o, two.both, *two.near = meet(o, two.both, *two.near)
        two.finish()
        three.cross_one()
        w_out = Weight(two.arrays(), OUT_TILES)
        h, m = middle_forward(images, x, o, vec, w_out, me)
        h, m, three.ring, three.one = meet(h, m, three.ring, three.one)
        three.cross_two()
        three.send_near(0, 1)
        bias_up = vec[7 : 7 + FF // D].reshape(FF // D, 1, D)
        w_up = Weight(two.arrays(), UP_TILES, 3)
        act, slope = up_forward(images, m, w_up, bias_up, me)
        act, three.two, three.both, *three.near = meet(act, three.two, three.both, *three.near)
        three.finish()
        w_down = Weight(three.arrays(), DOWN_TILES, quarters=True)
        w_proj = Weight(three.arrays(), PROJ_TILES, 12)
        all_text = jnp.zeros((16, 128), bf16)
    else:
        me = jnp.zeros((4,), jnp.int32)
        placed = slot_place(owner_list, slots)
        hits = placed[None, :] == jnp.arange(n_rep * slots, dtype=jnp.int32)[:, None]
        tile_ids = jnp.arange(owner_list.shape[0], dtype=jnp.int32)[None, :]
        tile_of_slot = jnp.where(jnp.any(hits, axis=1), jnp.sum(jnp.where(hits, tile_ids, 0), axis=1), 1 << 20)
        text = text_emb.astype(f32)
        own_text = (text * lax.rsqrt(jnp.sum(text * text, axis=-1, keepdims=True) + unit_eps)).astype(bf16)
        all_text = lax.all_gather(own_text, AXES, axis=0, tiled=True)
        tiles = gather_weights(master, placed).reshape(-1, TR, D)
        w_qkv = Weight([tiles[:QKV_TILES]], QKV_TILES)
        w_out = Weight([tiles[QKV_TILES : QKV_TILES + OUT_TILES]], OUT_TILES)
        w_up = Weight([tiles[QKV_TILES + OUT_TILES : DOWN_FIRST]], UP_TILES)
        w_down = Weight([tiles[DOWN_FIRST:PROJ_FIRST].reshape(DOWN_TILES, TR // 4, FF)], DOWN_TILES, quarters=True)
        w_proj = Weight([tiles[PROJ_FIRST:VEC_TILE]], PROJ_TILES)
        a, qkv, vec = qkv_forward(images, x, tiles[VEC_TILE, :16].astype(f32), w_qkv, me)
        bias_up = vec[7 : 7 + FF // D].reshape(FF // D, 1, D)
        o, lse = attention_forward(images, qkv, mask_row)
        h, m = middle_forward(images, x, o, vec, w_out, me)
        act, slope = up_forward(images, m, w_up, bias_up, me)
    block_out, pooled = down_forward(images, act, w_down, h, vec, sel, inv_count, me)

    pooled_all = lax.all_to_all(jnp.broadcast_to(pooled[None, :images], (n_dp * n_rep, images, D)), AXES, 0, 0)
    act_sum = act_sums(images, act, sel)
    probabilities = attention_again(images, qkv, lse, col)
    if fast:
        pooled_all, act_sum, probabilities = meet(pooled_all, act_sum, probabilities)
    dz_all, rank, spread, hidden, pooled_all = loss_backward(
        me, first_image, pooled_all, all_text, order, w_proj, w_down, inv_count
    )

    both = jnp.concatenate([rank[:images], act_sum[:images]], axis=1)
    if fast:
        packed = jnp.concatenate([both[:, at * PACK : (at + 1) * PACK] for at in range(3)], axis=0)
        ranks = Spread()
        packed = jnp.pad(packed, ((0, 16 - 3 * images), (0, 0)))
        beside = send(packed, SWAP_Z)
        dm, g_bias_up, other, mine = up_backward(images, slope, m, w_up, hidden, col, me)
        dm, other, mine, packed, beside = meet(dm, other, mine, packed, beside)
        up_sum = PieceSum(other, me)
        pair = jnp.stack([packed, beside])
        far = send(pair, SWAP_ZZ)
        dh, do, g_out, g_two = middle_backward(images, h, dm, col, spread, o, w_out, vec, me)
        dh, do, up_sum.mine, up_sum.one, pair, far = meet(dh, do, mine, up_sum.one, pair, far)
        up_sum.cross_one()
        dqkv, g_bias = attention_backward(images, qkv, do, probabilities)
        dqkv, up_sum.two, pair, far = meet(dqkv, up_sum.two, pair, far)
        up_sum.cross_two()
        ranks.cross_one(jnp.concatenate([pair, far]))
        dqkv, _ = meet(dqkv, up_sum.part)
        other = qkv_weight_grad_fast(images, dqkv, a, g_out, me, True)
        other, dqkv = meet(other, dqkv)
        qkv_sum = PieceSum(other, me)
        mine = qkv_weight_grad_fast(images, dqkv, a, g_out, me, False)
        up_sum.partial()
        dqkv, up_sum.sums, up_sum.three, qkv_sum.mine, qkv_sum.one, ranks.ring, ranks.one = meet(
            dqkv, up_sum.sums, up_sum.three, mine, qkv_sum.one, ranks.ring, ranks.one
        )
        qkv_sum.cross_one()
        up_sum.cross_z()
        ranks.both = send(ranks.one, CROSS_TWO)
        input_grad, vec_sum = input_backward(images, x, dqkv, w_qkv, dh, vec, g_two, g_bias, g_bias_up, me)
        vec_sum, qkv_sum.two, ranks.ring, ranks.one, ranks.both, *up_sum.last = meet(
            vec_sum, qkv_sum.two, ranks.ring, ranks.one, ranks.both, *up_sum.last
        )
        qkv_sum.cross_two()
        near_vec = send(vec_sum, SWAP_CORE)
        ranks.two = send(ranks.ring, CROSS_TWO)
        ranks.send_near(0, 1)
        up_total = up_sum.total()
        vec_sum, near_vec, up_total = meet(vec_sum, near_vec, up_total)
        vec_sum += near_vec
        vec_sum += send(vec_sum, SWAP_ZZ)
        qkv_sum.partial()
        vec_sum, qkv_sum.sums, qkv_sum.three, up_total, ranks.two, ranks.both, *ranks.near = meet(
            vec_sum, qkv_sum.sums, qkv_sum.three, up_total, ranks.two, ranks.both, *ranks.near
        )
        qkv_sum.cross_z()
        near_up = send(up_total, SWAP_CORE)
        vec_sum += send(vec_sum, SWAP_Y)
        vec_sum += send(vec_sum, SWAP_Z)
        near_up, vec_sum, ranks.two, ranks.both, *qkv_sum.last = meet(
            near_up, vec_sum, ranks.two, ranks.both, *qkv_sum.last
        )
        qkv_total = qkv_sum.total()
        near_qkv = send(qkv_total, SWAP_CORE)
        ranks.finish()
        across = send(vec_sum, SWAP_X)
        near_qkv, across, *ranks.near = meet(near_qkv, across, *ranks.near)
        vec_total = vec_sum + across
        summed = return_to_owners((qkv_total, up_total, near_qkv, near_up), place)
        g_down, g_proj = rank_grads(images, kind, row, ranks.arrays(), dz_all, pooled_all)
        g_down, g_proj, vec_total, *summed = meet(g_down, g_proj, vec_total, *summed)
    else:
        both_all = lax.all_gather(both, AXES, axis=0, tiled=True)
        dm, g_bias_up, g_up = up_backward(images, slope, m, w_up, hidden, col, me)
        dh, do, g_out, g_two = middle_backward(images, h, dm, col, spread, o, w_out, vec, me)
        dqkv, g_bias = attention_backward(images, qkv, do, probabilities)
        g_qkv = qkv_weight_grad(images, dqkv, a)
        input_grad, vec_total = input_backward(images, x, dqkv, w_qkv, dh, vec, g_two, g_bias, g_bias_up, me)
        mine = lax.dynamic_slice_in_dim(tile_of_slot, rep_at * slots, slots)
        first_row = dp_at * part_rows
        is_down = (mine >= DOWN_FIRST) & (mine < PROJ_FIRST)
        is_proj = (mine >= PROJ_FIRST) & (mine < VEC_TILE)
        kind = jnp.where(is_down, DOWN, jnp.where(is_proj, PROJ, jnp.where(mine <= VEC_TILE, SUMMED, NONE)))
        kind = kind.astype(jnp.int32)
        each = part_rows * D // FF
        row = jnp.where(is_proj, (mine - PROJ_FIRST) * TR + first_row, 0)
        down_rows = jnp.clip(((mine - DOWN_FIRST) * TR + first_row) * D // FF, 0, D - each)
        g_down = tn(both_all[:, :D], both_all[:, D:])
        g_down = jnp.stack([lax.dynamic_slice_in_dim(g_down, at, each) for at in down_rows])
        g_down = jnp.pad(g_down, ((0, 0), (0, max(0, 8 - each)), (0, 0)))
        g_proj = tn(dz_all, pooled_all)
        last = jnp.pad(vec_total, ((0, TR - 16), (0, 0))).astype(bf16)
        tiles = jnp.concatenate([g_qkv, g_out, g_up, last], axis=0).reshape(-1, TR, D)
        index = jnp.where(tile_of_slot == VEC_TILE, DOWN_FIRST, jnp.where(tile_of_slot < DOWN_FIRST, tile_of_slot, 1 << 20))
        summed = [scatter_grads(tiles, index, slots, part_rows)]
    new_master, new_first, new_second = adam(
        kind, row, me, master, first_moment, second_moment, summed, g_down, g_proj, vec_total
    )
    return block_out, input_grad, new_master, new_first, new_second


def solution(mesh):
    in_specs = (
        P(("dp", "rep"), None, None),
        P(("dp", "rep"), None),
        P(("dp", "rep"), None),
        P(),
        P(),
        P("rep", None, "dp", None),
        P("rep", None, "dp", None),
        P("rep", None, "dp", None),
    )
    out_specs = (
        P(("dp", "rep"), None, None),
        P(("dp", "rep"), None, None),
        P("rep", None, "dp", None),
        P("rep", None, "dp", None),
        P("rep", None, "dp", None),
    )
    return jax.shard_map(shards, mesh=mesh, in_specs=in_specs, out_specs=out_specs, check_vma=False)
```

```python
import functools

import jax
import jax.numpy as jnp
from jax import lax
from jax.experimental import pallas as pl
from jax.experimental.pallas import tpu as pltpu
from jax.sharding import PartitionSpec as P

D = 768
HEADS = 12
HEAD = 64
FF = 3072
EMB = 512
PATCHES = 196
STEP = 10
ROWS = 208
TR = 128

logit_scale = 50.0
learn_rate = 0.03
beta_one = 0.9
beta_two = 0.999
adam_eps = 1e-08
decay_rate = 0.05
norm_eps = 1e-05
unit_eps = 1e-06
masked_score = -1000000000.0

bf16 = jnp.bfloat16
f32 = jnp.float32
AXES = ("dp", "rep")
MIB = 1 << 20

X, Z, Y, CORE = range(4)
PIECES = [(x, z, y) for x in range(2) for z in range(4) for y in range(2)]

QKV_TILES = 3 * D // TR
OUT_TILES = D // TR
UP_TILES = FF // TR
DOWN_TILES = FF // TR
PROJ_TILES = EMB // TR
DOWN_FIRST = QKV_TILES + OUT_TILES + UP_TILES
PROJ_FIRST = DOWN_FIRST + DOWN_TILES
VEC_TILE = PROJ_FIRST + PROJ_TILES
PACK = (D + FF) // 3
CHUNK_TILES = (
    (QKV_TILES // 2, 0),
    (OUT_TILES // 2, QKV_TILES),
    (UP_TILES // 2, QKV_TILES + OUT_TILES),
    (DOWN_TILES // 2, DOWN_FIRST),
    (PROJ_TILES // 2, PROJ_FIRST),
)
CHUNK_AT = ((0, 0), (1, 0), (1, 3), (2, 0), (2, 12))
SLABS = (10, 15, 15)
CHIPS = [(dz, dy) for dz in range(4) for dy in range(2)]


def nn(a, b):
    return lax.dot_general(a, b, (((1,), (0,)), ((), ())), preferred_element_type=f32)


def nt(a, b):
    return lax.dot_general(a, b, (((1,), (1,)), ((), ())), preferred_element_type=f32)


def tn(a, b):
    return lax.dot_general(a, b, (((0,), (0,)), ((), ())), preferred_element_type=f32)


def call(kernel, outs, ins, in_specs, out_specs, grid=None, scratch=(), flops=0, vmem=24, prefetch=0, in_hbm=(), out_hbm=(), vmem_in=(), vmem_out=()):
    ins = [
        pltpu.with_memory_space_constraint(a, pltpu.HBM) if k >= prefetch and (s.memory_space is pltpu.HBM or k in in_hbm) else a
        for k, (a, s) in enumerate(zip(ins, [None] * prefetch + list(in_specs), strict=True))
    ]
    ins = [pltpu.with_memory_space_constraint(a, pltpu.VMEM) if k in vmem_in else a for k, a in enumerate(ins)]
    moved = sum(a.size * a.dtype.itemsize for a in ins) + sum(o.size * o.dtype.itemsize for o in outs)
    spaces = {k: pltpu.HBM for k in out_hbm} | {k: pltpu.VMEM for k in vmem_out}
    outs = [spaces[k](o.shape, o.dtype) if k in spaces else o for k, o in enumerate(outs)]
    params = pltpu.CompilerParams(
        vmem_limit_bytes=vmem * MIB,
        dimension_semantics=("arbitrary",) * len(grid or ()) or None,
    )
    return pl.pallas_call(
        kernel,
        out_shape=tuple(outs),
        grid_spec=pltpu.PrefetchScalarGridSpec(
            num_scalar_prefetch=prefetch,
            grid=grid or (1,),
            in_specs=in_specs,
            out_specs=tuple(out_specs),
            scratch_shapes=list(scratch),
        ),
        compiler_params=params,
        cost_estimate=pl.CostEstimate(flops=1, bytes_accessed=1, transcendentals=0),
    )(*ins)


def whole(shape):
    return pl.BlockSpec(shape, lambda *_: (0,) * len(shape))


def rows_at(rows, cols):
    return pl.BlockSpec((rows, cols), lambda i, *_: (i, 0))


def cols_at(rows, cols):
    return pl.BlockSpec((rows, cols), lambda i, *_: (0, i))


def sds(shape, dtype):
    return jax.ShapeDtypeStruct(shape, dtype)


class Weight:
    def __init__(self, arrays, tiles, first=0, quarters=False):
        self.arrays, self.tiles, self.first, self.quarters = tuple(arrays), tiles, first, quarters
        self.pieces = len(arrays) > 1
        self.specs = [pl.BlockSpec(memory_space=pltpu.HBM)] * len(arrays)
        shape = (tiles, TR // 4, FF) if quarters else (tiles, TR, D)
        self.scratch = [pltpu.VMEM(shape, bf16), pltpu.SemaphoreType.DMA((32 if self.pieces else 1,))]

    def copies(self, me, refs, out, sems):
        if not self.pieces:
            return [lambda: pltpu.make_async_copy(refs[0], out, sems.at[0])]
        copies = []
        half = self.tiles // 2
        for at, (c, x, y) in enumerate(sources(me)):
            for back in range(4):
                z = me[Z] ^ back
                if self.quarters:
                    row, col = x * 16, z * D + y * 384
                else:
                    row, col = x * 64 + z * 16, y * 384
                rows = pl.ds(pl.multiple_of(row, 16), 16)
                cols = pl.ds(pl.multiple_of(col, 128), 384)
                source = refs[at].at[back, pl.ds(self.first, half)]
                place = out.at[pl.ds(half * c, half), rows, cols]
                copies.append(functools.partial(pltpu.make_async_copy, source, place, sems.at[len(copies)]))
        return copies

    def start(self, me, refs, out, sems):
        for copy in self.copies(me, refs, out, sems):
            copy().start()

    def wait(self, me, refs, out, sems, part=None, parts=1):
        copies = self.copies(me, refs, out, sems)
        if part is not None and not self.pieces:
            copies = copies if part == 0 else []
        elif part is not None:
            copies = copies[16 * part : 16 * part + 16] if parts == 2 else copies[part::4]
        for copy in copies:
            copy().wait()

    def load(self, me, refs, out, sems):
        @pl.when(pl.program_id(0) == 0)
        def _():
            self.start(me, refs, out, sems)
            self.wait(me, refs, out, sems)


def normalized(x):
    center = x - jnp.mean(x, axis=-1, keepdims=True)
    spread = jnp.mean(center * center, axis=-1, keepdims=True)
    inverse = lax.rsqrt(spread + norm_eps)
    return center * inverse, inverse


def norm_back(grad, hat, inverse, gain):
    scaled = grad * gain
    first = jnp.mean(scaled, axis=-1, keepdims=True)
    second = jnp.mean(scaled * hat, axis=-1, keepdims=True)
    return inverse * (scaled - first - hat * second)


def accumulate(i, ref, value):
    @pl.when(i == 0)
    def _():
        ref[...] = value

    @pl.when(i > 0)
    def _():
        ref[...] += value


def column_sum(x):
    return jnp.sum(x, axis=0, keepdims=True)


def third(j, me):
    return jnp.where(me[CORE] == 0, j, 2 - j)


def qkv_kernel(images, weight, me_ref, *refs):
    count = len(weight.arrays)
    pieces = refs[:count]
    x_ref, vec_in_ref, a_ref, qkv_ref, vec_ref, w_ref, sems, vec_half, vec_sems = refs[count:]
    j = pl.program_id(0)

    @pl.when(j == 0)
    def _():
        weight.start(me_ref, pieces, w_ref, sems)
        if weight.pieces:
            parts = []
            for at, (_, x, y) in list(enumerate(sources(me_ref)))[:4]:
                for back in range(4):
                    copy = pltpu.make_async_copy(pieces[at].at[back, 9], vec_half.at[y], vec_sems.at[len(parts)])
                    parts.append(((x == 0) & ((me_ref[Z] ^ back) == 0), copy))
            for here, copy in parts:
                pl.when(here)(copy.start)
            for here, copy in parts:
                pl.when(here)(copy.wait)
            vec_ref[...] = jnp.concatenate([vec_half[0], vec_half[1]], axis=1).astype(f32)
        else:
            vec_ref[...] = vec_in_ref[...]
        for i in range(images):
            hat, _ = normalized(x_ref[pl.ds(i * ROWS, ROWS), :].astype(f32))
            a_ref[pl.ds(i * ROWS, ROWS), :] = (hat * vec_ref[0:1, :] + vec_ref[1:2, :]).astype(bf16)
        weight.wait(me_ref, pieces, w_ref, sems, 0, 2)

    @pl.when(j == 1)
    def _():
        weight.wait(me_ref, pieces, w_ref, sems, 1, 2)

    j = third(j, me_ref)
    bias = jnp.where(j == 0, vec_ref[4:5, :], jnp.where(j == 2, vec_ref[5:6, :], 0.0))
    scale = jnp.where(j == 0, f32(HEAD**-0.5), f32(1.0))
    w = w_ref[pl.ds(6 * j, 6)].reshape(D, D)
    qkv_ref[...] = ((nt(a_ref[...], w) + bias) * scale).astype(bf16)


def qkv_forward(images, x, vec, weight, me):
    n = images * ROWS
    return call(
        functools.partial(qkv_kernel, images, weight),
        (sds((n, D), bf16), sds((n, 3 * D), bf16), sds((16, D), f32)),
        (me, *weight.arrays, x, vec),
        weight.specs + [whole((n, D)), whole((16, D))],
        [whole((n, D)), pl.BlockSpec((n, D), lambda j, me: (0, third(j, me))), whole((16, D))],
        grid=(3,),
        out_hbm=(0,),
        scratch=weight.scratch + [pltpu.VMEM((2, 16, 384), bf16), pltpu.SemaphoreType.DMA((16,))],
        flops=2 * n * D * 3 * D,
        prefetch=1,
    )


def attention_kernel(qkv_ref, mask_ref, o_ref, lse_ref):
    lane = lax.broadcasted_iota(jnp.int32, (ROWS, 2 * HEAD), 1)
    low_half = lane < HEAD
    valid = mask_ref[0] > 0.0
    lse_all = jnp.zeros((ROWS, 128), f32)
    for pair in range(HEADS // 2):
        at = pair * 2 * HEAD
        q = qkv_ref[:, at : at + 2 * HEAD]
        k = qkv_ref[:, D + at : D + at + 2 * HEAD]
        v = qkv_ref[:, 2 * D + at : 2 * D + at + 2 * HEAD]
        mixed = []
        for half in range(2):
            keep = low_half if half == 0 else jnp.logical_not(low_half)
            s = nt(q, jnp.where(keep, k, jnp.zeros_like(k)))
            s = jnp.where(valid, s, masked_score)
            top = jnp.max(s, axis=-1, keepdims=True)
            e = jnp.exp(s - top)
            total = jnp.sum(e, axis=-1, keepdims=True)
            p = e * (1.0 / total)
            mixed.append(nn(p.astype(bf16), v))
            lse_all = jnp.where(lane == 2 * pair + half, top + jnp.log(total), lse_all)
        o_ref[:, at : at + 2 * HEAD] = jnp.where(low_half, mixed[0], mixed[1]).astype(bf16)
    lse_ref[0] = jnp.transpose(lse_all)[0:16, :]


def attention_forward(images, qkv, mask_row):
    n = images * ROWS
    return call(
        attention_kernel,
        (sds((n, D), bf16), sds((images, 16, ROWS), f32)),
        (qkv, mask_row),
        [rows_at(ROWS, 3 * D), pl.BlockSpec((1, 1, ROWS), lambda i: (i, 0, 0))],
        [rows_at(ROWS, D), pl.BlockSpec((1, 16, ROWS), lambda i: (i, 0, 0))],
        grid=(images,),
        flops=4 * n * ROWS * D,
    )


def middle_kernel(weight, me_ref, *refs):
    count = len(weight.arrays)
    x_ref, o_ref, vec_ref, h_ref, m_ref, w_ref, sems = refs[count:]
    weight.load(me_ref, refs[:count], w_ref, sems)
    part = nt(o_ref[...], w_ref[...].reshape(D, D)) + vec_ref[6:7, :]
    middle = x_ref[...].astype(f32) + part
    h_ref[...] = middle
    hat, _ = normalized(middle)
    m_ref[...] = (hat * vec_ref[2:3, :] + vec_ref[3:4, :]).astype(bf16)


def middle_forward(images, x, o, vec, weight, me):
    n = images * ROWS
    return call(
        functools.partial(middle_kernel, weight),
        (sds((n, D), f32), sds((n, D), bf16)),
        (me, *weight.arrays, x, o, vec),
        weight.specs + [rows_at(ROWS, D), rows_at(ROWS, D), whole((16, D))],
        [rows_at(ROWS, D), rows_at(ROWS, D)],
        grid=(images,),
        scratch=weight.scratch,
        flops=2 * n * D * D,
        prefetch=1,
    )


def gelu_parts(u):
    phi = 0.5 + 0.5 * lax.erf(u * 0.7071067811865476)
    density = jnp.exp2(u * u * -0.7213475204444817) * 0.3989422804014327
    return u * phi, phi + u * density


def own_block(j, me):
    return (j // 2 + me[CORE]) % 2 * 2 + j % 2


def up_kernel(images, weight, me_ref, *refs):
    count = len(weight.arrays)
    m_ref, bias_ref, act_ref, slope_ref, w_ref, sems = refs[count:]
    j = pl.program_id(0)

    @pl.when(j == 0)
    def _():
        weight.start(me_ref, refs[:count], w_ref, sems)
        weight.wait(me_ref, refs[:count], w_ref, sems, 0, 2)

    @pl.when(j == 2)
    def _():
        weight.wait(me_ref, refs[:count], w_ref, sems, 1, 2)

    w = w_ref[pl.ds(6 * own_block(j, me_ref), 6)].reshape(D, D)
    for i in range(images):
        at = pl.ds(i * ROWS, ROWS)
        act, slope = gelu_parts(nt(m_ref[at, :], w) + bias_ref[0])
        act_ref[at, :] = act.astype(bf16)
        slope_ref[at, :] = slope.astype(bf16)


def up_forward(images, m, weight, bias, me):
    n = images * ROWS
    cols = pl.BlockSpec((n, D), lambda j, me: (0, own_block(j, me)))
    return call(
        functools.partial(up_kernel, images, weight),
        (sds((n, FF), bf16), sds((n, FF), bf16)),
        (me, *weight.arrays, m, bias),
        weight.specs + [whole((n, D)), pl.BlockSpec((1, 1, D), lambda j, me: (own_block(j, me), 0, 0))],
        [cols, cols],
        grid=(FF // D,),
        vmem_out=(0,),
        out_hbm=(1,),
        scratch=weight.scratch,
        flops=2 * n * D * FF,
        prefetch=1,
    )


def act_sum_kernel(images, act_ref, sel_ref, sum_ref):
    total = jnp.zeros(sum_ref.shape, f32)
    for i in range(images):
        total += nn(sel_ref[i], act_ref[pl.ds(i * ROWS, ROWS), :])
    sum_ref[...] = total.astype(bf16)


def act_sums(images, act, sel):
    n = images * ROWS
    return call(
        functools.partial(act_sum_kernel, images),
        (sds((16, FF), bf16),),
        (act, sel),
        [cols_at(n, D), whole((images, 16, ROWS))],
        [cols_at(16, D)],
        grid=(FF // D,),
        flops=32 * n * FF,
    )[0]


def down_kernel(images, weight, me_ref, *refs):
    count = len(weight.arrays)
    act_ref, h_ref, vec_ref, sel_ref, inv_ref, out_ref, pooled_ref, w_ref, sems = refs[count:]
    j = pl.program_id(0)

    @pl.when(j == 0)
    def _():
        weight.start(me_ref, refs[:count], w_ref, sems)
        weight.wait(me_ref, refs[:count], w_ref, sems, 0, 2)

    @pl.when(j == 1)
    def _():
        weight.wait(me_ref, refs[:count], w_ref, sems, 1, 2)

    tiles = DOWN_TILES // 3
    w = w_ref[pl.ds(tiles * third(j, me_ref), tiles)].reshape(D // 3, FF)
    y = nt(act_ref[...], w)
    total = jnp.zeros((16, D // 3), f32)
    for i in range(images):
        rows = slice(i * ROWS, i * ROWS + ROWS)
        out = (h_ref[rows, :] + (y[rows] + vec_ref[11:12, :])).astype(bf16)
        out_ref[i] = out[0:PATCHES, :]
        total += nn(sel_ref[i], out)
    pooled_ref[...] = (total * inv_ref[:, 0:1]).astype(bf16)


def down_forward(images, act, weight, h, vec, sel, inv_count, me):
    n = images * ROWS

    def cols(rows):
        return pl.BlockSpec((rows, D // 3), lambda j, me: (0, third(j, me)))

    return call(
        functools.partial(down_kernel, images, weight),
        (sds((images, PATCHES, D), bf16), sds((16, D), bf16)),
        (me, *weight.arrays, act, h, vec, sel, inv_count),
        weight.specs[:-1]
        + [
            pl.BlockSpec(memory_space=pl.ANY),
            pl.BlockSpec(memory_space=pltpu.VMEM),
            cols(n),
            cols(16),
            whole((images, 16, ROWS)),
            whole((16, 128)),
        ],
        [pl.BlockSpec((images, PATCHES, D // 3), lambda j, me: (0, 0, third(j, me))), cols(16)],
        grid=(3,),
        vmem_in=(1 + len(weight.arrays),),
        scratch=weight.scratch,
        flops=2 * n * D * FF,
        prefetch=1,
    )


def loss_kernel(total_images, proj, down, me_ref, first_ref, *refs):
    count = len(proj.arrays)
    pieces = refs[:count]
    if proj.pieces:
        down_pieces, rest = pieces, refs[count:]
    else:
        down_pieces, rest = refs[count : count + 1], refs[count + 1 :]
    text_ref, pooled_ref, order_ref, inv_ref, dz_ref, rank_ref, spread_ref, hidden_ref, all_ref = rest[:9]
    proj_ref, proj_sems, down_ref, down_sems, rows_ref = rest[9:14]
    down_copies = down.copies(me_ref, down_pieces, down_ref, down_sems)
    proj_copies = proj.copies(me_ref, pieces, proj_ref, proj_sems)
    if proj.pieces:
        slab_ref, slab_sems = rest[14:]
        for at, (c, x, y) in enumerate(sources(me_ref)):
            for back in range(4):
                device = x * 16 + (me_ref[Z] ^ back) * 4 + y * 2 + c
                out = slab_ref.at[pl.ds(pl.multiple_of(device * 16, 16), 16)]
                source = pieces[at].at[back, 14]
                proj_copies.append(
                    functools.partial(pltpu.make_async_copy, source, out, slab_sems.at[at * 4 + back])
                )
    for copy in proj_copies + down_copies:
        copy().start()
    for copy in proj_copies:
        copy().wait()
    if proj.pieces:
        images = total_images // 32
        shape = (total_images, 512)
        row = lax.broadcasted_iota(jnp.int32, shape, 0)
        col = lax.broadcasted_iota(jnp.int32, shape, 1)
        start = row // images * 16 + row % images
        held = slab_ref[...]
        left = nn(jnp.where(col == start, 1.0, 0.0).astype(bf16), held)
        right = nn(jnp.where(col == start + 8, 1.0, 0.0).astype(bf16), held[:, 0:128])
        text = jnp.concatenate([left, right], axis=1).astype(bf16)
    else:
        text = text_ref[...]
    proj_w = proj_ref[...].reshape(EMB, D)
    each = total_images // pooled_ref.shape[0]
    for d in range(pooled_ref.shape[0]):
        rows_ref[d * each : d * each + each, :] = pooled_ref[d].astype(f32)
    pooled = rows_ref[...].astype(bf16)
    all_ref[...] = pooled
    z = nt(pooled, proj_w)
    square = jnp.sum(z * z, axis=-1, keepdims=True) + unit_eps
    inverse = lax.rsqrt(square)
    image = (z * inverse).astype(bf16)
    s = logit_scale * nt(image, text)
    shape = (total_images, total_images)
    hit = jnp.where(order_ref[:, 0:1] == lax.broadcasted_iota(jnp.int32, shape, 1), 1.0, 0.0)
    part = 1.0 / (2.0 * total_images)

    def grad_of(axis):
        top = jnp.max(s, axis=axis, keepdims=True)
        lse = top + jnp.log(jnp.sum(jnp.exp(s - top), axis=axis, keepdims=True))
        return ((jnp.exp(s - lse) - hit) * part).astype(bf16)

    de = logit_scale * (nn(grad_of(1), text) + nn(grad_of(0), text))
    dz = inverse * de - z * (inverse * inverse * inverse * jnp.sum(z * de, axis=-1, keepdims=True))
    dz = dz.astype(bf16)
    dz_ref[...] = dz
    pick = lax.broadcasted_iota(jnp.int32, (16, total_images), 1) == (
        first_ref[0] + lax.broadcasted_iota(jnp.int32, (16, total_images), 0)
    )
    own = nn(jnp.where(pick, 1.0, 0.0).astype(bf16), dz).astype(bf16)
    spread = nn(own, proj_w) * inv_ref[:, 0:1]
    spread_ref[...] = spread
    rank = spread.astype(bf16)
    rank_ref[...] = rank
    for copy in down_copies:
        copy().wait()
    hidden_ref[...] = nn(rank, down_ref[...].reshape(D, FF))


def loss_backward(me, first, pooled, text, order, proj, down, inv_count):
    total = pooled.shape[0] * pooled.shape[1]
    if proj.pieces:
        arrays, extra = proj.arrays, [pltpu.VMEM((512, 384), bf16), pltpu.SemaphoreType.DMA((32,))]
    else:
        arrays, extra = proj.arrays + down.arrays, []
    return call(
        functools.partial(loss_kernel, total, proj, down),
        (sds((total, EMB), bf16), sds((16, D), bf16), sds((16, D), f32), sds((16, FF), f32), sds((total, D), bf16)),
        (me, first, *arrays, text, pooled, order, inv_count),
        [pl.BlockSpec(memory_space=pltpu.HBM)] * len(arrays)
        + [whole(text.shape), whole(pooled.shape), whole((total, 128)), whole((16, 128))],
        [whole((total, EMB)), whole((16, D)), whole((16, D)), whole((16, FF)), whole((total, D))],
        scratch=proj.scratch + down.scratch + [pltpu.VMEM((total, D), f32)] + extra,
        flops=6 * total * total * EMB + 2 * total * D * EMB + 32 * D * FF,
        vmem=32,
        prefetch=2,
    )


def weave(ref, value):
    for t in range(value.shape[0] // TR):
        for x, z, y in PIECES:
            row = t * TR + x * 64 + z * 16
            ref[x * 8 + z * 2 + y, pl.ds(t * 16, 16), :] = value[row : row + 16, y * 384 : y * 384 + 384]


def half_block(j, me):
    return (j // 2 + 1 - me[CORE]) % 2 * 2 + j % 2


DM_COLS = 256


def up_back_kernel(images, weight, me_ref, *refs):
    count = len(weight.arrays)
    slope_ref, m_ref, hidden_ref, col_ref, dm_ref, db_ref = refs[count : count + 6]
    w_ref, sems, du_ref = refs[-3:]
    j = pl.program_id(0)
    blocks = FF // D

    @pl.when(j == 0)
    def _():
        weight.start(me_ref, refs[:count], w_ref, sems)

    @pl.when(j < blocks)
    def _():
        cols = pl.ds(pl.multiple_of(half_block(j, me_ref) * D, 128), D)
        total = jnp.zeros((1, D), f32)
        for i in range(images):
            at = pl.ds(i * ROWS, ROWS)
            du = (slope_ref[at, :].astype(f32) * (col_ref[at, 0:1] * hidden_ref[i : i + 1, :])).astype(bf16)
            du_ref[at, cols] = du
            total += column_sum(du.astype(f32))
        db_ref[...] = jnp.broadcast_to(total, db_ref.shape)
        dw = tn(du_ref[:, cols], m_ref[...]).astype(bf16)
        if not weight.pieces:
            refs[count + 6][...] = dw
            return
        send_ref, keep_ref = refs[count + 6 : count + 8]

        @pl.when(j < 2)
        def _():
            weave(send_ref, dw)

        @pl.when(j >= 2)
        def _():
            weave(keep_ref, dw)

    @pl.when(j == blocks)
    def _():
        weight.wait(me_ref, refs[:count], w_ref, sems)

    @pl.when(j >= blocks)
    def _():
        for k in range(D // DM_COLS):

            @pl.when(j == blocks + k)
            def _():
                dm_ref[...] = nn(du_ref[...], w_ref[:, :, k * DM_COLS : (k + 1) * DM_COLS].reshape(FF, DM_COLS))


def up_backward(images, slope, m, weight, hidden, col, me):
    n = images * ROWS
    blocks = FF // D
    steps = D // DM_COLS

    def block(j, me):
        return half_block(jnp.minimum(j, blocks - 1), me)

    def cols(rows):
        return pl.BlockSpec((rows, D), lambda j, me: (0, block(j, me)))

    if weight.pieces:
        shapes = (sds((16, 192, 384), bf16),) * 2
        specs = [
            pl.BlockSpec((16, 96, 384), lambda j, me: (0, jnp.minimum(j, 1), 0)),
            pl.BlockSpec((16, 96, 384), lambda j, me: (0, jnp.clip(j - 2, 0, 1), 0)),
        ]
    else:
        shapes = (sds((FF, D), bf16),)
        specs = [pl.BlockSpec((D, D), lambda j, me: (block(j, me), 0))]
    return call(
        functools.partial(up_back_kernel, images, weight),
        (sds((n, D), f32), sds((8, FF), f32)) + shapes,
        (me, *weight.arrays, slope, m, hidden, col),
        weight.specs + [cols(n), whole((n, D)), cols(16), whole((n, 128))],
        [pl.BlockSpec((n, DM_COLS), lambda j, me: (0, jnp.maximum(j - blocks, 0))), cols(8)] + specs,
        grid=(blocks + steps,),
        vmem=34,
        scratch=weight.scratch + [pltpu.VMEM((n, FF), bf16)],
        flops=4 * n * D * FF,
        prefetch=1,
    )


def middle_back_kernel(images, weight, me_ref, *refs):
    count = len(weight.arrays)
    h_ref, dm_ref, col_ref, spread_ref, o_ref, vec_ref = refs[count : count + 6]
    dh_ref, do_ref, dw_ref, dvec_ref, w_ref, sems, dat_ref = refs[count + 6 :]
    i = pl.program_id(0)

    @pl.when(i == 0)
    def _():
        weight.start(me_ref, refs[:count], w_ref, sems)

    @pl.when(i < images)
    def _():
        hat, inverse = normalized(h_ref[...])
        dm = dm_ref[...]
        part = norm_back(dm, hat, inverse, vec_ref[2:3, :])
        here = spread_ref[pl.ds(i, 1), :]
        dh = col_ref[:, 0:1] * here + part
        dh_ref[...] = dh
        dat = dh.astype(bf16)
        dat_ref[pl.ds(pl.multiple_of(i * ROWS, 16), ROWS), :] = dat
        sums = jnp.concatenate(
            [
                column_sum(dm * hat),
                column_sum(dm),
                column_sum(dat.astype(f32)),
                column_sum(col_ref[:, 0:1]) * here.astype(bf16).astype(f32),
                jnp.zeros((4, D), f32),
            ],
            axis=0,
        )
        accumulate(i, dvec_ref, sums)

    @pl.when(i == images)
    def _():
        dw = tn(dat_ref[...], o_ref[...]).astype(bf16)
        if weight.pieces:
            for half in range(2):
                weave(dw_ref.at[half], dw[half * 384 : half * 384 + 384])
        else:
            dw_ref[...] = dw
        weight.wait(me_ref, refs[:count], w_ref, sems)
        do_ref[...] = nn(dat_ref[...], w_ref[...].reshape(D, D)).astype(bf16)


def middle_backward(images, h, dm, col, spread, o, weight, vec, me):
    n = images * ROWS
    dw_shape = (2, 16, 48, 384) if weight.pieces else (D, D)

    def rows(cols):
        return pl.BlockSpec((ROWS, cols), lambda i, me: (jnp.minimum(i, images - 1), 0))

    return call(
        functools.partial(middle_back_kernel, images, weight),
        (sds((n, D), f32), sds((n, D), bf16), sds(dw_shape, bf16), sds((8, D), f32)),
        (me, *weight.arrays, h, dm, col, spread, o, vec),
        weight.specs + [rows(D), rows(D), rows(128), whole((16, D)), whole((n, D)), whole((16, D))],
        [rows(D), whole((n, D)), whole(dw_shape), whole((8, D))],
        grid=(images + 1,),
        in_hbm=(1 + len(weight.arrays),),
        vmem_in=(2 + len(weight.arrays),) if weight.pieces else (),
        scratch=weight.scratch + [pltpu.VMEM((n, D), bf16)],
        flops=4 * n * D * D,
        prefetch=1,
    )


def attention_again_kernel(qkv_ref, lse_ref, col_ref, p_ref):
    low_half = lax.broadcasted_iota(jnp.int32, (ROWS, 2 * HEAD), 1) < HEAD
    valid = jnp.broadcast_to(col_ref[:, 0:1], (ROWS, ROWS)) > 0.0
    for pair in range(HEADS // 2):
        at = pair * 2 * HEAD
        q = qkv_ref[:, at : at + 2 * HEAD]
        k = qkv_ref[:, D + at : D + at + 2 * HEAD]
        for half in range(2):
            keep = low_half if half == 0 else jnp.logical_not(low_half)
            head = 2 * pair + half
            s = jnp.where(valid, nt(jnp.where(keep, k, jnp.zeros_like(k)), q), masked_score)
            p_ref[0, head] = jnp.exp(s - lse_ref[0, head : head + 1, :]).astype(bf16)


def attention_again(images, qkv, lse, col):
    n = images * ROWS
    return call(
        attention_again_kernel,
        (sds((images, HEADS, ROWS, ROWS), bf16),),
        (qkv, lse, col),
        [rows_at(ROWS, 3 * D), pl.BlockSpec((1, 16, ROWS), lambda i: (i, 0, 0)), rows_at(ROWS, 128)],
        [pl.BlockSpec((1, HEADS, ROWS, ROWS), lambda i: (i, 0, 0, 0))],
        grid=(images,),
        vmem_out=(0,),
        flops=2 * n * ROWS * D,
    )[0]


def attention_back_kernel(qkv_ref, do_ref, p_ref, dqkv_ref, db_ref):
    i = pl.program_id(0)
    low_half = lax.broadcasted_iota(jnp.int32, (ROWS, 2 * HEAD), 1) < HEAD
    for pair in range(HEADS // 2):
        at = pair * 2 * HEAD
        q = qkv_ref[:, at : at + 2 * HEAD]
        k = qkv_ref[:, D + at : D + at + 2 * HEAD]
        v = qkv_ref[:, 2 * D + at : 2 * D + at + 2 * HEAD]
        do = do_ref[:, at : at + 2 * HEAD]
        dv, dk, dq = [], [], []
        for half in range(2):
            keep = low_half if half == 0 else jnp.logical_not(low_half)
            only_k = jnp.where(keep, k, jnp.zeros_like(k))
            only_v = jnp.where(keep, v, jnp.zeros_like(v))
            head = 2 * pair + half
            rounded = p_ref[0, head]
            p = rounded.astype(f32)
            dp = nt(only_v, do)
            share = jnp.sum(p * dp, axis=0, keepdims=True)
            ds = (p * (dp - share)).astype(bf16)
            dv.append(nn(rounded, do))
            dk.append(nn(ds, q))
            dq.append(tn(ds, only_k))
        dqkv_ref[:, at : at + 2 * HEAD] = ((dq[0] + dq[1]) * (HEAD**-0.5)).astype(bf16)
        dqkv_ref[:, D + at : D + at + 2 * HEAD] = jnp.where(low_half, dk[0], dk[1]).astype(bf16)
        dqkv_ref[:, 2 * D + at : 2 * D + at + 2 * HEAD] = jnp.where(low_half, dv[0], dv[1]).astype(bf16)
    accumulate(i, db_ref, nn(jnp.ones((16, ROWS), bf16), dqkv_ref[...]))


def attention_backward(images, qkv, do, p):
    n = images * ROWS
    return call(
        attention_back_kernel,
        (sds((n, 3 * D), bf16), sds((16, 3 * D), f32)),
        (qkv, do, p),
        [
            rows_at(ROWS, 3 * D),
            rows_at(ROWS, D),
            pl.BlockSpec((1, HEADS, ROWS, ROWS), lambda i: (i, 0, 0, 0)),
        ],
        [rows_at(ROWS, 3 * D), whole((16, 3 * D))],
        grid=(images,),
        vmem_in=(2,),
        flops=10 * n * ROWS * D,
    )


def qkv_grad_kernel(dqkv_ref, a_ref, dw_ref):
    dw_ref[...] = tn(dqkv_ref[...], a_ref[...]).astype(bf16)


def qkv_weight_grad(images, dqkv, a):
    n = images * ROWS
    return call(
        qkv_grad_kernel,
        (sds((3 * D, D), bf16),),
        (dqkv, a),
        [cols_at(n, D), whole((n, D))],
        [rows_at(D, D)],
        grid=(3,),
        flops=6 * n * D * D,
    )[0]


def qkv_grad_fast_kernel(_, dqkv_ref, a_ref, out_ref, pieces_ref):
    j = pl.program_id(0)

    @pl.when(j < 3)
    def _():
        weave(pieces_ref, tn(dqkv_ref[...], a_ref[...]).astype(bf16))

    @pl.when(j == 3)
    def _():
        pieces_ref[...] = out_ref[0]


def qkv_weight_grad_fast(images, dqkv, a, dw_out, me, other):
    n = images * ROWS

    def half(me):
        return 1 - me[CORE] if other else me[CORE]

    return call(
        qkv_grad_fast_kernel,
        (sds((16, 192, 384), bf16),),
        (me, dqkv, a, dw_out),
        [
            pl.BlockSpec((n, 384), lambda j, me: (0, half(me) * 3 + jnp.minimum(j, 2))),
            whole((n, D)),
            pl.BlockSpec((1, 16, 48, 384), lambda j, me: (half(me), 0, 0, 0)),
        ],
        [pl.BlockSpec((16, 48, 384), lambda j, me: (0, j, 0))],
        grid=(4,),
        out_hbm=(0,),
        flops=3 * n * D * D,
        prefetch=1,
    )[0]


def input_back_kernel(weight, me_ref, *refs):
    count = len(weight.arrays)
    x_ref, dqkv_ref, dh_ref, vec_ref, two_ref, bias_ref, up_ref, out_ref, dvec_ref, w_ref, sems, sum_ref = refs[count:]
    i = pl.program_id(0)
    weight.load(me_ref, refs[:count], w_ref, sems)
    da = nn(dqkv_ref[...], w_ref[...].reshape(3 * D, D))
    hat, inverse = normalized(x_ref[...].astype(f32))
    out = dh_ref[...] + norm_back(da, hat, inverse, vec_ref[0:1, :])
    out_ref[0] = out[0:PATCHES, :]
    sums = jnp.concatenate([column_sum(da * hat), column_sum(da), jnp.zeros((6, D), f32)], axis=0)
    accumulate(i, sum_ref, sums)

    @pl.when(i == pl.num_programs(0) - 1)
    def _():
        dvec_ref[...] = jnp.zeros_like(dvec_ref)
        dvec_ref[0:2, :] = sum_ref[0:2, :]
        dvec_ref[2:4, :] = two_ref[0:2, :]
        dvec_ref[4:5, :] = bias_ref[0:1, 0:D]
        dvec_ref[5:6, :] = bias_ref[0:1, 2 * D : 3 * D]
        dvec_ref[6:7, :] = two_ref[2:3, :]
        for b in range(FF // D):
            dvec_ref[7 + b : 8 + b, :] = up_ref[0:1, b * D : (b + 1) * D]
        dvec_ref[7 + FF // D : 8 + FF // D, :] = two_ref[3:4, :]


def input_backward(images, x, dqkv, weight, dh, vec, g_two, g_bias, g_bias_up, me):
    n = images * ROWS
    return call(
        functools.partial(input_back_kernel, weight),
        (sds((images, PATCHES, D), f32), sds((16, D), f32)),
        (me, *weight.arrays, x, dqkv, dh, vec, g_two, g_bias, g_bias_up),
        weight.specs
        + [rows_at(ROWS, D), rows_at(ROWS, 3 * D), rows_at(ROWS, D)]
        + [whole(a.shape) for a in (vec, g_two, g_bias, g_bias_up)],
        [pl.BlockSpec((1, PATCHES, D), lambda i, *_: (i, 0, 0)), whole((16, D))],
        grid=(images,),
        scratch=weight.scratch + [pltpu.VMEM((8, D), f32)],
        flops=6 * n * D * D,
        prefetch=1,
    )


SUMMED, DOWN, PROJ, NONE, VEC = 0, 1, 2, 3, 4


def adam_kernel(part_rows, fast, each, kind_ref, row_ref, me_ref, *refs):
    master_ref, first_ref, second_ref, down_ref, proj_ref, vec_ref = refs[:6]
    summed_refs = refs[6:-5]
    new_master_ref, new_first_ref, new_second_ref, grad_ref, woven_ref = refs[-5:]
    wide = FF // D
    for k in range(each):
        slot = pl.program_id(0) * each + k
        kind = kind_ref[slot]

        @pl.when(kind == SUMMED)
        def _():
            if fast:
                for summed_ref, (dz, dy) in zip(summed_refs, CHIPS, strict=True):
                    rows = pl.ds(pl.multiple_of((me_ref[Z] ^ dz) * 16, 16), 16)
                    cols = pl.ds(pl.multiple_of((me_ref[Y] ^ dy) * 384, 128), 384)
                    grad_ref[rows, cols] = summed_ref[k].astype(f32)
            else:
                grad_ref[...] = summed_refs[0][k].astype(f32)

        @pl.when(kind == VEC)
        def _():
            grad_ref[...] = jnp.zeros_like(grad_ref)
            grad_ref[0 : vec_ref.shape[0], :] = vec_ref[...]

        @pl.when(kind == DOWN)
        def _():
            for c in range(D // 128):
                for b in range(wide):
                    lanes = slice(b * D + c * 128, b * D + c * 128 + 128)
                    woven_ref[c, pl.ds(b, part_rows // wide, stride=wide), :] = down_ref[k, 0 : part_rows // wide, lanes]
                grad_ref[:, c * 128 : (c + 1) * 128] = woven_ref[c]

        @pl.when(kind == PROJ)
        def _():
            at = pl.multiple_of(row_ref[slot], part_rows)
            grad_ref[...] = proj_ref[pl.ds(at, part_rows), :]

        @pl.when(kind == NONE)
        def _():
            grad_ref[...] = jnp.zeros_like(grad_ref)

        grad = grad_ref[...]
        master = master_ref[0, k]
        first = beta_one * first_ref[0, k] + (1.0 - beta_one) * grad
        second = beta_two * second_ref[0, k] + (1.0 - beta_two) * grad * grad
        new_first_ref[0, k] = first
        new_second_ref[0, k] = second
        direction = first / (1.0 - beta_one**STEP)
        size = jnp.sqrt(second / (1.0 - beta_two**STEP)) + adam_eps
        new_master_ref[0, k] = master - learn_rate * (direction / size + decay_rate * master)


def adam(kind, row, me, master, first, second, summed, down, proj, vec):
    slots, part_rows = master.shape[1:3]
    each = slots // 2
    block = pl.BlockSpec((1, each, part_rows, D), lambda s, *_: (0, s, 0, 0))
    fast = len(summed) > 1
    return call(
        functools.partial(adam_kernel, part_rows, fast, each),
        (sds(master.shape, f32),) * 3,
        (kind, row, me, master, first, second, down, proj, vec, *summed),
        [
            block,
            block,
            block,
            pl.BlockSpec((each,) + down.shape[1:], lambda s, *_: (s, 0, 0)),
            whole(proj.shape),
            whole(vec.shape),
        ]
        + [pl.BlockSpec((each,) + a.shape[1:], lambda s, *_: (s, 0, 0)) for a in summed],
        [block] * 3,
        grid=(slots // each,),
        scratch=[pltpu.VMEM((part_rows, D), f32), pltpu.VMEM((D // 128, part_rows, 128), f32)],
        flops=20 * slots * part_rows * D,
        in_hbm=(3, 4, 5),
        vmem_in=(6, 7) if fast else (),
        prefetch=3,
    )


def rank_grad_kernel(images, kind_ref, row_ref, *refs):
    dz_ref, pooled_ref, down_ref, proj_ref = refs[-4:]
    held = jnp.concatenate([ref[...].reshape(64, PACK) for ref in refs[:-4]], axis=0)
    row = lax.broadcasted_iota(jnp.int32, (D, 128), 0)
    col = lax.broadcasted_iota(jnp.int32, (D, 128), 1)
    wanted = jnp.full((D, 128), -1, jnp.int32)
    for s in range(8):
        first = jnp.where(kind_ref[s] == DOWN, row_ref[s], -D)
        wanted = jnp.where(col // 16 == s, first + col % 16, wanted)
    mine = nn(held[:, 0:D], jnp.where(row == wanted, 1.0, 0.0).astype(bf16)).astype(bf16)
    shape = (512, 512)
    row = lax.broadcasted_iota(jnp.int32, shape, 0)
    col = lax.broadcasted_iota(jnp.int32, shape, 1)
    first = 0
    for segment in range(3):
        here = (row - col == segment * images) & (row // 16 == col // 16) & (col % 16 < images)
        rank = nn(jnp.where(here, 1.0, 0.0).astype(bf16), mine).astype(bf16)
        part = held[:, D:PACK] if segment == 0 else held
        down_ref[:, :, first : first + part.shape[1]] = tn(rank, part).reshape(8, 16, part.shape[1])
        first += part.shape[1]
    proj_ref[...] = tn(dz_ref[...], pooled_ref[...])


def rank_grads(images, kind, row, arrays, dz, pooled):
    return call(
        functools.partial(rank_grad_kernel, images),
        (sds((8, 16, FF), f32), sds((EMB, D), f32)),
        (kind, row, *arrays, dz, pooled),
        [whole(a.shape) for a in arrays] + [whole(dz.shape), whole(pooled.shape)],
        [whole((8, 16, FF)), whole((EMB, D))],
        vmem_out=(0, 1),
        flops=256 * D * FF,
        prefetch=2,
    )


def slot_place(owner_list, slot_count):
    tile_count = owner_list.shape[0]
    earlier = jnp.tril(jnp.ones((tile_count, tile_count), jnp.int32), -1)
    same_owner = (owner_list[:, None] == owner_list[None, :]).astype(jnp.int32)
    return owner_list * slot_count + jnp.sum(same_owner * earlier, axis=1)


def gather_weights(master, placed):
    n_dp, n_rep = lax.axis_size("dp"), lax.axis_size("rep")
    slots, part_rows = master.shape[1:3]
    gathered = lax.all_gather(master.astype(bf16), AXES, axis=0, tiled=True)
    gathered = gathered.reshape(n_dp, n_rep * slots, part_rows, D)
    return jnp.transpose(jnp.take(gathered, placed, axis=1), (1, 0, 2, 3)).reshape(-1, D)


def scatter_grads(tiles, tile_of_slot, slots, part_rows):
    n_dp, n_rep = lax.axis_size("dp"), lax.axis_size("rep")
    count = tiles.shape[0]
    tiles = jnp.concatenate([tiles, jnp.zeros((1, TR, D), tiles.dtype)], axis=0)
    index = jnp.where(tile_of_slot < count, tile_of_slot, count)
    buffer = jnp.take(tiles, index, axis=0).reshape(n_rep * slots, n_dp, part_rows, D)
    buffer = jnp.transpose(buffer, (1, 0, 2, 3)).reshape(n_dp * n_rep, slots, part_rows, D)
    return lax.psum_scatter(buffer, AXES, scatter_dimension=0, tiled=True)[0]


def pairs(move):
    def number(x, z, y, c):
        return x * 16 + z * 4 + y * 2 + c

    return [(number(x, z, y, c), number(*move(x, z, y, c))) for x, z, y in PIECES for c in range(2)]


SWAP_CORE = pairs(lambda x, z, y, c: (x, z, y, 1 - c))
SWAP_X = pairs(lambda x, z, y, c: (1 - x, z, y, c))
SWAP_Y = pairs(lambda x, z, y, c: (x, z, 1 - y, c))
SWAP_Z = pairs(lambda x, z, y, c: (x, z ^ 1, y, c))
SWAP_ZZ = pairs(lambda x, z, y, c: (x, z ^ 2, y, c))
SWAP_XY = pairs(lambda x, z, y, c: (1 - x, z, 1 - y, c))
ACROSS_Z = [pairs(lambda x, z, y, c, k=k: (x, z ^ k, y, c)) for k in (1, 2, 3)]
CROSS_ONE = pairs(lambda x, z, y, c: (1 - x, z, y, c) if c == 0 else (x, z, 1 - y, c))
CROSS_TWO = pairs(lambda x, z, y, c: (x, z, 1 - y, c) if c == 0 else (1 - x, z, y, c))


def send(value, permutation):
    return lax.ppermute(value, AXES, permutation)


def add_kernel(count, pieces, outputs, _, *refs):
    for p in range(pieces):
        total = refs[p * count][0].astype(f32)
        for k in range(1, count):
            total += refs[p * count + k][0].astype(f32)
        outs = refs[pieces * count :]
        if outputs == 1:
            outs[0][p] = total.astype(outs[0].dtype)
        else:
            outs[p][...] = total.astype(outs[p].dtype)


def add_pieces(sources, me, pieces, steps=1, dtypes=(bf16,), near=()):
    rows = sources[0][0].shape[1]
    each = pieces // steps
    arrays, specs = [], []
    for p in range(each):
        for array, at in sources:
            arrays.append(array)
            specs.append(pl.BlockSpec((1, rows, 384), lambda i, me, p=p, at=at: (at(i * each + p, me), 0, 0)))
    if len(dtypes) == 1:
        shapes = (sds((pieces, rows, 384), dtypes[0]),)
        outs = [pl.BlockSpec((each, rows, 384), lambda i, me: (i, 0, 0))]
    else:
        shapes = tuple(sds((rows, 384), dtype) for dtype in dtypes)
        outs = [whole((rows, 384))] * pieces
    in_hbm = [k + 1 for k in range(len(arrays)) if k % len(sources) not in near]
    results = call(
        functools.partial(add_kernel, len(sources), each, len(dtypes)),
        shapes,
        (me, *arrays),
        specs,
        outs,
        grid=(steps,),
        flops=pieces * rows * D,
        in_hbm=in_hbm,
        prefetch=1,
    )
    return results[0] if len(dtypes) == 1 else results


class PieceSum:
    def __init__(self, other, me):
        self.me = me
        self.one = send(other, SWAP_CORE)

    def first_send(self, i, me):
        return jnp.where(me[CORE] == 0, (1 - me[X]) * 8 + i, i * 2 + 1 - me[Y])

    def kept(self, i, me):
        return jnp.where(me[CORE] == 0, me[X] * 8 + i, i * 2 + me[Y])

    def second_send(self, i, me):
        return jnp.where(me[CORE] == 0, 2 * i + 1 - me[Y], (1 - me[X]) * 4 + i)

    def second_keep(self, i, me):
        return jnp.where(me[CORE] == 0, 2 * i + me[Y], me[X] * 4 + i)

    def cross_one(self):
        parts = [(self.mine, self.first_send), (self.one, self.first_send)]
        self.two = send(add_pieces(parts, self.me, 8, 2, near=(1,)), CROSS_ONE)

    def cross_two(self):
        def own(i, me):
            return self.kept(self.second_send(i, me), me)

        parts = [(self.mine, own), (self.one, own), (self.two, self.second_send)]
        self.part = add_pieces(parts, self.me, 4, near=(2,))
        self.three = send(self.part, CROSS_TWO)

    def partial(self):
        def crossed(i, me):
            return self.second_keep(me[Z] ^ i, me)

        def own(i, me):
            return self.kept(crossed(i, me), me)

        parts = [(self.mine, own), (self.one, own), (self.two, crossed)]
        self.sums = add_pieces(parts, self.me, 4, dtypes=(f32,))

    def cross_z(self):
        parts = [(self.sums, lambda i, me: i), (self.three, lambda i, me: me[Z] ^ i)]
        self.own, *parts = add_pieces(parts, self.me, 4, dtypes=(f32, bf16, bf16, bf16), near=(0, 1))
        self.last = [send(part, move) for part, move in zip(parts, ACROSS_Z, strict=True)]

    def total(self):
        parts = [(part[None], lambda i, me: 0) for part in (self.own, *self.last)]
        return add_pieces(parts, self.me, 1, near=(0, 1, 2, 3))[0]


def place_kernel(index_ref, *refs):
    for k in range(64):
        at = index_ref[k]
        out_ref = refs[4 + k // 8]
        for q in range(4):

            @pl.when((at >= 12 * q) & (at < 12 * q + 12))
            def _():
                out_ref[k % 8] = refs[q][pl.ds(pl.multiple_of((at - 12 * q) * 16, 16), 16), :]

        @pl.when(at >= 48)
        def _():
            out_ref[k % 8] = jnp.zeros((16, 384), bf16)


def return_to_owners(sums, place):
    placed = call(
        place_kernel,
        (sds((8, 16, 384), bf16),) * 8,
        (place, *sums),
        [whole((192, 384))] * 4,
        [whole((8, 16, 384))] * 8,
        prefetch=1,
    )
    return exchange(placed)


def plan_kernel(owner_ref, me_ref, pick_ref, place_ref, kind_ref, row_ref, counts, placed, tile_of):
    x, c = me_ref[X], me_ref[CORE]
    rep = me_ref[Z] * 4 + me_ref[Y] * 2 + c

    @pl.loop(0, 16)
    def _(r):
        counts[r] = 0

    @pl.loop(0, 128)
    def _(k):
        tile_of[k] = 1 << 20

    @pl.loop(0, VEC_TILE + 1)
    def _(t):
        owner = owner_ref[t]
        at = owner * 8 + counts[owner]
        counts[owner] = counts[owner] + 1
        placed[t] = at
        tile_of[at] = t

    def slab(t):
        at = placed[t]
        owner = at // 8
        chip = (owner // 4 ^ me_ref[Z]) * 2 + (owner // 2 % 2 ^ me_ref[Y])
        return jnp.where(owner % 2 == c, 0, 64) + chip * 8 + at % 8

    def fill(first, count, tile):
        @pl.loop(0, count)
        def _(k):
            pick_ref[first + k] = slab(tile + k)

    base = 0
    for tiles, tile in CHUNK_TILES:
        fill(base, tiles, tile + tiles * c)
        base += tiles
    pick_ref[base] = slab(VEC_TILE)

    @pl.loop(0, 64)
    def _(k):
        chip = k // 8
        owner = (chip // 2 ^ me_ref[Z]) * 4 + (chip % 2 ^ me_ref[Y]) * 2 + c
        t = tile_of[owner * 8 + k % 8]
        u = t - QKV_TILES
        v = u - OUT_TILES
        half = jnp.where(t < QKV_TILES, t // 9, jnp.where(u < OUT_TILES, u // 3, v // 12))
        place = jnp.where(t < QKV_TILES, t % 9, jnp.where(u < OUT_TILES, 9 + u % 3, 12 + v % 12))
        place_ref[k] = jnp.where(t < DOWN_FIRST, jnp.where(half == c, place, 24 + place), 48)

    @pl.loop(0, 8)
    def _(k):
        t = tile_of[rep * 8 + k]
        is_down = (t >= DOWN_FIRST) & (t < PROJ_FIRST)
        is_proj = (t >= PROJ_FIRST) & (t < VEC_TILE)
        kind = jnp.where(t < DOWN_FIRST, SUMMED, jnp.where(is_down, DOWN, jnp.where(is_proj, PROJ, NONE)))
        kind_ref[k] = jnp.where((t == VEC_TILE) & (x == 0), VEC, kind)
        row_ref[k] = jnp.where(
            is_down, ((t - DOWN_FIRST) * TR + x * 64) // 4, jnp.where(is_proj, (t - PROJ_FIRST) * TR + x * 64, 0)
        )


def plan(owner_list, me):
    smem = pl.BlockSpec(memory_space=pltpu.SMEM)
    sizes = (sum(tiles for tiles, _ in CHUNK_TILES) + 1, 64, 8, 8)
    return pl.pallas_call(
        plan_kernel,
        out_shape=tuple(sds((size,), jnp.int32) for size in sizes),
        in_specs=[smem, smem],
        out_specs=(smem,) * 4,
        scratch_shapes=[pltpu.SMEM((16,), jnp.int32), pltpu.SMEM((128,), jnp.int32), pltpu.SMEM((128,), jnp.int32)],
    )(owner_list, me)


def prepare_kernel(owner_ref, me_ref, master_ref, *refs):
    out_refs, (lanes_ref, tile_ref) = refs[:8], refs[8:]
    rep = me_ref[Z] * 4 + me_ref[Y] * 2 + me_ref[CORE]
    for s in range(9):
        tile_ref[s] = 0

    def note(t, held):
        here = owner_ref[t] == rep

        @pl.when(here)
        def _():
            tile_ref[held] = t

        return held + jnp.where(here, 1, 0)

    lax.fori_loop(DOWN_FIRST, PROJ_FIRST, note, lax.fori_loop(0, DOWN_FIRST, note, 0))
    for s in range(8):
        down = (tile_ref[s] >= DOWN_FIRST) & (tile_ref[s] < PROJ_FIRST)

        @pl.when(jnp.logical_not(down))
        def _():
            for k, (dz, dy) in enumerate(CHIPS):
                rows = pl.ds(pl.multiple_of((me_ref[Z] ^ dz) * 16, 16), 16)
                cols = pl.ds(pl.multiple_of((me_ref[Y] ^ dy) * 384, 128), 384)
                out_refs[k][s] = master_ref[0, s, rows, cols].astype(bf16)

        @pl.when(down)
        def _():
            for k in range(6):
                lanes_ref[k] = master_ref[0, s, :, 128 * k : 128 * k + 128]
            for k, (dz, dy) in enumerate(CHIPS):
                for q in range(3):
                    part = lanes_ref[(me_ref[Y] ^ dy) * 3 + q, pl.ds(me_ref[Z] ^ dz, 16, stride=4), :]
                    out_refs[k][s, :, 128 * q : 128 * q + 128] = part.astype(bf16)


def pick_kernel(index_ref, mine_ref, theirs_ref, text_ref, one_ref, two_ref, three_ref):
    def slab(k, ref, j):
        at = index_ref[k]

        @pl.when(at < 64)
        def _():
            ref[j] = mine_ref[at]

        @pl.when(at >= 64)
        def _():
            ref[j] = theirs_ref[at - 64]

    k = 0
    for (tiles, _), (chunk, first) in zip(CHUNK_TILES, CHUNK_AT, strict=True):
        for j in range(tiles):
            slab(k, (one_ref, two_ref, three_ref)[chunk], first + j)
            k += 1
    slab(k, one_ref, 9)
    text = text_ref[...].astype(f32)
    count = text.shape[0]
    text = (text * lax.rsqrt(jnp.sum(text * text, axis=-1, keepdims=True) + unit_eps)).astype(bf16)
    three_ref[14] = jnp.zeros((16, 384), bf16)
    three_ref[14, 0:count, :] = text[:, 0:384]
    three_ref[14, 8 : 8 + count, 0:128] = text[:, 384:512]


class Spread:
    def __init__(self, block=None):
        if block is not None:
            self.parts = [block] + [send(block, move) for move in ACROSS_Z]

    def cross_one(self, ring=None):
        self.ring = jnp.stack(self.parts) if ring is None else ring
        self.one = send(self.ring, CROSS_ONE)
        self.two = None
        self.near = []

    def cross_two(self):
        if self.two is None:
            self.two = send(self.ring, CROSS_TWO)
        self.both = send(self.one, CROSS_TWO)

    def send_near(self, *which):
        for k in which:
            self.near.append(send(getattr(self, ("ring", "one", "two", "both")[k]), SWAP_CORE))

    def finish(self):
        self.send_near(*range(len(self.near), 4))

    def arrays(self):
        return (self.ring, self.one, self.two, self.both, *self.near)


def meet(*values):
    return lax.optimization_barrier(values)


def sources(me):
    for other in range(2):
        c = me[CORE] if other == 0 else 1 - me[CORE]
        for crossed in range(4):
            one, two = crossed % 2, crossed // 2
            flip_x = jnp.where(c == 0, one, two)
            flip_y = jnp.where(c == 0, two, one)
            yield c, me[X] + flip_x - 2 * me[X] * flip_x, me[Y] + flip_y - 2 * me[Y] * flip_y


def exchange(blocks):
    return [blocks[0]] + [
        send(blocks[k], pairs(lambda x, z, y, c, k=k: (x, z ^ CHIPS[k][0], y ^ CHIPS[k][1], c))) for k in range(1, 8)
    ]


def pick_slabs(master, text_emb, owner_list, me, *others):
    prepared = call(
        prepare_kernel,
        (sds((8, 16, 384), bf16),) * 8,
        (owner_list, me, master),
        [whole(master.shape)],
        [whole((8, 16, 384))] * 8,
        scratch=[pltpu.VMEM((6, 64, 128), f32), pltpu.SMEM((16,), jnp.int32)],
        in_hbm=(2,),
        prefetch=2,
    )
    pick, place, kind, row = plan(owner_list, me)
    *mine, pick = meet(*exchange(prepared), pick)
    mine = jnp.concatenate(mine)
    mine, *others = meet(mine, *others)
    blocks = call(
        pick_kernel,
        tuple(sds((slabs, 16, 384), bf16) for slabs in SLABS),
        (pick, mine, send(mine, SWAP_CORE), text_emb),
        [whole((64, 16, 384)), whole((64, 16, 384)), whole(text_emb.shape)],
        [whole((slabs, 16, 384)) for slabs in SLABS],
        prefetch=1,
    )
    return blocks, (place, kind, row), others


def shards(block_in, tissue, text_emb, text_order, owner_list, master, first_moment, second_moment):
    n_dp = lax.axis_size("dp")
    n_rep = lax.axis_size("rep")
    images = block_in.shape[0]
    slots, part_rows = master.shape[1:3]
    image_total = text_order.shape[0]
    n = images * ROWS
    dp_at, rep_at = lax.axis_index("dp"), lax.axis_index("rep")
    first_image = lax.axis_index(AXES) * images

    x = jnp.pad(block_in, ((0, 0), (0, ROWS - PATCHES), (0, 0))).reshape(n, D)
    valid = jnp.pad((tissue > 0).astype(f32), ((0, 0), (0, ROWS - PATCHES)))
    mask_row = valid[:, None, :]
    col = jnp.broadcast_to(valid.reshape(n, 1), (n, 128))
    numbers = jnp.arange(images, dtype=jnp.int32)
    sel = jnp.where(
        numbers[:, None, None] == jnp.arange(16, dtype=jnp.int32)[None, :, None], valid[:, None, :], 0.0
    ).astype(bf16)
    inv_count = jnp.pad(1.0 / jnp.sum(valid, axis=1), (0, 16 - images))
    inv_count = jnp.broadcast_to(inv_count[:, None], (16, 128))
    order = jnp.broadcast_to(text_order[:, None], (image_total, 128))
    first_image = first_image.astype(jnp.int32)[None]

    fast = (n_dp, n_rep, slots, part_rows) == (2, 16, 8, 64)
    if fast:
        me = jnp.stack([dp_at, rep_at // 4, rep_at // 2 % 2, rep_at % 2]).astype(jnp.int32)
        (block_one, block_two, block_three), (place, kind, row), others = pick_slabs(
            master, text_emb, owner_list, me, x, mask_row, col, sel, inv_count, order, first_image
        )
        x, mask_row, col, sel, inv_count, order, first_image = others
        one = Spread(block_one)
        *one.parts, block_two = meet(*one.parts, block_two)
        one.cross_one()
        one.two = send(one.ring, CROSS_TWO)
        two = Spread(block_two)
        one.ring, one.one, one.two = meet(one.ring, one.one, one.two)
        one.cross_two()
        one.ring, one.one, one.two, *two.parts = meet(one.ring, one.one, one.two, *two.parts)
        one.send_near(0, 1, 2)
        one.both, block_three = meet(one.both, block_three)
        one.finish()
        two.cross_one()
        two.two = send(two.ring, CROSS_TWO)
        three = Spread(block_three)
        w_qkv = Weight(one.arrays(), QKV_TILES)
        a, qkv, vec = qkv_forward(images, x, jnp.zeros((16, D), f32), w_qkv, me)
        qkv, two.ring, two.one, two.two, *three.parts = meet(qkv, two.ring, two.one, two.two, *three.parts)
        two.cross_two()
        two.send_near(0, 1, 2)
        o, lse = attention_forward(images, qkv, mask_row)
        o, two.both, *two.near = meet(o, two.both, *two.near)
        two.finish()
        three.cross_one()
        w_out = Weight(two.arrays(), OUT_TILES)
        h, m = middle_forward(images, x, o, vec, w_out, me)
        h, m, three.ring, three.one = meet(h, m, three.ring, three.one)
        three.cross_two()
        three.send_near(0, 1)
        bias_up = vec[7 : 7 + FF // D].reshape(FF // D, 1, D)
        w_up = Weight(two.arrays(), UP_TILES, 3)
        act, slope = up_forward(images, m, w_up, bias_up, me)
        act, three.two, three.both, *three.near = meet(act, three.two, three.both, *three.near)
        three.finish()
        w_down = Weight(three.arrays(), DOWN_TILES, quarters=True)
        w_proj = Weight(three.arrays(), PROJ_TILES, 12)
        all_text = jnp.zeros((16, 128), bf16)
    else:
        me = jnp.zeros((4,), jnp.int32)
        placed = slot_place(owner_list, slots)
        hits = placed[None, :] == jnp.arange(n_rep * slots, dtype=jnp.int32)[:, None]
        tile_ids = jnp.arange(owner_list.shape[0], dtype=jnp.int32)[None, :]
        tile_of_slot = jnp.where(jnp.any(hits, axis=1), jnp.sum(jnp.where(hits, tile_ids, 0), axis=1), 1 << 20)
        text = text_emb.astype(f32)
        own_text = (text * lax.rsqrt(jnp.sum(text * text, axis=-1, keepdims=True) + unit_eps)).astype(bf16)
        all_text = lax.all_gather(own_text, AXES, axis=0, tiled=True)
        tiles = gather_weights(master, placed).reshape(-1, TR, D)
        w_qkv = Weight([tiles[:QKV_TILES]], QKV_TILES)
        w_out = Weight([tiles[QKV_TILES : QKV_TILES + OUT_TILES]], OUT_TILES)
        w_up = Weight([tiles[QKV_TILES + OUT_TILES : DOWN_FIRST]], UP_TILES)
        w_down = Weight([tiles[DOWN_FIRST:PROJ_FIRST].reshape(DOWN_TILES, TR // 4, FF)], DOWN_TILES, quarters=True)
        w_proj = Weight([tiles[PROJ_FIRST:VEC_TILE]], PROJ_TILES)
        a, qkv, vec = qkv_forward(images, x, tiles[VEC_TILE, :16].astype(f32), w_qkv, me)
        bias_up = vec[7 : 7 + FF // D].reshape(FF // D, 1, D)
        o, lse = attention_forward(images, qkv, mask_row)
        h, m = middle_forward(images, x, o, vec, w_out, me)
        act, slope = up_forward(images, m, w_up, bias_up, me)
    block_out, pooled = down_forward(images, act, w_down, h, vec, sel, inv_count, me)

    pooled_all = lax.all_to_all(jnp.broadcast_to(pooled[None, :images], (n_dp * n_rep, images, D)), AXES, 0, 0)
    act_sum = act_sums(images, act, sel)
    probabilities = attention_again(images, qkv, lse, col)
    if fast:
        pooled_all, act_sum, probabilities = meet(pooled_all, act_sum, probabilities)
    dz_all, rank, spread, hidden, pooled_all = loss_backward(
        me, first_image, pooled_all, all_text, order, w_proj, w_down, inv_count
    )

    both = jnp.concatenate([rank[:images], act_sum[:images]], axis=1)
    if fast:
        packed = jnp.concatenate([both[:, at * PACK : (at + 1) * PACK] for at in range(3)], axis=0)
        ranks = Spread()
        packed = jnp.pad(packed, ((0, 16 - 3 * images), (0, 0)))
        beside = send(packed, SWAP_Z)
        dm, g_bias_up, other, mine = up_backward(images, slope, m, w_up, hidden, col, me)
        dm, other, mine, packed, beside = meet(dm, other, mine, packed, beside)
        up_sum = PieceSum(other, me)
        pair = jnp.stack([packed, beside])
        far = send(pair, SWAP_ZZ)
        dh, do, g_out, g_two = middle_backward(images, h, dm, col, spread, o, w_out, vec, me)
        dh, do, up_sum.mine, up_sum.one, pair, far = meet(dh, do, mine, up_sum.one, pair, far)
        up_sum.cross_one()
        dqkv, g_bias = attention_backward(images, qkv, do, probabilities)
        dqkv, up_sum.two, pair, far = meet(dqkv, up_sum.two, pair, far)
        up_sum.cross_two()
        ranks.cross_one(jnp.concatenate([pair, far]))
        dqkv, _ = meet(dqkv, up_sum.part)
        other = qkv_weight_grad_fast(images, dqkv, a, g_out, me, True)
        other, dqkv = meet(other, dqkv)
        qkv_sum = PieceSum(other, me)
        mine = qkv_weight_grad_fast(images, dqkv, a, g_out, me, False)
        up_sum.partial()
        dqkv, up_sum.sums, up_sum.three, qkv_sum.mine, qkv_sum.one, ranks.ring, ranks.one = meet(
            dqkv, up_sum.sums, up_sum.three, mine, qkv_sum.one, ranks.ring, ranks.one
        )
        qkv_sum.cross_one()
        up_sum.cross_z()
        ranks.both = send(ranks.one, CROSS_TWO)
        input_grad, vec_sum = input_backward(images, x, dqkv, w_qkv, dh, vec, g_two, g_bias, g_bias_up, me)
        vec_sum, qkv_sum.two, ranks.ring, ranks.one, ranks.both, *up_sum.last = meet(
            vec_sum, qkv_sum.two, ranks.ring, ranks.one, ranks.both, *up_sum.last
        )
        qkv_sum.cross_two()
        near_vec = send(vec_sum, SWAP_CORE)
        ranks.two = send(ranks.ring, CROSS_TWO)
        ranks.send_near(0, 1)
        up_total = up_sum.total()
        vec_sum, near_vec, up_total = meet(vec_sum, near_vec, up_total)
        vec_sum += near_vec
        vec_sum += send(vec_sum, SWAP_ZZ)
        qkv_sum.partial()
        vec_sum, qkv_sum.sums, qkv_sum.three, up_total, ranks.two, ranks.both, *ranks.near = meet(
            vec_sum, qkv_sum.sums, qkv_sum.three, up_total, ranks.two, ranks.both, *ranks.near
        )
        qkv_sum.cross_z()
        near_up = send(up_total, SWAP_CORE)
        vec_sum += send(vec_sum, SWAP_Y)
        vec_sum += send(vec_sum, SWAP_Z)
        near_up, vec_sum, ranks.two, ranks.both, *qkv_sum.last = meet(
            near_up, vec_sum, ranks.two, ranks.both, *qkv_sum.last
        )
        qkv_total = qkv_sum.total()
        near_qkv = send(qkv_total, SWAP_CORE)
        ranks.finish()
        across = send(vec_sum, SWAP_X)
        near_qkv, across, *ranks.near = meet(near_qkv, across, *ranks.near)
        vec_total = vec_sum + across
        summed = return_to_owners((qkv_total, up_total, near_qkv, near_up), place)
        g_down, g_proj = rank_grads(images, kind, row, ranks.arrays(), dz_all, pooled_all)
        g_down, g_proj, vec_total, *summed = meet(g_down, g_proj, vec_total, *summed)
    else:
        both_all = lax.all_gather(both, AXES, axis=0, tiled=True)
        dm, g_bias_up, g_up = up_backward(images, slope, m, w_up, hidden, col, me)
        dh, do, g_out, g_two = middle_backward(images, h, dm, col, spread, o, w_out, vec, me)
        dqkv, g_bias = attention_backward(images, qkv, do, probabilities)
        g_qkv = qkv_weight_grad(images, dqkv, a)
        input_grad, vec_total = input_backward(images, x, dqkv, w_qkv, dh, vec, g_two, g_bias, g_bias_up, me)
        mine = lax.dynamic_slice_in_dim(tile_of_slot, rep_at * slots, slots)
        first_row = dp_at * part_rows
        is_down = (mine >= DOWN_FIRST) & (mine < PROJ_FIRST)
        is_proj = (mine >= PROJ_FIRST) & (mine < VEC_TILE)
        kind = jnp.where(is_down, DOWN, jnp.where(is_proj, PROJ, jnp.where(mine <= VEC_TILE, SUMMED, NONE)))
        kind = kind.astype(jnp.int32)
        each = part_rows * D // FF
        row = jnp.where(is_proj, (mine - PROJ_FIRST) * TR + first_row, 0)
        down_rows = jnp.clip(((mine - DOWN_FIRST) * TR + first_row) * D // FF, 0, D - each)
        g_down = tn(both_all[:, :D], both_all[:, D:])
        g_down = jnp.stack([lax.dynamic_slice_in_dim(g_down, at, each) for at in down_rows])
        g_down = jnp.pad(g_down, ((0, 0), (0, max(0, 8 - each)), (0, 0)))
        g_proj = tn(dz_all, pooled_all)
        last = jnp.pad(vec_total, ((0, TR - 16), (0, 0))).astype(bf16)
        tiles = jnp.concatenate([g_qkv, g_out, g_up, last], axis=0).reshape(-1, TR, D)
        index = jnp.where(tile_of_slot == VEC_TILE, DOWN_FIRST, jnp.where(tile_of_slot < DOWN_FIRST, tile_of_slot, 1 << 20))
        summed = [scatter_grads(tiles, index, slots, part_rows)]
    new_master, new_first, new_second = adam(
        kind, row, me, master, first_moment, second_moment, summed, g_down, g_proj, vec_total
    )
    return block_out, input_grad, new_master, new_first, new_second


def solution(mesh):
    in_specs = (
        P(("dp", "rep"), None, None),
        P(("dp", "rep"), None),
        P(("dp", "rep"), None),
        P(),
        P(),
        P("rep", None, "dp", None),
        P("rep", None, "dp", None),
        P("rep", None, "dp", None),
    )
    out_specs = (
        P(("dp", "rep"), None, None),
        P(("dp", "rep"), None, None),
        P("rep", None, "dp", None),
        P("rep", None, "dp", None),
        P("rep", None, "dp", None),
    )
    return jax.shard_map(shards, mesh=mesh, in_specs=in_specs, out_specs=out_specs, check_vma=False)
```
